32 devices in a mesh: dp: 4 (over x, core), seq: 4 (over z), tensor: 2 (over y).
Axes of the slice: x: 2, y: 2, z: 4, core: 2. Of those that a mesh axis runs over, the one named last changes fastest.
Arguments:
- source: bfloat16 [4, 2048, 768], P('dp', 'seq'), may hold values from -6 to 6
- target: bfloat16 [4, 2048, 768], P('dp', 'seq'), may hold values from -6 to 6
- source_segments: int32 [4, 2048], P('dp'), may hold values from 0 to 3, never falling along the last dimension, each value on 1 to 1537 neighbouring positions
- target_segments: int32 [4, 2048], P('dp'), may hold values from 0 to 3, never falling along the last dimension, each value on 1 to 1537 neighbouring positions
- enc_qkv: bfloat16 [3, 768, 768], P(None, None, 'tensor'), may hold values from -0.21875 to 0.21875
- enc_qv_bias: bfloat16 [2, 768], P(None, 'tensor'), may hold values from -3 to 3
- enc_proj: bfloat16 [768, 768], P('tensor'), may hold values from -1.5 to 1.5
- enc_ff_in: bfloat16 [768, 3072], P(None, 'tensor'), may hold values from -0.21875 to 0.21875
- enc_ff_in_bias: bfloat16 [3072], P('tensor'), may hold values from -3 to 3
- enc_ff_out: bfloat16 [3072, 768], P('tensor'), may hold values from -0.109375 to 0.109375
- enc_bias: bfloat16 [2, 768], replicated, may hold values from -2 to 2
- enc_gains: bfloat16 [2, 768], replicated, may hold values from 0.5 to 1.5
- enc_shifts: bfloat16 [2, 768], replicated, may hold values from -2 to 2
- dec_self: bfloat16 [3, 768, 768], P(None, None, 'tensor'), may hold values from -0.21875 to 0.21875
- dec_self_bias: bfloat16 [2, 768], P(None, 'tensor'), may hold values from -3 to 3
- dec_self_proj: bfloat16 [768, 768], P('tensor'), may hold values from -1.5 to 1.5
- dec_cross: bfloat16 [3, 768, 768], P(None, None, 'tensor'), may hold values from -0.21875 to 0.21875
- dec_cross_bias: bfloat16 [2, 768], P(None, 'tensor'), may hold values from -3 to 3
- dec_cross_proj: bfloat16 [768, 768], P('tensor'), may hold values from -1.5 to 1.5
- dec_ff_in: bfloat16 [768, 3072], P(None, 'tensor'), may hold values from -0.21875 to 0.21875
- dec_ff_in_bias: bfloat16 [3072], P('tensor'), may hold values from -3 to 3
- dec_ff_out: bfloat16 [3072, 768], P('tensor'), may hold values from -0.109375 to 0.109375
- dec_bias: bfloat16 [3, 768], replicated, may hold values from -2 to 2
- dec_gains: bfloat16 [3, 768], replicated, may hold values from 0.5 to 1.5
- dec_shifts: bfloat16 [3, 768], replicated, may hold values from -2 to 2
- enc_cotangent: bfloat16 [4, 2048, 768], P('dp', 'seq'), may hold values from -6 to 6
- dec_cotangent: bfloat16 [4, 2048, 768], P('dp', 'seq'), may hold values from -6 to 6
Outputs:
- enc_output: bfloat16 [4, 2048, 768], P('dp', 'seq')
- dec_output: bfloat16 [4, 2048, 768], P('dp', 'seq')
- grad_source: float32 [4, 2048, 768], P('dp', 'seq')
- grad_target: float32 [4, 2048, 768], P('dp', 'seq')
- grad_enc_qkv: float32 [3, 768, 768], P(None, ('dp', 'seq'), 'tensor')
- grad_enc_qv_bias: float32 [2, 768], P(None, 'tensor')
- grad_enc_proj: float32 [768, 768], P('tensor', ('dp', 'seq'))
- grad_enc_ff_in: float32 [768, 3072], P(('dp', 'seq'), 'tensor')
- grad_enc_ff_in_bias: float32 [3072], P('tensor')
- grad_enc_ff_out: float32 [3072, 768], P('tensor', ('dp', 'seq'))
- grad_enc_bias: float32 [2, 768], replicated
- grad_enc_gains: float32 [2, 768], replicated
- grad_enc_shifts: float32 [2, 768], replicated
- grad_dec_self: float32 [3, 768, 768], P(None, ('dp', 'seq'), 'tensor')
- grad_dec_self_bias: float32 [2, 768], P(None, 'tensor')
- grad_dec_self_proj: float32 [768, 768], P('tensor', ('dp', 'seq'))
- grad_dec_cross: float32 [3, 768, 768], P(None, ('dp', 'seq'), 'tensor')
- grad_dec_cross_bias: float32 [2, 768], P(None, 'tensor')
- grad_dec_cross_proj: float32 [768, 768], P('tensor', ('dp', 'seq'))
- grad_dec_ff_in: float32 [768, 3072], P(('dp', 'seq'), 'tensor')
- grad_dec_ff_in_bias: float32 [3072], P('tensor')
- grad_dec_ff_out: float32 [3072, 768], P('tensor', ('dp', 'seq'))
- grad_dec_bias: float32 [3, 768], replicated
- grad_dec_gains: float32 [3, 768], replicated
- grad_dec_shifts: float32 [3, 768], replicated
The draws below stay inside these ranges and needn't reach their ends.
Inputs may be any that keep to these rules, and one draw needn't show every extreme that they name: `source_segments`: each row holds 4 documents in order, each of one position or more; one of them has exactly 1537 positions. `target_segments`: each row holds 4 documents in order, each of one position or more; one of them has exactly 1537 positions.
All inputs are finite; a program needn't handle non-finite values.
Results may differ from the reference program's by a relative error of at most 0.025.
Values may be sent and summed in bfloat16 or wider, within the bound.
A program may use at most 256 MiB of HBM per device.

```python
import math
import jax
import jax.numpy as jnp
import numpy as np
from jax import lax

D = 768
HEAD_DIM = 64
FF = 3072
TOK_DEV = 512
DOCS = 4
HD = 768
LEN = 2048
PAIRS = 4


def with_spikes(values, key, source, target, parts, factor):
    def block_of(axis_at):
        return (jnp.arange(values.shape[axis_at]) // (values.shape[axis_at] // parts)).reshape((-1,) + (1,) * (values.ndim - 1 - axis_at))

    one_side = jax.random.permutation(key, parts)[block_of(target)]
    second = (block_of(target) + parts // 2) % parts
    return jnp.where((block_of(source) == one_side) | (block_of(source) == second), factor * values, values)


def levels(key, dims, pieces, smallest, high):
    level = 1.0
    for position, shards_of in pieces:
        steps = jax.random.uniform(jax.random.fold_in(jax.random.fold_in(key, 6), position), (shards_of,), jnp.float32, smallest / len(pieces), high / len(pieces))
        level = level * jnp.repeat(jnp.exp(steps), dims[position] // shards_of).reshape((-1,) + (1,) * (len(dims) - 1 - position))
    return level


def profile(number_of, total, bound, slope):
    weights = [(1 << 20) // math.isqrt(standing ** slope) + 1 for standing in range(2, number_of + 1)]
    spare, counts = total - bound - (number_of - 1), [1] * (number_of - 1)
    while spare > 0:
        free = [i for i in range(number_of - 1) if counts[i] < bound]
        mass, remaining = sum([weights[i] for i in free]), spare
        for i in free:
            more = min(bound - counts[i], max(1, remaining * weights[i] // mass), spare)
            counts[i] = counts[i] + more
            spare = spare - more
    return np.array([bound] + counts)


def ragged(key, count, total, most, skew):
    if count == 2:
        one = jax.random.randint(key, (), max(1, total - most), min(most, total - 1) + 1)
        return jnp.stack([one, total - one])
    lengths = jnp.asarray(profile(count, total, most, skew), jnp.int32)
    twos = (count - 1) // 2
    giver, taker = lengths[1:1 + 2 * twos:2], lengths[2:2 + 2 * twos:2]
    slack = jnp.minimum(giver - 1, most - taker)
    moved = jax.random.randint(jax.random.fold_in(key, 1), (twos,), 0, 1 << 20) % (slack + 1)
    lengths = lengths.at[1:1 + 2 * twos:2].set(giver - moved).at[2:2 + 2 * twos:2].set(taker + moved)
    return lengths[jax.random.permutation(jax.random.fold_in(key, 2), count)]


def scatter_about(own_key, dims, scale, bound, cuts=(), kind=jnp.bfloat16):
    result = scale * jax.random.normal(own_key, dims, jnp.float32)
    if cuts:
        result = result * levels(own_key, dims, cuts, -0.22, 0.18)
    return jnp.clip(result, -bound, bound).astype(kind)


def gaussian_with(key, dims, width, most, pieces, heavy, kind=jnp.bfloat16):
    values = width * jax.random.normal(key, dims, jnp.float32)
    if pieces:
        values = values * levels(key, dims, pieces, -0.22, 0.18)
    return jnp.clip(with_spikes(values, jax.random.fold_in(key, 3), *heavy), -most, most).astype(kind)


def setup_inputs(seed: int = 0) -> dict:
    key_list = jax.random.split(jax.random.key(seed), 28)
    return {
        "source": scatter_about(key_list[0], (PAIRS, LEN, D), 1.0, 6.0, ((0, 4), (1, 4))),
        "target": scatter_about(key_list[1], (PAIRS, LEN, D), 1.0, 6.0, ((0, 4), (1, 4))),
        "source_segments": jax.vmap(lambda own: jnp.searchsorted(jnp.cumsum(ragged(own, DOCS, LEN, LEN - TOK_DEV + 1, 2)), jnp.arange(LEN), side="right"))(jax.random.split(key_list[2], PAIRS)).reshape((PAIRS, LEN)).astype(jnp.int32),
        "target_segments": jax.vmap(lambda own: jnp.searchsorted(jnp.cumsum(ragged(own, DOCS, LEN, LEN - TOK_DEV + 1, 2)), jnp.arange(LEN), side="right"))(jax.random.split(key_list[3], PAIRS)).reshape((PAIRS, LEN)).astype(jnp.int32),
        "enc_qkv": scatter_about(key_list[4], (3, D, HD), D ** -0.5, 0.21875, ((2, 2),)),
        "enc_qv_bias": scatter_about(key_list[5], (2, HD), 0.5, 3.0, ((1, 2),)),
        "enc_proj": scatter_about(key_list[6], (HD, D), (HEAD_DIM // 4) ** -0.5, 1.5, ((0, 2),)),
        "enc_ff_in": scatter_about(key_list[7], (D, FF), D ** -0.5, 0.21875, ((1, 2),)),
        "enc_ff_in_bias": scatter_about(key_list[8], (FF,), 0.5, 3.0, ((0, 2),)),
        "enc_ff_out": scatter_about(key_list[9], (FF, D), FF ** -0.5, 0.109375, ((0, 2),)),
        "enc_bias": scatter_about(key_list[10], (2, D), 0.3, 2.0),
        "enc_gains": jnp.clip(1.0 + 0.1 * jax.random.normal(key_list[11], (2, D), jnp.float32), 0.5, 1.5).astype(jnp.bfloat16),
        "enc_shifts": scatter_about(key_list[12], (2, D), 0.3, 2.0),
        "dec_self": scatter_about(key_list[13], (3, D, HD), D ** -0.5, 0.21875, ((2, 2),)),
        "dec_self_bias": scatter_about(key_list[14], (2, HD), 0.5, 3.0, ((1, 2),)),
        "dec_self_proj": scatter_about(key_list[15], (HD, D), (HEAD_DIM // 4) ** -0.5, 1.5, ((0, 2),)),
        "dec_cross": scatter_about(key_list[16], (3, D, HD), D ** -0.5, 0.21875, ((2, 2),)),
        "dec_cross_bias": scatter_about(key_list[17], (2, HD), 0.5, 3.0, ((1, 2),)),
        "dec_cross_proj": scatter_about(key_list[18], (HD, D), (HEAD_DIM // 4) ** -0.5, 1.5, ((0, 2),)),
        "dec_ff_in": scatter_about(key_list[19], (D, FF), D ** -0.5, 0.21875, ((1, 2),)),
        "dec_ff_in_bias": scatter_about(key_list[20], (FF,), 0.5, 3.0, ((0, 2),)),
        "dec_ff_out": scatter_about(key_list[21], (FF, D), FF ** -0.5, 0.109375, ((0, 2),)),
        "dec_bias": scatter_about(key_list[22], (3, D), 0.3, 2.0),
        "dec_gains": jnp.clip(1.0 + 0.1 * jax.random.normal(key_list[23], (3, D), jnp.float32), 0.5, 1.5).astype(jnp.bfloat16),
        "dec_shifts": scatter_about(key_list[24], (3, D), 0.3, 2.0),
        "enc_cotangent": gaussian_with(key_list[25], (PAIRS, LEN, D), 1.0, 6.0, ((0, 4), (1, 4)), (1, 2, 4, 2.0)),
        "dec_cotangent": gaussian_with(key_list[26], (PAIRS, LEN, D), 1.0, 6.0, ((0, 4), (1, 4)), (1, 2, 4, 2.0)),
    }


HIGH = lax.Precision.HIGHEST
EPS = 1e-05

@jax.custom_vjp
def low(v):
    return lax.optimization_barrier(v.astype(jnp.bfloat16)).astype(jnp.float32)

@jax.custom_vjp
def low_back(v):
    return v

def low_keep(v):
    return (low(v), None)

def low_pass(kept, grad):
    return (grad,)

def back_keep(v):
    return (v, None)

def back_low(kept, grad):
    return (low(grad),)
low.defvjp(low_keep, low_pass)
low_back.defvjp(back_keep, back_low)

def rounded(v):
    return low_back(low(v))

def dense(left, right):
    return jnp.dot(left, right, precision=HIGH, preferred_element_type=jnp.float32)

def norm(hidden, gain, shift):
    centered = hidden - lax.optimization_barrier(jnp.mean(hidden, axis=-1, keepdims=True))
    spread = lax.optimization_barrier(jnp.mean(centered * centered, axis=-1, keepdims=True))
    return centered * lax.rsqrt(spread + EPS) * gain + shift

@jax.checkpoint
def attention(queries, keys, values, allowed):
    length = queries.shape[0]
    query_heads = queries.reshape(length, -1, HEAD_DIM)
    key_heads = keys.reshape(keys.shape[0], -1, HEAD_DIM)
    value_heads = values.reshape(values.shape[0], -1, HEAD_DIM)
    raw = low_back(jnp.einsum('qhd,khd->hqk', query_heads, key_heads, precision=HIGH))
    scores = jnp.where(allowed[None], raw * HEAD_DIM ** (-0.5), -1e+30)
    probs = jax.nn.softmax(scores, axis=-1)
    mixed = jnp.einsum('hqk,khd->qhd', low(probs), value_heads, precision=HIGH)
    return rounded(mixed.reshape(length, -1))

def attend_block(query_in, key_in, qkv, qv_bias, out_weight, out_bias, allowed):
    queries = rounded(dense(query_in, qkv[0]) + qv_bias[0])
    keys = rounded(dense(key_in, qkv[1]))
    values = rounded(dense(key_in, qkv[2]) + qv_bias[1])
    return low_back(dense(attention(queries, keys, values, allowed), out_weight) + out_bias)

def feed_block(x_in, w_in, b_in, w_out, b_out):
    hidden = low_back(dense(x_in, w_in) + b_in)
    return low_back(dense(low(jax.nn.gelu(hidden, approximate=False)), w_out) + b_out)

def layer_pair(params, source, target, source_seg, target_seg):
    enc_qkv, enc_qv_bias, enc_proj, enc_ff_in, enc_ff_in_bias, enc_ff_out, enc_bias, enc_gains, enc_shifts, dec_self, dec_self_bias, dec_self_proj, dec_cross, dec_cross_bias, dec_cross_proj, dec_ff_in, dec_ff_in_bias, dec_ff_out, dec_bias, dec_gains, dec_shifts = params
    place = jnp.arange(source.shape[0], dtype=jnp.int32)
    same_source = source_seg[:, None] == source_seg[None, :]
    same_target = (target_seg[:, None] == target_seg[None, :]) & (place[None, :] <= place[:, None])
    across = target_seg[:, None] == source_seg[None, :]
    source_in = low(source)
    first = norm(source + attend_block(source_in, source_in, enc_qkv, enc_qv_bias, enc_proj, enc_bias[0], same_source), enc_gains[0], enc_shifts[0])
    encoded = norm(first + feed_block(low(first), enc_ff_in, enc_ff_in_bias, enc_ff_out, enc_bias[1]), enc_gains[1], enc_shifts[1])
    target_in = low(target)
    second = norm(target + attend_block(target_in, target_in, dec_self, dec_self_bias, dec_self_proj, dec_bias[0], same_target), dec_gains[0], dec_shifts[0])
    third = norm(second + attend_block(low(second), low(encoded), dec_cross, dec_cross_bias, dec_cross_proj, dec_bias[1], across), dec_gains[1], dec_shifts[1])
    decoded = norm(third + feed_block(low(third), dec_ff_in, dec_ff_in_bias, dec_ff_out, dec_bias[2]), dec_gains[2], dec_shifts[2])
    return (encoded, decoded)

def reference(source, target, source_segments, target_segments, enc_qkv, enc_qv_bias, enc_proj, enc_ff_in, enc_ff_in_bias, enc_ff_out, enc_bias, enc_gains, enc_shifts, dec_self, dec_self_bias, dec_self_proj, dec_cross, dec_cross_bias, dec_cross_proj, dec_ff_in, dec_ff_in_bias, dec_ff_out, dec_bias, dec_gains, dec_shifts, enc_cotangent, dec_cotangent):
    weights = tuple((item.astype(jnp.float32) for item in (enc_qkv, enc_qv_bias, enc_proj, enc_ff_in, enc_ff_in_bias, enc_ff_out, enc_bias, enc_gains, enc_shifts, dec_self, dec_self_bias, dec_self_proj, dec_cross, dec_cross_bias, dec_cross_proj, dec_ff_in, dec_ff_in_bias, dec_ff_out, dec_bias, dec_gains, dec_shifts)))

    def forward(params, source_rows, target_rows):
        return lax.map(lambda item: layer_pair(params, item[0], item[1], item[2], item[3]), (source_rows, target_rows, source_segments, target_segments))
    outputs, pullback = jax.vjp(forward, weights, source.astype(jnp.float32), target.astype(jnp.float32))
    grads, grad_source, grad_target = pullback((enc_cotangent.astype(jnp.float32), dec_cotangent.astype(jnp.float32)))
    return (outputs[0].astype(jnp.bfloat16), outputs[1].astype(jnp.bfloat16), grad_source, grad_target, grads[0], grads[1], grads[2], grads[3], grads[4], grads[5], grads[6], grads[7], grads[8], grads[9], grads[10], grads[11], grads[12], grads[13], grads[14], grads[15], grads[16], grads[17], grads[18], grads[19], grads[20])
```

```python
import functools

import jax
import jax.numpy as jnp
from jax import lax
from jax.experimental import pallas as pl
from jax.experimental.pallas import tpu as pltpu
from jax.sharding import PartitionSpec as P

HEAD_DIM = 64
EPS = 1e-05
NEG = -1e30
BF16 = jnp.bfloat16
F32 = jnp.float32
NT = (((1,), (1,)), ((), ()))
TN = (((0,), (0,)), ((), ()))
KEY_BLOCK = 512


def dot_plain(left, right):
    return jnp.dot(left, right, preferred_element_type=F32)


def dot_last(left, right):
    return lax.dot_general(left, right, NT, preferred_element_type=F32)


def dot_first(left, right):
    return lax.dot_general(left, right, TN, preferred_element_type=F32)


def column_sum(value):
    return jnp.sum(value.astype(F32), axis=0)


def rounded(value):
    return lax.reduce_precision(value, 8, 7)


def norm_forward(hidden, gain, shift):
    centered = hidden - jnp.mean(hidden, axis=-1, keepdims=True)
    spread = jnp.mean(centered * centered, axis=-1, keepdims=True)
    factor = lax.rsqrt(spread + EPS)
    normed = centered * factor
    return (normed * gain.astype(F32) + shift.astype(F32), (normed, factor))


def norm_backward(grad, saved, gain):
    normed, factor = saved
    scaled = grad * gain.astype(F32)
    centered = scaled - jnp.mean(scaled, axis=-1, keepdims=True)
    grad_hidden = factor * (centered - normed * jnp.mean(scaled * normed, axis=-1, keepdims=True))
    return (grad_hidden, jnp.sum(grad * normed, axis=0), jnp.sum(grad, axis=0))


def head_columns(head):
    return slice(head // 2 * 128, head // 2 * 128 + 128)


def head_rows(head):
    return slice(head * HEAD_DIM, (head + 1) * HEAD_DIM)


def own_lanes(shape, head):
    lanes = lax.broadcasted_iota(jnp.int32, shape, 1)
    return lanes >= HEAD_DIM if head % 2 else lanes < HEAD_DIM


def allowed_in(index, block, base, low_ref, high_ref, count):
    part = block // 2
    place = lax.broadcasted_iota(jnp.int32, (block, count), 0)
    place = place + jnp.where(place < part, base[2 * index], base[2 * index + 1] - part)
    return (place >= low_ref[...]) & (place < high_ref[...])


def over_blocks(flags, length, block, body, skipped):
    @pl.loop(0, length // block)
    def _(index):
        flag = flags[index]
        rows = pl.ds(pl.multiple_of(index * block, block), block)

        @pl.when(flag == 0)
        def _():
            skipped(rows)

        @pl.when(flag == 1)
        def _():
            body(index, rows, True)

        @pl.when(flag == 2)
        def _():
            body(index, rows, False)


def forward_kernel(
    block, flags, base, q_ref, kv_ref, low_ref, high_ref, out_ref, lse_ref, masked_q, acc, top
):
    count, width = q_ref.shape
    heads = width // HEAD_DIM
    for head in range(heads):
        pair = q_ref[:, head_columns(head)]
        masked_q[head] = jnp.where(own_lanes(pair.shape, head), pair, jnp.zeros_like(pair))
    acc[...] = jnp.zeros_like(acc)
    top[...] = jnp.full_like(top, NEG)

    def body(index, rows, partial):
        if partial:
            allowed = allowed_in(index, block, base, low_ref, high_ref, count)
        for head in range(heads):
            cols = head_columns(head)
            scores = lax.dot_general(
                kv_ref[rows, cols], masked_q[head], NT, preferred_element_type=F32
            )
            if partial:
                scores = jnp.where(allowed, scores, NEG)
            old = top[head : head + 1, :]
            new = jnp.maximum(old, jnp.max(scores, axis=0, keepdims=True))
            weights = jnp.exp(scores - new).astype(BF16)
            vals = kv_ref[rows, width + cols.start : width + cols.stop]
            vals = jnp.where(own_lanes(vals.shape, head), vals, jnp.ones_like(vals))
            acc[head] = acc[head] * jnp.exp(old - new) + lax.dot_general(
                vals, weights, TN, preferred_element_type=F32
            )
            top[head : head + 1, :] = new

    over_blocks(flags, kv_ref.shape[0], block, body, lambda rows: None)
    lse_ref[...] = jnp.zeros_like(lse_ref)
    for head in range(heads):
        first = head % 2 * HEAD_DIM
        total = acc[head, HEAD_DIM - first : HEAD_DIM - first + 1, :]
        out_ref[head_rows(head), :] = acc[head, first : first + HEAD_DIM, :] / total
        lse_ref[head : head + 1, :] = top[head : head + 1, :] + jnp.log(total)


def backward_kernel(
    block,
    flags,
    base,
    q_ref,
    kv_ref,
    do_ref,
    dot_ref,
    out_ref,
    lse_ref,
    low_ref,
    high_ref,
    dq_ref,
    dkv_ref,
    masked_q,
    masked_do,
    delta,
    dq,
):
    count, width = q_ref.shape
    heads = width // HEAD_DIM
    for head in range(heads):
        pair = q_ref[:, head_columns(head)]
        keep = own_lanes(pair.shape, head)
        masked_q[head] = jnp.where(keep, pair, jnp.zeros_like(pair))
        pair = do_ref[:, head_columns(head)]
        masked_do[head] = jnp.where(keep, pair, jnp.zeros_like(pair))
        part = head_rows(head)
        delta[head : head + 1, :] = jnp.sum(
            dot_ref[part, :].astype(F32) * out_ref[part, :], axis=0, keepdims=True
        )
    dq[...] = jnp.zeros_like(dq)

    def body(index, rows, partial):
        if partial:
            allowed = allowed_in(index, block, base, low_ref, high_ref, count)
        for pair in range(heads // 2):
            cols = head_columns(2 * pair)
            later = slice(width + cols.start, width + cols.stop)
            keys, vals = kv_ref[rows, cols], kv_ref[rows, later]
            dk = dv = 0.0
            for head in (2 * pair, 2 * pair + 1):
                scores = lax.dot_general(keys, masked_q[head], NT, preferred_element_type=F32)
                probs = jnp.exp(scores - lse_ref[head : head + 1, :])
                if partial:
                    probs = jnp.where(allowed, probs, 0.0)
                dprobs = lax.dot_general(vals, masked_do[head], NT, preferred_element_type=F32)
                draw = (probs * (dprobs - delta[head : head + 1, :])).astype(BF16)
                probs = probs.astype(BF16)
                dv = dv + jnp.dot(probs, masked_do[head], preferred_element_type=F32)
                dk = dk + jnp.dot(draw, masked_q[head], preferred_element_type=F32)
                first = head % 2 * HEAD_DIM
                both = lax.dot_general(keys, draw, TN, preferred_element_type=F32)
                dq[head_rows(head), :] += both[first : first + HEAD_DIM]
            dkv_ref[rows, cols] = dk.astype(BF16)
            dkv_ref[rows, later] = dv.astype(BF16)

    def skipped(rows):
        dkv_ref[rows, :] = jnp.zeros((block, 2 * width), BF16)

    over_blocks(flags, kv_ref.shape[0], block, body, skipped)
    dq_ref[...] = (dq[...] * HEAD_DIM ** (-0.5)).astype(BF16)


SCALARS = pl.BlockSpec(memory_space=pltpu.SMEM)
VECTORS = pl.BlockSpec(memory_space=pltpu.VMEM)


def kernel_call(kernel, inputs, scalars, shapes, scratch, work, limit):
    length, count, width = work
    product = 2 * length * count * width
    return pl.pallas_call(
        kernel,
        out_shape=shapes,
        in_specs=[SCALARS] * scalars + [VECTORS] * (len(inputs) - scalars),
        out_specs=(VECTORS,) * len(shapes),
        scratch_shapes=scratch,
        compiler_params=pltpu.CompilerParams(vmem_limit_bytes=limit),
        cost_estimate=pl.CostEstimate(
            flops=5 * product, bytes_accessed=8 * length * width, transcendentals=0
        ),
    )(*inputs)


def attend(queries, kv, mask):
    count, width = queries.shape
    heads = width // HEAD_DIM
    flags, base, low, high = mask
    return kernel_call(
        functools.partial(forward_kernel, KEY_BLOCK),
        (flags, base, queries, kv, low, high),
        2,
        (jax.ShapeDtypeStruct((width, count), F32), jax.ShapeDtypeStruct((8, count), F32)),
        [
            pltpu.VMEM((heads, count, 128), BF16),
            pltpu.VMEM((heads, 128, count), F32),
            pltpu.VMEM((8, count), F32),
        ],
        (kv.shape[0], count, width),
        40 << 20,
    )


def attend_back(queries, kv, grad_out, grad_out_t, output, lse, mask):
    count, width = queries.shape
    heads = width // HEAD_DIM
    flags, base, low, high = mask
    return kernel_call(
        functools.partial(backward_kernel, KEY_BLOCK),
        (flags, base, queries, kv, grad_out, grad_out_t, output, lse, low, high),
        2,
        (
            jax.ShapeDtypeStruct((width, count), BF16),
            jax.ShapeDtypeStruct(kv.shape, BF16),
        ),
        [
            pltpu.VMEM((heads, count, 128), BF16),
            pltpu.VMEM((heads, count, 128), BF16),
            pltpu.VMEM((8, count), F32),
            pltpu.VMEM((width, count), F32),
        ],
        (kv.shape[0], count, width),
        48 << 20,
    )


class Places:
    def __init__(self, pairs, ring):
        self.pairs, self.ring = pairs, ring
        self.d = lax.axis_index("dp")
        self.x, self.core = self.d // 2, self.d % 2
        self.y, self.z = lax.axis_index("tensor"), lax.axis_index("seq")

    def swap_core(self, value):
        return lax.ppermute(value, "dp", [(i, i ^ 1) for i in range(self.pairs)])

    def swap_y(self, value):
        return lax.ppermute(value, "tensor", [(0, 1), (1, 0)])

    def swap_x(self, value, bit):
        return lax.ppermute(value, "dp", [(i, i ^ (2 << bit)) for i in range(self.pairs)])

    def swap_z(self, value, bit):
        return lax.ppermute(value, "seq", [(i, i ^ (1 << bit)) for i in range(self.ring)])

    def from_z(self, value, step):
        return lax.ppermute(value, "seq", [((i + step) % self.ring, i) for i in range(self.ring)])

    def to_z(self, value, step):
        return lax.ppermute(value, "seq", [(i, (i + step) % self.ring) for i in range(self.ring)])

    def permute(self, value, source_of):
        moves = []
        for d in range(self.pairs):
            for y in range(2):
                source = source_of(d, y)
                if source is not None:
                    moves.append((source[0] * 2 + source[1], d * 2 + y))
        return lax.ppermute(value, ("dp", "tensor"), moves)

    def fetch_weight(self, value):
        return self.permute(value, lambda d, y: (d + 1, y) if d % 2 == 0 else (d - 1, 1 - y))

    def core_sum(self, partial):
        low = rounded(partial)
        return low + self.swap_core(low.astype(BF16)).astype(F32)

    def own_pair(self, rows):
        return jnp.where(self.core == self.y, rows, self.swap_core(rows))

    def hand_out(self, rows):
        other = self.permute(rows, lambda d, y: (d, 1 - y) if d % 2 != y else None)
        return jnp.where(self.core == self.y, rows, other)

    def gather_rows(self, own):
        part = own.shape[0] // 2
        half = lax.dynamic_slice_in_dim(own, self.core * part, part, 0)
        pieces = [own]
        for step in range(1, self.ring):
            mine = self.from_z(half, step)
            pieces += [mine, self.swap_core(mine)]
        return jnp.concatenate(pieces, axis=0)

    def bases(self, count):
        part = count // 2
        places = [self.z * count, self.z * count + part]
        for step in range(1, self.ring):
            shard = (self.z + step) % self.ring * count
            places += [shard + self.core * part, shard + (1 - self.core) * part]
        return jnp.stack(places).astype(jnp.int32)

    def return_rows(self, piece_of, count):
        part = count // 2
        total = None
        for step in list(range(1, self.ring)) + [0]:
            piece = rounded(piece_of(step))
            if step == 0:
                mine = lax.dynamic_slice_in_dim(piece, self.core * part, part, 0)
                others = lax.dynamic_slice_in_dim(piece, (1 - self.core) * part, part, 0)
            else:
                mine, others = piece[:part], piece[part:]
            both = mine + self.swap_core(others.astype(BF16)).astype(F32)
            if step:
                both = self.to_z(both.astype(BF16), step).astype(F32)
            total = both if total is None else total + both
        total = rounded(total)
        other = self.swap_core(total.astype(BF16)).astype(F32)
        return jnp.where(
            self.core == 0,
            jnp.concatenate([total, other]),
            jnp.concatenate([other, total]),
        )

    def scatter(self, grad, x_first):
        rows, columns = grad.shape
        owners = self.pairs // 2
        grad = grad.reshape(owners, 2, self.ring, rows // (self.pairs * self.ring), columns)
        for stage in "xyz" if x_first else "yxz":
            if stage == "y":
                kept = lax.dynamic_index_in_dim(grad, self.core, grad.ndim - 4, False)
                sent = lax.dynamic_index_in_dim(grad, 1 - self.core, grad.ndim - 4, False)
                first = self.permute(
                    sent, lambda d, y: (d + 1, 1 - y) if d % 2 == 0 else (d - 1, y)
                )
                second = self.permute(kept, lambda d, y: (d, 1 - y) if d % 2 else None)
                kept = jnp.where(self.core == 0, kept, second)
                grad = (kept.astype(F32) + first.astype(F32)).astype(BF16)
            else:
                axis = 0 if stage == "x" else grad.ndim - 3
                place, swap = (self.x, self.swap_x) if stage == "x" else (self.z, self.swap_z)
                size, bit = grad.shape[axis], 0
                while size > 1:
                    shape = grad.shape[:axis] + (size // 2, 2) + grad.shape[axis + 1 :]
                    grad = grad.reshape(shape)
                    mine = (place >> bit) & 1
                    kept = lax.dynamic_index_in_dim(grad, mine, axis + 1, False)
                    sent = lax.dynamic_index_in_dim(grad, 1 - mine, axis + 1, False)
                    grad = kept.astype(F32) + swap(sent, bit).astype(F32)
                    size, bit = size // 2, bit + 1
                    if stage == "x" or size > 1:
                        grad = grad.astype(BF16)
                grad = lax.squeeze(grad, (axis,))
        return grad.astype(F32)

    def all_sum(self, whole, halves):
        both = jnp.concatenate([whole, halves])
        for bit in range((self.pairs // 2).bit_length() - 1):
            both = both + self.swap_x(both, bit)
        for bit in range(self.ring.bit_length() - 1):
            both = both + self.swap_z(both, bit)
        whole, halves = both[: whole.shape[0]], both[whole.shape[0] :]
        whole = whole + self.swap_y(whole)
        whole = (whole + self.swap_core(whole)) * 0.5
        first = self.permute(halves, lambda d, y: (d + 1, 1 - y) if d % 2 == 0 else (d - 1, y))
        second = self.swap_y(halves)
        halves = jnp.where(self.core == 0, halves, second) + first
        return whole, halves


def mask_of(query_seg, key_seg, first_row, base, causal, count):
    low = jnp.sum(key_seg[None, :] < query_seg[:, None], axis=1, dtype=jnp.int32)
    high = jnp.sum(key_seg[None, :] <= query_seg[:, None], axis=1, dtype=jnp.int32)
    if causal:
        high = jnp.minimum(high, first_row + jnp.arange(count, dtype=jnp.int32) + 1)
    part = count // 2
    active = (jnp.min(low) < base + part) & (jnp.max(high) > base)
    full = (jnp.max(low) <= base) & (jnp.min(high) >= base + part)
    per = KEY_BLOCK // part
    active = jnp.any(active.reshape(-1, per), axis=1)
    full = jnp.all(full.reshape(-1, per), axis=1)
    flags = active.astype(jnp.int32) + full.astype(jnp.int32)
    return (flags, base, low[None], high[None])


def attention_forward(place, query_in, key_in, weights, out_weight, out_bias, mask):
    w_q, w_kv, b_q, b_kv = weights
    scale = HEAD_DIM ** (-0.5)
    queries = ((dot_plain(query_in, w_q) + b_q).astype(BF16) * scale).astype(BF16)
    kv = (dot_plain(key_in, w_kv) + b_kv).astype(BF16)
    output, lse = attend(queries, kv, mask)
    mixed = output.astype(BF16)
    branch = place.core_sum(dot_first(mixed, out_weight)) + out_bias.astype(F32)
    return (branch, (queries, kv, output, lse, mixed))


def attention_backward(grad_branch, saved, query_in, key_in, weights, out_weight, mask):
    queries, kv, output, lse, mixed = saved
    w_q, w_kv = weights[:2]
    count, width = queries.shape
    grad_mixed = dot_last(grad_branch, out_weight).astype(BF16)
    grad_mixed_t = dot_last(out_weight, grad_branch).astype(BF16)
    grad_q, grad_kv = attend_back(queries, kv, grad_mixed, grad_mixed_t, output, lse, mask)
    grad_query_in = dot_general_q(grad_q, w_q)

    def grad_key_in(step):
        return dot_last(grad_kv[step * count : (step + 1) * count], w_kv)

    grad_qkv = jnp.concatenate(
        [
            lax.dot_general(query_in, grad_q, (((0,), (1,)), ((), ())), preferred_element_type=F32),
            dot_first(key_in, grad_kv),
        ],
        axis=1,
    ).astype(BF16)
    grad_out = lax.dot_general(
        grad_branch, mixed, (((0,), (1,)), ((), ())), preferred_element_type=F32
    ).astype(BF16)
    grad_bias = jnp.concatenate(
        [jnp.sum(grad_q.astype(F32), axis=1), column_sum(grad_kv[:, width:])]
    )
    return (grad_query_in, grad_key_in, grad_qkv, grad_out, grad_bias)


def dot_general_q(grad_q, w_q):
    return lax.dot_general(grad_q, w_q, (((0,), (1,)), ((), ())), preferred_element_type=F32)


def feed_forward(place, x_in, w_in, b_in, w_out, b_out):
    hidden = dot_plain(x_in, w_in) + b_in.astype(F32)
    active = jax.nn.gelu(hidden, approximate=False).astype(BF16)
    branch = place.core_sum(dot_plain(active, w_out)) + b_out.astype(F32)
    return (branch, (hidden, active))


def feed_backward(place, grad_branch, saved, x_in, w_in, w_out):
    hidden, active = saved
    grad_active = dot_last(grad_branch, w_out)
    slope = jax.vjp(lambda value: jax.nn.gelu(value, approximate=False), hidden)[1](grad_active)[0]
    grad_hidden = slope.astype(BF16)
    grad_in = place.core_sum(dot_last(grad_hidden, w_in))
    return (
        grad_in,
        dot_first(x_in, grad_hidden).astype(BF16),
        column_sum(grad_hidden),
        dot_first(grad_branch, active).astype(BF16),
    )


def shards(
    source,
    target,
    source_segments,
    target_segments,
    enc_qkv,
    enc_qv_bias,
    enc_proj,
    enc_ff_in,
    enc_ff_in_bias,
    enc_ff_out,
    enc_bias,
    enc_gains,
    enc_shifts,
    dec_self,
    dec_self_bias,
    dec_self_proj,
    dec_cross,
    dec_cross_bias,
    dec_cross_proj,
    dec_ff_in,
    dec_ff_in_bias,
    dec_ff_out,
    dec_bias,
    dec_gains,
    dec_shifts,
    enc_cotangent,
    dec_cotangent,
):
    count = source.shape[1]
    model = source.shape[2]
    place = Places(lax.axis_size("dp"), lax.axis_size("seq"))
    first_row = place.z * count

    xs = place.own_pair(source[0])
    x_all = place.gather_rows(xs)
    enc_qkv = place.fetch_weight(enc_qkv)
    vectors = place.fetch_weight(
        jnp.concatenate(
            [
                enc_qv_bias.reshape(-1),
                dec_self_bias.reshape(-1),
                dec_cross_bias.reshape(-1),
                enc_ff_in_bias,
                dec_ff_in_bias,
            ]
        )
    )
    ts = place.own_pair(target[0])
    t_all = place.gather_rows(ts)
    segments = place.own_pair(jnp.concatenate([source_segments, target_segments]))
    dec_self = place.fetch_weight(dec_self)
    enc_proj = place.fetch_weight(enc_proj)
    enc_ff_in = place.fetch_weight(enc_ff_in)
    enc_ff_out = place.fetch_weight(enc_ff_out)
    dec_self_proj = place.fetch_weight(dec_self_proj)
    dec_cross = place.fetch_weight(dec_cross)
    dec_cross_proj = place.fetch_weight(dec_cross_proj)
    dec_ff_in = place.fetch_weight(dec_ff_in)
    dec_ff_out = place.fetch_weight(dec_ff_out)
    enc_cot = place.own_pair(enc_cotangent[0])
    dec_cot = place.own_pair(dec_cotangent[0])

    width = enc_qkv.shape[2]
    hidden_units = enc_ff_in.shape[1]
    marks = [0, 2 * width, 4 * width, 6 * width, 6 * width + hidden_units, 6 * width + 2 * hidden_units]
    enc_qv_bias, dec_self_bias, dec_cross_bias, enc_ff_in_bias, dec_ff_in_bias = (
        vectors[a:b] for a, b in zip(marks[:-1], marks[1:])
    )

    def prepared(qkv, bias):
        bias = bias.astype(F32)
        b_kv = jnp.concatenate([jnp.zeros((width,), F32), bias[width:]])
        return (qkv[0], jnp.concatenate([qkv[1], qkv[2]], axis=1), bias[:width], b_kv)

    enc_w = prepared(enc_qkv, enc_qv_bias)
    self_w = prepared(dec_self, dec_self_bias)
    cross_w = prepared(dec_cross, dec_cross_bias)

    source_keys, target_keys = segments[0], segments[1]
    source_own = lax.dynamic_slice_in_dim(source_keys, first_row, count, 0)
    target_own = lax.dynamic_slice_in_dim(target_keys, first_row, count, 0)
    base = place.bases(count)
    enc_mask = mask_of(source_own, source_keys, first_row, base, False, count)
    self_mask = mask_of(target_own, target_keys, first_row, base, True, count)
    cross_mask = mask_of(target_own, source_keys, first_row, base, False, count)

    branch, enc_attn = attention_forward(place, xs, x_all, enc_w, enc_proj, enc_bias[0], enc_mask)
    first, enc_norm_one = norm_forward(xs.astype(F32) + branch, enc_gains[0], enc_shifts[0])
    first_low = first.astype(BF16)
    branch, enc_feed = feed_forward(
        place, first_low, enc_ff_in, enc_ff_in_bias, enc_ff_out, enc_bias[1]
    )
    encoded, enc_norm_two = norm_forward(first + branch, enc_gains[1], enc_shifts[1])
    encoded_low = encoded.astype(BF16)
    e_all = place.gather_rows(encoded_low)

    branch, self_attn = attention_forward(
        place, ts, t_all, self_w, dec_self_proj, dec_bias[0], self_mask
    )
    second, dec_norm_one = norm_forward(ts.astype(F32) + branch, dec_gains[0], dec_shifts[0])
    second_low = second.astype(BF16)
    branch, cross_attn = attention_forward(
        place, second_low, e_all, cross_w, dec_cross_proj, dec_bias[1], cross_mask
    )
    third, dec_norm_two = norm_forward(second + branch, dec_gains[1], dec_shifts[1])
    third_low = third.astype(BF16)
    branch, dec_feed = feed_forward(
        place, third_low, dec_ff_in, dec_ff_in_bias, dec_ff_out, dec_bias[2]
    )
    decoded, dec_norm_three = norm_forward(third + branch, dec_gains[2], dec_shifts[2])

    grad_hidden, dec_gain_three, dec_shift_three = norm_backward(
        dec_cot.astype(F32), dec_norm_three, dec_gains[2]
    )
    grad_branch = grad_hidden.astype(BF16)
    feed_in, dec_w_in, dec_b_in, dec_w_out = feed_backward(
        place, grad_branch, dec_feed, third_low, dec_ff_in, dec_ff_out
    )
    dec_ff_grad = place.scatter(jnp.concatenate([dec_w_in, dec_w_out], axis=1), False)
    dec_bias_three = column_sum(grad_branch)
    grad_third = grad_hidden + feed_in
    grad_hidden, dec_gain_two, dec_shift_two = norm_backward(grad_third, dec_norm_two, dec_gains[1])
    grad_branch = grad_hidden.astype(BF16)
    query_part, key_part, cross_qkv, cross_proj, cross_bias = attention_backward(
        grad_branch, cross_attn, second_low, e_all, cross_w, dec_cross_proj, cross_mask
    )
    cross_grad = place.scatter(jnp.concatenate([cross_qkv, cross_proj], axis=1), True)
    dec_bias_two = column_sum(grad_branch)
    key_total = place.return_rows(key_part, count)
    grad_second = grad_hidden + place.core_sum(query_part)
    grad_hidden, dec_gain_one, dec_shift_one = norm_backward(
        grad_second, dec_norm_one, dec_gains[0]
    )
    grad_branch = grad_hidden.astype(BF16)
    query_part, key_part, self_qkv, self_proj, self_bias = attention_backward(
        grad_branch, self_attn, ts, t_all, self_w, dec_self_proj, self_mask
    )
    self_grad = place.scatter(jnp.concatenate([self_qkv, self_proj], axis=1), True)
    dec_bias_one = column_sum(grad_branch)

    def self_part(step, query_part=query_part, key_part=key_part):
        return key_part(step) if step else key_part(step) + query_part

    grad_target = grad_hidden + place.return_rows(self_part, count)
    grad_hidden, enc_gain_two, enc_shift_two = norm_backward(
        enc_cot.astype(F32) + key_total, enc_norm_two, enc_gains[1]
    )
    grad_branch = grad_hidden.astype(BF16)
    feed_in, enc_w_in, enc_b_in, enc_w_out = feed_backward(
        place, grad_branch, enc_feed, first_low, enc_ff_in, enc_ff_out
    )
    enc_ff_grad = place.scatter(jnp.concatenate([enc_w_in, enc_w_out], axis=1), True)
    enc_bias_two = column_sum(grad_branch)
    grad_first = grad_hidden + feed_in
    grad_hidden, enc_gain_one, enc_shift_one = norm_backward(grad_first, enc_norm_one, enc_gains[0])
    grad_branch = grad_hidden.astype(BF16)
    query_part, key_part, enc_qkv_grad, enc_proj_grad, enc_bias_grad = attention_backward(
        grad_branch, enc_attn, xs, x_all, enc_w, enc_proj, enc_mask
    )
    enc_grad = place.scatter(jnp.concatenate([enc_qkv_grad, enc_proj_grad], axis=1), False)
    enc_bias_one = column_sum(grad_branch)

    def enc_part(step, query_part=query_part, key_part=key_part):
        return key_part(step) if step else key_part(step) + query_part

    grad_source = grad_hidden + place.return_rows(enc_part, count)

    def attention_grads(grad):
        qkv = grad[:, : 3 * width].reshape(-1, 3, width).transpose(1, 0, 2)
        return (qkv, grad[:, 3 * width :].T)

    def feed_grads(grad):
        return (grad[:, :hidden_units], grad[:, hidden_units:].T)

    out_enc_qkv, out_enc_proj = attention_grads(enc_grad)
    out_self, out_self_proj = attention_grads(self_grad)
    out_cross, out_cross_proj = attention_grads(cross_grad)
    out_enc_in, out_enc_out = feed_grads(enc_ff_grad)
    out_dec_in, out_dec_out = feed_grads(dec_ff_grad)
    whole, halves = place.all_sum(
        jnp.concatenate(
            [
                enc_bias_one,
                enc_bias_two,
                enc_gain_one,
                enc_gain_two,
                enc_shift_one,
                enc_shift_two,
                dec_bias_one,
                dec_bias_two,
                dec_bias_three,
                dec_gain_one,
                dec_gain_two,
                dec_gain_three,
                dec_shift_one,
                dec_shift_two,
                dec_shift_three,
            ]
        ),
        jnp.concatenate([enc_bias_grad, self_bias, cross_bias, enc_b_in, dec_b_in]),
    )
    whole = whole.reshape(15, model)
    small = [halves[a:b] for a, b in zip(marks[:-1], marks[1:])]
    return (
        place.hand_out(encoded_low)[None],
        place.hand_out(decoded.astype(BF16))[None],
        place.hand_out(rounded(grad_source).astype(BF16)).astype(F32)[None],
        place.hand_out(rounded(grad_target).astype(BF16)).astype(F32)[None],
        out_enc_qkv,
        small[0].reshape(2, width),
        out_enc_proj,
        out_enc_in,
        small[3],
        out_enc_out,
        whole[0:2],
        whole[2:4],
        whole[4:6],
        out_self,
        small[1].reshape(2, width),
        out_self_proj,
        out_cross,
        small[2].reshape(2, width),
        out_cross_proj,
        out_dec_in,
        small[4],
        out_dec_out,
        whole[6:9],
        whole[9:12],
        whole[12:15],
    )


def solution(mesh):
    return jax.shard_map(
        shards,
        mesh=mesh,
        in_specs=(
            P("dp", "seq", None),
            P("dp", "seq", None),
            P("dp", None),
            P("dp", None),
            P(None, None, "tensor"),
            P(None, "tensor"),
            P("tensor", None),
            P(None, "tensor"),
            P("tensor"),
            P("tensor", None),
            P(),
            P(),
            P(),
            P(None, None, "tensor"),
            P(None, "tensor"),
            P("tensor", None),
            P(None, None, "tensor"),
            P(None, "tensor"),
            P("tensor", None),
            P(None, "tensor"),
            P("tensor"),
            P("tensor", None),
            P(),
            P(),
            P(),
            P("dp", "seq", None),
            P("dp", "seq", None),
        ),
        out_specs=(
            P("dp", "seq", None),
            P("dp", "seq", None),
            P("dp", "seq", None),
            P("dp", "seq", None),
            P(None, ("dp", "seq"), "tensor"),
            P(None, "tensor"),
            P("tensor", ("dp", "seq")),
            P(("dp", "seq"), "tensor"),
            P("tensor"),
            P("tensor", ("dp", "seq")),
            P(),
            P(),
            P(),
            P(None, ("dp", "seq"), "tensor"),
            P(None, "tensor"),
            P("tensor", ("dp", "seq")),
            P(None, ("dp", "seq"), "tensor"),
            P(None, "tensor"),
            P("tensor", ("dp", "seq")),
            P(("dp", "seq"), "tensor"),
            P("tensor"),
            P("tensor", ("dp", "seq")),
            P(),
            P(),
            P(),
        ),
        check_vma=False,
    )
```

```python
import functools

import jax
import jax.numpy as jnp
from jax import lax
from jax.experimental import pallas as pl
from jax.experimental.pallas import tpu as pltpu
from jax.sharding import PartitionSpec as P

HEAD_DIM = 64
EPS = 1e-05
NEG = -1e30
BF16 = jnp.bfloat16
F32 = jnp.float32
NT = (((1,), (1,)), ((), ()))
TN = (((0,), (0,)), ((), ()))
KEY_BLOCK = 512
DOCS = 4


def dot_plain(left, right):
    return jnp.dot(left, right, preferred_element_type=F32)


def dot_last(left, right):
    return lax.dot_general(left, right, NT, preferred_element_type=F32)


def dot_first(left, right):
    return lax.dot_general(left, right, TN, preferred_element_type=F32)


def column_sum(value):
    return jnp.sum(value.astype(F32), axis=0)


def rounded(value):
    return lax.reduce_precision(value, 8, 7)


def norm_forward(hidden, gain, shift):
    centered = hidden - jnp.mean(hidden, axis=-1, keepdims=True)
    spread = jnp.mean(centered * centered, axis=-1, keepdims=True)
    factor = lax.rsqrt(spread + EPS)
    normed = centered * factor
    return (normed * gain.astype(F32) + shift.astype(F32), (normed, factor))


def norm_backward(grad, saved, gain):
    normed, factor = saved
    scaled = grad * gain.astype(F32)
    centered = scaled - jnp.mean(scaled, axis=-1, keepdims=True)
    grad_hidden = factor * (centered - normed * jnp.mean(scaled * normed, axis=-1, keepdims=True))
    return (grad_hidden, jnp.sum(grad * normed, axis=0), jnp.sum(grad, axis=0))


def head_columns(head):
    return slice(head // 2 * 128, head // 2 * 128 + 128)


def head_rows(head):
    return slice(head * HEAD_DIM, (head + 1) * HEAD_DIM)


def own_lanes(shape, head):
    lanes = lax.broadcasted_iota(jnp.int32, shape, 1)
    return lanes >= HEAD_DIM if head % 2 else lanes < HEAD_DIM


class Mask:
    def __init__(self, causal, starts, segments, first_row):
        self.causal, self.starts, self.first_row = causal, starts, first_row
        segments = segments[...]
        low = high = jnp.zeros_like(segments)
        for number in range(DOCS):
            low = jnp.where(segments == number, starts[number], low)
            high = jnp.where(segments == number, starts[number + 1], high)
        self.count = segments.shape[1]
        if causal:
            place = first_row + lax.broadcasted_iota(jnp.int32, segments.shape, 1)
            high = jnp.minimum(high, place + 1)
        self.low, self.high = low, high

    def allowed(self, index, block):
        place = lax.broadcasted_iota(jnp.int32, (block, self.count), 0) + index * block
        return (place >= self.low) & (place < self.high)

    def flag(self, index, block, ends):
        start, stop = index * block, (index + 1) * block
        low, low_last = self.starts[ends[0]], self.starts[ends[1]]
        high_first, high = self.starts[ends[0] + 1], self.starts[ends[1] + 1]
        if self.causal:
            high = jnp.minimum(high, self.first_row + self.count)
            high_first = jnp.minimum(high_first, self.first_row + 1)
        active = (low < stop) & (high > start)
        full = (low_last <= start) & (high_first >= stop)
        return jnp.where(active, jnp.where(full, 2, 1), 0)


def over_blocks(mask, ends, length, block, body, skipped):
    @pl.loop(0, length // block)
    def _(index):
        flag = mask.flag(index, block, ends)
        rows = pl.ds(pl.multiple_of(index * block, block), block)

        @pl.when(flag == 0)
        def _():
            skipped(rows)

        @pl.when(flag == 1)
        def _():
            body(index, rows, True)

        @pl.when(flag == 2)
        def _():
            body(index, rows, False)


def forward_start(q_ref, masked_q, acc, top):
    heads = q_ref.shape[1] // HEAD_DIM
    for head in range(heads):
        pair = q_ref[:, head_columns(head)]
        masked_q[head] = jnp.where(own_lanes(pair.shape, head), pair, jnp.zeros_like(pair))
    acc[...] = jnp.zeros_like(acc)
    top[...] = jnp.full_like(top, NEG)


def forward_block(index, rows, partial, block, kv_ref, mask, masked_q, acc, top):
    heads, count = masked_q.shape[:2]
    width = heads * HEAD_DIM
    if partial:
        allowed = mask.allowed(index, block)
    for head in range(heads):
        cols = head_columns(head)
        scores = lax.dot_general(kv_ref[rows, cols], masked_q[head], NT, preferred_element_type=F32)
        if partial:
            scores = jnp.where(allowed, scores, NEG)
        old = top[head : head + 1, :]
        new = jnp.maximum(old, jnp.max(scores, axis=0, keepdims=True))
        weights = jnp.exp(scores - new).astype(BF16)
        vals = kv_ref[rows, width + cols.start : width + cols.stop]
        vals = jnp.where(own_lanes(vals.shape, head), vals, jnp.ones_like(vals))
        acc[head] = acc[head] * jnp.exp(old - new) + lax.dot_general(
            vals, weights, TN, preferred_element_type=F32
        )
        top[head : head + 1, :] = new


def forward_end(out_ref, lse_ref, acc, top):
    lse_ref[...] = jnp.zeros_like(lse_ref)
    for head in range(acc.shape[0]):
        first = head % 2 * HEAD_DIM
        total = acc[head, HEAD_DIM - first : HEAD_DIM - first + 1, :]
        out_ref[head_rows(head), :] = acc[head, first : first + HEAD_DIM, :] / total
        lse_ref[head : head + 1, :] = top[head : head + 1, :] + jnp.log(total)


def forward_kernel(
    block, causal, starts, ends, segments, q_ref, kv_ref, out_ref, lse_ref, masked_q, acc, top
):
    mask = Mask(causal, starts, segments, ends[2])
    forward_start(q_ref, masked_q, acc, top)

    def body(index, rows, partial):
        forward_block(index, rows, partial, block, kv_ref, mask, masked_q, acc, top)

    over_blocks(mask, ends, kv_ref.shape[0], block, body, lambda rows: None)
    forward_end(out_ref, lse_ref, acc, top)


def backward_start(q_ref, do_ref, dot_ref, out_ref, masked_q, masked_do, delta, dq):
    for head in range(masked_q.shape[0]):
        pair = q_ref[:, head_columns(head)]
        keep = own_lanes(pair.shape, head)
        masked_q[head] = jnp.where(keep, pair, jnp.zeros_like(pair))
        pair = do_ref[:, head_columns(head)]
        masked_do[head] = jnp.where(keep, pair, jnp.zeros_like(pair))
        part = head_rows(head)
        delta[head : head + 1, :] = jnp.sum(
            dot_ref[part, :].astype(F32) * out_ref[part, :], axis=0, keepdims=True
        )
    dq[...] = jnp.zeros_like(dq)


def backward_block(
    index, rows, partial, block, mask, kv_ref, lse_ref, dkv_ref, masked_q, masked_do, delta, dq
):
    heads = masked_q.shape[0]
    width = heads * HEAD_DIM
    if partial:
        allowed = mask.allowed(index, block)
    for pair in range(heads // 2):
        cols = head_columns(2 * pair)
        later = slice(width + cols.start, width + cols.stop)
        keys, vals = kv_ref[rows, cols], kv_ref[rows, later]
        dk = dv = 0.0
        for head in (2 * pair, 2 * pair + 1):
            scores = lax.dot_general(keys, masked_q[head], NT, preferred_element_type=F32)
            probs = jnp.exp(scores - lse_ref[head : head + 1, :])
            if partial:
                probs = jnp.where(allowed, probs, 0.0)
            dprobs = lax.dot_general(vals, masked_do[head], NT, preferred_element_type=F32)
            draw = (probs * (dprobs - delta[head : head + 1, :])).astype(BF16)
            probs = probs.astype(BF16)
            dv = dv + jnp.dot(probs, masked_do[head], preferred_element_type=F32)
            dk = dk + jnp.dot(draw, masked_q[head], preferred_element_type=F32)
            first = head % 2 * HEAD_DIM
            both = lax.dot_general(keys, draw, TN, preferred_element_type=F32)
            dq[head_rows(head), :] += both[first : first + HEAD_DIM]
        dkv_ref[rows, cols] = dk.astype(BF16)
        dkv_ref[rows, later] = dv.astype(BF16)


def backward_end(dq_ref, dq):
    dq_ref[...] = (dq[...] * HEAD_DIM ** (-0.5)).astype(BF16)


def backward_kernel(
    block,
    causal,
    tokens,
    starts,
    ends,
    segments,
    q_ref,
    kv_ref,
    do_ref,
    dot_ref,
    out_ref,
    lse_ref,
    *refs,
):
    dq_ref, dkv_ref, masked_q, masked_do, delta, dq = refs[tokens:]
    mask = Mask(causal, starts, segments, ends[2])
    backward_start(q_ref, do_ref, dot_ref, out_ref, masked_q, masked_do, delta, dq)

    def body(index, rows, partial):
        backward_block(
            index, rows, partial, block, mask, kv_ref, lse_ref, dkv_ref, masked_q, masked_do, delta, dq
        )

    def skipped(rows):
        dkv_ref[rows, :] = jnp.zeros((block, dkv_ref.shape[1]), BF16)

    over_blocks(mask, ends, kv_ref.shape[0], block, body, skipped)
    backward_end(dq_ref, dq)


SCALARS = pl.BlockSpec(memory_space=pltpu.SMEM)
VECTORS = pl.BlockSpec(memory_space=pltpu.VMEM)


ANYWHERE = pl.BlockSpec(memory_space=pl.ANY)


def cost_of(kv, count, width, products):
    flops = 2 * products * kv.shape[0] * count * width
    return pl.CostEstimate(flops=flops, bytes_accessed=flops // 512, transcendentals=0)


def forward_scratch(count, width):
    heads = width // HEAD_DIM
    return [
        pltpu.VMEM((heads, count, 128), BF16),
        pltpu.VMEM((heads, 128, count), F32),
        pltpu.VMEM((8, count), F32),
    ]


def backward_scratch(count, width):
    heads = width // HEAD_DIM
    return [
        pltpu.VMEM((heads, count, 128), BF16),
        pltpu.VMEM((heads, count, 128), BF16),
        pltpu.VMEM((8, count), F32),
        pltpu.VMEM((width, count), F32),
    ]


def attend(queries, kv, mask):
    count, width = queries.shape
    causal, starts, ends, segments = mask
    return pl.pallas_call(
        functools.partial(forward_kernel, KEY_BLOCK, causal),
        out_shape=(
            jax.ShapeDtypeStruct((width, count), F32),
            jax.ShapeDtypeStruct((8, count), F32),
        ),
        in_specs=[SCALARS] * 2 + [VECTORS] * 3,
        out_specs=(VECTORS,) * 2,
        scratch_shapes=forward_scratch(count, width),
        compiler_params=pltpu.CompilerParams(vmem_limit_bytes=40 << 20),
        cost_estimate=cost_of(kv, count, width, 2),
    )(starts, ends, segments, queries, kv)


def attend_back(queries, kv, grad_out, grad_out_t, output, lse, mask, tokens=()):
    count, width = queries.shape
    causal, starts, ends, segments = mask
    return pl.pallas_call(
        functools.partial(backward_kernel, KEY_BLOCK, causal, len(tokens)),
        out_shape=(
            jax.ShapeDtypeStruct((width, count), BF16),
            jax.ShapeDtypeStruct(kv.shape, BF16),
        ),
        in_specs=[SCALARS] * 2 + [VECTORS] * 7 + [ANYWHERE] * len(tokens),
        out_specs=(VECTORS,) * 2,
        scratch_shapes=backward_scratch(count, width),
        compiler_params=pltpu.CompilerParams(vmem_limit_bytes=48 << 20),
        cost_estimate=cost_of(kv, count, width, 5),
    )(starts, ends, segments, queries, kv, grad_out, grad_out_t, output, lse, *tokens)


MESH = pl.DeviceIdType.MESH
DMA = pltpu.SemaphoreType.DMA


class Here:
    def __init__(self, ring):
        self.ring = ring
        self.d, self.z, self.y = (lax.axis_index(a) for a in ("dp", "seq", "tensor"))
        self.core, self.x = lax.rem(self.d, 2), lax.div(self.d, 2)
        self.other_d = self.d + 1 - 2 * self.core
        self.partner = (self.other_d, self.z, self.y)
        self.right = (self.d, self.z + 1, self.y)
        self.left = (self.d, self.z - 1, self.y)

    def meet(self, devices):
        barrier = pltpu.get_barrier_semaphore()
        wanted = 0
        for condition, device in devices:

            @pl.when(condition)
            def _(device=device):
                pl.semaphore_signal(barrier, inc=1, device_id=device, device_id_type=MESH)

            wanted = wanted + jnp.where(condition, 1, 0)
        pl.semaphore_wait(barrier, wanted)

    def neighbours(self):
        return [
            (self.core >= 0, self.partner),
            (self.z + 1 < self.ring, self.right),
            (self.z > 0, self.left),
        ]


def remote(source, target, sent, received, device):
    return pltpu.make_async_remote_copy(
        src_ref=source,
        dst_ref=target,
        send_sem=sent,
        recv_sem=received,
        device_id=device,
        device_id_type=MESH,
    )


class Gather:
    def __init__(self, here, rows_ref, sems):
        self.here, self.rows_ref = here, rows_ref
        self.count = rows_ref.shape[0] // here.ring
        self.sent, self.got, self.core_sent, self.core_got = sems

    def half(self, shard, core):
        part = self.count // 2
        start = pl.multiple_of(shard * self.count + core * part, part)
        return self.rows_ref.at[pl.ds(start, part)]

    def ways(self, step):
        here = self.here
        z, ring = here.z, here.ring
        return [
            (0, z - step, z >= step, z - step + 1, (z + 1 < ring) & (z + 1 >= step), here.right),
            (1, z + step, z + step < ring, z + step - 1, (z > 0) & (z + step <= ring), here.left),
        ]

    def along(self, way, step, shard, device):
        view = self.half(shard, self.here.core)
        return remote(view, view, self.sent.at[way, step], self.got.at[way, step], device)

    def across(self, way, step, shard, core):
        view = self.half(shard, core)
        return remote(
            view, view, self.core_sent.at[way, step], self.core_got.at[way, step], self.here.partner
        )

    def start(self, step):
        for way, _, _, shard, sends, device in self.ways(step):

            @pl.when(sends)
            def _(way=way, shard=shard, device=device):
                self.along(way, step, shard, device).start()

    def arrive(self, step):
        for way, shard, comes, _, _, device in self.ways(step):

            @pl.when(comes)
            def _(way=way, shard=shard, device=device):
                self.along(way, step, shard, self.here.partner).wait_recv()
                self.across(way, step, shard, self.here.core).start()

    def finish(self, step):
        for way, shard, comes, out, sends, device in self.ways(step):

            @pl.when(sends)
            def _(way=way, out=out, device=device):
                self.along(way, step, out, device).wait_send()

            @pl.when(comes)
            def _(way=way, shard=shard):
                self.across(way, step, shard, self.here.core).wait_send()
                self.across(way, step, shard, 1 - self.here.core).wait_recv()


class Fetch:
    def __init__(self, here, inputs, outputs, sems):
        self.here, self.inputs, self.outputs = here, inputs, outputs
        self.y_sent, self.y_got, self.x_sent, self.x_got, self.core_sent, self.core_got = sems
        self.x_partner = (here.d + 2 - 4 * lax.rem(here.x, 2), here.z, here.y)
        self.y_partner = (here.other_d, here.z, 1 - here.y)

    def devices(self):
        here = self.here
        return [(here.core >= 0, self.y_partner), (here.core == 1, self.x_partner)]

    def part(self, ref, which):
        rows = ref.shape[0] // 2
        return ref.at[pl.ds(pl.multiple_of(which * rows, rows), rows)]

    def over_y(self, k):
        which = lax.rem(self.here.x, 2)
        return remote(
            self.part(self.inputs[k], which),
            self.part(self.outputs[k], which),
            self.y_sent.at[k],
            self.y_got.at[k],
            self.y_partner,
        )

    def over_x(self, k, which):
        view = self.part(self.outputs[k], which)
        return remote(view, view, self.x_sent.at[k], self.x_got.at[k], self.x_partner)

    def across(self, k):
        return remote(
            self.inputs[k], self.outputs[k], self.core_sent.at[k], self.core_got.at[k], self.here.partner
        )

    def begin(self):
        @pl.when(self.here.core == 0)
        def _():
            for k in range(min(2, len(self.inputs))):
                self.over_y(k).start()

        @pl.when(self.here.core == 1)
        def _():
            for k in range(len(self.inputs)):
                self.across(k).start()

    def advance(self, k):
        @pl.when(self.here.core == 0)
        def _():
            self.over_y(k).wait_send()
            if k + 2 < len(self.inputs):
                self.over_y(k + 2).start()

        @pl.when(self.here.core == 1)
        def _():
            self.over_y(k).wait_recv()
            self.over_x(k, lax.rem(self.here.x, 2)).start()

    def end(self):
        @pl.when(self.here.core == 0)
        def _():
            for k in range(len(self.inputs)):
                self.across(k).wait_recv()

        @pl.when(self.here.core == 1)
        def _():
            for k in range(len(self.inputs)):
                self.over_x(k, lax.rem(self.here.x, 2)).wait_send()
                self.over_x(k, 1 - lax.rem(self.here.x, 2)).wait_recv()
                self.across(k).wait_send()


def gather_sems(ring):
    return [DMA((2, ring))] * 4


def fetch_sems(number):
    return [DMA((number,))] * 6


def opening_kernel(ring, number, *refs):
    inputs, outputs, sems = refs[: 4 + number], refs[4 + number : 8 + 2 * number], refs[8 + 2 * number :]
    source, target, segments, vectors = inputs[:4]
    source_all, target_all, segments_out, vectors_out = outputs[:4]
    shard_sems, vector_sems = sems[:3], sems[3:6]
    here = Here(ring)
    fetch = Fetch(here, inputs[4:], outputs[4:], sems[14:])
    here.meet(here.neighbours() + fetch.devices())
    count = source.shape[0]
    own = pl.ds(pl.multiple_of(here.z * count, count), count)
    moves = [
        (source, source_all.at[own]),
        (target, target_all.at[own]),
        (segments, segments_out),
    ]
    owner = here.core == here.y

    def shard_copy(k):
        start, end = moves[k]
        sent, got, copied = shard_sems
        return (
            remote(start, end, sent.at[k], got.at[k], here.partner),
            pltpu.make_async_copy(start, end, copied.at[k]),
        )

    def vector_copy():
        sent, got, copied = vector_sems
        return (
            remote(vectors, vectors_out, sent, got, fetch.y_partner),
            pltpu.make_async_copy(vectors, vectors_out, copied),
        )

    def wait_shard(k):
        across, local = shard_copy(k)

        @pl.when(owner)
        def _():
            across.wait_send()
            local.wait()

        @pl.when(jnp.logical_not(owner))
        def _():
            across.wait_recv()

    @pl.when(owner)
    def _():
        for k in range(3):
            across, local = shard_copy(k)
            across.start()
            local.start()

    @pl.when(here.core == 0)
    def _():
        across, local = vector_copy()
        across.start()
        local.start()

    fetch.begin()
    gathers = [Gather(here, source_all, sems[6:10]), Gather(here, target_all, sems[10:14])]
    slots = 2 * (ring - 1)
    done = 0
    for k, gather in enumerate(gathers):
        wait_shard(k)
        for step in range(1, ring):
            gather.start(step)
            slot = k * (ring - 1) + step
            while done < number * slot // slots:
                fetch.advance(done)
                done += 1
            gather.arrive(step)
    for gather in gathers:
        for step in range(1, ring):
            gather.finish(step)
    wait_shard(2)
    fetch.end()
    across, local = vector_copy()

    @pl.when(here.core == 0)
    def _():
        across.wait_send()
        local.wait()

    @pl.when(here.core == 1)
    def _():
        across.wait_recv()


def opening(ring, source, target, segments, vectors, weights):
    inputs = (source, target, segments, vectors) + tuple(weights)
    count, model = source.shape
    rows = jax.ShapeDtypeStruct((ring * count, model), BF16)
    shapes = (rows, rows) + tuple(jax.ShapeDtypeStruct(v.shape, v.dtype) for v in inputs[2:])
    number = len(weights)
    return pl.pallas_call(
        functools.partial(opening_kernel, ring, number),
        out_shape=shapes,
        in_specs=[VECTORS] * 4 + [ANYWHERE] * number,
        out_specs=(ANYWHERE,) * 2 + (VECTORS,) * 2 + (ANYWHERE,) * number,
        scratch_shapes=[DMA((3,))] * 3 + [DMA] * 3 + gather_sems(ring) * 2 + fetch_sems(number),
        compiler_params=pltpu.CompilerParams(collective_id=1, has_side_effects=True),
    )(*inputs)


def gather_attend_kernel(block, causal, ring, tokens, starts, segments, q_ref, kv_ref, own_ref, *refs):
    out_ref, lse_ref, all_ref, masked_q, acc, top, copied = refs[tokens : tokens + 7]
    here = Here(ring)
    gather = Gather(here, all_ref, refs[tokens + 7 :])
    here.meet(here.neighbours())
    count = own_ref.shape[0]
    first_row = pl.multiple_of(here.z * count, count)
    local = pltpu.make_async_copy(own_ref, all_ref.at[pl.ds(first_row, count)], copied)
    local.start()
    local.wait()
    gather.start(1)
    mask = Mask(causal, starts, segments, first_row)
    forward_start(q_ref, masked_q, acc, top)

    @pl.loop(0, kv_ref.shape[0] // block)
    def _(index):
        rows = pl.ds(pl.multiple_of(index * block, block), block)
        forward_block(index, rows, True, block, kv_ref, mask, masked_q, acc, top)

        @pl.when((index >= 1) & (index < ring))
        def _():
            gather.arrive(index)

        @pl.when((index >= 1) & (index < ring - 1))
        def _():
            gather.start(index + 1)

    forward_end(out_ref, lse_ref, acc, top)

    @pl.loop(1, ring)
    def _(step):
        gather.finish(step)


def gather_attend(ring, queries, kv, mask, own, tokens):
    count, width = queries.shape
    causal, starts, _, segments = mask
    return pl.pallas_call(
        functools.partial(gather_attend_kernel, KEY_BLOCK, causal, ring, len(tokens)),
        out_shape=(
            jax.ShapeDtypeStruct((width, count), F32),
            jax.ShapeDtypeStruct((8, count), F32),
            jax.ShapeDtypeStruct((ring * own.shape[0], own.shape[1]), BF16),
        ),
        in_specs=[SCALARS] + [VECTORS] * 4 + [ANYWHERE] * len(tokens),
        out_specs=(VECTORS, VECTORS, ANYWHERE),
        scratch_shapes=forward_scratch(count, width) + [DMA] + gather_sems(ring),
        compiler_params=pltpu.CompilerParams(
            vmem_limit_bytes=40 << 20, collective_id=2, has_side_effects=True
        ),
        cost_estimate=cost_of(kv, count, width, 2),
    )(starts, segments, queries, kv, own, *tokens)


class Return:
    def __init__(self, here, terms_ref, query_ref, out_ref, refs):
        self.here, self.terms_ref, self.query_ref, self.out_ref = here, terms_ref, query_ref, out_ref
        self.mine, self.outgoing, self.from_core, self.arrived, self.total = refs[:5]
        self.core_sent, self.core_got, self.sent, self.got, self.end_sent, self.end_got = refs[5:]
        self.count = terms_ref.shape[0] // here.ring
        self.part = self.count // 2
        self.order = list(range(1, here.ring)) + [0]

    def devices(self):
        here = self.here
        found = [(here.core >= 0, here.partner)]
        for step in range(1, here.ring):
            found.append((here.core >= 0, self.to(step)))
        return found

    def to(self, step):
        here = self.here
        return (here.d, lax.rem(here.z + step, here.ring), here.y)

    def half(self, core):
        return pl.ds(pl.multiple_of(core * self.part, self.part), self.part)

    def rows(self, step, core):
        start = lax.rem(self.here.z + step, self.here.ring) * self.count + core * self.part
        return pl.ds(pl.multiple_of(start, self.part), self.part)

    def across(self, step):
        other = 1 - self.here.core
        if step == 0 and self.query_ref is not None:
            source = self.mine.at[self.half(other)]
        else:
            source = self.terms_ref.at[self.rows(step, other)]
        return remote(
            source,
            self.from_core.at[step],
            self.core_sent.at[step],
            self.core_got.at[step],
            self.here.partner,
        )

    def along(self, step):
        return remote(
            self.outgoing.at[step], self.arrived.at[step], self.sent.at[step], self.got.at[step], self.to(step)
        )

    def begin(self):
        if self.query_ref is not None:
            start = pl.multiple_of(self.here.z * self.count, self.count)
            own = self.terms_ref[pl.ds(start, self.count), :].astype(F32)
            self.mine[...] = (own + self.query_ref[...].astype(F32)).astype(BF16)
        for step in self.order:
            self.across(step).start()

    def send(self):
        for step in self.order:
            self.across(step).wait_recv()
            if step == 0 and self.query_ref is not None:
                local = self.mine[self.half(self.here.core), :]
            else:
                local = self.terms_ref[self.rows(step, self.here.core), :]
            both = local.astype(F32) + self.from_core[step].astype(F32)
            if step:
                self.outgoing[step] = both.astype(BF16)
                self.along(step).start()
            else:
                self.total[...] = both

    def end(self):
        for step in range(1, self.here.ring):
            self.along(step).wait_recv()
            self.total[...] += self.arrived[step].astype(F32)
        own, other = self.half(self.here.core), self.half(1 - self.here.core)
        self.out_ref[own, :] = self.total[...].astype(BF16)
        for half, waits in ((own, False), (other, True)):
            view = self.out_ref.at[half]
            copy = remote(view, view, self.end_sent, self.end_got, self.here.partner)
            if waits:
                copy.wait_recv()
            else:
                copy.start()
                copy.wait_send()
        for step in self.order:
            self.across(step).wait_send()
            if step:
                self.along(step).wait_send()


def return_scratch(ring, count, model):
    part = count // 2
    return (
        [pltpu.VMEM((count, model), BF16)]
        + [pltpu.VMEM((ring, part, model), BF16)] * 3
        + [pltpu.VMEM((part, model), F32)]
        + [DMA((ring,))] * 4
        + [DMA] * 2
    )


def return_kernel(ring, tokens, terms_ref, query_ref, *refs):
    returned = Return(Here(ring), terms_ref, query_ref, refs[tokens], refs[tokens + 1 :])
    returned.here.meet(returned.devices())
    returned.begin()
    returned.send()
    returned.end()


def return_rows(ring, number, terms, query, tokens=()):
    rows, model = terms.shape
    count = rows // ring
    return pl.pallas_call(
        functools.partial(return_kernel, ring, len(tokens)),
        out_shape=jax.ShapeDtypeStruct((count, model), BF16),
        in_specs=[VECTORS] * 2 + [ANYWHERE] * len(tokens),
        out_specs=VECTORS,
        scratch_shapes=return_scratch(ring, count, model),
        compiler_params=pltpu.CompilerParams(
            vmem_limit_bytes=40 << 20, collective_id=number, has_side_effects=True
        ),
    )(terms, query, *tokens)


def back_return_kernel(
    block,
    causal,
    ring,
    has_query,
    tokens,
    starts,
    segments,
    q_ref,
    kv_ref,
    do_ref,
    dot_ref,
    out_ref,
    lse_ref,
    terms_ref,
    *refs,
):
    query_ref, refs = (refs[0], refs[1:]) if has_query else (None, refs)
    dq_ref, dkv_ref, sum_ref, masked_q, masked_do, delta, dq = refs[tokens : tokens + 7]
    here = Here(ring)
    returned = Return(here, terms_ref, query_ref, sum_ref, refs[tokens + 7 :])
    here.meet(returned.devices())
    returned.begin()
    mask = Mask(causal, starts, segments, here.z * q_ref.shape[0])
    backward_start(q_ref, do_ref, dot_ref, out_ref, masked_q, masked_do, delta, dq)
    returned.send()

    @pl.loop(0, kv_ref.shape[0] // block)
    def _(index):
        rows = pl.ds(pl.multiple_of(index * block, block), block)
        backward_block(
            index, rows, True, block, mask, kv_ref, lse_ref, dkv_ref, masked_q, masked_do, delta, dq
        )

    backward_end(dq_ref, dq)
    returned.end()


def back_return(ring, number, queries, kv, grad_out, grad_out_t, output, lse, mask, terms, query, tokens):
    count, width = queries.shape
    model = terms.shape[1]
    causal, starts, _, segments = mask
    more = (terms,) if query is None else (terms, query)
    return pl.pallas_call(
        functools.partial(
            back_return_kernel, KEY_BLOCK, causal, ring, query is not None, len(tokens)
        ),
        out_shape=(
            jax.ShapeDtypeStruct((width, count), BF16),
            jax.ShapeDtypeStruct(kv.shape, BF16),
            jax.ShapeDtypeStruct((count, model), BF16),
        ),
        in_specs=[SCALARS] + [VECTORS] * (7 + len(more)) + [ANYWHERE] * len(tokens),
        out_specs=(VECTORS,) * 3,
        scratch_shapes=backward_scratch(count, width) + return_scratch(ring, count, model),
        compiler_params=pltpu.CompilerParams(
            vmem_limit_bytes=56 << 20, collective_id=number, has_side_effects=True
        ),
        cost_estimate=cost_of(kv, count, width, 5),
    )(starts, segments, queries, kv, grad_out, grad_out_t, output, lse, *more, *tokens)


class Places:
    def __init__(self, pairs, ring):
        self.pairs, self.ring = pairs, ring
        self.d = lax.axis_index("dp")
        self.x, self.core = self.d // 2, self.d % 2
        self.y, self.z = lax.axis_index("tensor"), lax.axis_index("seq")

    def swap_core(self, value):
        return lax.ppermute(value, "dp", [(i, i ^ 1) for i in range(self.pairs)])

    def swap_y(self, value):
        return lax.ppermute(value, "tensor", [(0, 1), (1, 0)])

    def swap_x(self, value, bit):
        return lax.ppermute(value, "dp", [(i, i ^ (2 << bit)) for i in range(self.pairs)])

    def swap_z(self, value, bit):
        return lax.ppermute(value, "seq", [(i, i ^ (1 << bit)) for i in range(self.ring)])

    def from_z(self, value, step):
        return lax.ppermute(value, "seq", [((i + step) % self.ring, i) for i in range(self.ring)])

    def to_z(self, value, step):
        return lax.ppermute(value, "seq", [(i, (i + step) % self.ring) for i in range(self.ring)])

    def permute(self, value, source_of):
        moves = []
        for d in range(self.pairs):
            for y in range(2):
                source = source_of(d, y)
                if source is not None:
                    moves.append((source[0] * 2 + source[1], d * 2 + y))
        return lax.ppermute(value, ("dp", "tensor"), moves)

    def fetch_weight(self, value):
        return self.permute(value, lambda d, y: (d + 1, y) if d % 2 == 0 else (d - 1, 1 - y))

    def core_sum(self, partial):
        low = rounded(partial)
        return low + self.swap_core(low.astype(BF16)).astype(F32)

    def own_pair(self, rows):
        return jnp.where(self.core == self.y, rows, self.swap_core(rows))

    def hand_out(self, rows):
        other = self.permute(rows, lambda d, y: (d, 1 - y) if d % 2 != y else None)
        return jnp.where(self.core == self.y, rows, other)

    def scatter(self, grad, x_first):
        rows, columns = grad.shape
        owners = self.pairs // 2
        grad = grad.reshape(owners, 2, self.ring, rows // (self.pairs * self.ring), columns)
        for stage in "xyz" if x_first else "yxz":
            if stage == "y":
                kept = lax.dynamic_index_in_dim(grad, self.core, grad.ndim - 4, False)
                sent = lax.dynamic_index_in_dim(grad, 1 - self.core, grad.ndim - 4, False)
                first = self.permute(
                    sent, lambda d, y: (d + 1, 1 - y) if d % 2 == 0 else (d - 1, y)
                )
                second = self.permute(kept, lambda d, y: (d, 1 - y) if d % 2 else None)
                kept = jnp.where(self.core == 0, kept, second)
                grad = (kept.astype(F32) + first.astype(F32)).astype(BF16)
            else:
                axis = 0 if stage == "x" else grad.ndim - 3
                place, swap = (self.x, self.swap_x) if stage == "x" else (self.z, self.swap_z)
                size, bit = grad.shape[axis], 0
                while size > 1:
                    shape = grad.shape[:axis] + (size // 2, 2) + grad.shape[axis + 1 :]
                    grad = grad.reshape(shape)
                    mine = (place >> bit) & 1
                    kept = lax.dynamic_index_in_dim(grad, mine, axis + 1, False)
                    sent = lax.dynamic_index_in_dim(grad, 1 - mine, axis + 1, False)
                    grad = kept.astype(F32) + swap(sent, bit).astype(F32)
                    size, bit = size // 2, bit + 1
                    if stage == "x" or size > 1:
                        grad = grad.astype(BF16)
                grad = lax.squeeze(grad, (axis,))
        return grad.astype(F32)

    def all_sum(self, whole, halves):
        both = jnp.concatenate([whole, halves])
        for bit in range((self.pairs // 2).bit_length() - 1):
            both = both + self.swap_x(both, bit)
        for bit in range(self.ring.bit_length() - 1):
            both = both + self.swap_z(both, bit)
        whole, halves = both[: whole.shape[0]], both[whole.shape[0] :]
        whole = whole + self.swap_y(whole)
        whole = (whole + self.swap_core(whole)) * 0.5
        first = self.permute(halves, lambda d, y: (d + 1, 1 - y) if d % 2 == 0 else (d - 1, y))
        second = self.swap_y(halves)
        halves = jnp.where(self.core == 0, halves, second) + first
        return whole, halves


def starts_of(segments):
    numbers = jnp.arange(8, dtype=jnp.int32)
    return jnp.sum(segments[None, :] < numbers[:, None], axis=1, dtype=jnp.int32)


def mask_of(query_seg, key_starts, first_row, causal):
    ends = jnp.stack([query_seg[0], query_seg[-1], first_row])
    return (causal, key_starts, ends, query_seg[None])


def projected(query_in, key_in, weights):
    w_q, w_kv, b_q, b_kv = weights
    scale = HEAD_DIM ** (-0.5)
    queries = ((dot_plain(query_in, w_q) + b_q).astype(BF16) * scale).astype(BF16)
    return queries, (dot_plain(key_in, w_kv) + b_kv).astype(BF16)


def attention_output(place, queries, kv, output, lse, out_weight, out_bias):
    mixed = output.astype(BF16)
    branch = place.core_sum(dot_first(mixed, out_weight)) + out_bias.astype(F32)
    return (branch, (queries, kv, output, lse, mixed))


def attention_backward(grad_branch, saved, query_in, key_in, weights, out_weight, back):
    queries, kv, output, lse, mixed = saved
    w_q, w_kv = weights[:2]
    width = queries.shape[1]
    grad_mixed = dot_last(grad_branch, out_weight).astype(BF16)
    grad_mixed_t = dot_last(out_weight, grad_branch).astype(BF16)
    grad_q, grad_kv, *more = back(queries, kv, grad_mixed, grad_mixed_t, output, lse)
    grad_query_in = dot_general_q(grad_q, w_q)
    grad_key_in = dot_last(grad_kv, w_kv).astype(BF16)
    grad_qkv = jnp.concatenate(
        [
            lax.dot_general(query_in, grad_q, (((0,), (1,)), ((), ())), preferred_element_type=F32),
            dot_first(key_in, grad_kv),
        ],
        axis=1,
    ).astype(BF16)
    grad_out = lax.dot_general(
        grad_branch, mixed, (((0,), (1,)), ((), ())), preferred_element_type=F32
    ).astype(BF16)
    grad_bias = jnp.concatenate(
        [jnp.sum(grad_q.astype(F32), axis=1), column_sum(grad_kv[:, width:])]
    )
    return (grad_query_in, grad_key_in, grad_qkv, grad_out, grad_bias, *more)


def dot_general_q(grad_q, w_q):
    return lax.dot_general(grad_q, w_q, (((0,), (1,)), ((), ())), preferred_element_type=F32)


def feed_forward(place, x_in, w_in, b_in, w_out, b_out):
    hidden = dot_plain(x_in, w_in) + b_in.astype(F32)
    active = jax.nn.gelu(hidden, approximate=False).astype(BF16)
    branch = place.core_sum(dot_plain(active, w_out)) + b_out.astype(F32)
    return (branch, (hidden, active))


def feed_backward(place, grad_branch, saved, x_in, w_in, w_out):
    hidden, active = saved
    grad_active = dot_last(grad_branch, w_out)
    slope = jax.vjp(lambda value: jax.nn.gelu(value, approximate=False), hidden)[1](grad_active)[0]
    grad_hidden = slope.astype(BF16)
    grad_in = place.core_sum(dot_last(grad_hidden, w_in))
    return (
        grad_in,
        dot_first(x_in, grad_hidden).astype(BF16),
        column_sum(grad_hidden),
        dot_first(grad_branch, active).astype(BF16),
    )


def shards(
    source,
    target,
    source_segments,
    target_segments,
    enc_qkv,
    enc_qv_bias,
    enc_proj,
    enc_ff_in,
    enc_ff_in_bias,
    enc_ff_out,
    enc_bias,
    enc_gains,
    enc_shifts,
    dec_self,
    dec_self_bias,
    dec_self_proj,
    dec_cross,
    dec_cross_bias,
    dec_cross_proj,
    dec_ff_in,
    dec_ff_in_bias,
    dec_ff_out,
    dec_bias,
    dec_gains,
    dec_shifts,
    enc_cotangent,
    dec_cotangent,
):
    count = source.shape[1]
    model = source.shape[2]
    place = Places(lax.axis_size("dp"), lax.axis_size("seq"))
    first_row = place.z * count

    ring = place.ring
    width = enc_qkv.shape[2]
    hidden_units = enc_ff_in.shape[1]

    vectors = jnp.concatenate(
        [
            enc_qv_bias.reshape(-1),
            dec_self_bias.reshape(-1),
            dec_cross_bias.reshape(-1),
            enc_ff_in_bias,
            dec_ff_in_bias,
        ]
    ).astype(F32)
    (
        x_all,
        t_all,
        segments,
        vectors,
        enc_qkv,
        dec_self,
        enc_proj,
        dec_self_proj,
        enc_ff_in,
        enc_ff_out,
        dec_cross,
        dec_cross_proj,
    ) = opening(
        ring,
        source[0],
        target[0],
        jnp.concatenate([source_segments, target_segments]),
        vectors.reshape(-1, 128),
        (
            enc_qkv.reshape(-1, width),
            dec_self.reshape(-1, width),
            enc_proj,
            dec_self_proj,
            enc_ff_in,
            enc_ff_out,
            dec_cross.reshape(-1, width),
            dec_cross_proj,
        ),
    )
    vectors = vectors.reshape(-1)
    xs = lax.dynamic_slice_in_dim(x_all, first_row, count, 0)
    ts = lax.dynamic_slice_in_dim(t_all, first_row, count, 0)
    dec_ff_in = place.fetch_weight(dec_ff_in)
    dec_ff_out = place.fetch_weight(dec_ff_out)
    enc_cot = place.own_pair(enc_cotangent[0])
    dec_cot = place.own_pair(dec_cotangent[0])

    marks = [0, 2 * width, 4 * width, 6 * width, 6 * width + hidden_units, 6 * width + 2 * hidden_units]
    enc_qv_bias, dec_self_bias, dec_cross_bias, enc_ff_in_bias, dec_ff_in_bias = (
        vectors[a:b] for a, b in zip(marks[:-1], marks[1:])
    )

    def prepared(qkv, bias):
        qkv = qkv.reshape(3, model, width)
        b_kv = jnp.concatenate([jnp.zeros((width,), F32), bias[width:]])
        return (qkv[0], jnp.concatenate([qkv[1], qkv[2]], axis=1), bias[:width], b_kv)

    enc_w = prepared(enc_qkv, enc_qv_bias)
    self_w = prepared(dec_self, dec_self_bias)
    cross_w = prepared(dec_cross, dec_cross_bias)

    source_keys, target_keys = segments[0], segments[1]
    source_own = lax.dynamic_slice_in_dim(source_keys, first_row, count, 0)
    target_own = lax.dynamic_slice_in_dim(target_keys, first_row, count, 0)
    source_starts, target_starts = starts_of(source_keys), starts_of(target_keys)
    enc_mask = mask_of(source_own, source_starts, first_row, False)
    self_mask = mask_of(target_own, target_starts, first_row, True)
    cross_mask = mask_of(target_own, source_starts, first_row, False)

    queries, kv = projected(xs, x_all, enc_w)
    output, lse = attend(queries, kv, enc_mask)
    branch, enc_attn = attention_output(place, queries, kv, output, lse, enc_proj, enc_bias[0])
    first, enc_norm_one = norm_forward(xs.astype(F32) + branch, enc_gains[0], enc_shifts[0])
    first_low = first.astype(BF16)
    branch, enc_feed = feed_forward(
        place, first_low, enc_ff_in, enc_ff_in_bias, enc_ff_out, enc_bias[1]
    )
    encoded, enc_norm_two = norm_forward(first + branch, enc_gains[1], enc_shifts[1])
    encoded_low = encoded.astype(BF16)

    queries, kv = projected(ts, t_all, self_w)
    output, lse, e_all = gather_attend(
        ring, queries, kv, self_mask, encoded_low, (dec_ff_in, dec_ff_out)
    )
    branch, self_attn = attention_output(
        place, queries, kv, output, lse, dec_self_proj, dec_bias[0]
    )
    second, dec_norm_one = norm_forward(ts.astype(F32) + branch, dec_gains[0], dec_shifts[0])
    second_low = second.astype(BF16)
    queries, kv = projected(second_low, e_all, cross_w)
    output, lse = attend(queries, kv, cross_mask)
    branch, cross_attn = attention_output(
        place, queries, kv, output, lse, dec_cross_proj, dec_bias[1]
    )
    third, dec_norm_two = norm_forward(second + branch, dec_gains[1], dec_shifts[1])
    third_low = third.astype(BF16)
    branch, dec_feed = feed_forward(
        place, third_low, dec_ff_in, dec_ff_in_bias, dec_ff_out, dec_bias[2]
    )
    decoded, dec_norm_three = norm_forward(third + branch, dec_gains[2], dec_shifts[2])

    grad_hidden, dec_gain_three, dec_shift_three = norm_backward(
        dec_cot.astype(F32), dec_norm_three, dec_gains[2]
    )
    grad_branch = grad_hidden.astype(BF16)
    feed_in, dec_w_in, dec_b_in, dec_w_out = feed_backward(
        place, grad_branch, dec_feed, third_low, dec_ff_in, dec_ff_out
    )
    dec_ff_grad = place.scatter(jnp.concatenate([dec_w_in, dec_w_out], axis=1), False)
    dec_bias_three = column_sum(grad_branch)
    grad_third = grad_hidden + feed_in
    grad_hidden, dec_gain_two, dec_shift_two = norm_backward(grad_third, dec_norm_two, dec_gains[1])
    grad_branch = grad_hidden.astype(BF16)
    query_part, key_part, cross_qkv, cross_proj, cross_bias = attention_backward(
        grad_branch,
        cross_attn,
        second_low,
        e_all,
        cross_w,
        dec_cross_proj,
        functools.partial(attend_back, mask=cross_mask),
    )
    cross_grad = place.scatter(jnp.concatenate([cross_qkv, cross_proj], axis=1), True)
    dec_bias_two = column_sum(grad_branch)
    grad_second = grad_hidden + place.core_sum(query_part)
    grad_hidden, dec_gain_one, dec_shift_one = norm_backward(
        grad_second, dec_norm_one, dec_gains[0]
    )
    grad_branch = grad_hidden.astype(BF16)
    query_part, key_part, self_qkv, self_proj, self_bias, key_total = attention_backward(
        grad_branch,
        self_attn,
        ts,
        t_all,
        self_w,
        dec_self_proj,
        lambda *parts: back_return(ring, 3, *parts, self_mask, key_part, None, ()),
    )
    self_grad = place.scatter(jnp.concatenate([self_qkv, self_proj], axis=1), True)
    dec_bias_one = column_sum(grad_branch)
    target_hidden = grad_hidden
    grad_hidden, enc_gain_two, enc_shift_two = norm_backward(
        enc_cot.astype(F32) + key_total.astype(F32), enc_norm_two, enc_gains[1]
    )
    grad_branch = grad_hidden.astype(BF16)
    feed_in, enc_w_in, enc_b_in, enc_w_out = feed_backward(
        place, grad_branch, enc_feed, first_low, enc_ff_in, enc_ff_out
    )
    enc_ff_grad = place.scatter(jnp.concatenate([enc_w_in, enc_w_out], axis=1), True)
    enc_bias_two = column_sum(grad_branch)
    grad_first = grad_hidden + feed_in
    grad_hidden, enc_gain_one, enc_shift_one = norm_backward(grad_first, enc_norm_one, enc_gains[0])
    grad_branch = grad_hidden.astype(BF16)
    target_query, target_key = query_part.astype(BF16), key_part
    query_part, key_part, enc_qkv_grad, enc_proj_grad, enc_bias_grad, target_total = (
        attention_backward(
            grad_branch,
            enc_attn,
            xs,
            x_all,
            enc_w,
            enc_proj,
            lambda *parts: back_return(
                ring, 4, *parts, enc_mask, target_key, target_query, (dec_ff_grad, cross_grad)
            ),
        )
    )
    grad_target = target_hidden + target_total.astype(F32)
    enc_grad = place.scatter(jnp.concatenate([enc_qkv_grad, enc_proj_grad], axis=1), False)
    enc_bias_one = column_sum(grad_branch)
    source_total = return_rows(
        ring, 5, key_part, query_part.astype(BF16), (self_grad, enc_ff_grad)
    )
    grad_source = grad_hidden + source_total.astype(F32)

    def attention_grads(grad):
        qkv = grad[:, : 3 * width].reshape(-1, 3, width).transpose(1, 0, 2)
        return (qkv, grad[:, 3 * width :].T)

    def feed_grads(grad):
        return (grad[:, :hidden_units], grad[:, hidden_units:].T)

    out_enc_qkv, out_enc_proj = attention_grads(enc_grad)
    out_self, out_self_proj = attention_grads(self_grad)
    out_cross, out_cross_proj = attention_grads(cross_grad)
    out_enc_in, out_enc_out = feed_grads(enc_ff_grad)
    out_dec_in, out_dec_out = feed_grads(dec_ff_grad)
    whole, halves = place.all_sum(
        jnp.concatenate(
            [
                enc_bias_one,
                enc_bias_two,
                enc_gain_one,
                enc_gain_two,
                enc_shift_one,
                enc_shift_two,
                dec_bias_one,
                dec_bias_two,
                dec_bias_three,
                dec_gain_one,
                dec_gain_two,
                dec_gain_three,
                dec_shift_one,
                dec_shift_two,
                dec_shift_three,
            ]
        ),
        jnp.concatenate([enc_bias_grad, self_bias, cross_bias, enc_b_in, dec_b_in]),
    )
    whole = whole.reshape(15, model)
    small = [halves[a:b] for a, b in zip(marks[:-1], marks[1:])]
    return (
        place.hand_out(encoded_low)[None],
        place.hand_out(decoded.astype(BF16))[None],
        place.hand_out(rounded(grad_source).astype(BF16)).astype(F32)[None],
        place.hand_out(rounded(grad_target).astype(BF16)).astype(F32)[None],
        out_enc_qkv,
        small[0].reshape(2, width),
        out_enc_proj,
        out_enc_in,
        small[3],
        out_enc_out,
        whole[0:2],
        whole[2:4],
        whole[4:6],
        out_self,
        small[1].reshape(2, width),
        out_self_proj,
        out_cross,
        small[2].reshape(2, width),
        out_cross_proj,
        out_dec_in,
        small[4],
        out_dec_out,
        whole[6:9],
        whole[9:12],
        whole[12:15],
    )


def solution(mesh):
    return jax.shard_map(
        shards,
        mesh=mesh,
        in_specs=(
            P("dp", "seq", None),
            P("dp", "seq", None),
            P("dp", None),
            P("dp", None),
            P(None, None, "tensor"),
            P(None, "tensor"),
            P("tensor", None),
            P(None, "tensor"),
            P("tensor"),
            P("tensor", None),
            P(),
            P(),
            P(),
            P(None, None, "tensor"),
            P(None, "tensor"),
            P("tensor", None),
            P(None, None, "tensor"),
            P(None, "tensor"),
            P("tensor", None),
            P(None, "tensor"),
            P("tensor"),
            P("tensor", None),
            P(),
            P(),
            P(),
            P("dp", "seq", None),
            P("dp", "seq", None),
        ),
        out_specs=(
            P("dp", "seq", None),
            P("dp", "seq", None),
            P("dp", "seq", None),
            P("dp", "seq", None),
            P(None, ("dp", "seq"), "tensor"),
            P(None, "tensor"),
            P("tensor", ("dp", "seq")),
            P(("dp", "seq"), "tensor"),
            P("tensor"),
            P("tensor", ("dp", "seq")),
            P(),
            P(),
            P(),
            P(None, ("dp", "seq"), "tensor"),
            P(None, "tensor"),
            P("tensor", ("dp", "seq")),
            P(None, ("dp", "seq"), "tensor"),
            P(None, "tensor"),
            P("tensor", ("dp", "seq")),
            P(("dp", "seq"), "tensor"),
            P("tensor"),
            P("tensor", ("dp", "seq")),
            P(),
            P(),
            P(),
        ),
        check_vma=False,
    )
```

```python
import functools

import jax
import jax.numpy as jnp
from jax import lax
from jax.experimental import pallas as pl
from jax.experimental.pallas import tpu as pltpu
from jax.sharding import PartitionSpec as P

HEAD_DIM = 64
EPS = 1e-05
NEG = -1e30
BF16 = jnp.bfloat16
F32 = jnp.float32
NT = (((1,), (1,)), ((), ()))
TN = (((0,), (0,)), ((), ()))
KEY_BLOCK = 512
DOCS = 4


def dot_plain(left, right):
    return jnp.dot(left, right, preferred_element_type=F32)


def dot_last(left, right):
    return lax.dot_general(left, right, NT, preferred_element_type=F32)


def dot_first(left, right):
    return lax.dot_general(left, right, TN, preferred_element_type=F32)


def column_sum(value):
    return jnp.sum(value.astype(F32), axis=0)


def rounded(value):
    return lax.reduce_precision(value, 8, 7)


def norm_forward(hidden, gain, shift):
    centered = hidden - jnp.mean(hidden, axis=-1, keepdims=True)
    spread = jnp.mean(centered * centered, axis=-1, keepdims=True)
    factor = lax.rsqrt(spread + EPS)
    normed = centered * factor
    return (normed * gain.astype(F32) + shift.astype(F32), (normed, factor))


def norm_backward(grad, saved, gain):
    normed, factor = saved
    scaled = grad * gain.astype(F32)
    centered = scaled - jnp.mean(scaled, axis=-1, keepdims=True)
    grad_hidden = factor * (centered - normed * jnp.mean(scaled * normed, axis=-1, keepdims=True))
    return (grad_hidden, jnp.sum(grad * normed, axis=0), jnp.sum(grad, axis=0))


def head_columns(head):
    return slice(head // 2 * 128, head // 2 * 128 + 128)


def head_rows(head):
    return slice(head * HEAD_DIM, (head + 1) * HEAD_DIM)


def own_lanes(shape, head):
    lanes = lax.broadcasted_iota(jnp.int32, shape, 1)
    return lanes >= HEAD_DIM if head % 2 else lanes < HEAD_DIM


class Mask:
    def __init__(self, causal, starts, segments, first_row):
        self.causal, self.starts, self.first_row = causal, starts, first_row
        segments = segments[...]
        low = high = jnp.zeros_like(segments)
        for number in range(DOCS):
            low = jnp.where(segments == number, starts[number], low)
            high = jnp.where(segments == number, starts[number + 1], high)
        self.count = segments.shape[1]
        if causal:
            place = first_row + lax.broadcasted_iota(jnp.int32, segments.shape, 1)
            high = jnp.minimum(high, place + 1)
        self.low, self.high = low, high

    def allowed(self, index, block):
        place = lax.broadcasted_iota(jnp.int32, (block, self.count), 0) + index * block
        return (place >= self.low) & (place < self.high)

    def flag(self, index, block, ends):
        start, stop = index * block, (index + 1) * block
        low, low_last = self.starts[ends[0]], self.starts[ends[1]]
        high_first, high = self.starts[ends[0] + 1], self.starts[ends[1] + 1]
        if self.causal:
            high = jnp.minimum(high, self.first_row + self.count)
            high_first = jnp.minimum(high_first, self.first_row + 1)
        active = (low < stop) & (high > start)
        full = (low_last <= start) & (high_first >= stop)
        return jnp.where(active, jnp.where(full, 2, 1), 0)


def over_blocks(mask, ends, length, block, body, skipped):
    @pl.loop(0, length // block)
    def _(index):
        flag = mask.flag(index, block, ends)
        rows = pl.ds(pl.multiple_of(index * block, block), block)

        @pl.when(flag == 0)
        def _():
            skipped(rows)

        @pl.when(flag == 1)
        def _():
            body(index, rows, True)

        @pl.when(flag == 2)
        def _():
            body(index, rows, False)


def forward_start(q_ref, masked_q, acc, top):
    heads = q_ref.shape[1] // HEAD_DIM
    for head in range(heads):
        pair = q_ref[:, head_columns(head)]
        masked_q[head] = jnp.where(own_lanes(pair.shape, head), pair, jnp.zeros_like(pair))
    acc[...] = jnp.zeros_like(acc)
    top[...] = jnp.full_like(top, NEG)


def forward_block(index, rows, partial, block, kv_ref, mask, masked_q, acc, top):
    heads, count = masked_q.shape[:2]
    width = heads * HEAD_DIM
    if partial:
        allowed = mask.allowed(index, block)
    for head in range(heads):
        cols = head_columns(head)
        scores = lax.dot_general(kv_ref[rows, cols], masked_q[head], NT, preferred_element_type=F32)
        if partial:
            scores = jnp.where(allowed, scores, NEG)
        old = top[head : head + 1, :]
        new = jnp.maximum(old, jnp.max(scores, axis=0, keepdims=True))
        weights = jnp.exp(scores - new).astype(BF16)
        vals = kv_ref[rows, width + cols.start : width + cols.stop]
        vals = jnp.where(own_lanes(vals.shape, head), vals, jnp.ones_like(vals))
        acc[head] = acc[head] * jnp.exp(old - new) + lax.dot_general(
            vals, weights, TN, preferred_element_type=F32
        )
        top[head : head + 1, :] = new


def forward_end(out_ref, lse_ref, acc, top):
    lse_ref[...] = jnp.zeros_like(lse_ref)
    for head in range(acc.shape[0]):
        first = head % 2 * HEAD_DIM
        total = acc[head, HEAD_DIM - first : HEAD_DIM - first + 1, :]
        out_ref[head_rows(head), :] = acc[head, first : first + HEAD_DIM, :] / total
        lse_ref[head : head + 1, :] = top[head : head + 1, :] + jnp.log(total)


def forward_kernel(
    block, causal, starts, ends, segments, q_ref, kv_ref, out_ref, lse_ref, masked_q, acc, top
):
    mask = Mask(causal, starts, segments, ends[2])
    forward_start(q_ref, masked_q, acc, top)

    def body(index, rows, partial):
        forward_block(index, rows, partial, block, kv_ref, mask, masked_q, acc, top)

    over_blocks(mask, ends, kv_ref.shape[0], block, body, lambda rows: None)
    forward_end(out_ref, lse_ref, acc, top)


def backward_start(q_ref, do_ref, dot_ref, out_ref, masked_q, masked_do, delta, dq):
    for head in range(masked_q.shape[0]):
        pair = q_ref[:, head_columns(head)]
        keep = own_lanes(pair.shape, head)
        masked_q[head] = jnp.where(keep, pair, jnp.zeros_like(pair))
        pair = do_ref[:, head_columns(head)]
        masked_do[head] = jnp.where(keep, pair, jnp.zeros_like(pair))
        part = head_rows(head)
        delta[head : head + 1, :] = jnp.sum(
            dot_ref[part, :].astype(F32) * out_ref[part, :], axis=0, keepdims=True
        )
    dq[...] = jnp.zeros_like(dq)


def backward_block(
    index, rows, partial, block, mask, kv_ref, lse_ref, dkv_ref, masked_q, masked_do, delta, dq
):
    heads = masked_q.shape[0]
    width = heads * HEAD_DIM
    if partial:
        allowed = mask.allowed(index, block)
    for pair in range(heads // 2):
        cols = head_columns(2 * pair)
        later = slice(width + cols.start, width + cols.stop)
        keys, vals = kv_ref[rows, cols], kv_ref[rows, later]
        dk = dv = 0.0
        for head in (2 * pair, 2 * pair + 1):
            scores = lax.dot_general(keys, masked_q[head], NT, preferred_element_type=F32)
            probs = jnp.exp(scores - lse_ref[head : head + 1, :])
            if partial:
                probs = jnp.where(allowed, probs, 0.0)
            dprobs = lax.dot_general(vals, masked_do[head], NT, preferred_element_type=F32)
            draw = (probs * (dprobs - delta[head : head + 1, :])).astype(BF16)
            probs = probs.astype(BF16)
            dv = dv + jnp.dot(probs, masked_do[head], preferred_element_type=F32)
            dk = dk + jnp.dot(draw, masked_q[head], preferred_element_type=F32)
            first = head % 2 * HEAD_DIM
            both = lax.dot_general(keys, draw, TN, preferred_element_type=F32)
            dq[head_rows(head), :] += both[first : first + HEAD_DIM]
        dkv_ref[rows, cols] = dk.astype(BF16)
        dkv_ref[rows, later] = dv.astype(BF16)


SCALARS = pl.BlockSpec(memory_space=pltpu.SMEM)
VECTORS = pl.BlockSpec(memory_space=pltpu.VMEM)


ANYWHERE = pl.BlockSpec(memory_space=pl.ANY)


def cost_of(kv, count, width, products):
    flops = 2 * products * kv.shape[0] * count * width
    return pl.CostEstimate(flops=flops, bytes_accessed=flops // 512, transcendentals=0)


def forward_scratch(count, width):
    heads = width // HEAD_DIM
    return [
        pltpu.VMEM((heads, count, 128), BF16),
        pltpu.VMEM((heads, 128, count), F32),
        pltpu.VMEM((8, count), F32),
    ]


def backward_scratch(count, width):
    heads = width // HEAD_DIM
    return [
        pltpu.VMEM((heads, count, 128), BF16),
        pltpu.VMEM((heads, count, 128), BF16),
        pltpu.VMEM((8, count), F32),
        pltpu.VMEM((width, count), F32),
    ]


def attend(queries, kv, mask):
    count, width = queries.shape
    causal, starts, ends, segments = mask
    return pl.pallas_call(
        functools.partial(forward_kernel, KEY_BLOCK, causal),
        out_shape=(
            jax.ShapeDtypeStruct((width, count), F32),
            jax.ShapeDtypeStruct((8, count), F32),
        ),
        in_specs=[SCALARS] * 2 + [VECTORS] * 3,
        out_specs=(VECTORS,) * 2,
        scratch_shapes=forward_scratch(count, width),
        compiler_params=pltpu.CompilerParams(vmem_limit_bytes=40 << 20),
        cost_estimate=cost_of(kv, count, width, 2),
    )(starts, ends, segments, queries, kv)


MESH = pl.DeviceIdType.MESH
DMA = pltpu.SemaphoreType.DMA


class Here:
    def __init__(self, ring):
        self.ring = ring
        self.d, self.z, self.y = (lax.axis_index(a) for a in ("dp", "seq", "tensor"))
        self.core, self.x = lax.rem(self.d, 2), lax.div(self.d, 2)
        self.other_d = self.d + 1 - 2 * self.core
        self.partner = (self.other_d, self.z, self.y)
        self.right = (self.d, self.z + 1, self.y)
        self.left = (self.d, self.z - 1, self.y)
        self.over_x = (self.d + 2 - 4 * lax.rem(self.x, 2), self.z, self.y)
        self.over_y = (self.d, self.z, 1 - self.y)
        self.diagonal = (self.other_d, self.z, 1 - self.y)

    def meet(self, devices):
        barrier = pltpu.get_barrier_semaphore()
        wanted = 0
        for condition, device in devices:

            @pl.when(condition)
            def _(device=device):
                pl.semaphore_signal(barrier, inc=1, device_id=device, device_id_type=MESH)

            wanted = wanted + jnp.where(condition, 1, 0)
        pl.semaphore_wait(barrier, wanted)

    def along_z(self, step):
        return (self.d, lax.rem(self.z + step, self.ring), self.y)

    def everyone(self):
        devices = [self.partner, self.over_x, self.over_y, self.diagonal]
        devices += [self.along_z(step) for step in range(1, self.ring)]
        return [(self.core >= 0, device) for device in devices]

    def neighbours(self):
        return [
            (self.core >= 0, self.partner),
            (self.z + 1 < self.ring, self.right),
            (self.z > 0, self.left),
        ]


def remote(source, target, sent, received, device):
    return pltpu.make_async_remote_copy(
        src_ref=source,
        dst_ref=target,
        send_sem=sent,
        recv_sem=received,
        device_id=device,
        device_id_type=MESH,
    )


class Gather:
    def __init__(self, here, rows_ref, sems):
        self.here, self.rows_ref = here, rows_ref
        self.count = rows_ref.shape[0] // here.ring
        self.sent, self.got, self.core_sent, self.core_got = sems

    def half(self, shard, core):
        part = self.count // 2
        start = pl.multiple_of(shard * self.count + core * part, part)
        return self.rows_ref.at[pl.ds(start, part)]

    def ways(self, step):
        here = self.here
        z, ring = here.z, here.ring
        return [
            (0, z - step, z >= step, z - step + 1, (z + 1 < ring) & (z + 1 >= step), here.right),
            (1, z + step, z + step < ring, z + step - 1, (z > 0) & (z + step <= ring), here.left),
        ]

    def along(self, way, step, shard, device):
        view = self.half(shard, self.here.core)
        return remote(view, view, self.sent.at[way, step], self.got.at[way, step], device)

    def across(self, way, step, shard, core):
        view = self.half(shard, core)
        return remote(
            view, view, self.core_sent.at[way, step], self.core_got.at[way, step], self.here.partner
        )

    def start(self, step):
        for way, _, _, shard, sends, device in self.ways(step):

            @pl.when(sends)
            def _(way=way, shard=shard, device=device):
                self.along(way, step, shard, device).start()

    def arrive(self, step):
        for way, shard, comes, _, _, device in self.ways(step):

            @pl.when(comes)
            def _(way=way, shard=shard, device=device):
                self.along(way, step, shard, self.here.partner).wait_recv()
                self.across(way, step, shard, self.here.core).start()

    def finish(self, step):
        for way, shard, comes, out, sends, device in self.ways(step):

            @pl.when(sends)
            def _(way=way, out=out, device=device):
                self.along(way, step, out, device).wait_send()

            @pl.when(comes)
            def _(way=way, shard=shard):
                self.across(way, step, shard, self.here.core).wait_send()
                self.across(way, step, shard, 1 - self.here.core).wait_recv()


class Fetch:
    def __init__(self, here, inputs, outputs, sems):
        self.here, self.inputs, self.outputs = here, inputs, outputs
        self.y_sent, self.y_got, self.x_sent, self.x_got, self.core_sent, self.core_got = sems
        self.x_partner = (here.d + 2 - 4 * lax.rem(here.x, 2), here.z, here.y)
        self.y_partner = (here.other_d, here.z, 1 - here.y)

    def devices(self):
        here = self.here
        return [(here.core >= 0, self.y_partner), (here.core == 1, self.x_partner)]

    def part(self, ref, which):
        rows = ref.shape[0] // 2
        return ref.at[pl.ds(pl.multiple_of(which * rows, rows), rows)]

    def over_y(self, k):
        which = lax.rem(self.here.x, 2)
        return remote(
            self.part(self.inputs[k], which),
            self.part(self.outputs[k], which),
            self.y_sent.at[k],
            self.y_got.at[k],
            self.y_partner,
        )

    def over_x(self, k, which):
        view = self.part(self.outputs[k], which)
        return remote(view, view, self.x_sent.at[k], self.x_got.at[k], self.x_partner)

    def across(self, k):
        return remote(
            self.inputs[k], self.outputs[k], self.core_sent.at[k], self.core_got.at[k], self.here.partner
        )

    def begin(self):
        @pl.when(self.here.core == 0)
        def _():
            for k in range(min(2, len(self.inputs))):
                self.over_y(k).start()

        @pl.when(self.here.core == 1)
        def _():
            for k in range(len(self.inputs)):
                self.across(k).start()

    def advance(self, k):
        @pl.when(self.here.core == 0)
        def _():
            self.over_y(k).wait_send()
            if k + 2 < len(self.inputs):
                self.over_y(k + 2).start()

        @pl.when(self.here.core == 1)
        def _():
            self.over_y(k).wait_recv()
            self.over_x(k, lax.rem(self.here.x, 2)).start()

    def end(self):
        @pl.when(self.here.core == 0)
        def _():
            for k in range(len(self.inputs)):
                self.across(k).wait_recv()

        @pl.when(self.here.core == 1)
        def _():
            for k in range(len(self.inputs)):
                self.over_x(k, lax.rem(self.here.x, 2)).wait_send()
                self.over_x(k, 1 - lax.rem(self.here.x, 2)).wait_recv()
                self.across(k).wait_send()


def gather_sems(ring):
    return [DMA((2, ring))] * 4


def fetch_sems(number):
    return [DMA((number,))] * 6


def opening_kernel(ring, number, *refs):
    inputs, outputs, sems = refs[: 4 + number], refs[4 + number : 8 + 2 * number], refs[8 + 2 * number :]
    source, target, segments, vectors = inputs[:4]
    source_all, target_all, segments_out, vectors_out = outputs[:4]
    shard_sems, vector_sems = sems[:3], sems[3:6]
    here = Here(ring)
    fetch = Fetch(here, inputs[4:], outputs[4:], sems[14:])
    here.meet(here.neighbours() + fetch.devices())
    count = source.shape[0]
    own = pl.ds(pl.multiple_of(here.z * count, count), count)
    moves = [
        (source, source_all.at[own]),
        (target, target_all.at[own]),
        (segments, segments_out),
    ]
    owner = here.core == here.y

    def shard_copy(k):
        start, end = moves[k]
        sent, got, copied = shard_sems
        return (
            remote(start, end, sent.at[k], got.at[k], here.partner),
            pltpu.make_async_copy(start, end, copied.at[k]),
        )

    def vector_copy():
        sent, got, copied = vector_sems
        return (
            remote(vectors, vectors_out, sent, got, fetch.y_partner),
            pltpu.make_async_copy(vectors, vectors_out, copied),
        )

    def wait_shard(k):
        across, local = shard_copy(k)

        @pl.when(owner)
        def _():
            across.wait_send()
            local.wait()

        @pl.when(jnp.logical_not(owner))
        def _():
            across.wait_recv()

    @pl.when(owner)
    def _():
        for k in range(3):
            across, local = shard_copy(k)
            across.start()
            local.start()

    @pl.when(here.core == 0)
    def _():
        across, local = vector_copy()
        across.start()
        local.start()

    fetch.begin()
    gathers = [Gather(here, source_all, sems[6:10]), Gather(here, target_all, sems[10:14])]
    slots = 2 * (ring - 1)
    done = 0
    for k, gather in enumerate(gathers):
        wait_shard(k)
        for step in range(1, ring):
            gather.start(step)
            slot = k * (ring - 1) + step
            while done < number * slot // slots:
                fetch.advance(done)
                done += 1
            gather.arrive(step)
    for gather in gathers:
        for step in range(1, ring):
            gather.finish(step)
    wait_shard(2)
    fetch.end()
    across, local = vector_copy()

    @pl.when(here.core == 0)
    def _():
        across.wait_send()
        local.wait()

    @pl.when(here.core == 1)
    def _():
        across.wait_recv()


def opening(ring, source, target, segments, vectors, weights):
    inputs = (source, target, segments, vectors) + tuple(weights)
    count, model = source.shape
    rows = jax.ShapeDtypeStruct((ring * count, model), BF16)
    shapes = (rows, rows) + tuple(jax.ShapeDtypeStruct(v.shape, v.dtype) for v in inputs[2:])
    number = len(weights)
    return pl.pallas_call(
        functools.partial(opening_kernel, ring, number),
        out_shape=shapes,
        in_specs=[VECTORS] * 4 + [ANYWHERE] * number,
        out_specs=(ANYWHERE,) * 2 + (VECTORS,) * 2 + (ANYWHERE,) * number,
        scratch_shapes=[DMA((3,))] * 3 + [DMA] * 3 + gather_sems(ring) * 2 + fetch_sems(number),
        compiler_params=pltpu.CompilerParams(collective_id=1, has_side_effects=True),
    )(*inputs)


def gather_attend_kernel(block, causal, ring, tokens, starts, segments, q_ref, kv_ref, own_ref, *refs):
    out_ref, lse_ref, all_ref, masked_q, acc, top, copied = refs[tokens : tokens + 7]
    here = Here(ring)
    gather = Gather(here, all_ref, refs[tokens + 7 :])
    here.meet(here.neighbours())
    count = own_ref.shape[0]
    first_row = pl.multiple_of(here.z * count, count)
    local = pltpu.make_async_copy(own_ref, all_ref.at[pl.ds(first_row, count)], copied)
    local.start()
    local.wait()
    gather.start(1)
    mask = Mask(causal, starts, segments, first_row)
    forward_start(q_ref, masked_q, acc, top)

    @pl.loop(0, kv_ref.shape[0] // block)
    def _(index):
        rows = pl.ds(pl.multiple_of(index * block, block), block)
        forward_block(index, rows, True, block, kv_ref, mask, masked_q, acc, top)

        @pl.when((index >= 1) & (index < ring))
        def _():
            gather.arrive(index)

        @pl.when((index >= 1) & (index < ring - 1))
        def _():
            gather.start(index + 1)

    forward_end(out_ref, lse_ref, acc, top)

    @pl.loop(1, ring)
    def _(step):
        gather.finish(step)


def gather_attend(ring, queries, kv, mask, own, tokens):
    count, width = queries.shape
    causal, starts, _, segments = mask
    return pl.pallas_call(
        functools.partial(gather_attend_kernel, KEY_BLOCK, causal, ring, len(tokens)),
        out_shape=(
            jax.ShapeDtypeStruct((width, count), F32),
            jax.ShapeDtypeStruct((8, count), F32),
            jax.ShapeDtypeStruct((ring * own.shape[0], own.shape[1]), BF16),
        ),
        in_specs=[SCALARS] + [VECTORS] * 4 + [ANYWHERE] * len(tokens),
        out_specs=(VECTORS, VECTORS, ANYWHERE),
        scratch_shapes=forward_scratch(count, width) + [DMA] + gather_sems(ring),
        compiler_params=pltpu.CompilerParams(
            vmem_limit_bytes=40 << 20, collective_id=2, has_side_effects=True
        ),
        cost_estimate=cost_of(kv, count, width, 2),
    )(starts, segments, queries, kv, own, *tokens)


class Part:
    def __init__(self, inputs, in_specs, out_shapes, scratch, bind):
        self.inputs, self.in_specs, self.out_shapes = inputs, in_specs, out_shapes
        self.scratch, self.bind = scratch, bind


def run_parts(number, body, parts, cost=None):
    ring = lax.axis_size("seq")
    counts = [(len(p.inputs), len(p.out_shapes), len(p.scratch)) for p in parts]

    def kernel(*refs):
        here = Here(ring)
        taken, offset = [[] for _ in parts], 0
        for kind in range(3):
            for refs_of, count in zip(taken, counts):
                refs_of.append(refs[offset : offset + count[kind]])
                offset += count[kind]
        here.meet(here.everyone())
        body(here, *(p.bind(here, *refs_of) for p, refs_of in zip(parts, taken)))

    results = pl.pallas_call(
        kernel,
        out_shape=[shape for p in parts for shape in p.out_shapes],
        in_specs=[spec for p in parts for spec in p.in_specs],
        out_specs=[VECTORS for p in parts for _ in p.out_shapes],
        scratch_shapes=[shape for p in parts for shape in p.scratch],
        compiler_params=pltpu.CompilerParams(
            vmem_limit_bytes=60 << 20, collective_id=number, has_side_effects=True
        ),
        cost_estimate=cost,
    )(*(array for p in parts for array in p.inputs))
    given = []
    for _, count, _ in counts:
        given.append(results[:count])
        results = results[count:]
    return given


class Stage:
    def __init__(self, here, kind, source, result, buffers, sems):
        self.here, self.kind, self.source, self.result = here, kind, source, result
        self.buffers, (self.sent, self.got) = buffers, sems
        rows = source.shape[0]
        if kind == "x":
            half = rows // 2
            self.kept = [half * here.x]
            self.given = [half * (1 - here.x)]
            self.size, self.to = half, here.over_x
        elif kind == "y":
            self.size = 192
            self.starts = list(range(0, rows, 2 * self.size))
        elif kind == "v":
            bit = lax.rem(here.z, 2)
            self.size = rows // 4
            self.kept = [self.size * bit, self.size * (bit + 2)]
            self.given = [self.size * (1 - bit), self.size * (3 - bit)]
            self.to = (here.d, here.z + 1 - 2 * bit, here.y)
        else:
            bit = lax.div(here.z, 2)
            self.size = rows // 2
            self.kept, self.given = [self.size * bit], [self.size * (1 - bit)]
            self.to = (here.d, here.z + 2 - 4 * bit, here.y)

    def rows(self, start):
        if not isinstance(start, int):
            start = pl.multiple_of(start, 16)
        return pl.ds(start, self.size)

    def move(self, start, place, buffer, sem, to):
        return remote(
            self.source.at[self.rows(start)],
            self.buffers[buffer].at[self.rows(place * self.size)],
            self.sent.at[sem],
            self.got.at[sem],
            to,
        )

    def moves(self):
        here = self.here
        if self.kind != "y":
            both = [
                (None, self.move(start, k, 0, k, self.to)) for k, start in enumerate(self.given)
            ]
            return both, both
        sends, arrivals = [], []
        for k, start in enumerate(self.starts):
            upper = start + self.size
            sends.append((here.core == 0, self.move(upper, k, 0, 2 * k, here.partner)))
            sends.append((here.core == 1, self.move(start, k, 0, 2 * k, here.diagonal)))
            sends.append((here.core == 1, self.move(upper, k, 1, 2 * k + 1, here.over_y)))
            arrivals.append((None, self.move(upper, k, 0, 2 * k, here.partner)))
            arrivals.append((here.core == 1, self.move(upper, k, 1, 2 * k + 1, here.over_y)))
        return sends, arrivals

    @staticmethod
    def each(moves, act):
        for condition, copy in moves:
            if condition is None:
                act(copy)
            else:
                pl.when(condition)(functools.partial(act, copy))

    def begin(self):
        self.each(self.moves()[0], lambda copy: copy.start())

    def end(self):
        sends, arrivals = self.moves()
        self.each(arrivals, lambda copy: copy.wait_recv())
        kept = self.kept if self.kind != "y" else self.starts
        for k, start in enumerate(kept):
            place = self.rows(k * self.size)

            def add(own_ref, own, place=place):
                both = own_ref[own, :].astype(F32) + self.buffers[0][place, :].astype(F32)
                self.result[place, :] = both.astype(self.result.dtype)

            if self.kind == "y":
                pl.when(self.here.core == 0)(functools.partial(add, self.source, self.rows(start)))
                pl.when(self.here.core == 1)(functools.partial(add, self.buffers[1], place))
            else:
                add(self.source, self.rows(start))
        self.each(sends, lambda copy: copy.wait_send())


class Chain:
    def __init__(self, stages, times):
        self.stages, self.times = stages, times

    def event(self, time):
        for k, own in enumerate(self.times):
            if own == time:
                if k:
                    self.stages[k - 1].end()
                if k < len(self.stages):
                    self.stages[k].begin()


def chain(array, kinds, times):
    rows, columns = array.shape
    scratch, shapes = [], []
    for kind in kinds:
        rows = rows // 2
        scratch += [pltpu.VMEM((rows, columns), BF16)] * (2 if kind == "y" else 1)
        scratch += [DMA((4,))] * 2
        shapes.append((rows, columns))
    scratch += [pltpu.VMEM(shape, BF16) for shape in shapes[:-1]]
    final = jax.ShapeDtypeStruct(shapes[-1], F32 if kinds[-1] == "w" else BF16)

    def bind(here, inputs, outputs, refs):
        refs = list(refs)
        results = refs[len(refs) - len(kinds) + 1 :] + [outputs[0]]
        source, stages = inputs[0], []
        for kind, result in zip(kinds, results):
            buffers = [refs.pop(0) for _ in range(2 if kind == "y" else 1)]
            sems = [refs.pop(0) for _ in range(2)]
            stages.append(Stage(here, kind, source, result, buffers, sems))
            source = result
        return Chain(stages, times)

    return Part((array,), [VECTORS], [final], scratch, bind)


def run_chains(number, chains, events):
    def body(here, *bound):
        for time in range(events):
            for one in bound:
                one.event(time)

    return [given[0] for given in run_parts(number, body, chains)]


class Back:
    def __init__(self, here, causal, apart, inputs, outputs, scratch):
        self.here, self.causal, self.apart = here, causal, apart
        self.starts, self.segments, self.q, self.kv, self.do, self.dot, self.out, self.lse = inputs[:8]
        self.w_q, self.w_kv = inputs[8:]
        self.dq_out, self.dkv, self.sum = outputs[:3]
        self.query_sum = outputs[3] if apart else None
        self.work, scratch = scratch[:4], scratch[4:]
        self.terms, self.from_core, self.outgoing, self.arrived, self.total = scratch[:5]
        self.core_sent, self.core_got, self.sent, self.got, self.end_sent, self.end_got = scratch[5:11]
        if apart:
            self.query_low, self.query_got, self.query_sems = scratch[11:]
        self.count = self.q.shape[0]
        self.part = self.count // 2
        self.mask = Mask(causal, self.starts, self.segments, here.z * self.count)

    def half(self, core):
        return pl.ds(pl.multiple_of(core * self.part, self.part), self.part)

    def across(self, step):
        return remote(
            self.terms.at[step, self.half(1 - self.here.core)],
            self.from_core.at[step],
            self.core_sent.at[step],
            self.core_got.at[step],
            self.here.partner,
        )

    def along(self, step):
        return remote(
            self.outgoing.at[step],
            self.arrived.at[step],
            self.sent.at[step],
            self.got.at[step],
            self.here.along_z(step),
        )

    def both(self, step):
        self.across(step).wait_recv()
        own = self.terms[step, self.half(self.here.core), :].astype(F32)
        return own + self.from_core[step].astype(F32)

    def forward(self, step):
        self.outgoing[step] = self.both(step).astype(BF16)
        self.along(step).start()

    def block(self, step):
        shard = lax.rem(self.here.z + step, self.here.ring)
        rows = pl.ds(pl.multiple_of(shard * self.count, self.count), self.count)
        backward_block(
            shard, rows, True, self.count, self.mask, self.kv, self.lse, self.dkv, *self.work
        )
        return dot_last(self.dkv[rows, :], self.w_kv[...])

    def run(self, event):
        ring = self.here.ring
        event(0)
        backward_start(self.q, self.do, self.dot, self.out, *self.work)

        @pl.loop(1, ring)
        def _(step):
            self.terms[step] = self.block(step).astype(BF16)
            self.across(step).start()

            @pl.when(step > 1)
            def _():
                self.forward(step - 1)

            for time in range(1, ring):
                pl.when(step == time)(functools.partial(event, time))

        own = self.block(0)
        self.forward(ring - 1)
        event(ring)
        low = (self.work[3][...] * HEAD_DIM ** (-0.5)).T.astype(BF16)
        self.dq_out[...] = low
        query = dot_last(low, self.w_q[...])
        if self.apart:
            self.query_low[...] = query.astype(BF16)
            exchange = remote(
                self.query_low, self.query_got, self.query_sems.at[0], self.query_sems.at[1], self.here.partner
            )
            exchange.start()
        else:
            own = own + query
        self.terms[0] = own.astype(BF16)
        self.across(0).start()
        if self.apart:
            exchange.wait()
            self.query_sum[...] = self.query_low[...].astype(F32) + self.query_got[...].astype(F32)
        self.total[...] = self.both(0)
        event(ring + 1)
        for step in range(1, ring):
            self.along(step).wait_recv()
            self.total[...] += self.arrived[step].astype(F32)
        own, other = self.half(self.here.core), self.half(1 - self.here.core)
        self.sum[own, :] = self.total[...].astype(BF16)
        for half, waits in ((own, False), (other, True)):
            view = self.sum.at[half]
            copy = remote(view, view, self.end_sent, self.end_got, self.here.partner)
            if waits:
                copy.wait_recv()
            else:
                copy.start()
                copy.wait_send()
        for step in range(ring):
            self.across(step).wait_send()
            if step:
                self.along(step).wait_send()
        event(ring + 2)


def attend_back(number, saved, grad_mixed, grad_mixed_t, weights, mask, apart, chains):
    queries, kv, output, lse, _ = saved
    causal, starts, segments = mask
    ring = lax.axis_size("seq")
    count, width = queries.shape
    model = weights[0].shape[0]
    part = count // 2
    shapes = [
        jax.ShapeDtypeStruct((count, width), BF16),
        jax.ShapeDtypeStruct(kv.shape, BF16),
        jax.ShapeDtypeStruct((count, model), BF16),
    ]
    scratch = backward_scratch(count, width) + [
        pltpu.VMEM((ring, count, model), BF16),
        *[pltpu.VMEM((ring, part, model), BF16)] * 3,
        pltpu.VMEM((part, model), F32),
        *[DMA((ring,))] * 4,
        *[DMA] * 2,
    ]
    if apart:
        shapes.append(jax.ShapeDtypeStruct((count, model), F32))
        scratch += [pltpu.VMEM((count, model), BF16)] * 2 + [DMA((2,))]
    main = Part(
        (starts, segments, queries, kv, grad_mixed, grad_mixed_t, output, lse, *weights[:2]),
        [SCALARS] + [VECTORS] * 9,
        shapes,
        scratch,
        lambda here, *refs: Back(here, causal, apart, *refs),
    )

    def body(here, back, *bound):
        def event(time):
            for one in bound:
                one.event(time)

        back.run(event)

    first, *rest = run_parts(number, body, [main] + list(chains), cost_of(kv, count, width, 7))
    return first, [given[0] for given in rest]


class Plan:
    def __init__(self, kernels):
        self.kernels = kernels

    def chains(self, wanted):
        return [chain(*one) for one in wanted] if self.kernels else []

    def given(self, wanted, results):
        return results if self.kernels else [one[0] for one in wanted]


class Places:
    def __init__(self, pairs, ring):
        self.pairs, self.ring = pairs, ring
        self.d = lax.axis_index("dp")
        self.x, self.core = self.d // 2, self.d % 2
        self.y, self.z = lax.axis_index("tensor"), lax.axis_index("seq")

    def swap_core(self, value):
        return lax.ppermute(value, "dp", [(i, i ^ 1) for i in range(self.pairs)])

    def swap_y(self, value):
        return lax.ppermute(value, "tensor", [(0, 1), (1, 0)])

    def swap_x(self, value, bit):
        return lax.ppermute(value, "dp", [(i, i ^ (2 << bit)) for i in range(self.pairs)])

    def swap_z(self, value, bit):
        return lax.ppermute(value, "seq", [(i, i ^ (1 << bit)) for i in range(self.ring)])

    def from_z(self, value, step):
        return lax.ppermute(value, "seq", [((i + step) % self.ring, i) for i in range(self.ring)])

    def to_z(self, value, step):
        return lax.ppermute(value, "seq", [(i, (i + step) % self.ring) for i in range(self.ring)])

    def permute(self, value, source_of):
        moves = []
        for d in range(self.pairs):
            for y in range(2):
                source = source_of(d, y)
                if source is not None:
                    moves.append((source[0] * 2 + source[1], d * 2 + y))
        return lax.ppermute(value, ("dp", "tensor"), moves)

    def fetch_weight(self, value):
        return self.permute(value, lambda d, y: (d + 1, y) if d % 2 == 0 else (d - 1, 1 - y))

    def core_sum(self, partial):
        low = rounded(partial)
        return low + self.swap_core(low.astype(BF16)).astype(F32)

    def own_pair(self, rows):
        return jnp.where(self.core == self.y, rows, self.swap_core(rows))

    def hand_out(self, rows):
        other = self.permute(rows, lambda d, y: (d, 1 - y) if d % 2 != y else None)
        return jnp.where(self.core == self.y, rows, other)

    def plan(self):
        return Plan(self.pairs == 4 and self.ring == 4)

    def scatter(self, grad, x_first):
        rows, columns = grad.shape
        owners = self.pairs // 2
        grad = grad.reshape(owners, 2, self.ring, rows // (self.pairs * self.ring), columns)
        for stage in "xyz" if x_first else "yxz":
            if stage == "y":
                kept = lax.dynamic_index_in_dim(grad, self.core, grad.ndim - 4, False)
                sent = lax.dynamic_index_in_dim(grad, 1 - self.core, grad.ndim - 4, False)
                first = self.permute(
                    sent, lambda d, y: (d + 1, 1 - y) if d % 2 == 0 else (d - 1, y)
                )
                second = self.permute(kept, lambda d, y: (d, 1 - y) if d % 2 else None)
                kept = jnp.where(self.core == 0, kept, second)
                grad = (kept.astype(F32) + first.astype(F32)).astype(BF16)
            else:
                axis = 0 if stage == "x" else grad.ndim - 3
                place, swap = (self.x, self.swap_x) if stage == "x" else (self.z, self.swap_z)
                size, bit = grad.shape[axis], 0
                while size > 1:
                    shape = grad.shape[:axis] + (size // 2, 2) + grad.shape[axis + 1 :]
                    grad = grad.reshape(shape)
                    mine = (place >> bit) & 1
                    kept = lax.dynamic_index_in_dim(grad, mine, axis + 1, False)
                    sent = lax.dynamic_index_in_dim(grad, 1 - mine, axis + 1, False)
                    grad = kept.astype(F32) + swap(sent, bit).astype(F32)
                    size, bit = size // 2, bit + 1
                    if stage == "x" or size > 1:
                        grad = grad.astype(BF16)
                grad = lax.squeeze(grad, (axis,))
        return grad.astype(F32)

    def all_sum(self, whole, halves):
        both = jnp.concatenate([whole, halves])
        for bit in range((self.pairs // 2).bit_length() - 1):
            both = both + self.swap_x(both, bit)
        for bit in range(self.ring.bit_length() - 1):
            both = both + self.swap_z(both, bit)
        whole, halves = both[: whole.shape[0]], both[whole.shape[0] :]
        whole = whole + self.swap_y(whole)
        whole = (whole + self.swap_core(whole)) * 0.5
        first = self.permute(halves, lambda d, y: (d + 1, 1 - y) if d % 2 == 0 else (d - 1, y))
        second = self.swap_y(halves)
        halves = jnp.where(self.core == 0, halves, second) + first
        return whole, halves


def starts_of(segments):
    numbers = jnp.arange(8, dtype=jnp.int32)
    return jnp.sum(segments[None, :] < numbers[:, None], axis=1, dtype=jnp.int32)


def mask_of(query_seg, key_starts, first_row, causal):
    ends = jnp.stack([query_seg[0], query_seg[-1], first_row])
    return (causal, key_starts, ends, query_seg[None])


def projected(query_in, key_in, weights):
    w_q, w_kv, b_q, b_kv = weights
    scale = HEAD_DIM ** (-0.5)
    queries = ((dot_plain(query_in, w_q) + b_q).astype(BF16) * scale).astype(BF16)
    return queries, (dot_plain(key_in, w_kv) + b_kv).astype(BF16)


def attention_output(place, queries, kv, output, lse, out_weight, out_bias):
    mixed = output.astype(BF16)
    branch = place.core_sum(dot_first(mixed, out_weight)) + out_bias.astype(F32)
    return (branch, (queries, kv, output, lse, mixed))


def attention_backward(
    number, grad_branch, saved, query_in, key_in, weights, out_weight, mask, apart, plan, wanted
):
    mixed = saved[4]
    width = saved[0].shape[1]
    grad_mixed = dot_last(grad_branch, out_weight).astype(BF16)
    grad_mixed_t = dot_last(out_weight, grad_branch).astype(BF16)
    (grad_q, grad_kv, *sums), given = attend_back(
        number, saved, grad_mixed, grad_mixed_t, weights, mask, apart, plan.chains(wanted)
    )
    grads = (
        dot_first(query_in, grad_q).astype(BF16),
        lax.dot_general(
            grad_branch, mixed, (((0,), (1,)), ((), ())), preferred_element_type=F32
        ).astype(BF16),
        dot_first(key_in, grad_kv).astype(BF16),
    )
    grad_bias = jnp.concatenate([column_sum(grad_q), column_sum(grad_kv[:, width:])])
    return (sums, grads, grad_bias, plan.given(wanted, given))


def feed_forward(place, x_in, w_in, b_in, w_out, b_out):
    hidden = dot_plain(x_in, w_in) + b_in.astype(F32)
    active = jax.nn.gelu(hidden, approximate=False).astype(BF16)
    branch = place.core_sum(dot_plain(active, w_out)) + b_out.astype(F32)
    return (branch, (hidden, active))


def feed_backward(place, grad_branch, saved, x_in, w_in, w_out):
    hidden, active = saved
    grad_active = dot_last(grad_branch, w_out)
    slope = jax.vjp(lambda value: jax.nn.gelu(value, approximate=False), hidden)[1](grad_active)[0]
    grad_hidden = slope.astype(BF16)
    grad_in = place.core_sum(dot_last(grad_hidden, w_in))
    return (
        grad_in,
        dot_first(x_in, grad_hidden).astype(BF16),
        column_sum(grad_hidden),
        dot_first(grad_branch, active).astype(BF16),
    )


def shards(
    source,
    target,
    source_segments,
    target_segments,
    enc_qkv,
    enc_qv_bias,
    enc_proj,
    enc_ff_in,
    enc_ff_in_bias,
    enc_ff_out,
    enc_bias,
    enc_gains,
    enc_shifts,
    dec_self,
    dec_self_bias,
    dec_self_proj,
    dec_cross,
    dec_cross_bias,
    dec_cross_proj,
    dec_ff_in,
    dec_ff_in_bias,
    dec_ff_out,
    dec_bias,
    dec_gains,
    dec_shifts,
    enc_cotangent,
    dec_cotangent,
):
    count = source.shape[1]
    model = source.shape[2]
    place = Places(lax.axis_size("dp"), lax.axis_size("seq"))
    first_row = place.z * count

    ring = place.ring
    width = enc_qkv.shape[2]
    hidden_units = enc_ff_in.shape[1]

    vectors = jnp.concatenate(
        [
            enc_qv_bias.reshape(-1),
            dec_self_bias.reshape(-1),
            dec_cross_bias.reshape(-1),
            enc_ff_in_bias,
            dec_ff_in_bias,
        ]
    ).astype(F32)
    (
        x_all,
        t_all,
        segments,
        vectors,
        enc_qkv,
        dec_self,
        enc_proj,
        dec_self_proj,
        enc_ff_in,
        enc_ff_out,
        dec_cross,
        dec_cross_proj,
    ) = opening(
        ring,
        source[0],
        target[0],
        jnp.concatenate([source_segments, target_segments]),
        vectors.reshape(-1, 128),
        (
            enc_qkv.reshape(-1, width),
            dec_self.reshape(-1, width),
            enc_proj,
            dec_self_proj,
            enc_ff_in,
            enc_ff_out,
            dec_cross.reshape(-1, width),
            dec_cross_proj,
        ),
    )
    vectors = vectors.reshape(-1)
    xs = lax.dynamic_slice_in_dim(x_all, first_row, count, 0)
    ts = lax.dynamic_slice_in_dim(t_all, first_row, count, 0)
    dec_ff_in = place.fetch_weight(dec_ff_in)
    dec_ff_out = place.fetch_weight(dec_ff_out)
    enc_cot = place.own_pair(enc_cotangent[0])
    dec_cot = place.own_pair(dec_cotangent[0])

    marks = [0, 2 * width, 4 * width, 6 * width, 6 * width + hidden_units, 6 * width + 2 * hidden_units]
    enc_qv_bias, dec_self_bias, dec_cross_bias, enc_ff_in_bias, dec_ff_in_bias = (
        vectors[a:b] for a, b in zip(marks[:-1], marks[1:])
    )

    def prepared(qkv, bias):
        qkv = qkv.reshape(3, model, width)
        b_kv = jnp.concatenate([jnp.zeros((width,), F32), bias[width:]])
        return (qkv[0], jnp.concatenate([qkv[1], qkv[2]], axis=1), bias[:width], b_kv)

    enc_w = prepared(enc_qkv, enc_qv_bias)
    self_w = prepared(dec_self, dec_self_bias)
    cross_w = prepared(dec_cross, dec_cross_bias)

    source_keys, target_keys = segments[0], segments[1]
    source_own = lax.dynamic_slice_in_dim(source_keys, first_row, count, 0)
    target_own = lax.dynamic_slice_in_dim(target_keys, first_row, count, 0)
    source_starts, target_starts = starts_of(source_keys), starts_of(target_keys)
    enc_mask = mask_of(source_own, source_starts, first_row, False)
    self_mask = mask_of(target_own, target_starts, first_row, True)
    cross_mask = mask_of(target_own, source_starts, first_row, False)

    queries, kv = projected(xs, x_all, enc_w)
    output, lse = attend(queries, kv, enc_mask)
    branch, enc_attn = attention_output(place, queries, kv, output, lse, enc_proj, enc_bias[0])
    first, enc_norm_one = norm_forward(xs.astype(F32) + branch, enc_gains[0], enc_shifts[0])
    first_low = first.astype(BF16)
    branch, enc_feed = feed_forward(
        place, first_low, enc_ff_in, enc_ff_in_bias, enc_ff_out, enc_bias[1]
    )
    encoded, enc_norm_two = norm_forward(first + branch, enc_gains[1], enc_shifts[1])
    encoded_low = encoded.astype(BF16)

    queries, kv = projected(ts, t_all, self_w)
    output, lse, e_all = gather_attend(
        ring, queries, kv, self_mask, encoded_low, (dec_ff_in, dec_ff_out)
    )
    branch, self_attn = attention_output(
        place, queries, kv, output, lse, dec_self_proj, dec_bias[0]
    )
    second, dec_norm_one = norm_forward(ts.astype(F32) + branch, dec_gains[0], dec_shifts[0])
    second_low = second.astype(BF16)
    queries, kv = projected(second_low, e_all, cross_w)
    output, lse = attend(queries, kv, cross_mask)
    branch, cross_attn = attention_output(
        place, queries, kv, output, lse, dec_cross_proj, dec_bias[1]
    )
    third, dec_norm_two = norm_forward(second + branch, dec_gains[1], dec_shifts[1])
    third_low = third.astype(BF16)
    branch, dec_feed = feed_forward(
        place, third_low, dec_ff_in, dec_ff_in_bias, dec_ff_out, dec_bias[2]
    )
    decoded, dec_norm_three = norm_forward(third + branch, dec_gains[2], dec_shifts[2])

    def back_mask(mask):
        return (mask[0], mask[1], mask[3])

    grad_hidden, dec_gain_three, dec_shift_three = norm_backward(
        dec_cot.astype(F32), dec_norm_three, dec_gains[2]
    )
    grad_branch = grad_hidden.astype(BF16)
    feed_in, dec_w_in, dec_b_in, dec_w_out = feed_backward(
        place, grad_branch, dec_feed, third_low, dec_ff_in, dec_ff_out
    )
    dec_bias_three = column_sum(grad_branch)
    grad_third = grad_hidden + feed_in
    grad_hidden, dec_gain_two, dec_shift_two = norm_backward(grad_third, dec_norm_two, dec_gains[1])
    grad_branch = grad_hidden.astype(BF16)
    plan = place.plan()
    (key_total, query_total), cross_grads, cross_bias, (dec_w_in, dec_w_out) = attention_backward(
        3,
        grad_branch,
        cross_attn,
        second_low,
        e_all,
        cross_w,
        dec_cross_proj,
        back_mask(cross_mask),
        True,
        plan,
        [(dec_w_in, "x", (0, 6)), (dec_w_out, "y", (0, 6))],
    )
    dec_bias_two = column_sum(grad_branch)
    grad_second = grad_hidden + query_total
    grad_hidden, dec_gain_one, dec_shift_one = norm_backward(
        grad_second, dec_norm_one, dec_gains[0]
    )
    grad_branch = grad_hidden.astype(BF16)
    cross_q, cross_proj, cross_kv = cross_grads
    (target_total,), self_grads, self_bias, given = attention_backward(
        4,
        grad_branch,
        self_attn,
        ts,
        t_all,
        self_w,
        dec_self_proj,
        back_mask(self_mask),
        False,
        plan,
            [
                (dec_w_in, "y", (0, 6)),
                (dec_w_out, "x", (0, 6)),
                (cross_kv, "x", (0, 6)),
                (cross_q, "y", (0, 6)),
                (cross_proj, "y", (0, 6)),
            ],
    )
    dec_w_in, dec_w_out, cross_kv, cross_q, cross_proj = given
    dec_bias_one = column_sum(grad_branch)
    grad_target = grad_hidden + target_total.astype(F32)
    grad_hidden, enc_gain_two, enc_shift_two = norm_backward(
        enc_cot.astype(F32) + key_total.astype(F32), enc_norm_two, enc_gains[1]
    )
    grad_branch = grad_hidden.astype(BF16)
    feed_in, enc_w_in, enc_b_in, enc_w_out = feed_backward(
        place, grad_branch, enc_feed, first_low, enc_ff_in, enc_ff_out
    )
    enc_bias_two = column_sum(grad_branch)
    grad_first = grad_hidden + feed_in
    grad_hidden, enc_gain_one, enc_shift_one = norm_backward(grad_first, enc_norm_one, enc_gains[0])
    grad_branch = grad_hidden.astype(BF16)
    self_q, self_proj, self_kv = self_grads
    (source_total,), enc_grads, enc_bias_grad, given = attention_backward(
        5,
        grad_branch,
        enc_attn,
        xs,
        x_all,
        enc_w,
        enc_proj,
        back_mask(enc_mask),
        False,
        plan,
            [
                (cross_kv, "y", (0, 6)),
                (cross_q, "x", (0, 6)),
                (cross_proj, "x", (0, 6)),
                (enc_w_in, "x", (0, 6)),
                (enc_w_out, "y", (0, 6)),
                (dec_w_in, "vw", (0, 4, 6)),
                (dec_w_out, "vw", (0, 4, 6)),
            ],
    )
    cross_kv, cross_q, cross_proj, enc_w_in, enc_w_out, dec_w_in, dec_w_out = given
    enc_bias_one = column_sum(grad_branch)
    grad_source = grad_hidden + source_total.astype(F32)
    enc_q, enc_proj_grad, enc_kv = enc_grads
    rest = [
        (enc_kv, "xyvw", (0, 2, 4, 5, 6)),
        (enc_q, "yxvw", (0, 2, 4, 5, 6)),
        (enc_proj_grad, "yxvw", (0, 2, 4, 5, 6)),
        (self_kv, "xyvw", (0, 1, 3, 4, 5)),
        (self_q, "yxvw", (0, 1, 3, 4, 5)),
        (self_proj, "yxvw", (0, 1, 3, 4, 5)),
        (enc_w_in, "yvw", (0, 2, 3, 4)),
        (enc_w_out, "xvw", (0, 2, 3, 4)),
        (cross_kv, "vw", (0, 1, 2)),
        (cross_q, "vw", (0, 1, 2)),
        (cross_proj, "vw", (0, 1, 2)),
    ]
    if plan.kernels:
        given = run_chains(6, plan.chains(rest), 7)
    else:
        given = [place.scatter(array, True) for array, _, _ in rest]
        dec_w_in, dec_w_out = (place.scatter(array, True) for array in (dec_w_in, dec_w_out))
    enc_kv, enc_q, enc_proj_grad, self_kv, self_q, self_proj = given[:6]
    enc_w_in, enc_w_out, cross_kv, cross_q, cross_proj = given[6:]

    def qkv_grads(of_q, of_kv):
        return jnp.stack([of_q, of_kv[:, :width], of_kv[:, width:]])

    whole, halves = place.all_sum(
        jnp.concatenate(
            [
                enc_bias_one,
                enc_bias_two,
                enc_gain_one,
                enc_gain_two,
                enc_shift_one,
                enc_shift_two,
                dec_bias_one,
                dec_bias_two,
                dec_bias_three,
                dec_gain_one,
                dec_gain_two,
                dec_gain_three,
                dec_shift_one,
                dec_shift_two,
                dec_shift_three,
            ]
        ),
        jnp.concatenate([enc_bias_grad, self_bias, cross_bias, enc_b_in, dec_b_in]),
    )
    whole = whole.reshape(15, model)
    small = [halves[a:b] for a, b in zip(marks[:-1], marks[1:])]
    return (
        place.hand_out(encoded_low)[None],
        place.hand_out(decoded.astype(BF16))[None],
        place.hand_out(rounded(grad_source).astype(BF16)).astype(F32)[None],
        place.hand_out(rounded(grad_target).astype(BF16)).astype(F32)[None],
        qkv_grads(enc_q, enc_kv),
        small[0].reshape(2, width),
        enc_proj_grad.T,
        enc_w_in,
        small[3],
        enc_w_out.T,
        whole[0:2],
        whole[2:4],
        whole[4:6],
        qkv_grads(self_q, self_kv),
        small[1].reshape(2, width),
        self_proj.T,
        qkv_grads(cross_q, cross_kv),
        small[2].reshape(2, width),
        cross_proj.T,
        dec_w_in,
        small[4],
        dec_w_out.T,
        whole[6:9],
        whole[9:12],
        whole[12:15],
    )


def solution(mesh):
    return jax.shard_map(
        shards,
        mesh=mesh,
        in_specs=(
            P("dp", "seq", None),
            P("dp", "seq", None),
            P("dp", None),
            P("dp", None),
            P(None, None, "tensor"),
            P(None, "tensor"),
            P("tensor", None),
            P(None, "tensor"),
            P("tensor"),
            P("tensor", None),
            P(),
            P(),
            P(),
            P(None, None, "tensor"),
            P(None, "tensor"),
            P("tensor", None),
            P(None, None, "tensor"),
            P(None, "tensor"),
            P("tensor", None),
            P(None, "tensor"),
            P("tensor"),
            P("tensor", None),
            P(),
            P(),
            P(),
            P("dp", "seq", None),
            P("dp", "seq", None),
        ),
        out_specs=(
            P("dp", "seq", None),
            P("dp", "seq", None),
            P("dp", "seq", None),
            P("dp", "seq", None),
            P(None, ("dp", "seq"), "tensor"),
            P(None, "tensor"),
            P("tensor", ("dp", "seq")),
            P(("dp", "seq"), "tensor"),
            P("tensor"),
            P("tensor", ("dp", "seq")),
            P(),
            P(),
            P(),
            P(None, ("dp", "seq"), "tensor"),
            P(None, "tensor"),
            P("tensor", ("dp", "seq")),
            P(None, ("dp", "seq"), "tensor"),
            P(None, "tensor"),
            P("tensor", ("dp", "seq")),
            P(("dp", "seq"), "tensor"),
            P("tensor"),
            P("tensor", ("dp", "seq")),
            P(),
            P(),
            P(),
        ),
        check_vma=False,
    )
```

```python
import functools

import jax
import jax.numpy as jnp
from jax import lax
from jax.experimental import pallas as pl
from jax.experimental.pallas import tpu as pltpu
from jax.sharding import PartitionSpec as P

HEAD_DIM = 64
EPS = 1e-05
NEG = -1e30
BF16 = jnp.bfloat16
F32 = jnp.float32
NT = (((1,), (1,)), ((), ()))
TN = (((0,), (0,)), ((), ()))
KEY_BLOCK = 512
DOCS = 4


def dot_plain(left, right):
    return jnp.dot(left, right, preferred_element_type=F32)


def dot_last(left, right):
    return lax.dot_general(left, right, NT, preferred_element_type=F32)


def dot_first(left, right):
    return lax.dot_general(left, right, TN, preferred_element_type=F32)


def column_sum(value):
    return jnp.sum(value.astype(F32), axis=0)


def rounded(value):
    return lax.reduce_precision(value, 8, 7)


def after(array):
    return jnp.minimum(jnp.abs(array[0, 0].astype(F32)), 0.0)


def norm_forward(hidden, gain, shift):
    centered = hidden - jnp.mean(hidden, axis=-1, keepdims=True)
    spread = jnp.mean(centered * centered, axis=-1, keepdims=True)
    factor = lax.rsqrt(spread + EPS)
    normed = centered * factor
    return (normed * gain.astype(F32) + shift.astype(F32), (normed, factor))


def norm_backward(grad, saved, gain):
    normed, factor = saved
    scaled = grad * gain.astype(F32)
    centered = scaled - jnp.mean(scaled, axis=-1, keepdims=True)
    grad_hidden = factor * (centered - normed * jnp.mean(scaled * normed, axis=-1, keepdims=True))
    return (grad_hidden, jnp.sum(grad * normed, axis=0), jnp.sum(grad, axis=0))


def head_columns(head):
    return slice(head // 2 * 128, head // 2 * 128 + 128)


def head_rows(head):
    return slice(head * HEAD_DIM, (head + 1) * HEAD_DIM)


def own_lanes(shape, head):
    lanes = lax.broadcasted_iota(jnp.int32, shape, 1)
    return lanes >= HEAD_DIM if head % 2 else lanes < HEAD_DIM


class Mask:
    def __init__(self, causal, starts, segments, first_row):
        self.causal, self.starts, self.first_row = causal, starts, first_row
        segments = segments[...]
        low = high = jnp.zeros_like(segments)
        for number in range(DOCS):
            low = jnp.where(segments == number, starts[number], low)
            high = jnp.where(segments == number, starts[number + 1], high)
        self.count = segments.shape[1]
        if causal:
            place = first_row + lax.broadcasted_iota(jnp.int32, segments.shape, 1)
            high = jnp.minimum(high, place + 1)
        self.low, self.high = low, high

    def allowed(self, index, block):
        place = lax.broadcasted_iota(jnp.int32, (block, self.count), 0) + index * block
        return (place >= self.low) & (place < self.high)

    def flag(self, index, block, ends):
        start, stop = index * block, (index + 1) * block
        low, low_last = self.starts[ends[0]], self.starts[ends[1]]
        high_first, high = self.starts[ends[0] + 1], self.starts[ends[1] + 1]
        if self.causal:
            high = jnp.minimum(high, self.first_row + self.count)
            high_first = jnp.minimum(high_first, self.first_row + 1)
        active = (low < stop) & (high > start)
        full = (low_last <= start) & (high_first >= stop)
        return jnp.where(active, jnp.where(full, 2, 1), 0)


def over_blocks(mask, ends, length, block, body, skipped):
    @pl.loop(0, length // block)
    def _(index):
        flag = mask.flag(index, block, ends)
        rows = pl.ds(pl.multiple_of(index * block, block), block)

        @pl.when(flag == 0)
        def _():
            skipped(rows)

        @pl.when(flag == 1)
        def _():
            body(index, rows, True)

        @pl.when(flag == 2)
        def _():
            body(index, rows, False)


def forward_start(q_ref, masked_q, acc, top):
    heads = q_ref.shape[1] // HEAD_DIM
    for head in range(heads):
        pair = q_ref[:, head_columns(head)]
        masked_q[head] = jnp.where(own_lanes(pair.shape, head), pair, jnp.zeros_like(pair))
    acc[...] = jnp.zeros_like(acc)
    top[...] = jnp.full_like(top, NEG)


def forward_block(index, rows, partial, block, kv_ref, mask, masked_q, acc, top):
    heads, count = masked_q.shape[:2]
    width = heads * HEAD_DIM
    if partial:
        allowed = mask.allowed(index, block)
    for head in range(heads):
        cols = head_columns(head)
        scores = lax.dot_general(kv_ref[rows, cols], masked_q[head], NT, preferred_element_type=F32)
        if partial:
            scores = jnp.where(allowed, scores, NEG)
        old = top[head : head + 1, :]
        new = jnp.maximum(old, jnp.max(scores, axis=0, keepdims=True))
        weights = jnp.exp(scores - new).astype(BF16)
        vals = kv_ref[rows, width + cols.start : width + cols.stop]
        vals = jnp.where(own_lanes(vals.shape, head), vals, jnp.ones_like(vals))
        acc[head] = acc[head] * jnp.exp(old - new) + lax.dot_general(
            vals, weights, TN, preferred_element_type=F32
        )
        top[head : head + 1, :] = new


def forward_end(out_ref, lse_ref, acc, top):
    lse_ref[...] = jnp.zeros_like(lse_ref)
    for head in range(acc.shape[0]):
        first = head % 2 * HEAD_DIM
        total = acc[head, HEAD_DIM - first : HEAD_DIM - first + 1, :]
        out_ref[head_rows(head), :] = acc[head, first : first + HEAD_DIM, :] / total
        lse_ref[head : head + 1, :] = top[head : head + 1, :] + jnp.log(total)


def forward_kernel(
    block, causal, starts, ends, segments, q_ref, kv_ref, out_ref, lse_ref, masked_q, acc, top
):
    mask = Mask(causal, starts, segments, ends[2])
    forward_start(q_ref, masked_q, acc, top)

    def body(index, rows, partial):
        forward_block(index, rows, partial, block, kv_ref, mask, masked_q, acc, top)

    over_blocks(mask, ends, kv_ref.shape[0], block, body, lambda rows: None)
    forward_end(out_ref, lse_ref, acc, top)


def backward_start(q_ref, do_ref, dot_ref, out_ref, masked_q, masked_do, delta, dq):
    for head in range(masked_q.shape[0]):
        pair = q_ref[:, head_columns(head)]
        keep = own_lanes(pair.shape, head)
        masked_q[head] = jnp.where(keep, pair, jnp.zeros_like(pair))
        pair = do_ref[:, head_columns(head)]
        masked_do[head] = jnp.where(keep, pair, jnp.zeros_like(pair))
        part = head_rows(head)
        delta[head : head + 1, :] = jnp.sum(
            dot_ref[part, :].astype(F32) * out_ref[part, :], axis=0, keepdims=True
        )
    dq[...] = jnp.zeros_like(dq)


def backward_block(
    index, rows, block, mask, kv_ref, lse_ref, dkv_ref, masked_q, masked_do, delta, dq, between
):
    heads = masked_q.shape[0]
    width = heads * HEAD_DIM
    allowed = mask.allowed(index, block)
    for pair in range(heads // 2):
        if pair == 1:
            between()
        cols = head_columns(2 * pair)
        later = slice(width + cols.start, width + cols.stop)
        keys, vals = kv_ref[rows, cols], kv_ref[rows, later]
        dk = dv = 0.0
        for head in (2 * pair, 2 * pair + 1):
            scores = lax.dot_general(keys, masked_q[head], NT, preferred_element_type=F32)
            probs = jnp.exp(scores - lse_ref[head : head + 1, :])
            probs = jnp.where(allowed, probs, 0.0)
            dprobs = lax.dot_general(vals, masked_do[head], NT, preferred_element_type=F32)
            draw = (probs * (dprobs - delta[head : head + 1, :])).astype(BF16)
            probs = probs.astype(BF16)
            dv = dv + jnp.dot(probs, masked_do[head], preferred_element_type=F32)
            dk = dk + jnp.dot(draw, masked_q[head], preferred_element_type=F32)
            first = head % 2 * HEAD_DIM
            both = lax.dot_general(keys, draw, TN, preferred_element_type=F32)
            dq[head_rows(head), :] += both[first : first + HEAD_DIM]
        dkv_ref[rows, cols] = dk.astype(BF16)
        dkv_ref[rows, later] = dv.astype(BF16)


SCALARS = pl.BlockSpec(memory_space=pltpu.SMEM)
VECTORS = pl.BlockSpec(memory_space=pltpu.VMEM)


ANYWHERE = pl.BlockSpec(memory_space=pl.ANY)


def cost_of(kv, count, width, products):
    flops = 2 * products * kv.shape[0] * count * width
    return pl.CostEstimate(flops=flops, bytes_accessed=flops // 512, transcendentals=0)


def forward_scratch(count, width):
    heads = width // HEAD_DIM
    return [
        pltpu.VMEM((heads, count, 128), BF16),
        pltpu.VMEM((heads, 128, count), F32),
        pltpu.VMEM((8, count), F32),
    ]


def backward_scratch(count, width):
    heads = width // HEAD_DIM
    return [
        pltpu.VMEM((heads, count, 128), BF16),
        pltpu.VMEM((heads, count, 128), BF16),
        pltpu.VMEM((8, count), F32),
        pltpu.VMEM((width, count), F32),
    ]


def attend(queries, kv, mask):
    count, width = queries.shape
    causal, starts, ends, segments = mask
    return pl.pallas_call(
        functools.partial(forward_kernel, KEY_BLOCK, causal),
        out_shape=(
            jax.ShapeDtypeStruct((width, count), F32),
            jax.ShapeDtypeStruct((8, count), F32),
        ),
        in_specs=[SCALARS] * 2 + [VECTORS] * 3,
        out_specs=(VECTORS,) * 2,
        scratch_shapes=forward_scratch(count, width),
        compiler_params=pltpu.CompilerParams(vmem_limit_bytes=40 << 20),
        cost_estimate=cost_of(kv, count, width, 2),
    )(starts, ends, segments, queries, kv)


MESH = pl.DeviceIdType.MESH
DMA = pltpu.SemaphoreType.DMA


class Here:
    def __init__(self, ring):
        self.ring = ring
        self.d, self.z, self.y = (lax.axis_index(a) for a in ("dp", "seq", "tensor"))
        self.core, self.x = lax.rem(self.d, 2), lax.div(self.d, 2)
        self.other_d = self.d + 1 - 2 * self.core
        self.partner = (self.other_d, self.z, self.y)
        self.right = (self.d, self.z + 1, self.y)
        self.left = (self.d, self.z - 1, self.y)
        self.over_x = (self.d + 2 - 4 * lax.rem(self.x, 2), self.z, self.y)
        self.over_y = (self.d, self.z, 1 - self.y)
        self.diagonal = (self.other_d, self.z, 1 - self.y)

    def meet(self, devices):
        barrier = pltpu.get_barrier_semaphore()
        wanted = 0
        for condition, device in devices:

            @pl.when(condition)
            def _(device=device):
                pl.semaphore_signal(barrier, inc=1, device_id=device, device_id_type=MESH)

            wanted = wanted + jnp.where(condition, 1, 0)
        pl.semaphore_wait(barrier, wanted)

    def along_z(self, step):
        return (self.d, lax.rem(self.z + step, self.ring), self.y)

    def everyone(self):
        devices = [self.partner, self.over_x, self.over_y, self.diagonal]
        devices += [self.along_z(step) for step in range(1, self.ring)]
        return [(self.core >= 0, device) for device in devices]

    def neighbours(self):
        return [
            (self.core >= 0, self.partner),
            (self.z + 1 < self.ring, self.right),
            (self.z > 0, self.left),
        ]


def remote(source, target, sent, received, device):
    return pltpu.make_async_remote_copy(
        src_ref=source,
        dst_ref=target,
        send_sem=sent,
        recv_sem=received,
        device_id=device,
        device_id_type=MESH,
    )


class Gather:
    def __init__(self, here, rows_ref, sems):
        self.here, self.rows_ref = here, rows_ref
        self.count = rows_ref.shape[0] // here.ring
        self.sent, self.got, self.core_sent, self.core_got = sems

    def half(self, shard, core):
        part = self.count // 2
        start = pl.multiple_of(shard * self.count + core * part, part)
        return self.rows_ref.at[pl.ds(start, part)]

    def ways(self, step):
        here = self.here
        z, ring = here.z, here.ring
        return [
            (0, z - step, z >= step, z - step + 1, (z + 1 < ring) & (z + 1 >= step), here.right),
            (1, z + step, z + step < ring, z + step - 1, (z > 0) & (z + step <= ring), here.left),
        ]

    def along(self, way, step, shard, device):
        view = self.half(shard, self.here.core)
        return remote(view, view, self.sent.at[way, step], self.got.at[way, step], device)

    def across(self, way, step, shard, core):
        view = self.half(shard, core)
        return remote(
            view, view, self.core_sent.at[way, step], self.core_got.at[way, step], self.here.partner
        )

    def start(self, step):
        for way, _, _, shard, sends, device in self.ways(step):

            @pl.when(sends)
            def _(way=way, shard=shard, device=device):
                self.along(way, step, shard, device).start()

    def arrive(self, step):
        for way, shard, comes, _, _, device in self.ways(step):

            @pl.when(comes)
            def _(way=way, shard=shard, device=device):
                self.along(way, step, shard, self.here.partner).wait_recv()
                self.across(way, step, shard, self.here.core).start()

    def finish(self, step):
        for way, shard, comes, out, sends, device in self.ways(step):

            @pl.when(sends)
            def _(way=way, out=out, device=device):
                self.along(way, step, out, device).wait_send()

            @pl.when(comes)
            def _(way=way, shard=shard):
                self.across(way, step, shard, self.here.core).wait_send()
                self.across(way, step, shard, 1 - self.here.core).wait_recv()


def pieces_of(weights):
    found = []
    for k, weight in enumerate(weights):
        rows, columns = weight.shape
        number = 3 if rows == 6 * columns else 1
        while 2 * rows * columns > 655360 * number and rows % (64 * number) == 0:
            number *= 2
        found += [(k, i * (rows // number), rows // number) for i in range(number)]
    return found


def beside(weight, model):
    rows, columns = weight.shape
    matrices = 3 if rows == 3 * model else 1
    return jax.ShapeDtypeStruct((rows // matrices, columns * matrices), weight.dtype)


class Fetch:
    def __init__(self, here, inputs, outputs, sems):
        self.here, self.inputs, self.outputs = here, inputs, outputs
        self.y_sent, self.y_got, self.x_sent, self.x_got, self.core_sent, self.core_got = sems
        self.pieces = pieces_of(inputs)
        self.matrices = [
            (k, matrix)
            for k, (given, out) in enumerate(zip(inputs, outputs))
            for matrix in range(given.shape[0] // out.shape[0])
        ]
        self.number = len(self.pieces)
        self.own = lax.rem(here.x, 2)

    def devices(self):
        here = self.here
        return [(here.core >= 0, here.diagonal), (here.core == 1, here.over_x)]

    def part(self, p, which):
        k, start, rows = self.pieces[p]
        first = pl.multiple_of(start + which * (rows // 2), 16)
        return self.inputs[k].at[pl.ds(first, rows // 2)]

    def place(self, p, which):
        k, start, rows = self.pieces[p]
        out = self.outputs[k]
        matrix, start = divmod(start, out.shape[0])
        columns = self.inputs[k].shape[1]
        first = pl.multiple_of(start + which * (rows // 2), 16)
        return out.at[pl.ds(first, rows // 2), pl.ds(matrix * columns, columns)]

    def over_y(self, p):
        return remote(
            self.part(p, self.own),
            self.place(p, self.own),
            self.y_sent.at[p],
            self.y_got.at[p],
            self.here.diagonal,
        )

    def over_x(self, p, which):
        view = self.place(p, which)
        return remote(view, view, self.x_sent.at[p], self.x_got.at[p], self.here.over_x)

    def across(self, m):
        k, matrix = self.matrices[m]
        rows, columns = self.outputs[k].shape[0], self.inputs[k].shape[1]
        return remote(
            self.inputs[k].at[pl.ds(matrix * rows, rows)],
            self.outputs[k].at[:, pl.ds(matrix * columns, columns)],
            self.core_sent.at[m],
            self.core_got.at[m],
            self.here.partner,
        )

    def begin(self):
        @pl.when(self.here.core == 0)
        def _():
            for p in range(min(2, self.number)):
                self.over_y(p).start()

        @pl.when(self.here.core == 1)
        def _():
            for m in range(len(self.matrices)):
                self.across(m).start()

    def advance(self, p):
        @pl.when(self.here.core == 0)
        def _():
            self.over_y(p).wait_send()
            if p + 2 < self.number:
                self.over_y(p + 2).start()

        @pl.when(self.here.core == 1)
        def _():
            self.over_y(p).wait_recv()
            self.over_x(p, self.own).start()

    def end(self):
        @pl.when(self.here.core == 0)
        def _():
            for m in range(len(self.matrices)):
                self.across(m).wait_recv()

        @pl.when(self.here.core == 1)
        def _():
            for p in range(self.number):
                self.over_x(p, self.own).wait_send()
                self.over_x(p, 1 - self.own).wait_recv()
            for m in range(len(self.matrices)):
                self.across(m).wait_send()


def gather_sems(ring):
    return [DMA((2, ring))] * 4


def fetch_sems(weights):
    number = len(pieces_of(weights))
    return [DMA((number,))] * 4 + [DMA((3 * len(weights),))] * 2


def opening_kernel(ring, number, *refs):
    inputs, outputs, sems = refs[: 4 + number], refs[4 + number : 8 + 2 * number], refs[8 + 2 * number :]
    source, target, segments, vectors = inputs[:4]
    source_all, target_all, segments_out, vectors_out = outputs[:4]
    shard_sems, vector_sems = sems[:3], sems[3:6]
    here = Here(ring)
    fetch = Fetch(here, inputs[4:], outputs[4:], sems[14:])
    here.meet(here.neighbours() + fetch.devices())
    count = source.shape[0]
    own = pl.ds(pl.multiple_of(here.z * count, count), count)
    moves = [
        (source, source_all.at[own]),
        (target, target_all.at[own]),
        (segments, segments_out),
    ]
    owner = here.core == here.y

    def shard_copy(k):
        start, end = moves[k]
        sent, got, copied = shard_sems
        return (
            remote(start, end, sent.at[k], got.at[k], here.partner),
            pltpu.make_async_copy(start, end, copied.at[k]),
        )

    def vector_copy():
        sent, got, copied = vector_sems
        return (
            remote(vectors, vectors_out, sent, got, here.diagonal),
            pltpu.make_async_copy(vectors, vectors_out, copied),
        )

    def wait_shard(k):
        across, local = shard_copy(k)

        @pl.when(owner)
        def _():
            across.wait_send()
            local.wait()

        @pl.when(jnp.logical_not(owner))
        def _():
            across.wait_recv()

    @pl.when(owner)
    def _():
        for k in range(3):
            across, local = shard_copy(k)
            across.start()
            local.start()

    @pl.when(here.core == 0)
    def _():
        across, local = vector_copy()
        across.start()
        local.start()

    fetch.begin()
    gathers = [Gather(here, source_all, sems[6:10]), Gather(here, target_all, sems[10:14])]
    slots = 2 * (ring - 1)
    done = 0
    for k, gather in enumerate(gathers):
        wait_shard(k)
        for step in range(1, ring):
            gather.start(step)
            slot = k * (ring - 1) + step
            while done < fetch.number * slot // slots:
                fetch.advance(done)
                done += 1
            gather.arrive(step)
    for gather in gathers:
        for step in range(1, ring):
            gather.finish(step)
    wait_shard(2)
    fetch.end()
    across, local = vector_copy()

    @pl.when(here.core == 0)
    def _():
        across.wait_send()
        local.wait()

    @pl.when(here.core == 1)
    def _():
        across.wait_recv()


def opening(ring, source, target, segments, vectors, weights):
    inputs = (source, target, segments, vectors) + tuple(weights)
    count, model = source.shape
    rows = jax.ShapeDtypeStruct((ring * count, model), BF16)
    shapes = (rows, rows) + tuple(jax.ShapeDtypeStruct(v.shape, v.dtype) for v in inputs[2:4])
    shapes += tuple(beside(weight, model) for weight in weights)
    number = len(weights)
    return pl.pallas_call(
        functools.partial(opening_kernel, ring, number),
        out_shape=shapes,
        in_specs=[VECTORS] * 4 + [ANYWHERE] * number,
        out_specs=(ANYWHERE,) * 2 + (VECTORS,) * 2 + (ANYWHERE,) * number,
        scratch_shapes=[DMA((3,))] * 3 + [DMA] * 3 + gather_sems(ring) * 2 + fetch_sems(weights),
        compiler_params=pltpu.CompilerParams(collective_id=1, has_side_effects=True),
    )(*inputs)


def gather_attend_kernel(
    block, causal, ring, number, tokens, starts, segments, q_ref, kv_ref, own_ref, *refs
):
    weights, refs = refs[:number], refs[number + tokens :]
    out_ref, lse_ref, all_ref = refs[:3]
    fetched, refs = refs[3 : 3 + number], refs[3 + number :]
    masked_q, acc, top, copied = refs[:4]
    here = Here(ring)
    gather = Gather(here, all_ref, refs[4:8])
    fetch = Fetch(here, weights, fetched, refs[8:])
    here.meet(here.neighbours() + fetch.devices())
    count = own_ref.shape[0]
    first_row = pl.multiple_of(here.z * count, count)
    local = pltpu.make_async_copy(own_ref, all_ref.at[pl.ds(first_row, count)], copied)
    local.start()
    fetch.begin()
    local.wait()
    gather.start(1)
    mask = Mask(causal, starts, segments, first_row)
    forward_start(q_ref, masked_q, acc, top)
    blocks = kv_ref.shape[0] // block

    @pl.loop(0, blocks)
    def _(index):
        rows = pl.ds(pl.multiple_of(index * block, block), block)
        forward_block(index, rows, True, block, kv_ref, mask, masked_q, acc, top)

        @pl.when((index >= 1) & (index < ring))
        def _():
            gather.arrive(index)

        @pl.when((index >= 1) & (index < ring - 1))
        def _():
            gather.start(index + 1)

        for p in range(min(fetch.number, blocks - 1)):
            pl.when(index == p + 1)(functools.partial(fetch.advance, p))

    forward_end(out_ref, lse_ref, acc, top)
    for p in range(min(fetch.number, blocks - 1), fetch.number):
        fetch.advance(p)

    @pl.loop(1, ring)
    def _(step):
        gather.finish(step)

    fetch.end()


def gather_attend(ring, queries, kv, mask, own, weights, tokens):
    count, width = queries.shape
    causal, starts, _, segments = mask
    number = len(weights)
    return pl.pallas_call(
        functools.partial(gather_attend_kernel, KEY_BLOCK, causal, ring, number, len(tokens)),
        out_shape=(
            jax.ShapeDtypeStruct((width, count), F32),
            jax.ShapeDtypeStruct((8, count), F32),
            jax.ShapeDtypeStruct((ring * own.shape[0], own.shape[1]), BF16),
        )
        + tuple(beside(weight, own.shape[1]) for weight in weights),
        in_specs=[SCALARS] + [VECTORS] * 4 + [ANYWHERE] * (number + len(tokens)),
        out_specs=(VECTORS, VECTORS) + (ANYWHERE,) * (1 + number),
        scratch_shapes=forward_scratch(count, width)
        + [DMA]
        + gather_sems(ring)
        + fetch_sems(weights),
        compiler_params=pltpu.CompilerParams(
            vmem_limit_bytes=40 << 20, collective_id=2, has_side_effects=True
        ),
        cost_estimate=cost_of(kv, count, width, 2),
    )(starts, segments, queries, kv, own, *weights, *tokens)


class Part:
    def __init__(self, inputs, in_specs, out_shapes, scratch, bind):
        self.inputs, self.in_specs, self.out_shapes = inputs, in_specs, out_shapes
        self.scratch, self.bind = scratch, bind


def run_parts(number, body, parts, cost=None):
    ring = lax.axis_size("seq")
    counts = [(len(p.inputs), len(p.out_shapes), len(p.scratch)) for p in parts]

    def kernel(*refs):
        here = Here(ring)
        taken, offset = [[] for _ in parts], 0
        for kind in range(3):
            for refs_of, count in zip(taken, counts):
                refs_of.append(refs[offset : offset + count[kind]])
                offset += count[kind]
        here.meet(here.everyone())
        body(here, *(p.bind(here, *refs_of) for p, refs_of in zip(parts, taken)))

    results = pl.pallas_call(
        kernel,
        out_shape=[shape for p in parts for shape in p.out_shapes],
        in_specs=[spec for p in parts for spec in p.in_specs],
        out_specs=[VECTORS for p in parts for _ in p.out_shapes],
        scratch_shapes=[shape for p in parts for shape in p.scratch],
        compiler_params=pltpu.CompilerParams(
            vmem_limit_bytes=60 << 20, collective_id=number, has_side_effects=True
        ),
        cost_estimate=cost,
    )(*(array for p in parts for array in p.inputs))
    given = []
    for _, count, _ in counts:
        given.append(results[:count])
        results = results[count:]
    return given


class Stage:
    def __init__(self, here, kind, source, result, buffers, sems):
        self.here, self.kind, self.source, self.result = here, kind, source, result
        self.buffers, (self.sent, self.got) = buffers, sems
        rows = source.shape[0]
        if kind == "x":
            half = rows // 2
            self.kept = [half * here.x]
            self.given = [half * (1 - here.x)]
            self.size, self.to = half, here.over_x
        elif kind == "y":
            self.size = 192
            self.starts = list(range(0, rows, 2 * self.size))
        elif kind == "v":
            bit = lax.rem(here.z, 2)
            self.size = rows // 4
            self.kept = [self.size * bit, self.size * (bit + 2)]
            self.given = [self.size * (1 - bit), self.size * (3 - bit)]
            self.to = (here.d, here.z + 1 - 2 * bit, here.y)
        else:
            bit = lax.div(here.z, 2)
            self.size = rows // 2
            self.kept, self.given = [self.size * bit], [self.size * (1 - bit)]
            self.to = (here.d, here.z + 2 - 4 * bit, here.y)

    def rows(self, start):
        if not isinstance(start, int):
            start = pl.multiple_of(start, 16)
        return pl.ds(start, self.size)

    def move(self, start, place, buffer, sem, to):
        return remote(
            self.source.at[self.rows(start)],
            self.buffers[buffer].at[self.rows(place * self.size)],
            self.sent.at[sem],
            self.got.at[sem],
            to,
        )

    def moves(self):
        here = self.here
        if self.kind != "y":
            both = [
                (None, self.move(start, k, 0, k, self.to)) for k, start in enumerate(self.given)
            ]
            return both, both
        sends, arrivals = [], []
        for k, start in enumerate(self.starts):
            upper = start + self.size
            sends.append((here.core == 0, self.move(upper, k, 0, 2 * k, here.partner)))
            sends.append((here.core == 1, self.move(start, k, 0, 2 * k, here.diagonal)))
            sends.append((here.core == 1, self.move(upper, k, 1, 2 * k + 1, here.over_y)))
            arrivals.append((None, self.move(upper, k, 0, 2 * k, here.partner)))
            arrivals.append((here.core == 1, self.move(upper, k, 1, 2 * k + 1, here.over_y)))
        return sends, arrivals

    @staticmethod
    def each(moves, act):
        for condition, copy in moves:
            if condition is None:
                act(copy)
            else:
                pl.when(condition)(functools.partial(act, copy))

    def begin(self):
        self.each(self.moves()[0], lambda copy: copy.start())

    def end(self):
        sends, arrivals = self.moves()
        self.each(arrivals, lambda copy: copy.wait_recv())
        kept = self.kept if self.kind != "y" else self.starts
        for k, start in enumerate(kept):
            place = self.rows(k * self.size)

            def add(own_ref, own, place=place):
                both = own_ref[own, :].astype(F32) + self.buffers[0][place, :].astype(F32)
                self.result[place, :] = both.astype(self.result.dtype)

            if self.kind == "y":
                pl.when(self.here.core == 0)(functools.partial(add, self.source, self.rows(start)))
                pl.when(self.here.core == 1)(functools.partial(add, self.buffers[1], place))
            else:
                add(self.source, self.rows(start))
        self.each(sends, lambda copy: copy.wait_send())


class Chain:
    def __init__(self, stages, times):
        self.stages, self.times = stages, times

    def event(self, time):
        for k, own in enumerate(self.times):
            if own == time:
                if k:
                    self.stages[k - 1].end()
                if k < len(self.stages):
                    self.stages[k].begin()


def chain(array, kinds, times):
    rows, columns = array.shape
    scratch, shapes = [], []
    for kind in kinds:
        rows = rows // 2
        scratch += [pltpu.VMEM((rows, columns), BF16)] * (2 if kind == "y" else 1)
        scratch += [DMA((4,))] * 2
        shapes.append((rows, columns))
    scratch += [pltpu.VMEM(shape, BF16) for shape in shapes[:-1]]
    final = jax.ShapeDtypeStruct(shapes[-1], F32 if kinds[-1] == "w" else BF16)

    def bind(here, inputs, outputs, refs):
        refs = list(refs)
        results = refs[len(refs) - len(kinds) + 1 :] + [outputs[0]]
        source, stages = inputs[0], []
        for kind, result in zip(kinds, results):
            buffers = [refs.pop(0) for _ in range(2 if kind == "y" else 1)]
            sems = [refs.pop(0) for _ in range(2)]
            stages.append(Stage(here, kind, source, result, buffers, sems))
            source = result
        return Chain(stages, times)

    return Part((array,), [VECTORS], [final], scratch, bind)


class Small:
    def __init__(self, here, rows, held_rows, given, result, refs, times):
        self.here, self.given, self.result, self.times = here, given, result, times
        self.rows, self.held_rows = rows, held_rows
        self.arrived, self.sent, self.got = refs
        self.bits = [lax.rem(here.z, 2), lax.div(here.z, 2)]

    def copies(self, stage):
        here = self.here
        low, high = self.bits

        def to(device, slot, source=self.result, target=None):
            target = self.arrived.at[slot] if target is None else target
            return remote(source, target, self.sent.at[slot], self.got.at[slot], device)

        if stage < 3:
            device = (
                here.over_x,
                (here.d, here.z + 1 - 2 * low, here.y),
                (here.d, here.z + 2 - 4 * high, here.y),
            )[stage]
            both = [(None, to(device, stage))]
            return both, both
        if stage == 3:
            sends = [
                (None, to(here.over_y, 3)),
                (here.core == 0, to(here.partner, 4)),
                (here.core == 1, to(here.diagonal, 4)),
            ]
            return sends, sends[:1] + [(None, to(here.partner, 4))]
        return [(here.core == 0, to(here.partner, 5))], [(here.core == 1, to(here.partner, 5))]

    def end(self, stage):
        sends, arrivals = self.copies(stage)
        Stage.each(arrivals, lambda copy: copy.wait_recv())
        Stage.each(sends, lambda copy: copy.wait_send())
        core = self.here.core
        if stage < 3:
            self.result[...] += self.arrived[stage]
        elif stage == 3:
            whole, halves = slice(0, self.held_rows), slice(self.held_rows, self.rows)
            self.result[whole, :] += self.arrived[3, whole, :]
            own = jnp.where(core == 0, self.result[halves, :], self.arrived[3, halves, :])
            self.result[halves, :] = own + self.arrived[4, halves, :]
        else:
            whole = slice(0, self.held_rows)

            @pl.when(core == 1)
            def _():
                self.result[whole, :] = self.arrived[5, whole, :]

    def event(self, time):
        for k, own in enumerate(self.times):
            if own == time:
                if k == 0:
                    self.result[...] = self.given[...]
                else:
                    self.end(k - 1)
                if k < 5:
                    Stage.each(self.copies(k)[0], lambda copy: copy.start())


def small_sums(whole, halves, times):
    both = jnp.concatenate([whole, halves])
    rows, columns = both.shape
    shape = jax.ShapeDtypeStruct(both.shape, F32)
    part = Part(
        (both,),
        [VECTORS],
        [shape],
        [pltpu.VMEM((6, rows, columns), F32), DMA((6,)), DMA((6,))],
        lambda here, inputs, outputs, refs: Small(
            here, rows, whole.shape[0], inputs[0], outputs[0], refs, times
        ),
    )
    part.rows, part.vectors = whole.shape[0], (whole.reshape(-1), halves.reshape(-1))
    return part


def run_chains(number, chains, events):
    def body(here, *bound):
        for time in range(events):
            for one in bound:
                one.event(time)

    return [given[0] for given in run_parts(number, body, chains)]


class Back:
    def __init__(self, here, causal, apart, inputs, outputs, scratch):
        self.here, self.causal, self.apart = here, causal, apart
        self.starts, self.segments, self.q, self.kv, self.do, self.dot, self.out, self.lse = inputs[:8]
        self.weights = inputs[8]
        self.dq_out, self.dkv, self.sum = outputs[:3]
        self.query_sum = outputs[3] if apart else None
        self.work, scratch = scratch[:4], scratch[4:]
        self.terms, self.from_core, self.outgoing, self.arrived, self.total = scratch[:5]
        self.core_sent, self.core_got, self.sent, self.got, self.end_sent, self.end_got = scratch[5:11]
        if apart:
            self.query_low, self.query_got, self.query_sems = scratch[11:]
        self.count, self.width = self.q.shape
        self.part = self.count // 2
        self.mask = Mask(causal, self.starts, self.segments, here.z * self.count)

    def half(self, core):
        return pl.ds(pl.multiple_of(core * self.part, self.part), self.part)

    def shard_at(self, turn):
        ring, z, shard = self.here.ring, self.here.z, 0
        for device in range(ring):
            others = [t for t in range(ring) if t != device]
            others.sort(key=lambda t: (ring - t + device) if t > device else (t + ring - device))
            for k, other in enumerate(others):
                shard = jnp.where((z == device) & (turn == k + 1), other, shard)
        return shard

    def across(self, shard):
        return remote(
            self.terms.at[shard, self.half(1 - self.here.core)],
            self.from_core.at[shard],
            self.core_sent.at[shard],
            self.core_got.at[shard],
            self.here.partner,
        )

    def along(self, way, shard, device):
        return remote(
            self.outgoing.at[shard],
            self.arrived.at[way, shard],
            self.sent.at[shard],
            self.got.at[way, shard],
            device,
        )

    def both(self, shard):
        self.across(shard).wait_recv()
        own = self.terms[shard, self.half(self.here.core), :].astype(F32)
        return own + self.from_core[shard].astype(F32)

    def forward(self, shard):
        here = self.here
        self.total[...] = self.both(shard)
        for way, mine, comes, device in (
            (0, shard > here.z, here.z > 0, here.right),
            (1, shard < here.z, here.z + 1 < here.ring, here.left),
        ):

            @pl.when(mine & comes)
            def _(way=way):
                self.along(way, shard, here.partner).wait_recv()
                self.total[...] += self.arrived[way, shard].astype(F32)

        self.outgoing[shard] = self.total[...].astype(BF16)
        for way, mine, device in ((0, shard > here.z, here.right), (1, shard < here.z, here.left)):

            @pl.when(mine)
            def _(way=way, device=device):
                self.along(way, shard, device).start()

    def block(self, shard, between):
        rows = pl.ds(pl.multiple_of(shard * self.count, self.count), self.count)
        backward_block(
            shard, rows, self.count, self.mask, self.kv, self.lse, self.dkv, *self.work, between
        )
        return dot_last(self.dkv[rows, :], self.weights[:, self.width :])

    def run(self, event):
        here, ring = self.here, self.here.ring
        at_end = (here.z == 0) | (here.z == ring - 1)
        event(0)
        backward_start(self.q, self.do, self.dot, self.out, *self.work)

        @pl.loop(1, ring)
        def _(turn):
            shard = self.shard_at(turn)

            def between():
                @pl.when((turn > 1) & at_end)
                def _():
                    self.forward(self.shard_at(turn - 1))

            self.terms[shard] = self.block(shard, between).astype(BF16)
            self.across(shard).start()
            for time in range(1, ring):
                pl.when(turn == time)(functools.partial(event, time))

        def between():
            self.forward(self.shard_at(jnp.where(at_end, ring - 1, 1)))

        own = self.block(here.z, between)
        event(ring)
        low = (self.work[3][...] * HEAD_DIM ** (-0.5)).T.astype(BF16)
        self.dq_out[...] = low
        query = dot_last(low, self.weights[:, : self.width])
        if self.apart:
            self.query_low[...] = query.astype(BF16)
            exchange = remote(
                self.query_low, self.query_got, self.query_sems.at[0], self.query_sems.at[1], here.partner
            )
            exchange.start()
        else:
            own = own + query
        self.terms[here.z] = own.astype(BF16)
        self.across(here.z).start()
        if self.apart:
            exchange.wait()
            self.query_sum[...] = self.query_low[...].astype(F32) + self.query_got[...].astype(F32)

        @pl.when(jnp.logical_not(at_end))
        def _():
            @pl.loop(2, ring)
            def _(turn):
                self.forward(self.shard_at(turn))

        event(ring + 1)
        self.total[...] = self.both(here.z)
        for way, comes in ((0, here.z > 0), (1, here.z + 1 < ring)):

            @pl.when(comes)
            def _(way=way):
                self.along(way, here.z, here.partner).wait_recv()
                self.total[...] += self.arrived[way, here.z].astype(F32)

        own, other = self.half(here.core), self.half(1 - here.core)
        self.sum[own, :] = self.total[...].astype(BF16)
        for half, waits in ((own, False), (other, True)):
            view = self.sum.at[half]
            copy = remote(view, view, self.end_sent, self.end_got, here.partner)
            if waits:
                copy.wait_recv()
            else:
                copy.start()
                copy.wait_send()
        for shard in range(ring):
            self.across(shard).wait_send()

            @pl.when(here.z != shard)
            def _(shard=shard):
                self.along(0, shard, here.partner).wait_send()

        event(ring + 2)


def attend_back(number, saved, grad_mixed, grad_mixed_t, weights, mask, apart, chains):
    queries, kv, output, lse, _ = saved
    causal, starts, segments = mask
    ring = lax.axis_size("seq")
    count, width = queries.shape
    model = weights[0].shape[0]
    part = count // 2
    shapes = [
        jax.ShapeDtypeStruct((count, width), BF16),
        jax.ShapeDtypeStruct(kv.shape, BF16),
        jax.ShapeDtypeStruct((count, model), BF16),
    ]
    scratch = backward_scratch(count, width) + [
        pltpu.VMEM((ring, count, model), BF16),
        *[pltpu.VMEM((ring, part, model), BF16)] * 2,
        pltpu.VMEM((2, ring, part, model), BF16),
        pltpu.VMEM((part, model), F32),
        *[DMA((ring,))] * 3,
        DMA((2, ring)),
        *[DMA] * 2,
    ]
    if apart:
        shapes.append(jax.ShapeDtypeStruct((count, model), F32))
        scratch += [pltpu.VMEM((count, model), BF16)] * 2 + [DMA((2,))]
    main = Part(
        (starts, segments, queries, kv, grad_mixed, grad_mixed_t, output, lse, weights[0]),
        [SCALARS] + [VECTORS] * 8,
        shapes,
        scratch,
        lambda here, *refs: Back(here, causal, apart, *refs),
    )

    def body(here, back, *bound):
        def event(time):
            for one in bound:
                one.event(time)

        back.run(event)

    first, *rest = run_parts(number, body, [main] + list(chains), cost_of(kv, count, width, 7))
    return first, [given[0] for given in rest]


class Plan:
    def __init__(self, kernels):
        self.kernels = kernels

    def chains(self, wanted):
        return [chain(*one) for one in wanted] if self.kernels else []

    def given(self, wanted, results):
        return results if self.kernels else [one[0] for one in wanted]


class Places:
    def __init__(self, pairs, ring):
        self.pairs, self.ring = pairs, ring
        self.d = lax.axis_index("dp")
        self.x, self.core = self.d // 2, self.d % 2
        self.y, self.z = lax.axis_index("tensor"), lax.axis_index("seq")

    def swap_core(self, value):
        return lax.ppermute(value, "dp", [(i, i ^ 1) for i in range(self.pairs)])

    def swap_y(self, value):
        return lax.ppermute(value, "tensor", [(0, 1), (1, 0)])

    def swap_x(self, value, bit):
        return lax.ppermute(value, "dp", [(i, i ^ (2 << bit)) for i in range(self.pairs)])

    def swap_z(self, value, bit):
        return lax.ppermute(value, "seq", [(i, i ^ (1 << bit)) for i in range(self.ring)])

    def from_z(self, value, step):
        return lax.ppermute(value, "seq", [((i + step) % self.ring, i) for i in range(self.ring)])

    def to_z(self, value, step):
        return lax.ppermute(value, "seq", [(i, (i + step) % self.ring) for i in range(self.ring)])

    def permute(self, value, source_of):
        moves = []
        for d in range(self.pairs):
            for y in range(2):
                source = source_of(d, y)
                if source is not None:
                    moves.append((source[0] * 2 + source[1], d * 2 + y))
        return lax.ppermute(value, ("dp", "tensor"), moves)

    def fetch_weight(self, value):
        return self.permute(value, lambda d, y: (d + 1, y) if d % 2 == 0 else (d - 1, 1 - y))

    def core_sum(self, partial):
        low = rounded(partial)
        return low + self.swap_core(low.astype(BF16)).astype(F32)

    def own_pair(self, rows):
        return jnp.where(self.core == self.y, rows, self.swap_core(rows))

    def hand_out(self, rows):
        other = self.permute(rows, lambda d, y: (d, 1 - y) if d % 2 != y else None)
        return jnp.where(self.core == self.y, rows, other)

    def plan(self):
        return Plan(self.pairs == 4 and self.ring == 4)

    def scatter(self, grad, x_first):
        rows, columns = grad.shape
        owners = self.pairs // 2
        grad = grad.reshape(owners, 2, self.ring, rows // (self.pairs * self.ring), columns)
        for stage in "xyz" if x_first else "yxz":
            if stage == "y":
                kept = lax.dynamic_index_in_dim(grad, self.core, grad.ndim - 4, False)
                sent = lax.dynamic_index_in_dim(grad, 1 - self.core, grad.ndim - 4, False)
                first = self.permute(
                    sent, lambda d, y: (d + 1, 1 - y) if d % 2 == 0 else (d - 1, y)
                )
                second = self.permute(kept, lambda d, y: (d, 1 - y) if d % 2 else None)
                kept = jnp.where(self.core == 0, kept, second)
                grad = (kept.astype(F32) + first.astype(F32)).astype(BF16)
            else:
                axis = 0 if stage == "x" else grad.ndim - 3
                place, swap = (self.x, self.swap_x) if stage == "x" else (self.z, self.swap_z)
                size, bit = grad.shape[axis], 0
                while size > 1:
                    shape = grad.shape[:axis] + (size // 2, 2) + grad.shape[axis + 1 :]
                    grad = grad.reshape(shape)
                    mine = (place >> bit) & 1
                    kept = lax.dynamic_index_in_dim(grad, mine, axis + 1, False)
                    sent = lax.dynamic_index_in_dim(grad, 1 - mine, axis + 1, False)
                    grad = kept.astype(F32) + swap(sent, bit).astype(F32)
                    size, bit = size // 2, bit + 1
                    if stage == "x" or size > 1:
                        grad = grad.astype(BF16)
                grad = lax.squeeze(grad, (axis,))
        return grad.astype(F32)

    def all_sum(self, whole, halves):
        both = jnp.concatenate([whole, halves])
        for bit in range((self.pairs // 2).bit_length() - 1):
            both = both + self.swap_x(both, bit)
        for bit in range(self.ring.bit_length() - 1):
            both = both + self.swap_z(both, bit)
        whole, halves = both[: whole.shape[0]], both[whole.shape[0] :]
        whole = whole + self.swap_y(whole)
        whole = (whole + self.swap_core(whole)) * 0.5
        first = self.permute(halves, lambda d, y: (d + 1, 1 - y) if d % 2 == 0 else (d - 1, y))
        second = self.swap_y(halves)
        halves = jnp.where(self.core == 0, halves, second) + first
        return whole, halves


def starts_of(segments):
    numbers = jnp.arange(8, dtype=jnp.int32)
    return jnp.sum(segments[None, :] < numbers[:, None], axis=1, dtype=jnp.int32)


def mask_of(query_seg, key_starts, first_row, causal):
    ends = jnp.stack([query_seg[0], query_seg[-1], first_row])
    return (causal, key_starts, ends, query_seg[None])


def projected(query_in, key_in, weights):
    w_all, b_q, b_kv = weights
    width = b_q.shape[0]
    scale = HEAD_DIM ** (-0.5)
    queries = ((dot_plain(query_in, w_all[:, :width]) + b_q).astype(BF16) * scale).astype(BF16)
    return queries, (dot_plain(key_in, w_all[:, width:]) + b_kv).astype(BF16)


def attention_output(place, queries, kv, output, lse, out_weight, out_bias):
    mixed = output.astype(BF16)
    branch = place.core_sum(dot_first(mixed, out_weight)) + out_bias.astype(F32)
    return (branch, (queries, kv, output, lse, mixed))


def attention_backward(
    number, grad_branch, saved, query_in, key_in, weights, out_weight, mask, apart, plan, wanted
):
    mixed = saved[4]
    width = saved[0].shape[1]
    grad_mixed = dot_last(grad_branch, out_weight).astype(BF16)
    grad_mixed_t = dot_last(out_weight, grad_branch).astype(BF16)
    (grad_q, grad_kv, *sums), given = attend_back(
        number, saved, grad_mixed, grad_mixed_t, weights, mask, apart, plan.chains(wanted)
    )
    grads = (
        dot_first(query_in, grad_q).astype(BF16),
        lax.dot_general(
            grad_branch, mixed, (((0,), (1,)), ((), ())), preferred_element_type=F32
        ).astype(BF16),
        dot_first(key_in, grad_kv).astype(BF16),
    )
    grad_bias = jnp.concatenate([column_sum(grad_q), column_sum(grad_kv[:, width:])])
    return (sums, grads, grad_bias, plan.given(wanted, given))


def feed_forward(place, x_in, w_in, b_in, w_out, b_out):
    hidden = dot_plain(x_in, w_in) + b_in.astype(F32)
    active = jax.nn.gelu(hidden, approximate=False).astype(BF16)
    branch = place.core_sum(dot_plain(active, w_out)) + b_out.astype(F32)
    return (branch, (hidden, active))


def feed_backward(place, grad_branch, saved, x_in, w_in, w_out):
    hidden, active = saved
    grad_active = dot_last(grad_branch, w_out)
    slope = jax.vjp(lambda value: jax.nn.gelu(value, approximate=False), hidden)[1](grad_active)[0]
    grad_hidden = slope.astype(BF16)
    grad_in = place.core_sum(dot_last(grad_hidden, w_in))
    return (
        grad_in,
        dot_first(x_in, grad_hidden).astype(BF16),
        column_sum(grad_hidden),
        dot_first(grad_branch, active).astype(BF16),
    )


def shards(
    source,
    target,
    source_segments,
    target_segments,
    enc_qkv,
    enc_qv_bias,
    enc_proj,
    enc_ff_in,
    enc_ff_in_bias,
    enc_ff_out,
    enc_bias,
    enc_gains,
    enc_shifts,
    dec_self,
    dec_self_bias,
    dec_self_proj,
    dec_cross,
    dec_cross_bias,
    dec_cross_proj,
    dec_ff_in,
    dec_ff_in_bias,
    dec_ff_out,
    dec_bias,
    dec_gains,
    dec_shifts,
    enc_cotangent,
    dec_cotangent,
):
    count = source.shape[1]
    model = source.shape[2]
    place = Places(lax.axis_size("dp"), lax.axis_size("seq"))
    first_row = place.z * count

    ring = place.ring
    width = enc_qkv.shape[2]
    hidden_units = enc_ff_in.shape[1]

    vectors = jnp.concatenate(
        [
            enc_qv_bias.reshape(-1),
            dec_self_bias.reshape(-1),
            dec_cross_bias.reshape(-1),
            enc_ff_in_bias,
            dec_ff_in_bias,
        ]
    ).astype(F32)
    (
        x_all,
        t_all,
        segments,
        vectors,
        enc_qkv,
        dec_self,
        enc_proj,
        dec_self_proj,
        enc_ff_in,
        enc_ff_out,
    ) = opening(
        ring,
        source[0],
        target[0],
        jnp.concatenate([source_segments, target_segments]),
        vectors.reshape(-1, 128),
        (
            enc_qkv.reshape(-1, width),
            dec_self.reshape(-1, width),
            enc_proj,
            dec_self_proj,
            enc_ff_in,
            enc_ff_out,
        ),
    )
    vectors = vectors.reshape(-1)
    xs = lax.dynamic_slice_in_dim(x_all, first_row, count, 0)
    ts = lax.dynamic_slice_in_dim(t_all, first_row, count, 0)
    dec_ff_in = place.fetch_weight(dec_ff_in)
    dec_ff_out = place.fetch_weight(dec_ff_out)
    enc_cot = place.own_pair(enc_cotangent[0])
    dec_cot = place.own_pair(dec_cotangent[0])

    marks = [0, 2 * width, 4 * width, 6 * width, 6 * width + hidden_units, 6 * width + 2 * hidden_units]
    enc_qv_bias, dec_self_bias, dec_cross_bias, enc_ff_in_bias, dec_ff_in_bias = (
        vectors[a:b] for a, b in zip(marks[:-1], marks[1:])
    )

    def prepared(qkv, bias):
        b_kv = jnp.concatenate([jnp.zeros((width,), F32), bias[width:]])
        return (qkv, bias[:width], b_kv)

    enc_w = prepared(enc_qkv, enc_qv_bias)
    self_w = prepared(dec_self, dec_self_bias)

    source_keys, target_keys = segments[0], segments[1]
    source_own = lax.dynamic_slice_in_dim(source_keys, first_row, count, 0)
    target_own = lax.dynamic_slice_in_dim(target_keys, first_row, count, 0)
    source_starts, target_starts = starts_of(source_keys), starts_of(target_keys)
    enc_mask = mask_of(source_own, source_starts, first_row, False)
    self_mask = mask_of(target_own, target_starts, first_row, True)
    cross_mask = mask_of(target_own, source_starts, first_row, False)

    queries, kv = projected(xs, x_all, enc_w)
    output, lse = attend(queries, kv, enc_mask)
    branch, enc_attn = attention_output(place, queries, kv, output, lse, enc_proj, enc_bias[0])
    first, enc_norm_one = norm_forward(xs.astype(F32) + branch, enc_gains[0], enc_shifts[0])
    first_low = first.astype(BF16)
    enc_ff_in_bias = enc_ff_in_bias + after(dec_ff_in)
    branch, enc_feed = feed_forward(
        place, first_low, enc_ff_in, enc_ff_in_bias, enc_ff_out, enc_bias[1]
    )
    encoded, enc_norm_two = norm_forward(first + branch, enc_gains[1], enc_shifts[1])
    encoded_low = encoded.astype(BF16)

    queries, kv = projected(ts, t_all, self_w)
    output, lse, e_all, dec_cross, dec_cross_proj = gather_attend(
        ring,
        queries,
        kv,
        self_mask,
        encoded_low,
        (dec_cross.reshape(-1, width), dec_cross_proj),
        (dec_ff_out,),
    )
    cross_w = prepared(dec_cross, dec_cross_bias)
    branch, self_attn = attention_output(
        place, queries, kv, output, lse, dec_self_proj, dec_bias[0]
    )
    second, dec_norm_one = norm_forward(ts.astype(F32) + branch, dec_gains[0], dec_shifts[0])
    second_low = second.astype(BF16)
    queries, kv = projected(second_low, e_all, cross_w)
    output, lse = attend(queries, kv, cross_mask)
    branch, cross_attn = attention_output(
        place, queries, kv, output, lse, dec_cross_proj, dec_bias[1]
    )
    third, dec_norm_two = norm_forward(second + branch, dec_gains[1], dec_shifts[1])
    third_low = third.astype(BF16)
    branch, dec_feed = feed_forward(
        place, third_low, dec_ff_in, dec_ff_in_bias, dec_ff_out, dec_bias[2]
    )
    decoded, dec_norm_three = norm_forward(third + branch, dec_gains[2], dec_shifts[2])

    def back_mask(mask):
        return (mask[0], mask[1], mask[3])

    grad_hidden, dec_gain_three, dec_shift_three = norm_backward(
        dec_cot.astype(F32), dec_norm_three, dec_gains[2]
    )
    grad_branch = grad_hidden.astype(BF16)
    feed_in, dec_w_in, dec_b_in, dec_w_out = feed_backward(
        place, grad_branch, dec_feed, third_low, dec_ff_in, dec_ff_out
    )
    dec_bias_three = column_sum(grad_branch)
    grad_third = grad_hidden + feed_in
    grad_hidden, dec_gain_two, dec_shift_two = norm_backward(grad_third, dec_norm_two, dec_gains[1])
    grad_branch = grad_hidden.astype(BF16)
    plan = place.plan()
    (key_total, query_total), cross_grads, cross_bias, (dec_w_in, dec_w_out) = attention_backward(
        3,
        grad_branch,
        cross_attn,
        second_low,
        e_all,
        cross_w,
        dec_cross_proj,
        back_mask(cross_mask),
        True,
        plan,
        [(dec_w_in, "x", (0, 6)), (dec_w_out, "y", (0, 6))],
    )
    dec_bias_two = column_sum(grad_branch)
    grad_second = grad_hidden + query_total
    grad_hidden, dec_gain_one, dec_shift_one = norm_backward(
        grad_second, dec_norm_one, dec_gains[0]
    )
    grad_branch = grad_hidden.astype(BF16)
    cross_q, cross_proj, cross_kv = cross_grads
    (target_total,), self_grads, self_bias, given = attention_backward(
        4,
        grad_branch,
        self_attn,
        ts,
        t_all,
        self_w,
        dec_self_proj,
        back_mask(self_mask),
        False,
        plan,
            [
                (dec_w_in, "yvw", (0, 3, 5, 6)),
                (dec_w_out, "xvw", (0, 3, 5, 6)),
                (cross_kv, "x", (1, 6)),
                (cross_q, "y", (1, 6)),
                (cross_proj, "y", (1, 6)),
            ],
    )
    dec_w_in, dec_w_out, cross_kv, cross_q, cross_proj = given
    dec_bias_one = column_sum(grad_branch)
    grad_target = grad_hidden + target_total.astype(F32)
    grad_hidden, enc_gain_two, enc_shift_two = norm_backward(
        enc_cot.astype(F32) + key_total.astype(F32), enc_norm_two, enc_gains[1]
    )
    grad_branch = grad_hidden.astype(BF16)
    feed_in, enc_w_in, enc_b_in, enc_w_out = feed_backward(
        place, grad_branch, enc_feed, first_low, enc_ff_in, enc_ff_out
    )
    enc_bias_two = column_sum(grad_branch)
    grad_first = grad_hidden + feed_in
    grad_hidden, enc_gain_one, enc_shift_one = norm_backward(grad_first, enc_norm_one, enc_gains[0])
    grad_branch = grad_hidden.astype(BF16)
    self_q, self_proj, self_kv = self_grads
    (source_total,), enc_grads, enc_bias_grad, given = attention_backward(
        5,
        grad_branch,
        enc_attn,
        xs,
        x_all,
        enc_w,
        enc_proj,
        back_mask(enc_mask),
        False,
        plan,
            [
                (cross_kv, "yvw", (0, 3, 5, 6)),
                (cross_q, "xvw", (0, 3, 5, 6)),
                (cross_proj, "xvw", (0, 3, 5, 6)),
                (enc_w_in, "x", (0, 6)),
                (enc_w_out, "y", (0, 6)),
                (self_kv, "x", (2, 6)),
                (self_q, "y", (2, 6)),
                (self_proj, "y", (2, 6)),
            ],
    )
    cross_kv, cross_q, cross_proj, enc_w_in, enc_w_out, self_kv, self_q, self_proj = given
    enc_bias_one = column_sum(grad_branch)
    grad_source = grad_hidden + source_total.astype(F32)
    enc_q, enc_proj_grad, enc_kv = enc_grads
    rest = [
        (enc_w_in, "yvw", (0, 1, 2, 4)),
        (enc_w_out, "xvw", (0, 1, 2, 4)),
        (self_kv, "yvw", (0, 1, 2, 4)),
        (self_q, "xvw", (0, 1, 2, 4)),
        (self_proj, "xvw", (0, 1, 2, 4)),
        (enc_kv, "xyvw", (1, 3, 4, 5, 6)),
        (enc_q, "yxvw", (1, 3, 4, 5, 6)),
        (enc_proj_grad, "yxvw", (1, 3, 4, 5, 6)),
    ]
    small = small_sums(
        jnp.concatenate(
            [
                enc_bias_one,
                enc_bias_two,
                enc_gain_one,
                enc_gain_two,
                enc_shift_one,
                enc_shift_two,
                dec_bias_one,
                dec_bias_two,
                dec_bias_three,
                dec_gain_one,
                dec_gain_two,
                dec_gain_three,
                dec_shift_one,
                dec_shift_two,
                dec_shift_three,
            ]
        ).reshape(15, model),
        jnp.concatenate([enc_bias_grad, self_bias, cross_bias, enc_b_in, dec_b_in]).reshape(-1, model),
        (0, 1, 2, 3, 4, 5),
    )
    if plan.kernels:
        vectors, *given = run_chains(6, [small] + plan.chains(rest), 7)
        whole, halves = vectors[: small.rows], vectors[small.rows :]
    else:
        whole, halves = place.all_sum(*small.vectors)
        given = [place.scatter(array, True) for array, _, _ in rest]
        dec_w_in, dec_w_out, cross_kv, cross_q, cross_proj = (
            place.scatter(array, True)
            for array in (dec_w_in, dec_w_out, cross_kv, cross_q, cross_proj)
        )
    enc_w_in, enc_w_out, self_kv, self_q, self_proj, enc_kv, enc_q, enc_proj_grad = given

    def qkv_grads(of_q, of_kv):
        return jnp.stack([of_q, of_kv[:, :width], of_kv[:, width:]])

    whole, halves = whole.reshape(-1, model), halves.reshape(-1)
    small = [halves[a:b] for a, b in zip(marks[:-1], marks[1:])]
    return (
        place.hand_out(encoded_low)[None],
        place.hand_out(decoded.astype(BF16))[None],
        place.hand_out(rounded(grad_source).astype(BF16)).astype(F32)[None],
        place.hand_out(rounded(grad_target).astype(BF16)).astype(F32)[None],
        qkv_grads(enc_q, enc_kv),
        small[0].reshape(2, width),
        enc_proj_grad.T,
        enc_w_in,
        small[3],
        enc_w_out.T,
        whole[0:2],
        whole[2:4],
        whole[4:6],
        qkv_grads(self_q, self_kv),
        small[1].reshape(2, width),
        self_proj.T,
        qkv_grads(cross_q, cross_kv),
        small[2].reshape(2, width),
        cross_proj.T,
        dec_w_in,
        small[4],
        dec_w_out.T,
        whole[6:9],
        whole[9:12],
        whole[12:15],
    )


def solution(mesh):
    return jax.shard_map(
        shards,
        mesh=mesh,
        in_specs=(
            P("dp", "seq", None),
            P("dp", "seq", None),
            P("dp", None),
            P("dp", None),
            P(None, None, "tensor"),
            P(None, "tensor"),
            P("tensor", None),
            P(None, "tensor"),
            P("tensor"),
            P("tensor", None),
            P(),
            P(),
            P(),
            P(None, None, "tensor"),
            P(None, "tensor"),
            P("tensor", None),
            P(None, None, "tensor"),
            P(None, "tensor"),
            P("tensor", None),
            P(None, "tensor"),
            P("tensor"),
            P("tensor", None),
            P(),
            P(),
            P(),
            P("dp", "seq", None),
            P("dp", "seq", None),
        ),
        out_specs=(
            P("dp", "seq", None),
            P("dp", "seq", None),
            P("dp", "seq", None),
            P("dp", "seq", None),
            P(None, ("dp", "seq"), "tensor"),
            P(None, "tensor"),
            P("tensor", ("dp", "seq")),
            P(("dp", "seq"), "tensor"),
            P("tensor"),
            P("tensor", ("dp", "seq")),
            P(),
            P(),
            P(),
            P(None, ("dp", "seq"), "tensor"),
            P(None, "tensor"),
            P("tensor", ("dp", "seq")),
            P(None, ("dp", "seq"), "tensor"),
            P(None, "tensor"),
            P("tensor", ("dp", "seq")),
            P(("dp", "seq"), "tensor"),
            P("tensor"),
            P("tensor", ("dp", "seq")),
            P(),
            P(),
            P(),
        ),
        check_vma=False,
    )
```

```python
import functools
import math

import jax
import jax.numpy as jnp
from jax import lax
from jax.experimental import pallas as pl
from jax.experimental.pallas import tpu as pltpu
from jax.sharding import PartitionSpec as P

HEAD_DIM = 64
EPS = 1e-05
NEG = -1e30
BF16 = jnp.bfloat16
F32 = jnp.float32
NT = (((1,), (1,)), ((), ()))
TN = (((0,), (0,)), ((), ()))
KEY_BLOCK = 512
CHUNKS = 2
DOCS = 4


def dot_plain(left, right):
    return jnp.dot(left, right, preferred_element_type=F32)


def dot_last(left, right):
    return lax.dot_general(left, right, NT, preferred_element_type=F32)


def dot_first(left, right):
    return lax.dot_general(left, right, TN, preferred_element_type=F32)


def column_sum(value):
    return jnp.sum(value.astype(F32), axis=0)


def rounded(value):
    return lax.reduce_precision(value, 8, 7)


def after(array):
    return jnp.minimum(jnp.abs(array[0, 0].astype(F32)), 0.0)


def norm_forward(hidden, gain, shift):
    centered = hidden - jnp.mean(hidden, axis=-1, keepdims=True)
    spread = jnp.mean(centered * centered, axis=-1, keepdims=True)
    factor = lax.rsqrt(spread + EPS)
    normed = centered * factor
    return (normed * gain.astype(F32) + shift.astype(F32), (normed, factor))


def norm_backward(grad, saved, gain):
    normed, factor = saved
    scaled = grad * gain.astype(F32)
    centered = scaled - jnp.mean(scaled, axis=-1, keepdims=True)
    grad_hidden = factor * (centered - normed * jnp.mean(scaled * normed, axis=-1, keepdims=True))
    return (grad_hidden, jnp.sum(grad * normed, axis=0), jnp.sum(grad, axis=0))


def head_columns(head):
    return slice(head // 2 * 128, head // 2 * 128 + 128)


def head_rows(head):
    return slice(head * HEAD_DIM, (head + 1) * HEAD_DIM)


def own_lanes(shape, head):
    lanes = lax.broadcasted_iota(jnp.int32, shape, 1)
    return lanes >= HEAD_DIM if head % 2 else lanes < HEAD_DIM


class Mask:
    def __init__(self, causal, starts, segments, first_row):
        self.causal, self.starts, self.first_row = causal, starts, first_row
        segments = segments[...]
        low = high = jnp.zeros_like(segments)
        for number in range(DOCS):
            low = jnp.where(segments == number, starts[number], low)
            high = jnp.where(segments == number, starts[number + 1], high)
        self.count = segments.shape[1]
        if causal:
            place = first_row + lax.broadcasted_iota(jnp.int32, segments.shape, 1)
            high = jnp.minimum(high, place + 1)
        self.low, self.high = low, high

    def allowed(self, index, block):
        place = lax.broadcasted_iota(jnp.int32, (block, self.count), 0) + index * block
        return (place >= self.low) & (place < self.high)

    def flag(self, index, block, ends):
        start, stop = index * block, (index + 1) * block
        low, low_last = self.starts[ends[0]], self.starts[ends[1]]
        high_first, high = self.starts[ends[0] + 1], self.starts[ends[1] + 1]
        if self.causal:
            high = jnp.minimum(high, self.first_row + self.count)
            high_first = jnp.minimum(high_first, self.first_row + 1)
        active = (low < stop) & (high > start)
        full = (low_last <= start) & (high_first >= stop)
        return jnp.where(active, jnp.where(full, 2, 1), 0)


def over_blocks(mask, ends, length, block, body, skipped):
    @pl.loop(0, length // block)
    def _(index):
        flag = mask.flag(index, block, ends)
        rows = pl.ds(pl.multiple_of(index * block, block), block)

        @pl.when(flag == 0)
        def _():
            skipped(rows)

        @pl.when(flag == 1)
        def _():
            body(index, rows, True)

        @pl.when(flag == 2)
        def _():
            body(index, rows, False)


def forward_start(q_ref, masked_q, acc, top):
    heads = q_ref.shape[1] // HEAD_DIM
    for head in range(heads):
        pair = q_ref[:, head_columns(head)]
        masked_q[head] = jnp.where(own_lanes(pair.shape, head), pair, jnp.zeros_like(pair))
    acc[...] = jnp.zeros_like(acc)
    top[...] = jnp.full_like(top, NEG)


def forward_block(index, rows, partial, block, kv_ref, mask, masked_q, acc, top):
    heads, count = masked_q.shape[:2]
    width = heads * HEAD_DIM
    if partial:
        allowed = mask.allowed(index, block)
    for head in range(heads):
        cols = head_columns(head)
        scores = lax.dot_general(kv_ref[rows, cols], masked_q[head], NT, preferred_element_type=F32)
        if partial:
            scores = jnp.where(allowed, scores, NEG)
        old = top[head : head + 1, :]
        new = jnp.maximum(old, jnp.max(scores, axis=0, keepdims=True))
        weights = jnp.exp(scores - new).astype(BF16)
        vals = kv_ref[rows, width + cols.start : width + cols.stop]
        vals = jnp.where(own_lanes(vals.shape, head), vals, jnp.ones_like(vals))
        acc[head] = acc[head] * jnp.exp(old - new) + lax.dot_general(
            vals, weights, TN, preferred_element_type=F32
        )
        top[head : head + 1, :] = new


def forward_end(out_ref, lse_ref, acc, top):
    lse_ref[...] = jnp.zeros_like(lse_ref)
    for head in range(acc.shape[0]):
        first = head % 2 * HEAD_DIM
        total = acc[head, HEAD_DIM - first : HEAD_DIM - first + 1, :]
        out_ref[head_rows(head), :] = acc[head, first : first + HEAD_DIM, :] / total
        lse_ref[head : head + 1, :] = top[head : head + 1, :] + jnp.log(total)


def forward_kernel(
    block, causal, starts, ends, segments, q_ref, kv_ref, out_ref, lse_ref, masked_q, acc, top
):
    mask = Mask(causal, starts, segments, ends[2])
    forward_start(q_ref, masked_q, acc, top)

    def body(index, rows, partial):
        forward_block(index, rows, partial, block, kv_ref, mask, masked_q, acc, top)

    over_blocks(mask, ends, kv_ref.shape[0], block, body, lambda rows: None)
    forward_end(out_ref, lse_ref, acc, top)


def backward_start(q_ref, do_ref, dot_ref, out_ref, masked_q, masked_do, delta, dq):
    for head in range(masked_q.shape[0]):
        pair = q_ref[:, head_columns(head)]
        keep = own_lanes(pair.shape, head)
        masked_q[head] = jnp.where(keep, pair, jnp.zeros_like(pair))
        pair = do_ref[:, head_columns(head)]
        masked_do[head] = jnp.where(keep, pair, jnp.zeros_like(pair))
        part = head_rows(head)
        delta[head : head + 1, :] = jnp.sum(
            dot_ref[part, :].astype(F32) * out_ref[part, :], axis=0, keepdims=True
        )
    dq[...] = jnp.zeros_like(dq)


def backward_block(
    index, rows, block, mask, kv_ref, lse_ref, dkv_ref, masked_q, masked_do, delta, dq, between
):
    heads = masked_q.shape[0]
    width = heads * HEAD_DIM
    allowed = mask.allowed(index, block)
    for pair in range(heads // 2):
        if pair == 1:
            between()
        cols = head_columns(2 * pair)
        later = slice(width + cols.start, width + cols.stop)
        keys, vals = kv_ref[rows, cols], kv_ref[rows, later]
        dk = dv = 0.0
        for head in (2 * pair, 2 * pair + 1):
            scores = lax.dot_general(keys, masked_q[head], NT, preferred_element_type=F32)
            probs = jnp.exp(scores - lse_ref[head : head + 1, :])
            probs = jnp.where(allowed, probs, 0.0)
            dprobs = lax.dot_general(vals, masked_do[head], NT, preferred_element_type=F32)
            draw = (probs * (dprobs - delta[head : head + 1, :])).astype(BF16)
            probs = probs.astype(BF16)
            dv = dv + jnp.dot(probs, masked_do[head], preferred_element_type=F32)
            dk = dk + jnp.dot(draw, masked_q[head], preferred_element_type=F32)
            first = head % 2 * HEAD_DIM
            both = lax.dot_general(keys, draw, TN, preferred_element_type=F32)
            dq[head_rows(head), :] += both[first : first + HEAD_DIM]
        dkv_ref[rows, cols] = dk.astype(BF16)
        dkv_ref[rows, later] = dv.astype(BF16)


SCALARS = pl.BlockSpec(memory_space=pltpu.SMEM)
VECTORS = pl.BlockSpec(memory_space=pltpu.VMEM)


ANYWHERE = pl.BlockSpec(memory_space=pl.ANY)


def cost_of(kv, count, width, products):
    flops = 2 * products * kv.shape[0] * count * width
    return pl.CostEstimate(flops=flops, bytes_accessed=flops // 512, transcendentals=0)


def forward_scratch(count, width):
    heads = width // HEAD_DIM
    return [
        pltpu.VMEM((heads, count, 128), BF16),
        pltpu.VMEM((heads, 128, count), F32),
        pltpu.VMEM((8, count), F32),
    ]


def backward_scratch(count, width):
    heads = width // HEAD_DIM
    return [
        pltpu.VMEM((heads, count, 128), BF16),
        pltpu.VMEM((heads, count, 128), BF16),
        pltpu.VMEM((8, count), F32),
        pltpu.VMEM((width, count), F32),
    ]


def attend(queries, kv, mask):
    count, width = queries.shape
    causal, starts, ends, segments = mask
    return pl.pallas_call(
        functools.partial(forward_kernel, KEY_BLOCK, causal),
        out_shape=(
            jax.ShapeDtypeStruct((width, count), F32),
            jax.ShapeDtypeStruct((8, count), F32),
        ),
        in_specs=[SCALARS] * 2 + [VECTORS] * 3,
        out_specs=(VECTORS,) * 2,
        scratch_shapes=forward_scratch(count, width),
        compiler_params=pltpu.CompilerParams(vmem_limit_bytes=40 << 20),
        cost_estimate=cost_of(kv, count, width, 2),
    )(starts, ends, segments, queries, kv)


MESH = pl.DeviceIdType.MESH
DMA = pltpu.SemaphoreType.DMA


class Here:
    def __init__(self, ring):
        self.ring = ring
        self.d, self.z, self.y = (lax.axis_index(a) for a in ("dp", "seq", "tensor"))
        self.core, self.x = lax.rem(self.d, 2), lax.div(self.d, 2)
        self.other_d = self.d + 1 - 2 * self.core
        self.partner = (self.other_d, self.z, self.y)
        self.right = (self.d, self.z + 1, self.y)
        self.left = (self.d, self.z - 1, self.y)
        self.over_x = (self.d + 2 - 4 * lax.rem(self.x, 2), self.z, self.y)
        self.over_y = (self.d, self.z, 1 - self.y)
        self.diagonal = (self.other_d, self.z, 1 - self.y)

    def meet(self, devices):
        barrier = pltpu.get_barrier_semaphore()
        wanted = 0
        for condition, device in devices:

            @pl.when(condition)
            def _(device=device):
                pl.semaphore_signal(barrier, inc=1, device_id=device, device_id_type=MESH)

            wanted = wanted + jnp.where(condition, 1, 0)
        pl.semaphore_wait(barrier, wanted)

    def along_z(self, step):
        return (self.d, lax.rem(self.z + step, self.ring), self.y)

    def everyone(self):
        devices = [self.partner, self.over_x, self.over_y, self.diagonal]
        devices += [self.along_z(step) for step in range(1, self.ring)]
        return [(self.core >= 0, device) for device in devices]

    def crosswise(self):
        return [
            (self.z + 1 < self.ring, (self.other_d, self.z + 1, self.y)),
            (self.z > 0, (self.other_d, self.z - 1, self.y)),
        ]

    def neighbours(self):
        return [
            (self.core >= 0, self.partner),
            (self.z + 1 < self.ring, self.right),
            (self.z > 0, self.left),
        ]


def remote(source, target, sent, received, device):
    return pltpu.make_async_remote_copy(
        src_ref=source,
        dst_ref=target,
        send_sem=sent,
        recv_sem=received,
        device_id=device,
        device_id_type=MESH,
    )


class Gather:
    def __init__(self, here, rows_ref, sems, source=None, owner=None):
        self.here, self.rows_ref, self.source, self.owner = here, rows_ref, source, owner
        self.count = rows_ref.shape[0] // here.ring
        self.size = self.count // (2 * CHUNKS)
        self.sent, self.got, self.core_sent, self.core_got = sems

    def chunk(self, shard, core, chunk):
        start = shard * self.count + core * (self.count // 2) + chunk * self.size
        return self.rows_ref.at[pl.ds(pl.multiple_of(start, self.size), self.size)]

    def ways(self, step):
        here = self.here
        z, ring = here.z, here.ring
        return [
            (0, z - step, z >= step, z - step + 1, (z + 1 < ring) & (z + 1 >= step), here.right),
            (1, z + step, z + step < ring, z + step - 1, (z > 0) & (z + step <= ring), here.left),
        ]

    def along(self, way, step, shard, chunk, device):
        view = self.chunk(shard, self.here.core, chunk)
        k = way * CHUNKS + chunk
        return remote(view, view, self.sent.at[k, step], self.got.at[k, step], device)

    def across(self, way, step, shard, core, chunk):
        view = self.chunk(shard, core, chunk)
        k = way * CHUNKS + chunk
        return remote(
            view, view, self.core_sent.at[k, step], self.core_got.at[k, step], self.here.partner
        )

    def firsts(self):
        found = []
        for chunk in range(CHUNKS):
            for way, _, _, shard, sends, device in self.ways(1):
                if self.source is None:
                    found.append((sends, self.along(way, 1, shard, chunk, device)))
                    continue
                for core in range(2):
                    k = way * CHUNKS + chunk
                    start = core * (self.count // 2) + chunk * self.size
                    to = (self.here.d - self.here.core + core, *device[1:])
                    copy = remote(
                        self.source.at[pl.ds(start, self.size)],
                        self.chunk(shard, core, chunk),
                        self.sent.at[k, core],
                        self.got.at[k, 1],
                        to,
                    )
                    found.append((sends & self.owner, copy))
        return found

    def begin(self):
        for condition, copy in self.firsts():
            pl.when(condition)(copy.start)

    def advance(self, step):
        for chunk in range(CHUNKS):
            for way, shard, comes, _, _, _ in self.ways(step):

                @pl.when(comes)
                def _(way=way, shard=shard, chunk=chunk):
                    self.along(way, step, shard, chunk, self.here.partner).wait_recv()

                _, _, _, _, sends, device = self.ways(step + 1)[way]

                @pl.when(sends)
                def _(way=way, shard=shard, chunk=chunk, device=device):
                    self.along(way, step + 1, shard, chunk, device).start()

                @pl.when(comes)
                def _(way=way, shard=shard, chunk=chunk):
                    self.across(way, step, shard, self.here.core, chunk).start()

    def finish(self):
        for condition, copy in self.firsts():
            pl.when(condition)(copy.wait_send)

        @pl.loop(1, self.here.ring)
        def _(step):
            for chunk in range(CHUNKS):
                for way, shard, comes, out, sends, device in self.ways(step):

                    @pl.when(sends & (step > 1))
                    def _(way=way, out=out, device=device, chunk=chunk):
                        self.along(way, step, out, chunk, device).wait_send()

                    @pl.when(comes)
                    def _(way=way, shard=shard, chunk=chunk):
                        core = self.here.core
                        self.across(way, step, shard, core, chunk).wait_send()
                        self.across(way, step, shard, 1 - core, chunk).wait_recv()


def pieces_of(weights):
    found = []
    for k, weight in enumerate(weights):
        rows, columns = weight.shape
        number = 1 if rows % 3 else 3
        while 2 * rows * columns > 655360 * number and rows % (64 * number) == 0:
            number *= 2
        found += [(k, i * (rows // number), rows // number) for i in range(number)]
    return found


def beside(weight, model):
    rows, columns = weight.shape
    matrices = 3 if rows == 3 * model else 1
    return jax.ShapeDtypeStruct((rows // matrices, columns * matrices), weight.dtype)


AHEAD = 4


class Fetch:
    def __init__(self, here, inputs, outputs, sems):
        self.here, self.inputs, self.outputs = here, inputs, outputs
        self.y_sent, self.y_got, self.x_sent, self.x_got, self.core_sent, self.core_got = sems
        self.pieces = pieces_of(inputs)
        self.matrices = [
            (k, matrix)
            for k, (given, out) in enumerate(zip(inputs, outputs))
            for matrix in range(given.shape[0] // out.shape[0])
        ]
        self.number = len(self.pieces)
        self.own = lax.rem(here.x, 2)

    def devices(self):
        here = self.here
        return [(here.core >= 0, here.diagonal), (here.core == 1, here.over_x)]

    def part(self, p, which):
        k, start, rows = self.pieces[p]
        first = pl.multiple_of(start + which * (rows // 2), 16)
        return self.inputs[k].at[pl.ds(first, rows // 2)]

    def place(self, p, which):
        k, start, rows = self.pieces[p]
        out = self.outputs[k]
        matrix, start = divmod(start, out.shape[0])
        columns = self.inputs[k].shape[1]
        first = pl.multiple_of(start + which * (rows // 2), 16)
        return out.at[pl.ds(first, rows // 2), pl.ds(matrix * columns, columns)]

    def over_y(self, p):
        return remote(
            self.part(p, self.own),
            self.place(p, self.own),
            self.y_sent.at[p],
            self.y_got.at[p],
            self.here.diagonal,
        )

    def over_x(self, p, which):
        view = self.place(p, which)
        return remote(view, view, self.x_sent.at[p], self.x_got.at[p], self.here.over_x)

    def across(self, m):
        k, matrix = self.matrices[m]
        rows, columns = self.outputs[k].shape[0], self.inputs[k].shape[1]
        return remote(
            self.inputs[k].at[pl.ds(matrix * rows, rows)],
            self.outputs[k].at[:, pl.ds(matrix * columns, columns)],
            self.core_sent.at[m],
            self.core_got.at[m],
            self.here.partner,
        )

    def begin(self):
        @pl.when(self.here.core == 0)
        def _():
            for p in range(min(AHEAD, self.number)):
                self.over_y(p).start()

        @pl.when(self.here.core == 1)
        def _():
            for m in range(len(self.matrices)):
                self.across(m).start()

    def advance(self, p):
        @pl.when(self.here.core == 0)
        def _():
            self.over_y(p).wait_send()
            if p + AHEAD < self.number:
                self.over_y(p + AHEAD).start()

        @pl.when(self.here.core == 1)
        def _():
            self.over_y(p).wait_recv()
            self.over_x(p, self.own).start()

    def end(self):
        @pl.when(self.here.core == 0)
        def _():
            for m in range(len(self.matrices)):
                self.across(m).wait_recv()

        @pl.when(self.here.core == 1)
        def _():
            for p in range(self.number):
                self.over_x(p, self.own).wait_send()
                self.over_x(p, 1 - self.own).wait_recv()
            for m in range(len(self.matrices)):
                self.across(m).wait_send()


def gather_sems(ring):
    return [DMA((2 * CHUNKS, ring))] * 4


def fetch_sems(weights):
    number = len(pieces_of(weights))
    return [DMA((number,))] * 4 + [DMA((3 * len(weights),))] * 2


def opening_kernel(ring, number, *refs):
    inputs, outputs, sems = refs[: 4 + number], refs[4 + number : 8 + 2 * number], refs[8 + 2 * number :]
    source, target, segments, vectors = inputs[:4]
    source_all, target_out, segments_out, vectors_out = outputs[:4]
    shard_sems, vector_sems = sems[:3], sems[3:6]
    here = Here(ring)
    fetch = Fetch(here, inputs[4:], outputs[4:], sems[10:])
    here.meet(here.neighbours() + here.crosswise() + fetch.devices())
    count = source.shape[0]
    own = pl.ds(pl.multiple_of(here.z * count, count), count)
    moves = [
        (source, source_all.at[own]),
        (target, target_out),
        (segments, segments_out),
    ]
    owner = here.core == here.y

    def shard_copy(k):
        start, end = moves[k]
        sent, got, copied = shard_sems
        return (
            remote(start, end, sent.at[k], got.at[k], here.partner),
            pltpu.make_async_copy(start, end, copied.at[k]),
        )

    def vector_copy():
        sent, got, copied = vector_sems
        return (
            remote(vectors, vectors_out, sent, got, here.diagonal),
            pltpu.make_async_copy(vectors, vectors_out, copied),
        )

    def wait_shard(k):
        across, local = shard_copy(k)

        @pl.when(owner)
        def _():
            across.wait_send()
            local.wait()

        @pl.when(jnp.logical_not(owner))
        def _():
            across.wait_recv()

    @pl.when(owner)
    def _():
        for k in range(3):
            across, local = shard_copy(k)
            across.start()
            local.start()

    @pl.when(here.core == 0)
    def _():
        across, local = vector_copy()
        across.start()
        local.start()

    gather = Gather(here, source_all, sems[6:10], source, owner)
    gather.begin()
    fetch.begin()
    done = 0
    for step in range(1, ring):
        while done < fetch.number * (2 * step - 1) // (2 * ring - 2):
            fetch.advance(done)
            done += 1
        gather.advance(step)
    while done < fetch.number:
        fetch.advance(done)
        done += 1
    gather.finish()
    wait_shard(0)
    wait_shard(1)
    wait_shard(2)
    fetch.end()
    across, local = vector_copy()

    @pl.when(here.core == 0)
    def _():
        across.wait_send()
        local.wait()

    @pl.when(here.core == 1)
    def _():
        across.wait_recv()


def opening(ring, source, target, segments, vectors, weights):
    inputs = (source, target, segments, vectors) + tuple(weights)
    count, model = source.shape
    rows = jax.ShapeDtypeStruct((ring * count, model), BF16)
    shapes = (rows, jax.ShapeDtypeStruct(target.shape, BF16)) + tuple(jax.ShapeDtypeStruct(v.shape, v.dtype) for v in inputs[2:4])
    shapes += tuple(beside(weight, model) for weight in weights)
    number = len(weights)
    return pl.pallas_call(
        functools.partial(opening_kernel, ring, number),
        out_shape=shapes,
        in_specs=[VECTORS] * 4 + [ANYWHERE] * number,
        out_specs=(ANYWHERE,) + (VECTORS,) * 3 + (ANYWHERE,) * number,
        scratch_shapes=[DMA((3,))] * 3 + [DMA] * 3 + gather_sems(ring) + fetch_sems(weights),
        compiler_params=pltpu.CompilerParams(collective_id=1, has_side_effects=True),
    )(*inputs)


def gather_attend_kernel(
    block, causal, ring, number, tokens, starts, segments, q_ref, kv_ref, own_ref, *refs
):
    weights, refs = refs[:number], refs[number + tokens :]
    out_ref, lse_ref, all_ref = refs[:3]
    fetched, refs = refs[3 : 3 + number], refs[3 + number :]
    masked_q, acc, top, copied = refs[:4]
    here = Here(ring)
    gather = Gather(here, all_ref, refs[4:8])
    fetch = Fetch(here, weights, fetched, refs[8:])
    here.meet(here.neighbours() + fetch.devices())
    count = own_ref.shape[0]
    first_row = pl.multiple_of(here.z * count, count)
    local = pltpu.make_async_copy(own_ref, all_ref.at[pl.ds(first_row, count)], copied)
    local.start()
    fetch.begin()
    local.wait()
    gather.begin()
    mask = Mask(causal, starts, segments, first_row)
    forward_start(q_ref, masked_q, acc, top)
    blocks = kv_ref.shape[0] // block

    @pl.loop(0, blocks)
    def _(index):
        rows = pl.ds(pl.multiple_of(index * block, block), block)
        forward_block(index, rows, True, block, kv_ref, mask, masked_q, acc, top)

        @pl.when((index >= 1) & (index < ring))
        def _():
            gather.advance(index)

        for p in range(fetch.number):
            pl.when(index == 1 + p * (blocks - 1) // fetch.number)(
                functools.partial(fetch.advance, p)
            )

    forward_end(out_ref, lse_ref, acc, top)

    gather.finish()
    fetch.end()


def gather_attend(number, ring, queries, kv, mask, own, weights, tokens=()):
    count, width = queries.shape
    causal, starts, _, segments = mask
    fetched = len(weights)
    return pl.pallas_call(
        functools.partial(gather_attend_kernel, KEY_BLOCK, causal, ring, fetched, len(tokens)),
        out_shape=(
            jax.ShapeDtypeStruct((width, count), F32),
            jax.ShapeDtypeStruct((8, count), F32),
            jax.ShapeDtypeStruct((ring * own.shape[0], own.shape[1]), BF16),
        )
        + tuple(beside(weight, own.shape[1]) for weight in weights),
        in_specs=[SCALARS] + [VECTORS] * 4 + [ANYWHERE] * (fetched + len(tokens)),
        out_specs=(VECTORS, VECTORS) + (ANYWHERE,) * (1 + fetched),
        scratch_shapes=forward_scratch(count, width)
        + [DMA]
        + gather_sems(ring)
        + fetch_sems(weights),
        compiler_params=pltpu.CompilerParams(
            vmem_limit_bytes=40 << 20, collective_id=number, has_side_effects=True
        ),
        cost_estimate=cost_of(kv, count, width, 2),
    )(starts, segments, queries, kv, own, *weights, *tokens)


class Part:
    def __init__(self, inputs, in_specs, out_shapes, scratch, bind):
        self.inputs, self.in_specs, self.out_shapes = inputs, in_specs, out_shapes
        self.scratch, self.bind = scratch, bind


def run_parts(number, body, parts, cost=None):
    ring = lax.axis_size("seq")
    counts = [(len(p.inputs), len(p.out_shapes), len(p.scratch)) for p in parts]

    def kernel(*refs):
        here = Here(ring)
        taken, offset = [[] for _ in parts], 0
        for kind in range(3):
            for refs_of, count in zip(taken, counts):
                refs_of.append(refs[offset : offset + count[kind]])
                offset += count[kind]
        here.meet(here.everyone())
        body(here, *(p.bind(here, *refs_of) for p, refs_of in zip(parts, taken)))

    results = pl.pallas_call(
        kernel,
        out_shape=[shape for p in parts for shape in p.out_shapes],
        in_specs=[spec for p in parts for spec in p.in_specs],
        out_specs=[VECTORS for p in parts for _ in p.out_shapes],
        scratch_shapes=[shape for p in parts for shape in p.scratch],
        compiler_params=pltpu.CompilerParams(
            vmem_limit_bytes=62 << 20, collective_id=number, has_side_effects=True
        ),
        cost_estimate=cost,
    )(*(array for p in parts for array in p.inputs))
    given = []
    for _, count, _ in counts:
        given.append(results[:count])
        results = results[count:]
    return given


class Stage:
    def __init__(self, here, kind, source, result, buffers, sems):
        self.here, self.kind, self.source, self.result = here, kind, source, result
        self.buffers, (self.sent, self.got) = buffers, sems
        rows = source.shape[0]
        if kind == "x":
            half = rows // 2
            self.kept = [half * here.x]
            self.given = [half * (1 - here.x)]
            self.size, self.to = half, here.over_x
        elif kind == "y":
            self.size = 192
            self.starts = list(range(0, rows, 2 * self.size))
        elif kind == "v":
            bit = lax.rem(here.z, 2)
            self.size = rows // 4
            self.kept = [self.size * bit, self.size * (bit + 2)]
            self.given = [self.size * (1 - bit), self.size * (3 - bit)]
            self.to = (here.d, here.z + 1 - 2 * bit, here.y)
        else:
            bit = lax.div(here.z, 2)
            self.size = rows // 2
            self.kept, self.given = [self.size * bit], [self.size * (1 - bit)]
            self.to = (here.d, here.z + 2 - 4 * bit, here.y)

    def rows(self, start):
        if not isinstance(start, int):
            start = pl.multiple_of(start, 16)
        return pl.ds(start, self.size)

    def move(self, start, place, buffer, sem, to):
        return remote(
            self.source.at[self.rows(start)],
            self.buffers[buffer].at[self.rows(place * self.size)],
            self.sent.at[sem],
            self.got.at[sem],
            to,
        )

    def moves(self):
        here = self.here
        if self.kind != "y":
            both = [
                (None, self.move(start, k, 0, k, self.to)) for k, start in enumerate(self.given)
            ]
            return both, both
        sends, arrivals = [], []
        for k, start in enumerate(self.starts):
            upper = start + self.size
            sends.append((here.core == 0, self.move(upper, k, 0, 2 * k, here.partner)))
            sends.append((here.core == 1, self.move(start, k, 0, 2 * k, here.diagonal)))
            sends.append((here.core == 1, self.move(upper, k, 1, 2 * k + 1, here.over_y)))
            arrivals.append((None, self.move(upper, k, 0, 2 * k, here.partner)))
            arrivals.append((here.core == 1, self.move(upper, k, 1, 2 * k + 1, here.over_y)))
        return sends, arrivals

    @staticmethod
    def each(moves, act):
        for condition, copy in moves:
            if condition is None:
                act(copy)
            else:
                pl.when(condition)(functools.partial(act, copy))

    def begin(self):
        self.each(self.moves()[0], lambda copy: copy.start())

    def end(self):
        sends, arrivals = self.moves()
        self.each(arrivals, lambda copy: copy.wait_recv())
        kept = self.kept if self.kind != "y" else self.starts
        for k, start in enumerate(kept):
            place = self.rows(k * self.size)

            def add(own_ref, own, place=place):
                both = own_ref[own, :].astype(F32) + self.buffers[0][place, :].astype(F32)
                self.result[place, :] = both.astype(self.result.dtype)

            if self.kind == "y":
                pl.when(self.here.core == 0)(functools.partial(add, self.source, self.rows(start)))
                pl.when(self.here.core == 1)(functools.partial(add, self.buffers[1], place))
            else:
                add(self.source, self.rows(start))
        self.each(sends, lambda copy: copy.wait_send())


class Chain:
    def __init__(self, stages, times):
        self.stages, self.times = stages, times

    def event(self, time):
        for k, own in enumerate(self.times):
            if own == time:
                if k:
                    self.stages[k - 1].end()
                if k < len(self.stages):
                    self.stages[k].begin()


def chain(array, kinds, times):
    rows, columns = array.shape
    scratch, shapes = [], []
    for kind in kinds:
        rows = rows // 2
        scratch += [pltpu.VMEM((rows, columns), BF16)] * (2 if kind == "y" else 1)
        scratch += [DMA((4,))] * 2
        shapes.append((rows, columns))
    scratch += [pltpu.VMEM(shape, BF16) for shape in shapes[:-1]]
    final = jax.ShapeDtypeStruct(shapes[-1], F32 if kinds[-1] == "w" else BF16)

    def bind(here, inputs, outputs, refs):
        refs = list(refs)
        results = refs[len(refs) - len(kinds) + 1 :] + [outputs[0]]
        source, stages = inputs[0], []
        for kind, result in zip(kinds, results):
            buffers = [refs.pop(0) for _ in range(2 if kind == "y" else 1)]
            sems = [refs.pop(0) for _ in range(2)]
            stages.append(Stage(here, kind, source, result, buffers, sems))
            source = result
        return Chain(stages, times)

    return Part((array,), [VECTORS], [final], scratch, bind)


class Small:
    def __init__(self, here, rows, held_rows, given, result, refs, times):
        self.here, self.given, self.result, self.times = here, given, result, times
        self.rows, self.held_rows = rows, held_rows
        self.arrived, self.sent, self.got = refs
        self.bits = [lax.rem(here.z, 2), lax.div(here.z, 2)]

    def copies(self, stage):
        here = self.here
        low, high = self.bits

        def to(device, slot, source=self.result, target=None):
            target = self.arrived.at[slot] if target is None else target
            return remote(source, target, self.sent.at[slot], self.got.at[slot], device)

        if stage < 3:
            device = (
                here.over_x,
                (here.d, here.z + 1 - 2 * low, here.y),
                (here.d, here.z + 2 - 4 * high, here.y),
            )[stage]
            both = [(None, to(device, stage))]
            return both, both
        if stage == 3:
            sends = [
                (None, to(here.over_y, 3)),
                (here.core == 0, to(here.partner, 4)),
                (here.core == 1, to(here.diagonal, 4)),
            ]
            return sends, sends[:1] + [(None, to(here.partner, 4))]
        return [(here.core == 0, to(here.partner, 5))], [(here.core == 1, to(here.partner, 5))]

    def end(self, stage):
        sends, arrivals = self.copies(stage)
        Stage.each(arrivals, lambda copy: copy.wait_recv())
        Stage.each(sends, lambda copy: copy.wait_send())
        core = self.here.core
        if stage < 3:
            self.result[...] += self.arrived[stage]
        elif stage == 3:
            whole, halves = slice(0, self.held_rows), slice(self.held_rows, self.rows)
            self.result[whole, :] += self.arrived[3, whole, :]
            own = jnp.where(core == 0, self.result[halves, :], self.arrived[3, halves, :])
            self.result[halves, :] = own + self.arrived[4, halves, :]
        else:
            whole = slice(0, self.held_rows)

            @pl.when(core == 1)
            def _():
                self.result[whole, :] = self.arrived[5, whole, :]

    def event(self, time):
        for k, own in enumerate(self.times):
            if own == time:
                if k == 0:
                    self.result[...] = self.given[...]
                else:
                    self.end(k - 1)
                if k < 5:
                    Stage.each(self.copies(k)[0], lambda copy: copy.start())


def small_sums(whole, halves, times):
    both = jnp.concatenate([whole, halves])
    rows, columns = both.shape
    shape = jax.ShapeDtypeStruct(both.shape, F32)
    part = Part(
        (both,),
        [VECTORS],
        [shape],
        [pltpu.VMEM((6, rows, columns), F32), DMA((6,)), DMA((6,))],
        lambda here, inputs, outputs, refs: Small(
            here, rows, whole.shape[0], inputs[0], outputs[0], refs, times
        ),
    )
    part.rows, part.vectors = whole.shape[0], (whole.reshape(-1), halves.reshape(-1))
    return part


def run_chains(number, chains, events):
    def body(here, *bound):
        for time in range(events):
            for one in bound:
                one.event(time)

    return [given[0] for given in run_parts(number, body, chains)]


class Back:
    def __init__(self, here, causal, apart, inputs, outputs, scratch):
        self.here, self.causal, self.apart = here, causal, apart
        self.starts, self.segments, self.q, self.kv, self.do, self.dot, self.out, self.lse = inputs[:8]
        self.weights = inputs[8]
        self.dq_out, self.dkv, self.sum = outputs[:3]
        self.query_sum = outputs[3] if apart else None
        self.work, scratch = scratch[:4], scratch[4:]
        self.terms, self.from_core, self.outgoing, self.arrived, self.total = scratch[:5]
        self.core_sent, self.core_got, self.sent, self.got, self.end_sent, self.end_got = scratch[5:11]
        if apart:
            self.query_low, self.query_got, self.query_sems = scratch[11:]
        self.count, self.width = self.q.shape
        self.part = self.count // 2
        self.mask = Mask(causal, self.starts, self.segments, here.z * self.count)

    def half(self, core):
        return pl.ds(pl.multiple_of(core * self.part, self.part), self.part)

    def shard_at(self, turn):
        ring, z, shard = self.here.ring, self.here.z, 0
        for device in range(ring):
            others = [t for t in range(ring) if t != device]
            others.sort(key=lambda t: (ring - t + device) if t > device else (t + ring - device))
            for k, other in enumerate(others):
                shard = jnp.where((z == device) & (turn == k + 1), other, shard)
        return shard

    def across(self, shard):
        return remote(
            self.terms.at[shard, self.half(1 - self.here.core)],
            self.from_core.at[shard],
            self.core_sent.at[shard],
            self.core_got.at[shard],
            self.here.partner,
        )

    def along(self, way, shard, device):
        return remote(
            self.outgoing.at[shard],
            self.arrived.at[way, shard],
            self.sent.at[shard],
            self.got.at[way, shard],
            device,
        )

    def both(self, shard):
        self.across(shard).wait_recv()
        own = self.terms[shard, self.half(self.here.core), :].astype(F32)
        return own + self.from_core[shard].astype(F32)

    def forward(self, shard):
        here = self.here
        self.total[...] = self.both(shard)
        for way, mine, comes, device in (
            (0, shard > here.z, here.z > 0, here.right),
            (1, shard < here.z, here.z + 1 < here.ring, here.left),
        ):

            @pl.when(mine & comes)
            def _(way=way):
                self.along(way, shard, here.partner).wait_recv()
                self.total[...] += self.arrived[way, shard].astype(F32)

        self.outgoing[shard] = self.total[...].astype(BF16)
        for way, mine, device in ((0, shard > here.z, here.right), (1, shard < here.z, here.left)):

            @pl.when(mine)
            def _(way=way, device=device):
                self.along(way, shard, device).start()

    def block(self, shard, between):
        rows = pl.ds(pl.multiple_of(shard * self.count, self.count), self.count)
        backward_block(
            shard, rows, self.count, self.mask, self.kv, self.lse, self.dkv, *self.work, between
        )
        return dot_last(self.dkv[rows, :], self.weights[:, self.width :])

    def run(self, event):
        here, ring = self.here, self.here.ring
        at_end = (here.z == 0) | (here.z == ring - 1)
        event(0)
        backward_start(self.q, self.do, self.dot, self.out, *self.work)

        @pl.loop(1, ring)
        def _(turn):
            shard = self.shard_at(turn)

            def between():
                @pl.when((turn > 1) & at_end)
                def _():
                    self.forward(self.shard_at(turn - 1))

            self.terms[shard] = self.block(shard, between).astype(BF16)
            self.across(shard).start()
            for time in range(1, ring):
                pl.when(turn == time)(functools.partial(event, time))

        def between():
            self.forward(self.shard_at(jnp.where(at_end, ring - 1, 1)))

        own = self.block(here.z, between)
        event(ring)
        low = (self.work[3][...] * HEAD_DIM ** (-0.5)).T.astype(BF16)
        self.dq_out[...] = low
        query = dot_last(low, self.weights[:, : self.width])
        if self.apart:
            self.query_low[...] = query.astype(BF16)
            exchange = remote(
                self.query_low, self.query_got, self.query_sems.at[0], self.query_sems.at[1], here.partner
            )
            exchange.start()
        else:
            own = own + query
        self.terms[here.z] = own.astype(BF16)
        self.across(here.z).start()
        if self.apart:
            exchange.wait()
            self.query_sum[...] = self.query_low[...].astype(F32) + self.query_got[...].astype(F32)

        @pl.when(jnp.logical_not(at_end))
        def _():
            @pl.loop(2, ring)
            def _(turn):
                self.forward(self.shard_at(turn))

        event(ring + 1)
        self.total[...] = self.both(here.z)
        for way, comes in ((0, here.z > 0), (1, here.z + 1 < ring)):

            @pl.when(comes)
            def _(way=way):
                self.along(way, here.z, here.partner).wait_recv()
                self.total[...] += self.arrived[way, here.z].astype(F32)

        own, other = self.half(here.core), self.half(1 - here.core)
        self.sum[own, :] = self.total[...].astype(BF16)
        for half, waits in ((own, False), (other, True)):
            view = self.sum.at[half]
            copy = remote(view, view, self.end_sent, self.end_got, here.partner)
            if waits:
                copy.wait_recv()
            else:
                copy.start()
                copy.wait_send()
        for shard in range(ring):
            self.across(shard).wait_send()

            @pl.when(here.z != shard)
            def _(shard=shard):
                self.along(0, shard, here.partner).wait_send()

        event(ring + 2)


class Products:
    def __init__(self, back, inputs, outputs, scratch, time):
        self.back, self.time = back, time
        self.block, self.copied = scratch
        self.query_in, self.key_in, self.grad_branch, self.mixed = inputs
        self.of_q, self.of_out, self.of_kv, self.of_bias = outputs

    def event(self, time):
        if time != self.time:
            return
        dq, dkv = self.back.dq_out, self.back.dkv
        width = dq.shape[1]
        self.of_q[...] = dot_first(self.query_in[...], dq[...]).astype(BF16)
        self.of_out[...] = dot_first(self.grad_branch[...], self.mixed[...].T).astype(BF16)
        self.of_bias[0:1, :] = jnp.sum(dq[...].astype(F32), axis=0, keepdims=True)
        self.of_bias[1:2, :] = jnp.sum(dkv[:, width:].astype(F32), axis=0, keepdims=True)

        @pl.loop(0, self.of_kv.shape[0] // 256)
        def _(index):
            part = pl.ds(pl.multiple_of(index * 256, 256), 256)
            copy = pltpu.make_async_copy(self.key_in.at[:, part], self.block, self.copied)
            copy.start()
            copy.wait()
            self.of_kv[part, :] = dot_first(self.block[...], dkv[...]).astype(BF16)


def products(box, query_in, key_in, grad_branch, mixed, time):
    model, width = query_in.shape[1], mixed.shape[0]
    return Part(
        (query_in, key_in, grad_branch, mixed),
        [VECTORS, ANYWHERE, VECTORS, VECTORS],
        [
            jax.ShapeDtypeStruct((model, width), BF16),
            jax.ShapeDtypeStruct((model, width), BF16),
            jax.ShapeDtypeStruct((model, 2 * width), BF16),
            jax.ShapeDtypeStruct((2, width), F32),
        ],
        [pltpu.VMEM((key_in.shape[0], 256), BF16), DMA],
        lambda here, inputs, outputs, refs: Products(box["back"], inputs, outputs, refs, time),
    )


class FeedBack:
    def __init__(self, here, inputs, outputs, scratch, time):
        self.here, self.time = here, time
        self.grad, self.x_in = inputs[:2]
        self.streamed = inputs[2:]
        self.sum, self.of_bias, self.of_in, self.of_out = outputs
        self.blocks, (self.low, self.got, self.copied, self.sems) = scratch[:4], scratch[4:]

    def event(self, time):
        if time != self.time:
            return
        span = self.blocks[0].shape[2]
        number = self.of_in.shape[1] // span
        self.sum[...] = jnp.zeros_like(self.sum)

        def columns(index):
            return pl.ds(pl.multiple_of(index * span, span), span)

        def copies(index):
            slot, part = lax.rem(index, 2), columns(index)
            return [
                pltpu.make_async_copy(
                    ref.at[part] if k == 3 else ref.at[:, part],
                    self.blocks[k].at[slot],
                    self.copied.at[k, slot],
                )
                for k, ref in enumerate(self.streamed)
            ]

        for copy in copies(0):
            copy.start()

        @pl.loop(0, number)
        def _(index):
            part = columns(index)

            @pl.when(index + 1 < number)
            def _():
                for copy in copies(index + 1):
                    copy.start()

            for copy in copies(index):
                copy.wait()
            slope, active, w_in, w_out = (block.at[lax.rem(index, 2)] for block in self.blocks)
            hidden = (slope[...] * dot_last(self.grad[...], w_out[...])).astype(BF16)
            self.of_bias[:, part] = jnp.sum(hidden.astype(F32), axis=0, keepdims=True)
            self.sum[...] += dot_last(hidden, w_in[...])
            self.of_in[:, part] = dot_first(self.x_in[...], hidden).astype(BF16)
            self.of_out[:, part] = dot_first(self.grad[...], active[...]).astype(BF16)

        self.low[...] = self.sum[...].astype(BF16)
        exchange = remote(self.low, self.got, self.sems.at[0], self.sems.at[1], self.here.partner)
        exchange.start()
        exchange.wait()
        self.sum[...] = self.low[...].astype(F32) + self.got[...].astype(F32)


def feed_back(grad_branch, slope, w_in, w_out, x_in, active, time):
    count, model = x_in.shape
    units = w_in.shape[1]
    span = 256
    return Part(
        (grad_branch, x_in, slope, active, w_in, w_out),
        [VECTORS] * 2 + [ANYWHERE] * 4,
        [
            jax.ShapeDtypeStruct((count, model), F32),
            jax.ShapeDtypeStruct((1, units), F32),
            jax.ShapeDtypeStruct((model, units), BF16),
            jax.ShapeDtypeStruct((model, units), BF16),
        ],
        [
            pltpu.VMEM((2, count, span), slope.dtype),
            pltpu.VMEM((2, count, span), BF16),
            pltpu.VMEM((2, model, span), BF16),
            pltpu.VMEM((2, span, model), BF16),
            pltpu.VMEM((count, model), BF16),
            pltpu.VMEM((count, model), BF16),
            DMA((4, 2)),
            DMA((2,)),
        ],
        lambda here, *refs: FeedBack(here, *refs, time),
    )


def attend_back(number, saved, grad_mixed, grad_mixed_t, weights, mask, apart, more, box):
    queries, kv, output, lse, _ = saved
    causal, starts, segments = mask
    ring = lax.axis_size("seq")
    count, width = queries.shape
    model = weights[0].shape[0]
    part = count // 2
    shapes = [
        jax.ShapeDtypeStruct((count, width), BF16),
        jax.ShapeDtypeStruct(kv.shape, BF16),
        jax.ShapeDtypeStruct((count, model), BF16),
    ]
    scratch = backward_scratch(count, width) + [
        pltpu.VMEM((ring, count, model), BF16),
        *[pltpu.VMEM((ring, part, model), BF16)] * 2,
        pltpu.VMEM((2, ring, part, model), BF16),
        pltpu.VMEM((part, model), F32),
        *[DMA((ring,))] * 3,
        DMA((2, ring)),
        *[DMA] * 2,
    ]
    if apart:
        shapes.append(jax.ShapeDtypeStruct((count, model), F32))
        scratch += [pltpu.VMEM((count, model), BF16)] * 2 + [DMA((2,))]
    main = Part(
        (starts, segments, queries, kv, grad_mixed, grad_mixed_t, output, lse, weights[0]),
        [SCALARS] + [VECTORS] * 8,
        shapes,
        scratch,
        lambda here, *refs: box.setdefault("back", Back(here, causal, apart, *refs)),
    )

    def body(here, back, *bound):
        def event(time):
            for one in bound:
                one.event(time)

        back.run(event)

    return run_parts(number, body, [main] + list(more), cost_of(kv, count, width, 7))


class Plan:
    def __init__(self, kernels):
        self.kernels = kernels

    def chains(self, wanted):
        return [chain(*one) for one in wanted] if self.kernels else []

    def given(self, wanted, results):
        return results if self.kernels else [one[0] for one in wanted]


class Places:
    def __init__(self, pairs, ring):
        self.pairs, self.ring = pairs, ring
        self.d = lax.axis_index("dp")
        self.x, self.core = self.d // 2, self.d % 2
        self.y, self.z = lax.axis_index("tensor"), lax.axis_index("seq")

    def swap_core(self, value):
        return lax.ppermute(value, "dp", [(i, i ^ 1) for i in range(self.pairs)])

    def swap_y(self, value):
        return lax.ppermute(value, "tensor", [(0, 1), (1, 0)])

    def swap_x(self, value, bit):
        return lax.ppermute(value, "dp", [(i, i ^ (2 << bit)) for i in range(self.pairs)])

    def swap_z(self, value, bit):
        return lax.ppermute(value, "seq", [(i, i ^ (1 << bit)) for i in range(self.ring)])

    def from_z(self, value, step):
        return lax.ppermute(value, "seq", [((i + step) % self.ring, i) for i in range(self.ring)])

    def to_z(self, value, step):
        return lax.ppermute(value, "seq", [(i, (i + step) % self.ring) for i in range(self.ring)])

    def permute(self, value, source_of):
        moves = []
        for d in range(self.pairs):
            for y in range(2):
                source = source_of(d, y)
                if source is not None:
                    moves.append((source[0] * 2 + source[1], d * 2 + y))
        return lax.ppermute(value, ("dp", "tensor"), moves)

    def fetch_weight(self, value):
        return self.permute(value, lambda d, y: (d + 1, y) if d % 2 == 0 else (d - 1, 1 - y))

    def core_sum(self, partial):
        low = rounded(partial)
        return low + self.swap_core(low.astype(BF16)).astype(F32)

    def own_pair(self, rows):
        return jnp.where(self.core == self.y, rows, self.swap_core(rows))

    def hand_out(self, rows):
        other = self.permute(rows, lambda d, y: (d, 1 - y) if d % 2 != y else None)
        return jnp.where(self.core == self.y, rows, other)

    def plan(self):
        return Plan(self.pairs == 4 and self.ring == 4)

    def scatter(self, grad, x_first):
        rows, columns = grad.shape
        owners = self.pairs // 2
        grad = grad.reshape(owners, 2, self.ring, rows // (self.pairs * self.ring), columns)
        for stage in "xyz" if x_first else "yxz":
            if stage == "y":
                kept = lax.dynamic_index_in_dim(grad, self.core, grad.ndim - 4, False)
                sent = lax.dynamic_index_in_dim(grad, 1 - self.core, grad.ndim - 4, False)
                first = self.permute(
                    sent, lambda d, y: (d + 1, 1 - y) if d % 2 == 0 else (d - 1, y)
                )
                second = self.permute(kept, lambda d, y: (d, 1 - y) if d % 2 else None)
                kept = jnp.where(self.core == 0, kept, second)
                grad = (kept.astype(F32) + first.astype(F32)).astype(BF16)
            else:
                axis = 0 if stage == "x" else grad.ndim - 3
                place, swap = (self.x, self.swap_x) if stage == "x" else (self.z, self.swap_z)
                size, bit = grad.shape[axis], 0
                while size > 1:
                    shape = grad.shape[:axis] + (size // 2, 2) + grad.shape[axis + 1 :]
                    grad = grad.reshape(shape)
                    mine = (place >> bit) & 1
                    kept = lax.dynamic_index_in_dim(grad, mine, axis + 1, False)
                    sent = lax.dynamic_index_in_dim(grad, 1 - mine, axis + 1, False)
                    grad = kept.astype(F32) + swap(sent, bit).astype(F32)
                    size, bit = size // 2, bit + 1
                    if stage == "x" or size > 1:
                        grad = grad.astype(BF16)
                grad = lax.squeeze(grad, (axis,))
        return grad.astype(F32)

    def all_sum(self, whole, halves):
        both = jnp.concatenate([whole, halves])
        for bit in range((self.pairs // 2).bit_length() - 1):
            both = both + self.swap_x(both, bit)
        for bit in range(self.ring.bit_length() - 1):
            both = both + self.swap_z(both, bit)
        whole, halves = both[: whole.shape[0]], both[whole.shape[0] :]
        whole = whole + self.swap_y(whole)
        whole = (whole + self.swap_core(whole)) * 0.5
        first = self.permute(halves, lambda d, y: (d + 1, 1 - y) if d % 2 == 0 else (d - 1, y))
        second = self.swap_y(halves)
        halves = jnp.where(self.core == 0, halves, second) + first
        return whole, halves


def starts_of(segments):
    numbers = jnp.arange(8, dtype=jnp.int32)
    return jnp.sum(segments[None, :] < numbers[:, None], axis=1, dtype=jnp.int32)


def mask_of(query_seg, key_starts, first_row, causal):
    ends = jnp.stack([query_seg[0], query_seg[-1], first_row])
    return (causal, key_starts, ends, query_seg[None])


def projected(query_in, key_in, weights):
    w_all, b_q, b_kv = weights
    width = b_q.shape[0]
    scale = HEAD_DIM ** (-0.5)
    queries = ((dot_plain(query_in, w_all[:, :width]) + b_q).astype(BF16) * scale).astype(BF16)
    return queries, (dot_plain(key_in, w_all[:, width:]) + b_kv).astype(BF16)


def attention_output(place, queries, kv, output, lse, out_weight, out_bias):
    mixed = output.astype(BF16)
    branch = place.core_sum(dot_first(mixed, out_weight)) + out_bias.astype(F32)
    return (branch, (queries, kv, output, lse, mixed))


def attention_backward(
    number, grad_branch, saved, query_in, key_in, weights, out_weight, mask, apart, plan, wanted, inside=()
):
    mixed = saved[4]
    grad_mixed = dot_last(grad_branch, out_weight).astype(BF16)
    grad_mixed_t = dot_last(out_weight, grad_branch).astype(BF16)
    box = {}
    more = []
    if plan.kernels:
        made = products(box, query_in, key_in, grad_branch, mixed, 5)
        more = [made, *plan.chains(wanted), *inside]
    (grad_q, grad_kv, *sums), *rest = attend_back(
        number, saved, grad_mixed, grad_mixed_t, weights, mask, apart, more, box
    )
    if plan.kernels:
        *grads, grad_bias = rest.pop(0)
    else:
        grads = (
            dot_first(query_in, grad_q).astype(BF16),
            dot_first(grad_branch, mixed.T).astype(BF16),
            dot_first(key_in, grad_kv).astype(BF16),
        )
        grad_bias = jnp.stack([column_sum(grad_q), column_sum(grad_kv[:, grad_q.shape[1] :])])
    given = [results[0] for results in rest[: len(rest) - len(inside)]]
    rest = rest[len(rest) - len(inside) :]
    return (sums, grads, grad_bias.reshape(-1), plan.given(wanted, given), rest)


def feed_forward(place, x_in, w_in, b_in, w_out, b_out):
    hidden = dot_plain(x_in, w_in) + b_in.astype(F32)
    spread = 0.5 * (1.0 + lax.erf(hidden * 0.5**0.5))
    active = (hidden * spread).astype(BF16)
    slope = spread + hidden * jnp.exp(-0.5 * hidden * hidden) * (2.0 * math.pi) ** (-0.5)
    branch = place.core_sum(dot_plain(active, w_out)) + b_out.astype(F32)
    return (branch, (slope, active))


def feed_backward(place, grad_branch, saved, x_in, w_in, w_out):
    slope, active = saved
    grad_hidden = (slope * dot_last(grad_branch, w_out)).astype(BF16)
    grad_in = place.core_sum(dot_last(grad_hidden, w_in))
    return (
        grad_in,
        dot_first(x_in, grad_hidden).astype(BF16),
        column_sum(grad_hidden),
        dot_first(grad_branch, active).astype(BF16),
    )


def shards(
    source,
    target,
    source_segments,
    target_segments,
    enc_qkv,
    enc_qv_bias,
    enc_proj,
    enc_ff_in,
    enc_ff_in_bias,
    enc_ff_out,
    enc_bias,
    enc_gains,
    enc_shifts,
    dec_self,
    dec_self_bias,
    dec_self_proj,
    dec_cross,
    dec_cross_bias,
    dec_cross_proj,
    dec_ff_in,
    dec_ff_in_bias,
    dec_ff_out,
    dec_bias,
    dec_gains,
    dec_shifts,
    enc_cotangent,
    dec_cotangent,
):
    count = source.shape[1]
    model = source.shape[2]
    place = Places(lax.axis_size("dp"), lax.axis_size("seq"))
    first_row = place.z * count

    ring = place.ring
    width = enc_qkv.shape[2]
    hidden_units = enc_ff_in.shape[1]

    vectors = jnp.concatenate(
        [
            enc_qv_bias.reshape(-1),
            dec_self_bias.reshape(-1),
            dec_cross_bias.reshape(-1),
            enc_ff_in_bias,
            dec_ff_in_bias,
        ]
    ).astype(F32)
    (
        x_all,
        ts,
        segments,
        vectors,
        enc_qkv,
        enc_proj,
        dec_self,
        dec_self_proj,
    ) = opening(
        ring,
        source[0],
        target[0],
        jnp.concatenate([source_segments, target_segments]),
        vectors.reshape(-1, 128),
        (
            enc_qkv.reshape(-1, width),
            enc_proj,
            dec_self.reshape(-1, width),
            dec_self_proj,
        ),
    )
    vectors = vectors.reshape(-1)
    xs = lax.dynamic_slice_in_dim(x_all, first_row, count, 0)
    dec_ff_in = place.fetch_weight(dec_ff_in)
    dec_ff_out = place.fetch_weight(dec_ff_out)
    enc_cot = place.own_pair(enc_cotangent[0])
    dec_cot = place.own_pair(dec_cotangent[0])

    marks = [0, 2 * width, 4 * width, 6 * width, 6 * width + hidden_units, 6 * width + 2 * hidden_units]
    enc_qv_bias, dec_self_bias, dec_cross_bias, enc_ff_in_bias, dec_ff_in_bias = (
        vectors[a:b] for a, b in zip(marks[:-1], marks[1:])
    )

    def prepared(qkv, bias):
        b_kv = jnp.concatenate([jnp.zeros((width,), F32), bias[width:]])
        return (qkv, bias[:width], b_kv)

    enc_w = prepared(enc_qkv, enc_qv_bias)
    self_w = prepared(dec_self, dec_self_bias)

    source_keys, target_keys = segments[0], segments[1]
    source_own = lax.dynamic_slice_in_dim(source_keys, first_row, count, 0)
    target_own = lax.dynamic_slice_in_dim(target_keys, first_row, count, 0)
    source_starts, target_starts = starts_of(source_keys), starts_of(target_keys)
    enc_mask = mask_of(source_own, source_starts, first_row, False)
    self_mask = mask_of(target_own, target_starts, first_row, True)
    cross_mask = mask_of(target_own, source_starts, first_row, False)

    queries, kv = projected(xs, x_all, enc_w)
    output, lse, t_all, enc_ff_in, enc_ff_out = gather_attend(
        7, ring, queries, kv, enc_mask, ts, (enc_ff_in, enc_ff_out)
    )
    branch, enc_attn = attention_output(place, queries, kv, output, lse, enc_proj, enc_bias[0])
    first, enc_norm_one = norm_forward(xs.astype(F32) + branch, enc_gains[0], enc_shifts[0])
    first_low = first.astype(BF16)
    enc_ff_in_bias = enc_ff_in_bias + after(dec_ff_in)
    branch, enc_feed = feed_forward(
        place, first_low, enc_ff_in, enc_ff_in_bias, enc_ff_out, enc_bias[1]
    )
    encoded, enc_norm_two = norm_forward(first + branch, enc_gains[1], enc_shifts[1])
    encoded_low = encoded.astype(BF16)

    queries, kv = projected(ts, t_all, self_w)
    output, lse, e_all, dec_cross, dec_cross_proj = gather_attend(
        2,
        ring,
        queries,
        kv,
        self_mask,
        encoded_low,
        (dec_cross.reshape(-1, width), dec_cross_proj),
        (dec_ff_out,),
    )
    cross_w = prepared(dec_cross, dec_cross_bias)
    branch, self_attn = attention_output(
        place, queries, kv, output, lse, dec_self_proj, dec_bias[0]
    )
    second, dec_norm_one = norm_forward(ts.astype(F32) + branch, dec_gains[0], dec_shifts[0])
    second_low = second.astype(BF16)
    queries, kv = projected(second_low, e_all, cross_w)
    output, lse = attend(queries, kv, cross_mask)
    branch, cross_attn = attention_output(
        place, queries, kv, output, lse, dec_cross_proj, dec_bias[1]
    )
    third, dec_norm_two = norm_forward(second + branch, dec_gains[1], dec_shifts[1])
    third_low = third.astype(BF16)
    branch, dec_feed = feed_forward(
        place, third_low, dec_ff_in, dec_ff_in_bias, dec_ff_out, dec_bias[2]
    )
    decoded, dec_norm_three = norm_forward(third + branch, dec_gains[2], dec_shifts[2])

    def back_mask(mask):
        return (mask[0], mask[1], mask[3])

    grad_hidden, dec_gain_three, dec_shift_three = norm_backward(
        dec_cot.astype(F32), dec_norm_three, dec_gains[2]
    )
    grad_branch = grad_hidden.astype(BF16)
    feed_in, dec_w_in, dec_b_in, dec_w_out = feed_backward(
        place, grad_branch, dec_feed, third_low, dec_ff_in, dec_ff_out
    )
    dec_bias_three = column_sum(grad_branch)
    grad_third = grad_hidden + feed_in
    grad_hidden, dec_gain_two, dec_shift_two = norm_backward(grad_third, dec_norm_two, dec_gains[1])
    grad_branch = grad_hidden.astype(BF16)
    plan = place.plan()
    (key_total, query_total), cross_grads, cross_bias, (dec_w_in, dec_w_out), _ = attention_backward(
        3,
        grad_branch,
        cross_attn,
        second_low,
        e_all,
        cross_w,
        dec_cross_proj,
        back_mask(cross_mask),
        True,
        plan,
        [(dec_w_in, "x", (0, 6)), (dec_w_out, "y", (0, 6))],
    )
    dec_bias_two = column_sum(grad_branch)
    grad_second = grad_hidden + query_total
    grad_hidden, dec_gain_one, dec_shift_one = norm_backward(
        grad_second, dec_norm_one, dec_gains[0]
    )
    grad_branch = grad_hidden.astype(BF16)
    cross_q, cross_proj, cross_kv = cross_grads
    target_hidden, target_branch = grad_hidden, grad_branch
    grad_hidden, enc_gain_two, enc_shift_two = norm_backward(
        enc_cot.astype(F32) + key_total.astype(F32), enc_norm_two, enc_gains[1]
    )
    grad_branch = grad_hidden.astype(BF16)
    enc_bias_two = column_sum(grad_branch)
    slope, active = enc_feed
    (target_total,), self_grads, self_bias, given, inside = attention_backward(
        4,
        target_branch,
        self_attn,
        ts,
        t_all,
        self_w,
        dec_self_proj,
        back_mask(self_mask),
        False,
        plan,
            [
                (dec_w_in, "yvw", (0, 3, 5, 6)),
                (dec_w_out, "xvw", (0, 3, 5, 6)),
                (cross_kv, "x", (1, 6)),
                (cross_q, "y", (1, 6)),
                (cross_proj, "y", (1, 6)),
            ],
        [feed_back(grad_branch, slope, enc_ff_in, enc_ff_out, first_low, active, 5)]
        if plan.kernels
        else (),
    )
    dec_w_in, dec_w_out, cross_kv, cross_q, cross_proj = given
    if plan.kernels:
        feed_in, enc_b_in, enc_w_in, enc_w_out = inside[0]
        enc_b_in = enc_b_in.reshape(-1)
    else:
        feed_in, enc_w_in, enc_b_in, enc_w_out = feed_backward(
            place, grad_branch, enc_feed, first_low, enc_ff_in, enc_ff_out
        )
    dec_bias_one = column_sum(target_branch)
    grad_target = target_hidden + target_total.astype(F32)
    grad_first = grad_hidden + feed_in
    grad_hidden, enc_gain_one, enc_shift_one = norm_backward(grad_first, enc_norm_one, enc_gains[0])
    grad_branch = grad_hidden.astype(BF16)
    self_q, self_proj, self_kv = self_grads
    (source_total,), enc_grads, enc_bias_grad, given, _ = attention_backward(
        5,
        grad_branch,
        enc_attn,
        xs,
        x_all,
        enc_w,
        enc_proj,
        back_mask(enc_mask),
        False,
        plan,
            [
                (cross_kv, "yvw", (0, 3, 5, 6)),
                (cross_q, "xvw", (0, 3, 5, 6)),
                (cross_proj, "xvw", (0, 3, 5, 6)),
                (enc_w_in, "x", (0, 6)),
                (enc_w_out, "y", (0, 6)),
                (self_kv, "x", (2, 6)),
                (self_q, "y", (2, 6)),
                (self_proj, "y", (2, 6)),
            ],
    )
    cross_kv, cross_q, cross_proj, enc_w_in, enc_w_out, self_kv, self_q, self_proj = given
    enc_bias_one = column_sum(grad_branch)
    grad_source = grad_hidden + source_total.astype(F32)
    enc_q, enc_proj_grad, enc_kv = enc_grads
    rest = [
        (enc_w_in, "yvw", (0, 1, 2, 4)),
        (enc_w_out, "xvw", (0, 1, 2, 4)),
        (self_kv, "yvw", (0, 1, 2, 4)),
        (self_q, "xvw", (0, 1, 2, 4)),
        (self_proj, "xvw", (0, 1, 2, 4)),
        (enc_kv, "xyvw", (1, 3, 4, 5, 6)),
        (enc_q, "yxvw", (1, 3, 4, 5, 6)),
        (enc_proj_grad, "yxvw", (1, 3, 4, 5, 6)),
    ]
    small = small_sums(
        jnp.concatenate(
            [
                enc_bias_one,
                enc_bias_two,
                enc_gain_one,
                enc_gain_two,
                enc_shift_one,
                enc_shift_two,
                dec_bias_one,
                dec_bias_two,
                dec_bias_three,
                dec_gain_one,
                dec_gain_two,
                dec_gain_three,
                dec_shift_one,
                dec_shift_two,
                dec_shift_three,
            ]
        ).reshape(15, model),
        jnp.concatenate([enc_bias_grad, self_bias, cross_bias, enc_b_in, dec_b_in]).reshape(-1, model),
        (0, 1, 2, 3, 4, 5),
    )
    if plan.kernels:
        vectors, *given = run_chains(6, [small] + plan.chains(rest), 7)
        whole, halves = vectors[: small.rows], vectors[small.rows :]
    else:
        whole, halves = place.all_sum(*small.vectors)
        given = [place.scatter(array, True) for array, _, _ in rest]
        dec_w_in, dec_w_out, cross_kv, cross_q, cross_proj = (
            place.scatter(array, True)
            for array in (dec_w_in, dec_w_out, cross_kv, cross_q, cross_proj)
        )
    enc_w_in, enc_w_out, self_kv, self_q, self_proj, enc_kv, enc_q, enc_proj_grad = given

    def qkv_grads(of_q, of_kv):
        return jnp.stack([of_q, of_kv[:, :width], of_kv[:, width:]])

    whole, halves = whole.reshape(-1, model), halves.reshape(-1)
    small = [halves[a:b] for a, b in zip(marks[:-1], marks[1:])]
    return (
        place.hand_out(encoded_low)[None],
        place.hand_out(decoded.astype(BF16))[None],
        place.hand_out(rounded(grad_source).astype(BF16)).astype(F32)[None],
        place.hand_out(rounded(grad_target).astype(BF16)).astype(F32)[None],
        qkv_grads(enc_q, enc_kv),
        small[0].reshape(2, width),
        enc_proj_grad.T,
        enc_w_in,
        small[3],
        enc_w_out.T,
        whole[0:2],
        whole[2:4],
        whole[4:6],
        qkv_grads(self_q, self_kv),
        small[1].reshape(2, width),
        self_proj.T,
        qkv_grads(cross_q, cross_kv),
        small[2].reshape(2, width),
        cross_proj.T,
        dec_w_in,
        small[4],
        dec_w_out.T,
        whole[6:9],
        whole[9:12],
        whole[12:15],
    )


def solution(mesh):
    return jax.shard_map(
        shards,
        mesh=mesh,
        in_specs=(
            P("dp", "seq", None),
            P("dp", "seq", None),
            P("dp", None),
            P("dp", None),
            P(None, None, "tensor"),
            P(None, "tensor"),
            P("tensor", None),
            P(None, "tensor"),
            P("tensor"),
            P("tensor", None),
            P(),
            P(),
            P(),
            P(None, None, "tensor"),
            P(None, "tensor"),
            P("tensor", None),
            P(None, None, "tensor"),
            P(None, "tensor"),
            P("tensor", None),
            P(None, "tensor"),
            P("tensor"),
            P("tensor", None),
            P(),
            P(),
            P(),
            P("dp", "seq", None),
            P("dp", "seq", None),
        ),
        out_specs=(
            P("dp", "seq", None),
            P("dp", "seq", None),
            P("dp", "seq", None),
            P("dp", "seq", None),
            P(None, ("dp", "seq"), "tensor"),
            P(None, "tensor"),
            P("tensor", ("dp", "seq")),
            P(("dp", "seq"), "tensor"),
            P("tensor"),
            P("tensor", ("dp", "seq")),
            P(),
            P(),
            P(),
            P(None, ("dp", "seq"), "tensor"),
            P(None, "tensor"),
            P("tensor", ("dp", "seq")),
            P(None, ("dp", "seq"), "tensor"),
            P(None, "tensor"),
            P("tensor", ("dp", "seq")),
            P(("dp", "seq"), "tensor"),
            P("tensor"),
            P("tensor", ("dp", "seq")),
            P(),
            P(),
            P(),
        ),
        check_vma=False,
    )
```

```python
import functools
import math

import jax
import jax.numpy as jnp
from jax import lax
from jax.experimental import pallas as pl
from jax.experimental.pallas import tpu as pltpu
from jax.sharding import PartitionSpec as P

HEAD_DIM = 64
EPS = 1e-05
NEG = -1e30
BF16 = jnp.bfloat16
F32 = jnp.float32
NT = (((1,), (1,)), ((), ()))
TN = (((0,), (0,)), ((), ()))
KEY_BLOCK = 512
CHUNKS = 2
DOCS = 4


def dot_plain(left, right):
    return jnp.dot(left, right, preferred_element_type=F32)


def dot_last(left, right):
    return lax.dot_general(left, right, NT, preferred_element_type=F32)


def dot_first(left, right):
    return lax.dot_general(left, right, TN, preferred_element_type=F32)


def column_sum(value):
    return jnp.sum(value.astype(F32), axis=0)


def rounded(value):
    return lax.reduce_precision(value, 8, 7)


def after(array):
    return jnp.minimum(jnp.abs(array[0, 0].astype(F32)), 0.0)


def norm_forward(hidden, gain, shift):
    centered = hidden - jnp.mean(hidden, axis=-1, keepdims=True)
    spread = jnp.mean(centered * centered, axis=-1, keepdims=True)
    factor = lax.rsqrt(spread + EPS)
    normed = centered * factor
    return (normed * gain.astype(F32) + shift.astype(F32), (normed, factor))


def norm_backward(grad, saved, gain):
    normed, factor = saved
    scaled = grad * gain.astype(F32)
    centered = scaled - jnp.mean(scaled, axis=-1, keepdims=True)
    grad_hidden = factor * (centered - normed * jnp.mean(scaled * normed, axis=-1, keepdims=True))
    return (grad_hidden, jnp.sum(grad * normed, axis=0), jnp.sum(grad, axis=0))


def head_columns(head):
    return slice(head // 2 * 128, head // 2 * 128 + 128)


def head_rows(head):
    return slice(head * HEAD_DIM, (head + 1) * HEAD_DIM)


def own_lanes(shape, head):
    lanes = lax.broadcasted_iota(jnp.int32, shape, 1)
    return lanes >= HEAD_DIM if head % 2 else lanes < HEAD_DIM


class Mask:
    def __init__(self, causal, starts, segments, first_row):
        self.causal, self.starts, self.first_row = causal, starts, first_row
        segments = segments[...]
        low = high = jnp.zeros_like(segments)
        for number in range(DOCS):
            low = jnp.where(segments == number, starts[number], low)
            high = jnp.where(segments == number, starts[number + 1], high)
        self.count = segments.shape[1]
        if causal:
            place = first_row + lax.broadcasted_iota(jnp.int32, segments.shape, 1)
            high = jnp.minimum(high, place + 1)
        self.low, self.high = low, high

    def allowed(self, index, block):
        place = lax.broadcasted_iota(jnp.int32, (block, self.count), 0) + index * block
        return (place >= self.low) & (place < self.high)

    def flag(self, index, block, ends):
        start, stop = index * block, (index + 1) * block
        low, low_last = self.starts[ends[0]], self.starts[ends[1]]
        high_first, high = self.starts[ends[0] + 1], self.starts[ends[1] + 1]
        if self.causal:
            high = jnp.minimum(high, self.first_row + self.count)
            high_first = jnp.minimum(high_first, self.first_row + 1)
        active = (low < stop) & (high > start)
        full = (low_last <= start) & (high_first >= stop)
        return jnp.where(active, jnp.where(full, 2, 1), 0)


def over_blocks(mask, ends, length, block, body, skipped):
    @pl.loop(0, length // block)
    def _(index):
        flag = mask.flag(index, block, ends)
        rows = pl.ds(pl.multiple_of(index * block, block), block)

        @pl.when(flag == 0)
        def _():
            skipped(rows)

        @pl.when(flag == 1)
        def _():
            body(index, rows, True)

        @pl.when(flag == 2)
        def _():
            body(index, rows, False)


def forward_start(q_ref, masked_q, acc, top):
    heads = q_ref.shape[1] // HEAD_DIM
    for head in range(heads):
        pair = q_ref[:, head_columns(head)]
        masked_q[head] = jnp.where(own_lanes(pair.shape, head), pair, jnp.zeros_like(pair))
    acc[...] = jnp.zeros_like(acc)
    top[...] = jnp.full_like(top, NEG)


def forward_block(index, rows, partial, block, kv_ref, mask, masked_q, acc, top):
    heads, count = masked_q.shape[:2]
    width = heads * HEAD_DIM
    if partial:
        allowed = mask.allowed(index, block)
    for head in range(heads):
        cols = head_columns(head)
        scores = lax.dot_general(kv_ref[rows, cols], masked_q[head], NT, preferred_element_type=F32)
        if partial:
            scores = jnp.where(allowed, scores, NEG)
        old = top[head : head + 1, :]
        new = jnp.maximum(old, jnp.max(scores, axis=0, keepdims=True))
        weights = jnp.exp(scores - new).astype(BF16)
        vals = kv_ref[rows, width + cols.start : width + cols.stop]
        vals = jnp.where(own_lanes(vals.shape, head), vals, jnp.ones_like(vals))
        acc[head] = acc[head] * jnp.exp(old - new) + lax.dot_general(
            vals, weights, TN, preferred_element_type=F32
        )
        top[head : head + 1, :] = new


def forward_end(out_ref, lse_ref, acc, top):
    lse_ref[...] = jnp.zeros_like(lse_ref)
    for head in range(acc.shape[0]):
        first = head % 2 * HEAD_DIM
        total = acc[head, HEAD_DIM - first : HEAD_DIM - first + 1, :]
        out_ref[head_rows(head), :] = acc[head, first : first + HEAD_DIM, :] / total
        lse_ref[head : head + 1, :] = top[head : head + 1, :] + jnp.log(total)


def forward_kernel(block, causal, tokens, starts, ends, segments, q_ref, kv_ref, *refs):
    out_ref, lse_ref, masked_q, acc, top = refs[tokens:]
    mask = Mask(causal, starts, segments, ends[2])
    forward_start(q_ref, masked_q, acc, top)

    def body(index, rows, partial):
        forward_block(index, rows, partial, block, kv_ref, mask, masked_q, acc, top)

    over_blocks(mask, ends, kv_ref.shape[0], block, body, lambda rows: None)
    forward_end(out_ref, lse_ref, acc, top)


def backward_start(q_ref, do_ref, dot_ref, out_ref, masked_q, masked_do, delta, dq):
    for head in range(masked_q.shape[0]):
        pair = q_ref[:, head_columns(head)]
        keep = own_lanes(pair.shape, head)
        masked_q[head] = jnp.where(keep, pair, jnp.zeros_like(pair))
        pair = do_ref[:, head_columns(head)]
        masked_do[head] = jnp.where(keep, pair, jnp.zeros_like(pair))
        part = head_rows(head)
        delta[head : head + 1, :] = jnp.sum(
            dot_ref[part, :].astype(F32) * out_ref[part, :], axis=0, keepdims=True
        )
    dq[...] = jnp.zeros_like(dq)


def backward_block(
    index, rows, block, mask, kv_ref, lse_ref, dkv_ref, masked_q, masked_do, delta, dq, between
):
    heads = masked_q.shape[0]
    width = heads * HEAD_DIM
    allowed = mask.allowed(index, block)
    for pair in range(heads // 2):
        if pair == 1:
            between()
        cols = head_columns(2 * pair)
        later = slice(width + cols.start, width + cols.stop)
        keys, vals = kv_ref[rows, cols], kv_ref[rows, later]
        dk = dv = 0.0
        for head in (2 * pair, 2 * pair + 1):
            scores = lax.dot_general(keys, masked_q[head], NT, preferred_element_type=F32)
            probs = jnp.exp(scores - lse_ref[head : head + 1, :])
            probs = jnp.where(allowed, probs, 0.0)
            dprobs = lax.dot_general(vals, masked_do[head], NT, preferred_element_type=F32)
            draw = (probs * (dprobs - delta[head : head + 1, :])).astype(BF16)
            probs = probs.astype(BF16)
            dv = dv + jnp.dot(probs, masked_do[head], preferred_element_type=F32)
            dk = dk + jnp.dot(draw, masked_q[head], preferred_element_type=F32)
            first = head % 2 * HEAD_DIM
            both = lax.dot_general(keys, draw, TN, preferred_element_type=F32)
            dq[head_rows(head), :] += both[first : first + HEAD_DIM]
        dkv_ref[rows, cols] = dk.astype(BF16)
        dkv_ref[rows, later] = dv.astype(BF16)


SCALARS = pl.BlockSpec(memory_space=pltpu.SMEM)
VECTORS = pl.BlockSpec(memory_space=pltpu.VMEM)


ANYWHERE = pl.BlockSpec(memory_space=pl.ANY)


def cost_of(kv, count, width, products):
    flops = 2 * products * kv.shape[0] * count * width
    return pl.CostEstimate(flops=flops, bytes_accessed=flops // 512, transcendentals=0)


def forward_scratch(count, width):
    heads = width // HEAD_DIM
    return [
        pltpu.VMEM((heads, count, 128), BF16),
        pltpu.VMEM((heads, 128, count), F32),
        pltpu.VMEM((8, count), F32),
    ]


def backward_scratch(count, width):
    heads = width // HEAD_DIM
    return [
        pltpu.VMEM((heads, count, 128), BF16),
        pltpu.VMEM((heads, count, 128), BF16),
        pltpu.VMEM((8, count), F32),
        pltpu.VMEM((width, count), F32),
    ]


def attend(queries, kv, mask, tokens):
    count, width = queries.shape
    causal, starts, ends, segments = mask
    return pl.pallas_call(
        functools.partial(forward_kernel, KEY_BLOCK, causal, len(tokens)),
        out_shape=(
            jax.ShapeDtypeStruct((width, count), F32),
            jax.ShapeDtypeStruct((8, count), F32),
        ),
        in_specs=[SCALARS] * 2 + [VECTORS] * 3 + [ANYWHERE] * len(tokens),
        out_specs=(VECTORS,) * 2,
        scratch_shapes=forward_scratch(count, width),
        compiler_params=pltpu.CompilerParams(vmem_limit_bytes=40 << 20),
        cost_estimate=cost_of(kv, count, width, 2),
    )(starts, ends, segments, queries, kv, *tokens)


MESH = pl.DeviceIdType.MESH
DMA = pltpu.SemaphoreType.DMA


class Here:
    def __init__(self, ring):
        self.ring = ring
        self.d, self.z, self.y = (lax.axis_index(a) for a in ("dp", "seq", "tensor"))
        self.core, self.x = lax.rem(self.d, 2), lax.div(self.d, 2)
        self.other_d = self.d + 1 - 2 * self.core
        self.partner = (self.other_d, self.z, self.y)
        self.right = (self.d, self.z + 1, self.y)
        self.left = (self.d, self.z - 1, self.y)
        self.over_x = (self.d + 2 - 4 * lax.rem(self.x, 2), self.z, self.y)
        self.over_y = (self.d, self.z, 1 - self.y)
        self.diagonal = (self.other_d, self.z, 1 - self.y)

    def meet(self, devices):
        barrier = pltpu.get_barrier_semaphore()
        wanted = 0
        for condition, device in devices:

            @pl.when(condition)
            def _(device=device):
                pl.semaphore_signal(barrier, inc=1, device_id=device, device_id_type=MESH)

            wanted = wanted + jnp.where(condition, 1, 0)
        pl.semaphore_wait(barrier, wanted)

    def along_z(self, step):
        return (self.d, lax.rem(self.z + step, self.ring), self.y)

    def everyone(self):
        devices = [self.partner, self.over_x, self.over_y, self.diagonal]
        devices += [self.along_z(step) for step in range(1, self.ring)]
        return [(self.core >= 0, device) for device in devices]

    def crosswise(self):
        return [
            (self.z + 1 < self.ring, (self.other_d, self.z + 1, self.y)),
            (self.z > 0, (self.other_d, self.z - 1, self.y)),
        ]

    def neighbours(self):
        return [
            (self.core >= 0, self.partner),
            (self.z + 1 < self.ring, self.right),
            (self.z > 0, self.left),
        ]


def remote(source, target, sent, received, device):
    return pltpu.make_async_remote_copy(
        src_ref=source,
        dst_ref=target,
        send_sem=sent,
        recv_sem=received,
        device_id=device,
        device_id_type=MESH,
    )


class Gather:
    def __init__(self, here, rows_ref, sems, source=None, owner=None):
        self.here, self.rows_ref, self.source, self.owner = here, rows_ref, source, owner
        self.count = rows_ref.shape[0] // here.ring
        self.size = self.count // (2 * CHUNKS)
        self.sent, self.got, self.core_sent, self.core_got = sems

    def chunk(self, shard, core, chunk):
        start = shard * self.count + core * (self.count // 2) + chunk * self.size
        return self.rows_ref.at[pl.ds(pl.multiple_of(start, self.size), self.size)]

    def ways(self, step):
        here = self.here
        z, ring = here.z, here.ring
        return [
            (0, z - step, z >= step, z - step + 1, (z + 1 < ring) & (z + 1 >= step), here.right),
            (1, z + step, z + step < ring, z + step - 1, (z > 0) & (z + step <= ring), here.left),
        ]

    def along(self, way, step, shard, chunk, device):
        view = self.chunk(shard, self.here.core, chunk)
        k = way * CHUNKS + chunk
        return remote(view, view, self.sent.at[k, step], self.got.at[k, step], device)

    def across(self, way, step, shard, core, chunk):
        view = self.chunk(shard, core, chunk)
        k = way * CHUNKS + chunk
        return remote(
            view, view, self.core_sent.at[k, step], self.core_got.at[k, step], self.here.partner
        )

    def firsts(self):
        found = []
        for chunk in range(CHUNKS):
            for way, _, _, shard, sends, device in self.ways(1):
                if self.source is None:
                    found.append((sends, self.along(way, 1, shard, chunk, device)))
                    continue
                for core in range(2):
                    k = way * CHUNKS + chunk
                    start = core * (self.count // 2) + chunk * self.size
                    to = (self.here.d - self.here.core + core, *device[1:])
                    copy = remote(
                        self.source.at[pl.ds(start, self.size)],
                        self.chunk(shard, core, chunk),
                        self.sent.at[k, core],
                        self.got.at[k, 1],
                        to,
                    )
                    found.append((sends & self.owner, copy))
        return found

    def begin(self):
        for condition, copy in self.firsts():
            pl.when(condition)(copy.start)

    def advance(self, step):
        for chunk in range(CHUNKS):
            for way, shard, comes, _, _, _ in self.ways(step):

                @pl.when(comes)
                def _(way=way, shard=shard, chunk=chunk):
                    self.along(way, step, shard, chunk, self.here.partner).wait_recv()

                _, _, _, _, sends, device = self.ways(step + 1)[way]

                @pl.when(sends)
                def _(way=way, shard=shard, chunk=chunk, device=device):
                    self.along(way, step + 1, shard, chunk, device).start()

                @pl.when(comes)
                def _(way=way, shard=shard, chunk=chunk):
                    self.across(way, step, shard, self.here.core, chunk).start()

    def finish(self):
        for condition, copy in self.firsts():
            pl.when(condition)(copy.wait_send)

        @pl.loop(1, self.here.ring)
        def _(step):
            for chunk in range(CHUNKS):
                for way, shard, comes, out, sends, device in self.ways(step):

                    @pl.when(sends & (step > 1))
                    def _(way=way, out=out, device=device, chunk=chunk):
                        self.along(way, step, out, chunk, device).wait_send()

                    @pl.when(comes)
                    def _(way=way, shard=shard, chunk=chunk):
                        core = self.here.core
                        self.across(way, step, shard, core, chunk).wait_send()
                        self.across(way, step, shard, 1 - core, chunk).wait_recv()


def pieces_of(weights):
    found = []
    for k, weight in enumerate(weights):
        rows, columns = weight.shape[-2:]
        number = 1 if rows % 3 else 3
        while 2 * rows * columns > 655360 * number and rows % (64 * number) == 0:
            number *= 2
        for matrix in range(matrices_of(weight)):
            found += [(k, matrix, i * (rows // number), rows // number) for i in range(number)]
    return found


def matrices_of(weight):
    return weight.shape[0] if len(weight.shape) == 3 else 1


def beside(weight):
    rows, columns = weight.shape[-2:]
    return jax.ShapeDtypeStruct((rows, columns * matrices_of(weight)), weight.dtype)


AHEAD = 4


class Fetch:
    def __init__(self, here, inputs, outputs, sems):
        self.here, self.inputs, self.outputs = here, inputs, outputs
        self.y_sent, self.y_got, self.x_sent, self.x_got, self.core_sent, self.core_got = sems
        self.pieces = pieces_of(inputs)
        self.matrices = [
            (k, matrix)
            for k, given in enumerate(inputs)
            for matrix in range(matrices_of(given))
        ]
        self.number = len(self.pieces)
        self.own = lax.rem(here.x, 2)

    def devices(self):
        here = self.here
        return [(here.core >= 0, here.diagonal), (here.core == 1, here.over_x)]

    def matrix(self, k, matrix):
        given = self.inputs[k]
        return given.at[matrix] if len(given.shape) == 3 else given

    def part(self, p, which):
        k, matrix, start, rows = self.pieces[p]
        first = pl.multiple_of(start + which * (rows // 2), 16)
        return self.matrix(k, matrix).at[pl.ds(first, rows // 2)]

    def place(self, p, which):
        k, matrix, start, rows = self.pieces[p]
        columns = self.inputs[k].shape[-1]
        first = pl.multiple_of(start + which * (rows // 2), 16)
        return self.outputs[k].at[pl.ds(first, rows // 2), pl.ds(matrix * columns, columns)]

    def over_y(self, p):
        return remote(
            self.part(p, self.own),
            self.place(p, self.own),
            self.y_sent.at[p],
            self.y_got.at[p],
            self.here.diagonal,
        )

    def over_x(self, p, which):
        view = self.place(p, which)
        return remote(view, view, self.x_sent.at[p], self.x_got.at[p], self.here.over_x)

    def across(self, m):
        k, matrix = self.matrices[m]
        columns = self.inputs[k].shape[-1]
        return remote(
            self.matrix(k, matrix),
            self.outputs[k].at[:, pl.ds(matrix * columns, columns)],
            self.core_sent.at[m],
            self.core_got.at[m],
            self.here.partner,
        )

    def begin(self):
        @pl.when(self.here.core == 0)
        def _():
            for p in range(min(AHEAD, self.number)):
                self.over_y(p).start()

        @pl.when(self.here.core == 1)
        def _():
            for m in range(len(self.matrices)):
                self.across(m).start()

    def advance(self, p):
        @pl.when(self.here.core == 0)
        def _():
            self.over_y(p).wait_send()
            if p + AHEAD < self.number:
                self.over_y(p + AHEAD).start()

        @pl.when(self.here.core == 1)
        def _():
            self.over_y(p).wait_recv()
            self.over_x(p, self.own).start()

    def end(self):
        @pl.when(self.here.core == 0)
        def _():
            for m in range(len(self.matrices)):
                self.across(m).wait_recv()

        @pl.when(self.here.core == 1)
        def _():
            for p in range(self.number):
                self.over_x(p, self.own).wait_send()
                self.over_x(p, 1 - self.own).wait_recv()
            for m in range(len(self.matrices)):
                self.across(m).wait_send()


def gather_sems(ring):
    return [DMA((2 * CHUNKS, ring))] * 4


def fetch_sems(weights):
    number = len(pieces_of(weights))
    return [DMA((number,))] * 4 + [DMA((3 * len(weights),))] * 2


def opening_kernel(ring, number, *refs):
    inputs, refs = refs[: 9 + number], refs[9 + number :]
    outputs, (vectors, *sems) = refs[: 5 + number], refs[5 + number :]
    source, target, source_seg, target_seg = inputs[:4]
    source_all, target_out, source_seg_out, target_seg_out, vectors_out = outputs[:5]
    shard_sems, vector_sems = sems[:3], sems[3:6]
    here = Here(ring)
    fetch = Fetch(here, inputs[9:], outputs[5:], sems[10:])
    here.meet(here.neighbours() + here.crosswise() + fetch.devices())
    count = source.shape[0]
    own = pl.ds(pl.multiple_of(here.z * count, count), count)
    moves = [
        (source, source_all.at[own]),
        (target, target_out),
        (source_seg, source_seg_out),
        (target_seg, target_seg_out),
    ]
    owner = here.core == here.y

    def shard_copy(k):
        start, end = moves[k]
        sent, got, copied = shard_sems
        return (
            remote(start, end, sent.at[k], got.at[k], here.partner),
            pltpu.make_async_copy(start, end, copied.at[k]),
        )

    def vector_copy():
        sent, got, copied = vector_sems
        return (
            remote(vectors, vectors_out, sent, got, here.diagonal),
            pltpu.make_async_copy(vectors, vectors_out, copied),
        )

    def wait_shard(k):
        across, local = shard_copy(k)

        @pl.when(owner)
        def _():
            across.wait_send()
            local.wait()

        @pl.when(jnp.logical_not(owner))
        def _():
            across.wait_recv()

    gather = Gather(here, source_all, sems[6:10], source, owner)
    gather.begin()

    @pl.when(owner)
    def _():
        for k in range(len(moves)):
            across, local = shard_copy(k)
            across.start()
            local.start()

    fetch.begin()

    vectors[...] = jnp.zeros_like(vectors)
    for row, bias in enumerate(inputs[4:7]):
        width = bias.shape[1]
        for part in range(2):
            value = bias[part : part + 1, :].astype(F32)
            vectors[row : row + 1, 2 * part * width : (2 * part + 1) * width] = value
    for row, bias in enumerate(inputs[7:9]):
        vectors[3 + row : 4 + row, :] = bias[...].astype(F32).reshape(1, -1)

    @pl.when(here.core == 0)
    def _():
        across, local = vector_copy()
        across.start()
        local.start()

    done = 0
    for step in range(1, ring):
        while done < fetch.number * (2 * step - 1) // (2 * ring - 2):
            fetch.advance(done)
            done += 1
        gather.advance(step)
    while done < fetch.number:
        fetch.advance(done)
        done += 1
    gather.finish()
    for k in range(len(moves)):
        wait_shard(k)
    fetch.end()
    across, local = vector_copy()

    @pl.when(here.core == 0)
    def _():
        across.wait_send()
        local.wait()

    @pl.when(here.core == 1)
    def _():
        across.wait_recv()


def opening(ring, source, target, source_seg, target_seg, biases, weights):
    inputs = (source, target, source_seg, target_seg, *biases, *weights)
    count, model = source.shape
    number = len(weights)
    units = biases[-1].shape[0]
    shapes = (
        jax.ShapeDtypeStruct((ring * count, model), BF16),
        jax.ShapeDtypeStruct(target.shape, BF16),
        jax.ShapeDtypeStruct(source_seg.shape, jnp.int32),
        jax.ShapeDtypeStruct(target_seg.shape, jnp.int32),
        jax.ShapeDtypeStruct((8, units), F32),
    ) + tuple(beside(weight) for weight in weights)
    return pl.pallas_call(
        functools.partial(opening_kernel, ring, number),
        out_shape=shapes,
        in_specs=[VECTORS] * 9 + [ANYWHERE] * number,
        out_specs=(ANYWHERE,) + (VECTORS,) * 4 + (ANYWHERE,) * number,
        scratch_shapes=[pltpu.VMEM((8, units), F32)]
        + [DMA((4,))] * 3
        + [DMA] * 3
        + gather_sems(ring)
        + fetch_sems(weights),
        compiler_params=pltpu.CompilerParams(collective_id=1, has_side_effects=True),
    )(*inputs)


def gather_attend_kernel(
    block, causal, ring, number, tokens, starts, segments, bias_ref, own_ref, rows_ref, proj_ref, *refs
):
    weights, refs = refs[:number], refs[number + tokens :]
    q_ref, kv_ref, out_ref, lse_ref, all_ref = refs[:5]
    fetched, refs = refs[5 : 5 + number], refs[5 + number :]
    masked_q, acc, top, rows_in, proj, copied, rows_copied, proj_copied = refs[:8]
    here = Here(ring)
    gather = Gather(here, all_ref, refs[8:12])
    fetch = Fetch(here, weights, fetched, refs[12:])
    count, width = q_ref.shape
    first_row = pl.multiple_of(here.z * count, count)

    def rows_copy(shard):
        rows = pl.ds(pl.multiple_of(shard * count, count), count)
        return pltpu.make_async_copy(rows_ref.at[rows], rows_in.at[rows], rows_copied.at[shard])

    proj_copy = pltpu.make_async_copy(proj_ref, proj, proj_copied)
    proj_copy.start()
    for shard in range(ring):
        rows_copy(shard).start()
    here.meet(here.neighbours() + fetch.devices())
    local = pltpu.make_async_copy(own_ref, all_ref.at[pl.ds(first_row, count)], copied)
    local.start()
    fetch.begin()
    local.wait()
    gather.begin()
    mask = Mask(causal, starts, segments, first_row)
    proj_copy.wait()
    for shard in range(ring):
        rows_copy(shard).wait()
    queries = dot_plain(rows_in[pl.ds(first_row, count), :], proj[:, :width]) + bias_ref[:, :width]
    q_ref[...] = (queries.astype(BF16).astype(F32) * HEAD_DIM ** (-0.5)).astype(BF16)
    forward_start(q_ref, masked_q, acc, top)
    blocks = kv_ref.shape[0] // block

    @pl.loop(0, blocks)
    def _(index):
        rows = pl.ds(pl.multiple_of(index * block, block), block)
        both = dot_plain(rows_in[rows, :], proj[:, width:]) + bias_ref[:, width:]
        kv_ref[rows, :] = both.astype(BF16)
        forward_block(index, rows, True, block, kv_ref, mask, masked_q, acc, top)

        @pl.when((index >= 1) & (index < ring))
        def _():
            gather.advance(index)

        for p in range(fetch.number):
            pl.when(index == 1 + p * (blocks - 1) // fetch.number)(
                functools.partial(fetch.advance, p)
            )

    forward_end(out_ref, lse_ref, acc, top)
    gather.finish()
    fetch.end()


def gather_attend(number, ring, rows, proj, bias, mask, own, weights, tokens=()):
    length, model = rows.shape
    count, width = length // ring, proj.shape[1] // 3
    causal, starts, _, segments = mask
    fetched = len(weights)
    kv = jax.ShapeDtypeStruct((length, 2 * width), BF16)
    return pl.pallas_call(
        functools.partial(gather_attend_kernel, KEY_BLOCK, causal, ring, fetched, len(tokens)),
        out_shape=(
            jax.ShapeDtypeStruct((count, width), BF16),
            kv,
            jax.ShapeDtypeStruct((width, count), F32),
            jax.ShapeDtypeStruct((8, count), F32),
            jax.ShapeDtypeStruct((ring * own.shape[0], own.shape[1]), BF16),
        )
        + tuple(beside(weight) for weight in weights),
        in_specs=[SCALARS] + [VECTORS] * 3 + [ANYWHERE] * (2 + fetched + len(tokens)),
        out_specs=(VECTORS,) * 4 + (ANYWHERE,) * (1 + fetched),
        scratch_shapes=forward_scratch(count, width)
        + [
            pltpu.VMEM((length, model), BF16),
            pltpu.VMEM(proj.shape, BF16),
            DMA,
            DMA((ring,)),
            DMA,
        ]
        + gather_sems(ring)
        + fetch_sems(weights),
        compiler_params=pltpu.CompilerParams(
            vmem_limit_bytes=50 << 20, collective_id=number, has_side_effects=True
        ),
        cost_estimate=cost_of(kv, count, width, 4),
    )(starts, segments, bias, own, rows, proj, *weights, *tokens)


class Part:
    def __init__(self, inputs, in_specs, out_shapes, scratch, bind):
        self.inputs, self.in_specs, self.out_shapes = inputs, in_specs, out_shapes
        self.scratch, self.bind = scratch, bind


def run_parts(number, body, parts, cost=None):
    ring = lax.axis_size("seq")
    counts = [(len(p.inputs), len(p.out_shapes), len(p.scratch)) for p in parts]

    def kernel(*refs):
        here = Here(ring)
        taken, offset = [[] for _ in parts], 0
        for kind in range(3):
            for refs_of, count in zip(taken, counts):
                refs_of.append(refs[offset : offset + count[kind]])
                offset += count[kind]
        here.meet(here.everyone())
        body(here, *(p.bind(here, *refs_of) for p, refs_of in zip(parts, taken)))

    results = pl.pallas_call(
        kernel,
        out_shape=[shape for p in parts for shape in p.out_shapes],
        in_specs=[spec for p in parts for spec in p.in_specs],
        out_specs=[VECTORS for p in parts for _ in p.out_shapes],
        scratch_shapes=[shape for p in parts for shape in p.scratch],
        compiler_params=pltpu.CompilerParams(
            vmem_limit_bytes=62 << 20, collective_id=number, has_side_effects=True
        ),
        cost_estimate=cost,
    )(*(array for p in parts for array in p.inputs))
    given = []
    for _, count, _ in counts:
        given.append(results[:count])
        results = results[count:]
    return given


class Stage:
    def __init__(self, here, kind, source, result, buffers, sems):
        self.here, self.kind, self.source, self.result = here, kind, source, result
        self.buffers, (self.sent, self.got) = buffers, sems
        rows = source.shape[0]
        if kind == "x":
            half = rows // 2
            self.kept = [half * here.x]
            self.given = [half * (1 - here.x)]
            self.size, self.to = half, here.over_x
        elif kind == "y":
            self.size = 192
            self.starts = list(range(0, rows, 2 * self.size))
        elif kind == "v":
            bit = lax.rem(here.z, 2)
            self.size = rows // 4
            self.kept = [self.size * bit, self.size * (bit + 2)]
            self.given = [self.size * (1 - bit), self.size * (3 - bit)]
            self.to = (here.d, here.z + 1 - 2 * bit, here.y)
        else:
            bit = lax.div(here.z, 2)
            self.size = rows // 2
            self.kept, self.given = [self.size * bit], [self.size * (1 - bit)]
            self.to = (here.d, here.z + 2 - 4 * bit, here.y)

    def rows(self, start):
        if not isinstance(start, int):
            start = pl.multiple_of(start, 16)
        return pl.ds(start, self.size)

    def move(self, start, place, buffer, sem, to):
        return remote(
            self.source.at[self.rows(start)],
            self.buffers[buffer].at[self.rows(place * self.size)],
            self.sent.at[sem],
            self.got.at[sem],
            to,
        )

    def moves(self):
        here = self.here
        if self.kind != "y":
            both = [
                (None, self.move(start, k, 0, k, self.to)) for k, start in enumerate(self.given)
            ]
            return both, both
        sends, arrivals = [], []
        for k, start in enumerate(self.starts):
            upper = start + self.size
            sends.append((here.core == 0, self.move(upper, k, 0, 2 * k, here.partner)))
            sends.append((here.core == 1, self.move(start, k, 0, 2 * k, here.diagonal)))
            sends.append((here.core == 1, self.move(upper, k, 1, 2 * k + 1, here.over_y)))
            arrivals.append((None, self.move(upper, k, 0, 2 * k, here.partner)))
            arrivals.append((here.core == 1, self.move(upper, k, 1, 2 * k + 1, here.over_y)))
        return sends, arrivals

    @staticmethod
    def each(moves, act):
        for condition, copy in moves:
            if condition is None:
                act(copy)
            else:
                pl.when(condition)(functools.partial(act, copy))

    def begin(self):
        self.each(self.moves()[0], lambda copy: copy.start())

    def end(self):
        sends, arrivals = self.moves()
        self.each(arrivals, lambda copy: copy.wait_recv())
        kept = self.kept if self.kind != "y" else self.starts
        for k, start in enumerate(kept):
            place = self.rows(k * self.size)

            def add(own_ref, own, place=place):
                both = own_ref[own, :].astype(F32) + self.buffers[0][place, :].astype(F32)
                self.result[place, :] = both.astype(self.result.dtype)

            if self.kind == "y":
                pl.when(self.here.core == 0)(functools.partial(add, self.source, self.rows(start)))
                pl.when(self.here.core == 1)(functools.partial(add, self.buffers[1], place))
            else:
                add(self.source, self.rows(start))
        self.each(sends, lambda copy: copy.wait_send())


class Chain:
    def __init__(self, stages, times):
        self.stages, self.times = stages, times

    def event(self, time):
        for k, own in enumerate(self.times):
            if own == time:
                if k:
                    self.stages[k - 1].end()
                if k < len(self.stages):
                    self.stages[k].begin()


def chain(array, kinds, times, made=None):
    rows, columns = made[2] if made else array.shape
    scratch, shapes = [], []
    for kind in kinds:
        rows = rows // 2
        scratch += [pltpu.VMEM((rows, columns), BF16)] * (2 if kind == "y" else 1)
        scratch += [DMA((4,))] * 2
        shapes.append((rows, columns))
    scratch += [pltpu.VMEM(shape, BF16) for shape in shapes[:-1]]
    final = jax.ShapeDtypeStruct(shapes[-1], F32 if kinds[-1] == "w" else BF16)

    def bind(here, inputs, outputs, refs):
        refs = list(refs)
        results = refs[len(refs) - len(kinds) + 1 :] + [outputs[0]]
        source, stages = made[0][made[1]] if made else inputs[0], []
        for kind, result in zip(kinds, results):
            buffers = [refs.pop(0) for _ in range(2 if kind == "y" else 1)]
            sems = [refs.pop(0) for _ in range(2)]
            stages.append(Stage(here, kind, source, result, buffers, sems))
            source = result
        return Chain(stages, times)

    inputs = () if made else (array,)
    return Part(inputs, [VECTORS] * len(inputs), [final], scratch, bind)


def closing_kernel(flag, *refs):
    own_source, other_source, own_target, other_target, vectors = refs[:5]
    grads, outputs = refs[5:18], refs[18:]
    keeps = flag[0] == 1
    for own, other, out in (
        (own_source, other_source, outputs[0]),
        (own_target, other_target, outputs[1]),
    ):
        out[...] = jnp.where(keeps, own[...], other[...]).astype(F32)
    for k in range(3):
        of_q, of_out, of_kv = grads[3 * k : 3 * k + 3]
        qkv, out = outputs[2 + 2 * k : 4 + 2 * k]
        width = of_q.shape[1]
        qkv[0] = of_q[...]
        qkv[1] = of_kv[:, :width]
        qkv[2] = of_kv[:, width:]
        out[...] = of_out[...].T
    for k in range(2):
        of_in, of_out = grads[9 + 2 * k : 11 + 2 * k]
        outputs[8 + 2 * k][...] = of_in[...]
        outputs[9 + 2 * k][...] = of_out[...].T
    row = 0
    for out in outputs[12:18]:
        out[...] = vectors[row : row + out.shape[0], :]
        row += out.shape[0]
    for out in outputs[18:21]:
        width = out.shape[1]
        out[0:1, :] = vectors[row : row + 1, :width]
        out[1:2, :] = vectors[row : row + 1, width:]
        row += 1
    for out in outputs[21:]:
        for part in range(out.shape[1] // vectors.shape[1]):
            span = slice(part * vectors.shape[1], (part + 1) * vectors.shape[1])
            out[:, span] = vectors[row : row + 1, :]
            row += 1


def closing(flag, rows, vectors, grads, sizes):
    part, width = grads[0].shape
    units = grads[9].shape[1]
    model = vectors.shape[1]
    shapes = [rows[0].shape] * 2
    shapes += [(3, part, width), (width, part)] * 3 + [(part, units), (units, part)] * 2
    shapes += [(size, model) for size in sizes] + [(2, width)] * 3 + [(1, units)] * 2
    inputs = (flag, *rows, vectors, *grads)
    return pl.pallas_call(
        closing_kernel,
        out_shape=[jax.ShapeDtypeStruct(shape, F32) for shape in shapes],
        in_specs=[SCALARS] + [VECTORS] * (len(inputs) - 1),
        out_specs=[VECTORS] * len(shapes),
        compiler_params=pltpu.CompilerParams(vmem_limit_bytes=50 << 20),
    )(*inputs)


class Small:
    def __init__(self, here, rows, held_rows, given, result, refs, times):
        self.here, self.given, self.result, self.times = here, given, result, times
        self.rows, self.held_rows = rows, held_rows
        self.arrived, self.sent, self.got = refs
        self.bits = [lax.rem(here.z, 2), lax.div(here.z, 2)]

    def copies(self, stage):
        here = self.here
        low, high = self.bits

        def to(device, slot, source=self.result, target=None):
            target = self.arrived.at[slot] if target is None else target
            return remote(source, target, self.sent.at[slot], self.got.at[slot], device)

        if stage < 3:
            device = (
                here.over_x,
                (here.d, here.z + 1 - 2 * low, here.y),
                (here.d, here.z + 2 - 4 * high, here.y),
            )[stage]
            both = [(None, to(device, stage))]
            return both, both
        if stage == 3:
            sends = [
                (None, to(here.over_y, 3)),
                (here.core == 0, to(here.partner, 4)),
                (here.core == 1, to(here.diagonal, 4)),
            ]
            return sends, sends[:1] + [(None, to(here.partner, 4))]
        return [(here.core == 0, to(here.partner, 5))], [(here.core == 1, to(here.partner, 5))]

    def end(self, stage):
        sends, arrivals = self.copies(stage)
        Stage.each(arrivals, lambda copy: copy.wait_recv())
        Stage.each(sends, lambda copy: copy.wait_send())
        core = self.here.core
        if stage < 3:
            self.result[...] += self.arrived[stage]
        elif stage == 3:
            whole, halves = slice(0, self.held_rows), slice(self.held_rows, self.rows)
            self.result[whole, :] += self.arrived[3, whole, :]
            own = jnp.where(core == 0, self.result[halves, :], self.arrived[3, halves, :])
            self.result[halves, :] = own + self.arrived[4, halves, :]
        else:
            whole = slice(0, self.held_rows)

            @pl.when(core == 1)
            def _():
                self.result[whole, :] = self.arrived[5, whole, :]

    def event(self, time):
        for k, own in enumerate(self.times):
            if own == time:
                if k == 0:
                    self.result[...] = self.given[...]
                else:
                    self.end(k - 1)
                if k < 5:
                    Stage.each(self.copies(k)[0], lambda copy: copy.start())


def small_sums(whole, halves, times):
    both = jnp.concatenate([whole, halves])
    rows, columns = both.shape
    shape = jax.ShapeDtypeStruct(both.shape, F32)
    part = Part(
        (both,),
        [VECTORS],
        [shape],
        [pltpu.VMEM((6, rows, columns), F32), DMA((6,)), DMA((6,))],
        lambda here, inputs, outputs, refs: Small(
            here, rows, whole.shape[0], inputs[0], outputs[0], refs, times
        ),
    )
    part.rows, part.vectors = whole.shape[0], (whole.reshape(-1), halves.reshape(-1))
    return part


def run_chains(number, chains, events):
    def body(here, *bound):
        for time in range(events):
            for one in bound:
                one.event(time)

    return [given[0] for given in run_parts(number, body, chains)]


class Back:
    def __init__(self, here, causal, apart, inputs, outputs, scratch):
        self.here, self.causal, self.apart = here, causal, apart
        self.starts, self.segments, self.q, self.kv, self.do, self.dot, self.out, self.lse = inputs[:8]
        self.weights = inputs[8]
        self.dq_out, self.dkv, self.sum = outputs[:3]
        self.query_sum = outputs[3] if apart else None
        self.work, scratch = scratch[:4], scratch[4:]
        self.terms, self.from_core, self.outgoing, self.arrived, self.total = scratch[:5]
        self.core_sent, self.core_got, self.sent, self.got, self.end_sent, self.end_got = scratch[5:11]
        if apart:
            self.query_low, self.query_got, self.query_sems = scratch[11:]
        self.count, self.width = self.q.shape
        self.part = self.count // 2
        self.mask = Mask(causal, self.starts, self.segments, here.z * self.count)

    def half(self, core):
        return pl.ds(pl.multiple_of(core * self.part, self.part), self.part)

    def shard_at(self, turn):
        ring, z, shard = self.here.ring, self.here.z, 0
        for device in range(ring):
            others = [t for t in range(ring) if t != device]
            others.sort(key=lambda t: (ring - t + device) if t > device else (t + ring - device))
            for k, other in enumerate(others):
                shard = jnp.where((z == device) & (turn == k + 1), other, shard)
        return shard

    def across(self, turn, shard):
        return remote(
            self.terms.at[lax.rem(turn, 2), self.half(1 - self.here.core)],
            self.from_core.at[shard],
            self.core_sent.at[shard],
            self.core_got.at[shard],
            self.here.partner,
        )

    def slot(self, way, shard, z):
        return jnp.where((way == 1) & (shard == z), self.here.ring, shard)

    def along(self, way, shard, device):
        return remote(
            self.outgoing.at[shard],
            self.arrived.at[self.slot(way, shard, device[1])],
            self.sent.at[shard],
            self.got.at[way, shard],
            device,
        )

    def put(self, turn, shard, terms):
        @pl.when(turn > 2)
        def _():
            self.across(turn - 2, self.shard_at(turn - 2)).wait_send()

        slot = lax.rem(turn, 2)
        self.terms[slot] = terms.astype(BF16)
        self.across(turn, shard).start()
        self.outgoing[shard] = self.terms[slot, self.half(self.here.core), :]

    def both(self, shard):
        self.across(0, shard).wait_recv()
        return self.outgoing[shard].astype(F32) + self.from_core[shard].astype(F32)

    def forward(self, shard):
        here = self.here
        self.total[...] = self.both(shard)
        for way, mine, comes, device in (
            (0, shard > here.z, here.z > 0, here.right),
            (1, shard < here.z, here.z + 1 < here.ring, here.left),
        ):

            @pl.when(mine & comes)
            def _(way=way):
                self.along(way, shard, here.partner).wait_recv()
                self.total[...] += self.arrived[self.slot(way, shard, here.z)].astype(F32)

        self.outgoing[shard] = self.total[...].astype(BF16)
        for way, mine, device in ((0, shard > here.z, here.right), (1, shard < here.z, here.left)):

            @pl.when(mine)
            def _(way=way, device=device):
                self.along(way, shard, device).start()

    def block(self, shard, between):
        rows = pl.ds(pl.multiple_of(shard * self.count, self.count), self.count)
        backward_block(
            shard, rows, self.count, self.mask, self.kv, self.lse, self.dkv, *self.work, between
        )
        return dot_last(self.dkv[rows, :], self.weights[:, self.width :])

    def run(self, event):
        here, ring = self.here, self.here.ring
        at_end = (here.z == 0) | (here.z == ring - 1)
        event(0)
        backward_start(self.q, self.do, self.dot, self.out, *self.work)

        @pl.loop(1, ring)
        def _(turn):
            shard = self.shard_at(turn)

            def between():
                @pl.when((turn > 1) & at_end)
                def _():
                    self.forward(self.shard_at(turn - 1))

            self.put(turn, shard, self.block(shard, between))
            for time in range(1, ring):
                pl.when(turn == time)(functools.partial(event, time))

        def between():
            self.forward(self.shard_at(jnp.where(at_end, ring - 1, 1)))

        own = self.block(here.z, between)
        event(ring)
        low = (self.work[3][...] * HEAD_DIM ** (-0.5)).T.astype(BF16)
        self.dq_out[...] = low
        query = dot_last(low, self.weights[:, : self.width])
        if self.apart:
            self.query_low[...] = query.astype(BF16)
            exchange = remote(
                self.query_low, self.query_got, self.query_sems.at[0], self.query_sems.at[1], here.partner
            )
            exchange.start()
        else:
            own = own + query
        self.put(jnp.int32(ring), here.z, own)
        if self.apart:
            exchange.wait()
            self.query_sum[...] = self.query_low[...].astype(F32) + self.query_got[...].astype(F32)

        @pl.when(jnp.logical_not(at_end))
        def _():
            @pl.loop(2, ring)
            def _(turn):
                self.forward(self.shard_at(turn))

        event(ring + 1)
        self.total[...] = self.both(here.z)
        for way, comes in ((0, here.z > 0), (1, here.z + 1 < ring)):

            @pl.when(comes)
            def _(way=way):
                self.along(way, here.z, here.partner).wait_recv()
                self.total[...] += self.arrived[self.slot(way, here.z, here.z)].astype(F32)

        own, other = self.half(here.core), self.half(1 - here.core)
        self.sum[own, :] = self.total[...].astype(BF16)
        for half, waits in ((own, False), (other, True)):
            view = self.sum.at[half]
            copy = remote(view, view, self.end_sent, self.end_got, here.partner)
            if waits:
                copy.wait_recv()
            else:
                copy.start()
                copy.wait_send()
        self.across(ring - 1, self.shard_at(ring - 1)).wait_send()
        self.across(ring, here.z).wait_send()
        for shard in range(ring):

            @pl.when(here.z != shard)
            def _(shard=shard):
                self.along(0, shard, here.partner).wait_send()

        event(ring + 2)


class Products:
    def __init__(self, back, inputs, of_bias, made, scratch, time):
        self.back, self.time = back, time
        self.query_in, self.key_in, self.grad_branch, self.mixed = inputs
        self.of_bias = of_bias
        self.of_q, self.of_out, self.of_kv = made
        self.blocks, self.copied = scratch

    def copy(self, index):
        part = pl.ds(pl.multiple_of(index * 256, 256), 256)
        slot = lax.rem(index, 2)
        return pltpu.make_async_copy(
            self.key_in.at[:, part], self.blocks.at[slot], self.copied.at[slot]
        )

    def event(self, time):
        if time == 0:
            self.copy(0).start()
        if time != self.time:
            return
        dq, dkv = self.back.dq_out, self.back.dkv
        width = dq.shape[1]
        number = self.of_kv.shape[0] // 256

        @pl.loop(0, number)
        def _(index):
            @pl.when(index + 1 < number)
            def _():
                self.copy(index + 1).start()

            self.copy(index).wait()
            part = pl.ds(pl.multiple_of(index * 256, 256), 256)
            block = self.blocks[lax.rem(index, 2)]
            self.of_kv[part, :] = dot_first(block, dkv[...]).astype(BF16)

        self.of_q[...] = dot_first(self.query_in[...], dq[...]).astype(BF16)
        self.of_out[...] = dot_first(self.grad_branch[...], self.mixed[...].T).astype(BF16)
        self.of_bias[0:1, :] = jnp.sum(dq[...].astype(F32), axis=0, keepdims=True)
        self.of_bias[1:2, :] = jnp.sum(dkv[:, width:].astype(F32), axis=0, keepdims=True)


def products(box, query_in, key_in, grad_branch, mixed, time, begins):
    model, width = query_in.shape[1], mixed.shape[0]
    shapes = ((model, width), (model, width), (model, 2 * width))

    def bind(here, inputs, outputs, refs):
        made = refs[2:] if begins else outputs[1:]
        for k in range(3):
            box[k] = made[k]
        return Products(box["back"], inputs, outputs[0], made, refs[:2], time)

    part = Part(
        (query_in, key_in, grad_branch, mixed),
        [VECTORS, ANYWHERE, VECTORS, VECTORS],
        [jax.ShapeDtypeStruct((2, width), F32)]
        + ([] if begins else [jax.ShapeDtypeStruct(shape, BF16) for shape in shapes]),
        [pltpu.VMEM((2, key_in.shape[0], 256), BF16), DMA((2,))]
        + ([pltpu.VMEM(shape, BF16) for shape in shapes] if begins else []),
        bind,
    )
    if not begins:
        return [part]
    firsts = [
        chain(None, kind, (time, 6), (box, k, shape)) for k, (kind, shape) in enumerate(zip("yyx", shapes))
    ]
    return [part, *firsts]


class FeedBack:
    def __init__(self, here, inputs, outputs, scratch, time):
        self.here, self.time = here, time
        self.grad, self.x_in = inputs[:2]
        self.streamed = inputs[2:]
        self.sum, self.of_bias, self.of_in, self.of_out = outputs
        self.blocks, (self.low, self.got, self.copied, self.sems) = scratch[:4], scratch[4:]

    def event(self, time):
        if time != self.time:
            return
        span = self.blocks[0].shape[2]
        number = self.of_in.shape[1] // span
        self.sum[...] = jnp.zeros_like(self.sum)

        def columns(index):
            return pl.ds(pl.multiple_of(index * span, span), span)

        def copies(index):
            slot, part = lax.rem(index, 2), columns(index)
            return [
                pltpu.make_async_copy(
                    ref.at[part] if k == 3 else ref.at[:, part],
                    self.blocks[k].at[slot],
                    self.copied.at[k, slot],
                )
                for k, ref in enumerate(self.streamed)
            ]

        for copy in copies(0):
            copy.start()

        @pl.loop(0, number)
        def _(index):
            part = columns(index)

            @pl.when(index + 1 < number)
            def _():
                for copy in copies(index + 1):
                    copy.start()

            for copy in copies(index):
                copy.wait()
            slope, active, w_in, w_out = (block.at[lax.rem(index, 2)] for block in self.blocks)
            hidden = (slope[...] * dot_last(self.grad[...], w_out[...])).astype(BF16)
            self.of_bias[:, part] = jnp.sum(hidden.astype(F32), axis=0, keepdims=True)
            self.sum[...] += dot_last(hidden, w_in[...])
            self.of_in[:, part] = dot_first(self.x_in[...], hidden).astype(BF16)
            self.of_out[:, part] = dot_first(self.grad[...], active[...]).astype(BF16)

        self.low[...] = self.sum[...].astype(BF16)
        exchange = remote(self.low, self.got, self.sems.at[0], self.sems.at[1], self.here.partner)
        exchange.start()
        exchange.wait()
        self.sum[...] = self.low[...].astype(F32) + self.got[...].astype(F32)


def feed_back(grad_branch, slope, w_in, w_out, x_in, active, time):
    count, model = x_in.shape
    units = w_in.shape[1]
    span = 256
    return Part(
        (grad_branch, x_in, slope, active, w_in, w_out),
        [VECTORS] * 2 + [ANYWHERE] * 4,
        [
            jax.ShapeDtypeStruct((count, model), F32),
            jax.ShapeDtypeStruct((1, units), F32),
            jax.ShapeDtypeStruct((model, units), BF16),
            jax.ShapeDtypeStruct((model, units), BF16),
        ],
        [
            pltpu.VMEM((2, count, span), slope.dtype),
            pltpu.VMEM((2, count, span), BF16),
            pltpu.VMEM((2, model, span), BF16),
            pltpu.VMEM((2, span, model), BF16),
            pltpu.VMEM((count, model), BF16),
            pltpu.VMEM((count, model), BF16),
            DMA((4, 2)),
            DMA((2,)),
        ],
        lambda here, *refs: FeedBack(here, *refs, time),
    )


def attend_back(number, saved, grad_mixed, grad_mixed_t, weights, mask, apart, more, box):
    queries, kv, output, lse, _ = saved
    causal, starts, segments = mask
    ring = lax.axis_size("seq")
    count, width = queries.shape
    model = weights.shape[0]
    part = count // 2
    shapes = [
        jax.ShapeDtypeStruct((count, width), BF16),
        jax.ShapeDtypeStruct(kv.shape, BF16),
        jax.ShapeDtypeStruct((count, model), BF16),
    ]
    scratch = backward_scratch(count, width) + [
        pltpu.VMEM((2, count, model), BF16),
        *[pltpu.VMEM((ring, part, model), BF16)] * 2,
        pltpu.VMEM((ring + 1, part, model), BF16),
        pltpu.VMEM((part, model), F32),
        *[DMA((ring,))] * 3,
        DMA((2, ring)),
        *[DMA] * 2,
    ]
    if apart:
        shapes.append(jax.ShapeDtypeStruct((count, model), F32))
        scratch += [pltpu.VMEM((count, model), BF16)] * 2 + [DMA((2,))]
    main = Part(
        (starts, segments, queries, kv, grad_mixed, grad_mixed_t, output, lse, weights),
        [SCALARS] + [VECTORS] * 8,
        shapes,
        scratch,
        lambda here, *refs: box.setdefault("back", Back(here, causal, apart, *refs)),
    )

    def body(here, back, *bound):
        def event(time):
            for one in bound:
                one.event(time)

        back.run(event)

    return run_parts(number, body, [main] + list(more), cost_of(kv, count, width, 7))


class Plan:
    def __init__(self, kernels):
        self.kernels = kernels

    def chains(self, wanted):
        return [chain(*one) for one in wanted] if self.kernels else []

    def given(self, wanted, results):
        return results if self.kernels else [one[0] for one in wanted]


class Places:
    def __init__(self, pairs, ring):
        self.pairs, self.ring = pairs, ring
        self.d = lax.axis_index("dp")
        self.x, self.core = self.d // 2, self.d % 2
        self.y, self.z = lax.axis_index("tensor"), lax.axis_index("seq")

    def swap_core(self, value):
        return lax.ppermute(value, "dp", [(i, i ^ 1) for i in range(self.pairs)])

    def swap_y(self, value):
        return lax.ppermute(value, "tensor", [(0, 1), (1, 0)])

    def swap_x(self, value, bit):
        return lax.ppermute(value, "dp", [(i, i ^ (2 << bit)) for i in range(self.pairs)])

    def swap_z(self, value, bit):
        return lax.ppermute(value, "seq", [(i, i ^ (1 << bit)) for i in range(self.ring)])

    def from_z(self, value, step):
        return lax.ppermute(value, "seq", [((i + step) % self.ring, i) for i in range(self.ring)])

    def to_z(self, value, step):
        return lax.ppermute(value, "seq", [(i, (i + step) % self.ring) for i in range(self.ring)])

    def permute(self, value, source_of):
        moves = []
        for d in range(self.pairs):
            for y in range(2):
                source = source_of(d, y)
                if source is not None:
                    moves.append((source[0] * 2 + source[1], d * 2 + y))
        return lax.ppermute(value, ("dp", "tensor"), moves)

    def fetch_weight(self, value):
        return self.permute(value, lambda d, y: (d + 1, y) if d % 2 == 0 else (d - 1, 1 - y))

    def core_sum(self, partial):
        low = rounded(partial)
        return low + self.swap_core(low.astype(BF16)).astype(F32)

    def own_pair(self, rows):
        return jnp.where(self.core == self.y, rows, self.swap_core(rows))

    def hand_out(self, rows):
        return jnp.where(self.core == self.y, rows, self.others(rows))

    def others(self, rows):
        return self.permute(rows, lambda d, y: (d, 1 - y) if d % 2 != y else None)

    def plan(self):
        return Plan(self.pairs == 4 and self.ring == 4)

    def scatter(self, grad, x_first):
        rows, columns = grad.shape
        owners = self.pairs // 2
        grad = grad.reshape(owners, 2, self.ring, rows // (self.pairs * self.ring), columns)
        for stage in "xyz" if x_first else "yxz":
            if stage == "y":
                kept = lax.dynamic_index_in_dim(grad, self.core, grad.ndim - 4, False)
                sent = lax.dynamic_index_in_dim(grad, 1 - self.core, grad.ndim - 4, False)
                first = self.permute(
                    sent, lambda d, y: (d + 1, 1 - y) if d % 2 == 0 else (d - 1, y)
                )
                second = self.permute(kept, lambda d, y: (d, 1 - y) if d % 2 else None)
                kept = jnp.where(self.core == 0, kept, second)
                grad = (kept.astype(F32) + first.astype(F32)).astype(BF16)
            else:
                axis = 0 if stage == "x" else grad.ndim - 3
                place, swap = (self.x, self.swap_x) if stage == "x" else (self.z, self.swap_z)
                size, bit = grad.shape[axis], 0
                while size > 1:
                    shape = grad.shape[:axis] + (size // 2, 2) + grad.shape[axis + 1 :]
                    grad = grad.reshape(shape)
                    mine = (place >> bit) & 1
                    kept = lax.dynamic_index_in_dim(grad, mine, axis + 1, False)
                    sent = lax.dynamic_index_in_dim(grad, 1 - mine, axis + 1, False)
                    grad = kept.astype(F32) + swap(sent, bit).astype(F32)
                    size, bit = size // 2, bit + 1
                    if stage == "x" or size > 1:
                        grad = grad.astype(BF16)
                grad = lax.squeeze(grad, (axis,))
        return grad.astype(F32)

    def all_sum(self, whole, halves):
        both = jnp.concatenate([whole, halves])
        for bit in range((self.pairs // 2).bit_length() - 1):
            both = both + self.swap_x(both, bit)
        for bit in range(self.ring.bit_length() - 1):
            both = both + self.swap_z(both, bit)
        whole, halves = both[: whole.shape[0]], both[whole.shape[0] :]
        whole = whole + self.swap_y(whole)
        whole = (whole + self.swap_core(whole)) * 0.5
        first = self.permute(halves, lambda d, y: (d + 1, 1 - y) if d % 2 == 0 else (d - 1, y))
        second = self.swap_y(halves)
        halves = jnp.where(self.core == 0, halves, second) + first
        return whole, halves


def starts_of(segments):
    numbers = jnp.arange(8, dtype=jnp.int32)
    return jnp.sum(segments[None, :] < numbers[:, None], axis=1, dtype=jnp.int32)


def mask_of(query_seg, key_starts, first_row, causal):
    ends = jnp.stack([query_seg[0], query_seg[-1], first_row])
    return (causal, key_starts, ends, query_seg[None])


def projected(query_in, key_in, weights, bias):
    width = bias.shape[1] // 3
    queries = (dot_plain(query_in, weights[:, :width]) + bias[:, :width]).astype(BF16)
    kv = (dot_plain(key_in, weights[:, width:]) + bias[:, width:]).astype(BF16)
    return (queries * HEAD_DIM ** (-0.5)).astype(BF16), kv


def attention_output(place, queries, kv, output, lse, out_weight, out_bias):
    mixed = output.astype(BF16)
    branch = place.core_sum(dot_first(mixed, out_weight)) + out_bias.astype(F32)
    return (branch, (queries, kv, output, lse, mixed))


def attention_backward(
    number,
    grad_branch,
    saved,
    query_in,
    key_in,
    weights,
    out_weight,
    mask,
    apart,
    plan,
    wanted,
    inside=(),
    begins=False,
):
    mixed = saved[4]
    grad_mixed = dot_last(grad_branch, out_weight).astype(BF16)
    grad_mixed_t = dot_last(out_weight, grad_branch).astype(BF16)
    box = {}
    more = []
    if plan.kernels:
        made = products(box, query_in, key_in, grad_branch, mixed, 5, begins)
        more = [*made, *plan.chains(wanted), *inside]
    (grad_q, grad_kv, *sums), *rest = attend_back(
        number, saved, grad_mixed, grad_mixed_t, weights, mask, apart, more, box
    )
    if plan.kernels:
        (grad_bias, *grads), *rest = rest
        if begins:
            grads, rest = [first[0] for first in rest[:3]], rest[3:]
    else:
        grads = (
            dot_first(query_in, grad_q).astype(BF16),
            dot_first(grad_branch, mixed.T).astype(BF16),
            dot_first(key_in, grad_kv).astype(BF16),
        )
        grad_bias = jnp.stack([column_sum(grad_q), column_sum(grad_kv[:, grad_q.shape[1] :])])
    given = [results[0] for results in rest[: len(rest) - len(inside)]]
    rest = rest[len(rest) - len(inside) :]
    return (sums, grads, grad_bias.reshape(-1), plan.given(wanted, given), rest)


def feed_forward(place, x_in, w_in, b_in, w_out, b_out):
    hidden = dot_plain(x_in, w_in) + b_in.astype(F32)
    spread = 0.5 * (1.0 + lax.erf(hidden * 0.5**0.5))
    active = (hidden * spread).astype(BF16)
    slope = spread + hidden * jnp.exp(-0.5 * hidden * hidden) * (2.0 * math.pi) ** (-0.5)
    branch = place.core_sum(dot_plain(active, w_out)) + b_out.astype(F32)
    return (branch, (slope, active))


def feed_backward(place, grad_branch, saved, x_in, w_in, w_out):
    slope, active = saved
    grad_hidden = (slope * dot_last(grad_branch, w_out)).astype(BF16)
    grad_in = place.core_sum(dot_last(grad_hidden, w_in))
    return (
        grad_in,
        dot_first(x_in, grad_hidden).astype(BF16),
        column_sum(grad_hidden),
        dot_first(grad_branch, active).astype(BF16),
    )


def shards(
    source,
    target,
    source_segments,
    target_segments,
    enc_qkv,
    enc_qv_bias,
    enc_proj,
    enc_ff_in,
    enc_ff_in_bias,
    enc_ff_out,
    enc_bias,
    enc_gains,
    enc_shifts,
    dec_self,
    dec_self_bias,
    dec_self_proj,
    dec_cross,
    dec_cross_bias,
    dec_cross_proj,
    dec_ff_in,
    dec_ff_in_bias,
    dec_ff_out,
    dec_bias,
    dec_gains,
    dec_shifts,
    enc_cotangent,
    dec_cotangent,
):
    count = source.shape[1]
    model = source.shape[2]
    place = Places(lax.axis_size("dp"), lax.axis_size("seq"))
    first_row = place.z * count

    ring = place.ring
    width = enc_qkv.shape[2]
    hidden_units = enc_ff_in.shape[1]

    x_all, ts, source_keys, target_keys, vectors, enc_qkv, enc_proj, dec_self = opening(
        ring,
        source[0],
        target[0],
        source_segments,
        target_segments,
        (
            enc_qv_bias,
            dec_self_bias,
            dec_cross_bias,
            enc_ff_in_bias,
            dec_ff_in_bias,
        ),
        (enc_qkv, enc_proj, dec_self),
    )
    source_keys, target_keys = source_keys[0], target_keys[0]
    xs = lax.dynamic_slice_in_dim(x_all, first_row, count, 0)
    enc_cot = place.own_pair(enc_cotangent[0])
    dec_cot = place.own_pair(dec_cotangent[0])
    enc_b, self_b, cross_b = (vectors[k : k + 1, : 3 * width] for k in range(3))
    enc_ff_in_bias, dec_ff_in_bias = vectors[3], vectors[4]
    source_own = lax.dynamic_slice_in_dim(source_keys, first_row, count, 0)
    target_own = lax.dynamic_slice_in_dim(target_keys, first_row, count, 0)
    source_starts, target_starts = starts_of(source_keys), starts_of(target_keys)
    enc_mask = mask_of(source_own, source_starts, first_row, False)
    self_mask = mask_of(target_own, target_starts, first_row, True)
    cross_mask = mask_of(target_own, source_starts, first_row, False)

    queries, kv, output, lse, t_all, enc_ff_in, enc_ff_out = gather_attend(
        7, ring, x_all, enc_qkv, enc_b, enc_mask, ts, (enc_ff_in, enc_ff_out)
    )
    dec_ff_in = place.fetch_weight(dec_ff_in + after(lse).astype(BF16))
    branch, enc_attn = attention_output(place, queries, kv, output, lse, enc_proj, enc_bias[0])
    first, enc_norm_one = norm_forward(xs.astype(F32) + branch, enc_gains[0], enc_shifts[0])
    first_low = first.astype(BF16)
    branch, enc_feed = feed_forward(
        place, first_low, enc_ff_in, enc_ff_in_bias, enc_ff_out, enc_bias[1]
    )
    encoded, enc_norm_two = norm_forward(first + branch, enc_gains[1], enc_shifts[1])
    encoded_low = encoded.astype(BF16)

    (
        queries,
        kv,
        output,
        lse,
        e_all,
        dec_self_proj,
        dec_cross,
        dec_cross_proj,
    ) = gather_attend(
        2,
        ring,
        t_all,
        dec_self,
        self_b,
        self_mask,
        encoded_low,
        (dec_self_proj, dec_cross, dec_cross_proj),
    )
    dec_ff_out = place.fetch_weight(dec_ff_out + after(lse).astype(BF16))
    branch, self_attn = attention_output(
        place, queries, kv, output, lse, dec_self_proj, dec_bias[0]
    )
    second, dec_norm_one = norm_forward(ts.astype(F32) + branch, dec_gains[0], dec_shifts[0])
    second_low = second.astype(BF16)
    queries, kv = projected(second_low, e_all, dec_cross, cross_b)
    output, lse = attend(queries, kv, cross_mask, (dec_ff_in,))
    branch, cross_attn = attention_output(
        place, queries, kv, output, lse, dec_cross_proj, dec_bias[1]
    )
    third, dec_norm_two = norm_forward(second + branch, dec_gains[1], dec_shifts[1])
    third_low = third.astype(BF16)
    branch, dec_feed = feed_forward(
        place, third_low, dec_ff_in, dec_ff_in_bias, dec_ff_out, dec_bias[2]
    )
    decoded, dec_norm_three = norm_forward(third + branch, dec_gains[2], dec_shifts[2])

    def back_mask(mask):
        return (mask[0], mask[1], mask[3])

    grad_hidden, dec_gain_three, dec_shift_three = norm_backward(
        dec_cot.astype(F32), dec_norm_three, dec_gains[2]
    )
    grad_branch = grad_hidden.astype(BF16)
    feed_in, dec_w_in, dec_b_in, dec_w_out = feed_backward(
        place, grad_branch, dec_feed, third_low, dec_ff_in, dec_ff_out
    )
    dec_bias_three = column_sum(grad_branch)
    grad_third = grad_hidden + feed_in
    grad_hidden, dec_gain_two, dec_shift_two = norm_backward(grad_third, dec_norm_two, dec_gains[1])
    grad_branch = grad_hidden.astype(BF16)
    plan = place.plan()
    (key_total, query_total), cross_grads, cross_bias, (dec_w_in, dec_w_out), _ = attention_backward(
        3,
        grad_branch,
        cross_attn,
        second_low,
        e_all,
        dec_cross,
        dec_cross_proj,
        back_mask(cross_mask),
        True,
        plan,
        [(dec_w_in, "x", (0, 6)), (dec_w_out, "y", (0, 6))],
    )
    dec_bias_two = column_sum(grad_branch)
    grad_second = grad_hidden + query_total
    grad_hidden, dec_gain_one, dec_shift_one = norm_backward(
        grad_second, dec_norm_one, dec_gains[0]
    )
    grad_branch = grad_hidden.astype(BF16)
    cross_q, cross_proj, cross_kv = cross_grads
    target_hidden, target_branch = grad_hidden, grad_branch
    grad_hidden, enc_gain_two, enc_shift_two = norm_backward(
        enc_cot.astype(F32) + key_total.astype(F32), enc_norm_two, enc_gains[1]
    )
    grad_branch = grad_hidden.astype(BF16)
    enc_bias_two = column_sum(grad_branch)
    slope, active = enc_feed
    (target_total,), self_grads, self_bias, given, inside = attention_backward(
        4,
        target_branch,
        self_attn,
        ts,
        t_all,
        dec_self,
        dec_self_proj,
        back_mask(self_mask),
        False,
        plan,
            [
                (dec_w_in, "yvw", (0, 3, 5, 6)),
                (dec_w_out, "xvw", (0, 3, 5, 6)),
                (cross_kv, "x", (3, 6)),
                (cross_q, "y", (3, 6)),
                (cross_proj, "y", (3, 6)),
            ],
        [feed_back(grad_branch, slope, enc_ff_in, enc_ff_out, first_low, active, 5)]
        if plan.kernels
        else (),
        begins=True,
    )
    dec_w_in, dec_w_out, cross_kv, cross_q, cross_proj = given
    if plan.kernels:
        feed_in, enc_b_in, enc_w_in, enc_w_out = inside[0]
        enc_b_in = enc_b_in.reshape(-1)
    else:
        feed_in, enc_w_in, enc_b_in, enc_w_out = feed_backward(
            place, grad_branch, enc_feed, first_low, enc_ff_in, enc_ff_out
        )
    dec_bias_one = column_sum(target_branch)
    grad_target = target_hidden + target_total.astype(F32)
    grad_first = grad_hidden + feed_in
    grad_hidden, enc_gain_one, enc_shift_one = norm_backward(grad_first, enc_norm_one, enc_gains[0])
    grad_branch = grad_hidden.astype(BF16)
    self_q, self_proj, self_kv = self_grads
    (source_total,), enc_grads, enc_bias_grad, given, _ = attention_backward(
        5,
        grad_branch,
        enc_attn,
        xs,
        x_all,
        enc_qkv,
        enc_proj,
        back_mask(enc_mask),
        False,
        plan,
            [
                (cross_kv, "yvw", (0, 1, 3, 6)),
                (cross_q, "xvw", (0, 1, 3, 6)),
                (cross_proj, "xvw", (0, 1, 3, 6)),
                (enc_w_in, "x", (1, 6)),
                (enc_w_out, "y", (1, 6)),
                (self_kv, "y", (4, 6)),
                (self_q, "x", (4, 6)),
                (self_proj, "x", (4, 6)),
            ],
    )
    cross_kv, cross_q, cross_proj, enc_w_in, enc_w_out, self_kv, self_q, self_proj = given
    enc_bias_one = column_sum(grad_branch)
    grad_source = grad_hidden + source_total.astype(F32)
    enc_q, enc_proj_grad, enc_kv = enc_grads
    rest = [
        (self_kv, "vw", (0, 1, 2)),
        (self_q, "vw", (0, 1, 2)),
        (self_proj, "vw", (0, 1, 2)),
        (enc_w_in, "yvw", (0, 2, 4, 7)),
        (enc_w_out, "xvw", (0, 2, 4, 7)),
        (enc_kv, "xyvw", (2, 3, 5, 6, 7)),
        (enc_q, "yxvw", (2, 3, 5, 6, 7)),
        (enc_proj_grad, "yxvw", (2, 3, 5, 6, 7)),
    ]
    source_low = rounded(grad_source).astype(BF16)
    target_low = rounded(grad_target).astype(BF16)
    rows = (source_low, place.others(source_low), target_low, place.others(target_low))
    small = small_sums(
        jnp.concatenate(
            [
                enc_bias_one,
                enc_bias_two,
                enc_gain_one,
                enc_gain_two,
                enc_shift_one,
                enc_shift_two,
                dec_bias_one,
                dec_bias_two,
                dec_bias_three,
                dec_gain_one,
                dec_gain_two,
                dec_gain_three,
                dec_shift_one,
                dec_shift_two,
                dec_shift_three,
            ]
        ).reshape(15, model),
        jnp.concatenate([enc_bias_grad, self_bias, cross_bias, enc_b_in, dec_b_in]).reshape(-1, model),
        (0, 1, 2, 3, 4, 5),
    )
    if plan.kernels:
        vectors, *given = run_chains(6, [small] + plan.chains(rest), 8)
    else:
        vectors = jnp.concatenate(place.all_sum(*small.vectors)).reshape(-1, model)
        given = [place.scatter(array, True) for array, _, _ in rest]
        dec_w_in, dec_w_out, cross_kv, cross_q, cross_proj = (
            place.scatter(array, True)
            for array in (dec_w_in, dec_w_out, cross_kv, cross_q, cross_proj)
        )
    self_kv, self_q, self_proj, enc_w_in, enc_w_out, enc_kv, enc_q, enc_proj_grad = given

    grads = (enc_q, enc_proj_grad, enc_kv, self_q, self_proj, self_kv, cross_q, cross_proj, cross_kv)
    grads += (enc_w_in, enc_w_out, dec_w_in, dec_w_out)
    flag = jnp.where(place.core == place.y, 1, 0).astype(jnp.int32).reshape(1)
    results = closing(flag, rows, vectors, grads, (2, 2, 2, 3, 3, 3))
    of_source, of_target, *of_matrices = results[:12]
    of_whole, of_halves = results[12:18], results[18:]
    return (
        place.hand_out(encoded_low)[None],
        place.hand_out(decoded.astype(BF16))[None],
        of_source[None],
        of_target[None],
        of_matrices[0],
        of_halves[0],
        of_matrices[1],
        of_matrices[6],
        of_halves[3].reshape(-1),
        of_matrices[7],
        *of_whole[:3],
        of_matrices[2],
        of_halves[1],
        of_matrices[3],
        of_matrices[4],
        of_halves[2],
        of_matrices[5],
        of_matrices[8],
        of_halves[4].reshape(-1),
        of_matrices[9],
        *of_whole[3:],
    )


def solution(mesh):
    return jax.shard_map(
        shards,
        mesh=mesh,
        in_specs=(
            P("dp", "seq", None),
            P("dp", "seq", None),
            P("dp", None),
            P("dp", None),
            P(None, None, "tensor"),
            P(None, "tensor"),
            P("tensor", None),
            P(None, "tensor"),
            P("tensor"),
            P("tensor", None),
            P(),
            P(),
            P(),
            P(None, None, "tensor"),
            P(None, "tensor"),
            P("tensor", None),
            P(None, None, "tensor"),
            P(None, "tensor"),
            P("tensor", None),
            P(None, "tensor"),
            P("tensor"),
            P("tensor", None),
            P(),
            P(),
            P(),
            P("dp", "seq", None),
            P("dp", "seq", None),
        ),
        out_specs=(
            P("dp", "seq", None),
            P("dp", "seq", None),
            P("dp", "seq", None),
            P("dp", "seq", None),
            P(None, ("dp", "seq"), "tensor"),
            P(None, "tensor"),
            P("tensor", ("dp", "seq")),
            P(("dp", "seq"), "tensor"),
            P("tensor"),
            P("tensor", ("dp", "seq")),
            P(),
            P(),
            P(),
            P(None, ("dp", "seq"), "tensor"),
            P(None, "tensor"),
            P("tensor", ("dp", "seq")),
            P(None, ("dp", "seq"), "tensor"),
            P(None, "tensor"),
            P("tensor", ("dp", "seq")),
            P(("dp", "seq"), "tensor"),
            P("tensor"),
            P("tensor", ("dp", "seq")),
            P(),
            P(),
            P(),
        ),
        check_vma=False,
    )
```

```python
import functools
import math

import jax
import jax.numpy as jnp
from jax import lax
from jax.experimental import pallas as pl
from jax.experimental.pallas import tpu as pltpu
from jax.sharding import PartitionSpec as P

HEAD_DIM = 64
EPS = 1e-05
NEG = -1e30
BF16 = jnp.bfloat16
F32 = jnp.float32
NT = (((1,), (1,)), ((), ()))
TN = (((0,), (0,)), ((), ()))
KEY_BLOCK = 512
CHUNKS = 2
DOCS = 4


def dot_plain(left, right):
    return jnp.dot(left, right, preferred_element_type=F32)


def dot_last(left, right):
    return lax.dot_general(left, right, NT, preferred_element_type=F32)


def dot_first(left, right):
    return lax.dot_general(left, right, TN, preferred_element_type=F32)


def column_sum(value):
    return jnp.sum(value.astype(F32), axis=0)


def rounded(value):
    return lax.reduce_precision(value, 8, 7)


def after(array):
    return jnp.minimum(jnp.abs(array[0, 0].astype(F32)), 0.0)


def norm_forward(hidden, gain, shift):
    centered = hidden - jnp.mean(hidden, axis=-1, keepdims=True)
    spread = jnp.mean(centered * centered, axis=-1, keepdims=True)
    factor = lax.rsqrt(spread + EPS)
    normed = centered * factor
    return (normed * gain.astype(F32) + shift.astype(F32), (normed, factor))


def norm_backward(grad, saved, gain):
    normed, factor = saved
    scaled = grad * gain.astype(F32)
    centered = scaled - jnp.mean(scaled, axis=-1, keepdims=True)
    grad_hidden = factor * (centered - normed * jnp.mean(scaled * normed, axis=-1, keepdims=True))
    return (grad_hidden, jnp.sum(grad * normed, axis=0), jnp.sum(grad, axis=0))


def head_columns(head):
    return slice(head // 2 * 128, head // 2 * 128 + 128)


def head_rows(head):
    return slice(head * HEAD_DIM, (head + 1) * HEAD_DIM)


def own_lanes(shape, head):
    lanes = lax.broadcasted_iota(jnp.int32, shape, 1)
    return lanes >= HEAD_DIM if head % 2 else lanes < HEAD_DIM


class Mask:
    def __init__(self, causal, starts, segments, first_row):
        self.causal, self.starts, self.first_row = causal, starts, first_row
        segments = segments[...]
        low = high = jnp.zeros_like(segments)
        for number in range(DOCS):
            low = jnp.where(segments == number, starts[number], low)
            high = jnp.where(segments == number, starts[number + 1], high)
        self.count = segments.shape[1]
        if causal:
            place = first_row + lax.broadcasted_iota(jnp.int32, segments.shape, 1)
            high = jnp.minimum(high, place + 1)
        self.low, self.high = low, high

    def allowed(self, index, block):
        place = lax.broadcasted_iota(jnp.int32, (block, self.count), 0) + index * block
        return (place >= self.low) & (place < self.high)

    def flag(self, index, block, ends):
        start, stop = index * block, (index + 1) * block
        low, low_last = self.starts[ends[0]], self.starts[ends[1]]
        high_first, high = self.starts[ends[0] + 1], self.starts[ends[1] + 1]
        if self.causal:
            high = jnp.minimum(high, self.first_row + self.count)
            high_first = jnp.minimum(high_first, self.first_row + 1)
        active = (low < stop) & (high > start)
        full = (low_last <= start) & (high_first >= stop)
        return jnp.where(active, jnp.where(full, 2, 1), 0)


def over_blocks(mask, ends, length, block, body, skipped):
    @pl.loop(0, length // block)
    def _(index):
        flag = mask.flag(index, block, ends)
        rows = pl.ds(pl.multiple_of(index * block, block), block)

        @pl.when(flag == 0)
        def _():
            skipped(rows)

        @pl.when(flag == 1)
        def _():
            body(index, rows, True)

        @pl.when(flag == 2)
        def _():
            body(index, rows, False)


def forward_start(q_ref, masked_q, acc, top):
    heads = q_ref.shape[1] // HEAD_DIM
    for head in range(heads):
        pair = q_ref[:, head_columns(head)]
        masked_q[head] = jnp.where(own_lanes(pair.shape, head), pair, jnp.zeros_like(pair))
    acc[...] = jnp.zeros_like(acc)
    top[...] = jnp.full_like(top, NEG)


def forward_block(index, rows, partial, block, kv_ref, mask, masked_q, acc, top):
    heads, count = masked_q.shape[:2]
    width = heads * HEAD_DIM
    if partial:
        allowed = mask.allowed(index, block)
    for head in range(heads):
        cols = head_columns(head)
        scores = lax.dot_general(kv_ref[rows, cols], masked_q[head], NT, preferred_element_type=F32)
        if partial:
            scores = jnp.where(allowed, scores, NEG)
        old = top[head : head + 1, :]
        new = jnp.maximum(old, jnp.max(scores, axis=0, keepdims=True))
        weights = jnp.exp(scores - new).astype(BF16)
        vals = kv_ref[rows, width + cols.start : width + cols.stop]
        vals = jnp.where(own_lanes(vals.shape, head), vals, jnp.ones_like(vals))
        acc[head] = acc[head] * jnp.exp(old - new) + lax.dot_general(
            vals, weights, TN, preferred_element_type=F32
        )
        top[head : head + 1, :] = new


def forward_end(out_ref, lse_ref, acc, top):
    lse_ref[...] = jnp.zeros_like(lse_ref)
    for head in range(acc.shape[0]):
        first = head % 2 * HEAD_DIM
        total = acc[head, HEAD_DIM - first : HEAD_DIM - first + 1, :]
        out_ref[head_rows(head), :] = acc[head, first : first + HEAD_DIM, :] / total
        lse_ref[head : head + 1, :] = top[head : head + 1, :] + jnp.log(total)


def forward_kernel(block, causal, tokens, starts, ends, segments, q_ref, kv_ref, *refs):
    out_ref, lse_ref, masked_q, acc, top = refs[tokens:]
    mask = Mask(causal, starts, segments, ends[2])
    forward_start(q_ref, masked_q, acc, top)

    def body(index, rows, partial):
        forward_block(index, rows, partial, block, kv_ref, mask, masked_q, acc, top)

    over_blocks(mask, ends, kv_ref.shape[0], block, body, lambda rows: None)
    forward_end(out_ref, lse_ref, acc, top)


def backward_start(q_ref, do_ref, dot_ref, out_ref, masked_q, masked_do, delta, dq):
    for head in range(masked_q.shape[0]):
        pair = q_ref[:, head_columns(head)]
        keep = own_lanes(pair.shape, head)
        masked_q[head] = jnp.where(keep, pair, jnp.zeros_like(pair))
        pair = do_ref[:, head_columns(head)]
        masked_do[head] = jnp.where(keep, pair, jnp.zeros_like(pair))
        part = head_rows(head)
        delta[head : head + 1, :] = jnp.sum(
            dot_ref[part, :].astype(F32) * out_ref[part, :], axis=0, keepdims=True
        )
    dq[...] = jnp.zeros_like(dq)


def backward_block(
    index, rows, block, mask, kv_ref, lse_ref, dkv_ref, masked_q, masked_do, delta, dq, between
):
    heads = masked_q.shape[0]
    width = heads * HEAD_DIM
    allowed = mask.allowed(index, block)
    for pair in range(heads // 2):
        if pair == 1:
            between()
        cols = head_columns(2 * pair)
        later = slice(width + cols.start, width + cols.stop)
        keys, vals = kv_ref[rows, cols], kv_ref[rows, later]
        dk = dv = 0.0
        for head in (2 * pair, 2 * pair + 1):
            scores = lax.dot_general(keys, masked_q[head], NT, preferred_element_type=F32)
            probs = jnp.exp(scores - lse_ref[head : head + 1, :])
            probs = jnp.where(allowed, probs, 0.0)
            dprobs = lax.dot_general(vals, masked_do[head], NT, preferred_element_type=F32)
            draw = (probs * (dprobs - delta[head : head + 1, :])).astype(BF16)
            probs = probs.astype(BF16)
            dv = dv + jnp.dot(probs, masked_do[head], preferred_element_type=F32)
            dk = dk + jnp.dot(draw, masked_q[head], preferred_element_type=F32)
            first = head % 2 * HEAD_DIM
            both = lax.dot_general(keys, draw, TN, preferred_element_type=F32)
            dq[head_rows(head), :] += both[first : first + HEAD_DIM]
        dkv_ref[rows, cols] = dk.astype(BF16)
        dkv_ref[rows, later] = dv.astype(BF16)


SCALARS = pl.BlockSpec(memory_space=pltpu.SMEM)
VECTORS = pl.BlockSpec(memory_space=pltpu.VMEM)


ANYWHERE = pl.BlockSpec(memory_space=pl.ANY)


def cost_of(kv, count, width, products):
    flops = 2 * products * kv.shape[0] * count * width
    return pl.CostEstimate(flops=flops, bytes_accessed=flops // 512, transcendentals=0)


def forward_scratch(count, width):
    heads = width // HEAD_DIM
    return [
        pltpu.VMEM((heads, count, 128), BF16),
        pltpu.VMEM((heads, 128, count), F32),
        pltpu.VMEM((8, count), F32),
    ]


def backward_scratch(count, width):
    heads = width // HEAD_DIM
    return [
        pltpu.VMEM((heads, count, 128), BF16),
        pltpu.VMEM((heads, count, 128), BF16),
        pltpu.VMEM((8, count), F32),
        pltpu.VMEM((width, count), F32),
    ]


def attend(queries, kv, mask, tokens):
    count, width = queries.shape
    causal, starts, ends, segments = mask
    return pl.pallas_call(
        functools.partial(forward_kernel, KEY_BLOCK, causal, len(tokens)),
        out_shape=(
            jax.ShapeDtypeStruct((width, count), F32),
            jax.ShapeDtypeStruct((8, count), F32),
        ),
        in_specs=[SCALARS] * 2 + [VECTORS] * 3 + [ANYWHERE] * len(tokens),
        out_specs=(VECTORS,) * 2,
        scratch_shapes=forward_scratch(count, width),
        compiler_params=pltpu.CompilerParams(vmem_limit_bytes=40 << 20),
        cost_estimate=cost_of(kv, count, width, 2),
    )(starts, ends, segments, queries, kv, *tokens)


MESH = pl.DeviceIdType.MESH
DMA = pltpu.SemaphoreType.DMA


class Here:
    def __init__(self, ring):
        self.ring = ring
        self.d, self.z, self.y = (lax.axis_index(a) for a in ("dp", "seq", "tensor"))
        self.core, self.x = lax.rem(self.d, 2), lax.div(self.d, 2)
        self.other_d = self.d + 1 - 2 * self.core
        self.partner = (self.other_d, self.z, self.y)
        self.right = (self.d, self.z + 1, self.y)
        self.left = (self.d, self.z - 1, self.y)
        self.over_x = (self.d + 2 - 4 * lax.rem(self.x, 2), self.z, self.y)
        self.over_y = (self.d, self.z, 1 - self.y)
        self.diagonal = (self.other_d, self.z, 1 - self.y)

    def meet(self, devices):
        barrier = pltpu.get_barrier_semaphore()
        wanted = 0
        for condition, device in devices:

            @pl.when(condition)
            def _(device=device):
                pl.semaphore_signal(barrier, inc=1, device_id=device, device_id_type=MESH)

            wanted = wanted + jnp.where(condition, 1, 0)
        pl.semaphore_wait(barrier, wanted)

    def along_z(self, step):
        return (self.d, lax.rem(self.z + step, self.ring), self.y)

    def everyone(self):
        devices = [self.partner, self.over_x, self.over_y, self.diagonal]
        devices += [self.along_z(step) for step in range(1, self.ring)]
        return [(self.core >= 0, device) for device in devices]

    def crosswise(self):
        return [
            (self.z + 1 < self.ring, (self.other_d, self.z + 1, self.y)),
            (self.z > 0, (self.other_d, self.z - 1, self.y)),
        ]

    def neighbours(self):
        return [
            (self.core >= 0, self.partner),
            (self.z + 1 < self.ring, self.right),
            (self.z > 0, self.left),
        ]


def remote(source, target, sent, received, device):
    return pltpu.make_async_remote_copy(
        src_ref=source,
        dst_ref=target,
        send_sem=sent,
        recv_sem=received,
        device_id=device,
        device_id_type=MESH,
    )


class Gather:
    def __init__(self, here, rows_ref, sems, source=None, owner=None):
        self.here, self.rows_ref, self.source, self.owner = here, rows_ref, source, owner
        self.count = rows_ref.shape[0] // here.ring
        self.size = self.count // (2 * CHUNKS)
        self.sent, self.got, self.core_sent, self.core_got = sems

    def chunk(self, shard, core, chunk):
        start = shard * self.count + core * (self.count // 2) + chunk * self.size
        return self.rows_ref.at[pl.ds(pl.multiple_of(start, self.size), self.size)]

    def ways(self, step):
        here = self.here
        z, ring = here.z, here.ring
        return [
            (0, z - step, z >= step, z - step + 1, (z + 1 < ring) & (z + 1 >= step), here.right),
            (1, z + step, z + step < ring, z + step - 1, (z > 0) & (z + step <= ring), here.left),
        ]

    def along(self, way, step, shard, chunk, device):
        view = self.chunk(shard, self.here.core, chunk)
        k = way * CHUNKS + chunk
        return remote(view, view, self.sent.at[k, step], self.got.at[k, step], device)

    def across(self, way, step, shard, core, chunk):
        view = self.chunk(shard, core, chunk)
        k = way * CHUNKS + chunk
        return remote(
            view, view, self.core_sent.at[k, step], self.core_got.at[k, step], self.here.partner
        )

    def firsts(self):
        found = []
        for chunk in range(CHUNKS):
            for way, _, _, shard, sends, device in self.ways(1):
                if self.source is None:
                    found.append((sends, self.along(way, 1, shard, chunk, device)))
                    continue
                for core in range(2):
                    k = way * CHUNKS + chunk
                    start = core * (self.count // 2) + chunk * self.size
                    to = (self.here.d - self.here.core + core, *device[1:])
                    copy = remote(
                        self.source.at[pl.ds(start, self.size)],
                        self.chunk(shard, core, chunk),
                        self.sent.at[k, core],
                        self.got.at[k, 1],
                        to,
                    )
                    found.append((sends & self.owner, copy))
        return found

    def begin(self):
        for condition, copy in self.firsts():
            pl.when(condition)(copy.start)

    def advance(self, step):
        for chunk in range(CHUNKS):
            for way, shard, comes, _, _, _ in self.ways(step):

                @pl.when(comes)
                def _(way=way, shard=shard, chunk=chunk):
                    self.along(way, step, shard, chunk, self.here.partner).wait_recv()

                _, _, _, _, sends, device = self.ways(step + 1)[way]

                @pl.when(sends)
                def _(way=way, shard=shard, chunk=chunk, device=device):
                    self.along(way, step + 1, shard, chunk, device).start()

                @pl.when(comes)
                def _(way=way, shard=shard, chunk=chunk):
                    self.across(way, step, shard, self.here.core, chunk).start()

    def finish(self):
        for condition, copy in self.firsts():
            pl.when(condition)(copy.wait_send)

        @pl.loop(1, self.here.ring)
        def _(step):
            for chunk in range(CHUNKS):
                for way, shard, comes, out, sends, device in self.ways(step):

                    @pl.when(sends & (step > 1))
                    def _(way=way, out=out, device=device, chunk=chunk):
                        self.along(way, step, out, chunk, device).wait_send()

                    @pl.when(comes)
                    def _(way=way, shard=shard, chunk=chunk):
                        core = self.here.core
                        self.across(way, step, shard, core, chunk).wait_send()
                        self.across(way, step, shard, 1 - core, chunk).wait_recv()


def pieces_of(weights):
    found = []
    for k, weight in enumerate(weights):
        rows, columns = weight.shape[-2:]
        number = 1 if rows % 3 else 3
        while 2 * rows * columns > 655360 * number and rows % (64 * number) == 0:
            number *= 2
        for matrix in range(matrices_of(weight)):
            found += [(k, matrix, i * (rows // number), rows // number) for i in range(number)]
    return found


def matrices_of(weight):
    return weight.shape[0] if len(weight.shape) == 3 else 1


def beside(weight):
    rows, columns = weight.shape[-2:]
    return jax.ShapeDtypeStruct((rows, columns * matrices_of(weight)), weight.dtype)


AHEAD = 4


class Fetch:
    def __init__(self, here, inputs, outputs, sems):
        self.here, self.inputs, self.outputs = here, inputs, outputs
        self.y_sent, self.y_got, self.x_sent, self.x_got, self.core_sent, self.core_got = sems
        self.pieces = pieces_of(inputs)
        self.matrices = [
            (k, matrix)
            for k, given in enumerate(inputs)
            for matrix in range(matrices_of(given))
        ]
        self.number = len(self.pieces)
        self.own = lax.rem(here.x, 2)

    def devices(self):
        here = self.here
        return [(here.core >= 0, here.diagonal), (here.core == 1, here.over_x)]

    def matrix(self, k, matrix):
        given = self.inputs[k]
        return given.at[matrix] if len(given.shape) == 3 else given

    def part(self, p, which):
        k, matrix, start, rows = self.pieces[p]
        first = pl.multiple_of(start + which * (rows // 2), 16)
        return self.matrix(k, matrix).at[pl.ds(first, rows // 2)]

    def place(self, p, which):
        k, matrix, start, rows = self.pieces[p]
        columns = self.inputs[k].shape[-1]
        first = pl.multiple_of(start + which * (rows // 2), 16)
        return self.outputs[k].at[pl.ds(first, rows // 2), pl.ds(matrix * columns, columns)]

    def over_y(self, p):
        return remote(
            self.part(p, self.own),
            self.place(p, self.own),
            self.y_sent.at[p],
            self.y_got.at[p],
            self.here.diagonal,
        )

    def over_x(self, p, which):
        view = self.place(p, which)
        return remote(view, view, self.x_sent.at[p], self.x_got.at[p], self.here.over_x)

    def across(self, m):
        k, matrix = self.matrices[m]
        columns = self.inputs[k].shape[-1]
        return remote(
            self.matrix(k, matrix),
            self.outputs[k].at[:, pl.ds(matrix * columns, columns)],
            self.core_sent.at[m],
            self.core_got.at[m],
            self.here.partner,
        )

    def begin(self):
        @pl.when(self.here.core == 0)
        def _():
            for p in range(min(AHEAD, self.number)):
                self.over_y(p).start()

        @pl.when(self.here.core == 1)
        def _():
            for m in range(len(self.matrices)):
                self.across(m).start()

    def advance(self, p):
        @pl.when(self.here.core == 0)
        def _():
            self.over_y(p).wait_send()
            if p + AHEAD < self.number:
                self.over_y(p + AHEAD).start()

        @pl.when(self.here.core == 1)
        def _():
            self.over_y(p).wait_recv()
            self.over_x(p, self.own).start()

    def end(self):
        @pl.when(self.here.core == 0)
        def _():
            for m in range(len(self.matrices)):
                self.across(m).wait_recv()

        @pl.when(self.here.core == 1)
        def _():
            for p in range(self.number):
                self.over_x(p, self.own).wait_send()
                self.over_x(p, 1 - self.own).wait_recv()
            for m in range(len(self.matrices)):
                self.across(m).wait_send()


def gather_sems(ring):
    return [DMA((2 * CHUNKS, ring))] * 4


def fetch_sems(weights):
    number = len(pieces_of(weights))
    return [DMA((number,))] * 4 + [DMA((3 * len(weights),))] * 2


def opening_kernel(ring, number, *refs):
    inputs, refs = refs[: 9 + number], refs[9 + number :]
    outputs, (vectors, *sems) = refs[: 5 + number], refs[5 + number :]
    source, target, source_seg, target_seg = inputs[:4]
    source_all, target_out, source_seg_out, target_seg_out, vectors_out = outputs[:5]
    shard_sems, vector_sems = sems[:3], sems[3:6]
    here = Here(ring)
    fetch = Fetch(here, inputs[9:], outputs[5:], sems[10:])
    here.meet(here.neighbours() + here.crosswise() + fetch.devices())
    count = source.shape[0]
    own = pl.ds(pl.multiple_of(here.z * count, count), count)
    moves = [
        (source, source_all.at[own]),
        (target, target_out),
        (source_seg, source_seg_out),
        (target_seg, target_seg_out),
    ]
    owner = here.core == here.y

    def shard_copy(k):
        start, end = moves[k]
        sent, got, copied = shard_sems
        return (
            remote(start, end, sent.at[k], got.at[k], here.partner),
            pltpu.make_async_copy(start, end, copied.at[k]),
        )

    def vector_copy():
        sent, got, copied = vector_sems
        return (
            remote(vectors, vectors_out, sent, got, here.diagonal),
            pltpu.make_async_copy(vectors, vectors_out, copied),
        )

    def wait_shard(k):
        across, local = shard_copy(k)

        @pl.when(owner)
        def _():
            across.wait_send()
            local.wait()

        @pl.when(jnp.logical_not(owner))
        def _():
            across.wait_recv()

    gather = Gather(here, source_all, sems[6:10], source, owner)
    gather.begin()

    @pl.when(owner)
    def _():
        for k in range(len(moves)):
            across, local = shard_copy(k)
            across.start()
            local.start()

    fetch.begin()

    vectors[...] = jnp.zeros_like(vectors)
    for row, bias in enumerate(inputs[4:7]):
        width = bias.shape[1]
        for part in range(2):
            value = bias[part : part + 1, :].astype(F32)
            vectors[row : row + 1, 2 * part * width : (2 * part + 1) * width] = value
    for row, bias in enumerate(inputs[7:9]):
        vectors[3 + row : 4 + row, :] = bias[...].astype(F32).reshape(1, -1)

    @pl.when(here.core == 0)
    def _():
        across, local = vector_copy()
        across.start()
        local.start()

    done = 0
    for step in range(1, ring):
        while done < fetch.number * (2 * step - 1) // (2 * ring - 2):
            fetch.advance(done)
            done += 1
        gather.advance(step)
    while done < fetch.number:
        fetch.advance(done)
        done += 1
    gather.finish()
    for k in range(len(moves)):
        wait_shard(k)
    fetch.end()
    across, local = vector_copy()

    @pl.when(here.core == 0)
    def _():
        across.wait_send()
        local.wait()

    @pl.when(here.core == 1)
    def _():
        across.wait_recv()


def opening(ring, source, target, source_seg, target_seg, biases, weights):
    inputs = (source, target, source_seg, target_seg, *biases, *weights)
    count, model = source.shape
    number = len(weights)
    units = biases[-1].shape[0]
    shapes = (
        jax.ShapeDtypeStruct((ring * count, model), BF16),
        jax.ShapeDtypeStruct(target.shape, BF16),
        jax.ShapeDtypeStruct(source_seg.shape, jnp.int32),
        jax.ShapeDtypeStruct(target_seg.shape, jnp.int32),
        jax.ShapeDtypeStruct((8, units), F32),
    ) + tuple(beside(weight) for weight in weights)
    return pl.pallas_call(
        functools.partial(opening_kernel, ring, number),
        out_shape=shapes,
        in_specs=[VECTORS] * 9 + [ANYWHERE] * number,
        out_specs=(ANYWHERE,) + (VECTORS,) * 4 + (ANYWHERE,) * number,
        scratch_shapes=[pltpu.VMEM((8, units), F32)]
        + [DMA((4,))] * 3
        + [DMA] * 3
        + gather_sems(ring)
        + fetch_sems(weights),
        compiler_params=pltpu.CompilerParams(collective_id=1, has_side_effects=True),
    )(*inputs)


def gather_attend_kernel(
    block, causal, ring, number, tokens, starts, segments, bias_ref, own_ref, rows_ref, proj_ref, *refs
):
    weights, refs = refs[:number], refs[number + tokens :]
    q_ref, kv_ref, out_ref, lse_ref, all_ref = refs[:5]
    fetched, refs = refs[5 : 5 + number], refs[5 + number :]
    masked_q, acc, top, rows_in, proj, copied, rows_copied, proj_copied = refs[:8]
    here = Here(ring)
    gather = Gather(here, all_ref, refs[8:12])
    fetch = Fetch(here, weights, fetched, refs[12:])
    count, width = q_ref.shape
    first_row = pl.multiple_of(here.z * count, count)

    def rows_copy(shard):
        rows = pl.ds(pl.multiple_of(shard * count, count), count)
        return pltpu.make_async_copy(rows_ref.at[rows], rows_in.at[rows], rows_copied.at[shard])

    proj_copy = pltpu.make_async_copy(proj_ref, proj, proj_copied)
    proj_copy.start()
    for shard in range(ring):
        rows_copy(shard).start()
    here.meet(here.neighbours() + fetch.devices())
    local = pltpu.make_async_copy(own_ref, all_ref.at[pl.ds(first_row, count)], copied)
    local.start()
    fetch.begin()
    local.wait()
    gather.begin()
    mask = Mask(causal, starts, segments, first_row)
    proj_copy.wait()
    for shard in range(ring):
        rows_copy(shard).wait()
    queries = dot_plain(rows_in[pl.ds(first_row, count), :], proj[:, :width]) + bias_ref[:, :width]
    q_ref[...] = (queries.astype(BF16).astype(F32) * HEAD_DIM ** (-0.5)).astype(BF16)
    forward_start(q_ref, masked_q, acc, top)
    blocks = kv_ref.shape[0] // block

    @pl.loop(0, blocks)
    def _(index):
        rows = pl.ds(pl.multiple_of(index * block, block), block)
        both = dot_plain(rows_in[rows, :], proj[:, width:]) + bias_ref[:, width:]
        kv_ref[rows, :] = both.astype(BF16)
        forward_block(index, rows, True, block, kv_ref, mask, masked_q, acc, top)

        @pl.when((index >= 1) & (index < ring))
        def _():
            gather.advance(index)

        for p in range(fetch.number):
            pl.when(index == 1 + p * (blocks - 1) // fetch.number)(
                functools.partial(fetch.advance, p)
            )

    forward_end(out_ref, lse_ref, acc, top)
    gather.finish()
    fetch.end()


def gather_attend(number, ring, rows, proj, bias, mask, own, weights, tokens=()):
    length, model = rows.shape
    count, width = length // ring, proj.shape[1] // 3
    causal, starts, _, segments = mask
    fetched = len(weights)
    kv = jax.ShapeDtypeStruct((length, 2 * width), BF16)
    return pl.pallas_call(
        functools.partial(gather_attend_kernel, KEY_BLOCK, causal, ring, fetched, len(tokens)),
        out_shape=(
            jax.ShapeDtypeStruct((count, width), BF16),
            kv,
            jax.ShapeDtypeStruct((width, count), F32),
            jax.ShapeDtypeStruct((8, count), F32),
            jax.ShapeDtypeStruct((ring * own.shape[0], own.shape[1]), BF16),
        )
        + tuple(beside(weight) for weight in weights),
        in_specs=[SCALARS] + [VECTORS] * 3 + [ANYWHERE] * (2 + fetched + len(tokens)),
        out_specs=(VECTORS,) * 4 + (ANYWHERE,) * (1 + fetched),
        scratch_shapes=forward_scratch(count, width)
        + [
            pltpu.VMEM((length, model), BF16),
            pltpu.VMEM(proj.shape, BF16),
            DMA,
            DMA((ring,)),
            DMA,
        ]
        + gather_sems(ring)
        + fetch_sems(weights),
        compiler_params=pltpu.CompilerParams(
            vmem_limit_bytes=50 << 20, collective_id=number, has_side_effects=True
        ),
        cost_estimate=cost_of(kv, count, width, 4),
    )(starts, segments, bias, own, rows, proj, *weights, *tokens)


class Part:
    def __init__(self, inputs, in_specs, out_shapes, scratch, bind):
        self.inputs, self.in_specs, self.out_shapes = inputs, in_specs, out_shapes
        self.scratch, self.bind = scratch, bind


def run_parts(number, body, parts, cost=None):
    ring = lax.axis_size("seq")
    counts = [(len(p.inputs), len(p.out_shapes), len(p.scratch)) for p in parts]

    def kernel(*refs):
        here = Here(ring)
        taken, offset = [[] for _ in parts], 0
        for kind in range(3):
            for refs_of, count in zip(taken, counts):
                refs_of.append(refs[offset : offset + count[kind]])
                offset += count[kind]
        here.meet(here.everyone())
        body(here, *(p.bind(here, *refs_of) for p, refs_of in zip(parts, taken)))

    results = pl.pallas_call(
        kernel,
        out_shape=[shape for p in parts for shape in p.out_shapes],
        in_specs=[spec for p in parts for spec in p.in_specs],
        out_specs=[VECTORS for p in parts for _ in p.out_shapes],
        scratch_shapes=[shape for p in parts for shape in p.scratch],
        compiler_params=pltpu.CompilerParams(
            vmem_limit_bytes=62 << 20, collective_id=number, has_side_effects=True
        ),
        cost_estimate=cost,
    )(*(array for p in parts for array in p.inputs))
    given = []
    for _, count, _ in counts:
        given.append(results[:count])
        results = results[count:]
    return given


class Stage:
    def __init__(self, here, kind, source, result, buffers, sems):
        self.here, self.kind, self.source, self.result = here, kind, source, result
        self.buffers, (self.sent, self.got) = buffers, sems
        rows = source.shape[0]
        if kind == "x":
            half = rows // 2
            self.kept = [half * here.x]
            self.given = [half * (1 - here.x)]
            self.size, self.to = half, here.over_x
        elif kind == "y":
            self.size = 192
            self.starts = list(range(0, rows, 2 * self.size))
        elif kind == "v":
            bit = lax.rem(here.z, 2)
            self.size = rows // 4
            self.kept = [self.size * bit, self.size * (bit + 2)]
            self.given = [self.size * (1 - bit), self.size * (3 - bit)]
            self.to = (here.d, here.z + 1 - 2 * bit, here.y)
        else:
            bit = lax.div(here.z, 2)
            self.size = rows // 2
            self.kept, self.given = [self.size * bit], [self.size * (1 - bit)]
            self.to = (here.d, here.z + 2 - 4 * bit, here.y)

    def rows(self, start):
        if not isinstance(start, int):
            start = pl.multiple_of(start, 16)
        return pl.ds(start, self.size)

    def move(self, start, place, buffer, sem, to):
        return remote(
            self.source.at[self.rows(start)],
            self.buffers[buffer].at[self.rows(place * self.size)],
            self.sent.at[sem],
            self.got.at[sem],
            to,
        )

    def moves(self):
        here = self.here
        if self.kind != "y":
            both = [
                (None, self.move(start, k, 0, k, self.to)) for k, start in enumerate(self.given)
            ]
            return both, both
        sends, arrivals = [], []
        for k, start in enumerate(self.starts):
            upper = start + self.size
            sends.append((here.core == 0, self.move(upper, k, 0, 2 * k, here.partner)))
            sends.append((here.core == 1, self.move(start, k, 0, 2 * k, here.diagonal)))
            sends.append((here.core == 1, self.move(upper, k, 1, 2 * k + 1, here.over_y)))
            arrivals.append((None, self.move(upper, k, 0, 2 * k, here.partner)))
            arrivals.append((here.core == 1, self.move(upper, k, 1, 2 * k + 1, here.over_y)))
        return sends, arrivals

    @staticmethod
    def each(moves, act):
        for condition, copy in moves:
            if condition is None:
                act(copy)
            else:
                pl.when(condition)(functools.partial(act, copy))

    def begin(self):
        self.each(self.moves()[0], lambda copy: copy.start())

    def end(self):
        sends, arrivals = self.moves()
        self.each(arrivals, lambda copy: copy.wait_recv())
        kept = self.kept if self.kind != "y" else self.starts
        for k, start in enumerate(kept):
            place = self.rows(k * self.size)

            def add(own_ref, own, place=place):
                both = own_ref[own, :].astype(F32) + self.buffers[0][place, :].astype(F32)
                self.result[place, :] = both.astype(self.result.dtype)

            if self.kind == "y":
                pl.when(self.here.core == 0)(functools.partial(add, self.source, self.rows(start)))
                pl.when(self.here.core == 1)(functools.partial(add, self.buffers[1], place))
            else:
                add(self.source, self.rows(start))
        self.each(sends, lambda copy: copy.wait_send())


class Chain:
    def __init__(self, stages, times):
        self.stages, self.times = stages, times

    def event(self, time):
        for k, own in enumerate(self.times):
            if own == time:
                if k:
                    self.stages[k - 1].end()
                if k < len(self.stages):
                    self.stages[k].begin()


def chain(array, kinds, times, made=None):
    rows, columns = made[2] if made else array.shape
    scratch, shapes = [], []
    for kind in kinds:
        rows = rows // 2
        scratch += [pltpu.VMEM((rows, columns), BF16)] * (2 if kind == "y" else 1)
        scratch += [DMA((4,))] * 2
        shapes.append((rows, columns))
    scratch += [pltpu.VMEM(shape, BF16) for shape in shapes[:-1]]
    final = jax.ShapeDtypeStruct(shapes[-1], F32 if kinds[-1] == "w" else BF16)

    def bind(here, inputs, outputs, refs):
        refs = list(refs)
        results = refs[len(refs) - len(kinds) + 1 :] + [outputs[0]]
        source, stages = made[0][made[1]] if made else inputs[0], []
        for kind, result in zip(kinds, results):
            buffers = [refs.pop(0) for _ in range(2 if kind == "y" else 1)]
            sems = [refs.pop(0) for _ in range(2)]
            stages.append(Stage(here, kind, source, result, buffers, sems))
            source = result
        return Chain(stages, times)

    inputs = () if made else (array,)
    return Part(inputs, [VECTORS] * len(inputs), [final], scratch, bind)


def closing_kernel(flag, *refs):
    given, outputs, held, copied = refs[:22], refs[22:47], refs[47:69], refs[69]
    copies = [
        pltpu.make_async_copy(start, end, copied.at[k])
        for k, (start, end) in enumerate(zip(given, held))
    ]
    for copy in copies:
        copy.start()
    for copy in copies:
        copy.wait()
    rows, vectors, grads = held[:8], held[8], held[9:22]
    keeps = flag[0] == 1
    for k in range(4):
        own, other = rows[2 * k][...], rows[2 * k + 1][...]
        outputs[k][...] = jnp.where(keeps, own, other).astype(outputs[k].dtype)
    for k in range(3):
        of_q, of_kv = grads[3 * k], grads[3 * k + 2]
        qkv = outputs[4 + k]
        width = of_q.shape[1]
        qkv[0] = of_q[...]
        qkv[1] = of_kv[:, :width]
        qkv[2] = of_kv[:, width:]
    outputs[7][...] = grads[9][...]
    outputs[8][...] = grads[11][...]
    for k in range(3):
        outputs[9 + k][...] = grads[3 * k + 1][...]
    for k in range(2):
        outputs[12 + k][...] = grads[10 + 2 * k][...]
    row = 0
    for out in outputs[14:20]:
        out[...] = vectors[row : row + out.shape[0], :]
        row += out.shape[0]
    for out in outputs[20:23]:
        width = out.shape[1]
        out[0:1, :] = vectors[row : row + 1, :width]
        out[1:2, :] = vectors[row : row + 1, width:]
        row += 1
    columns = vectors.shape[1]
    for out in outputs[23:]:
        for part in range(out.shape[0] // columns):
            out[part * columns : (part + 1) * columns] = vectors[row, :]
            row += 1


def closing(flag, rows, vectors, grads, sizes):
    part, width = grads[0].shape
    units = grads[9].shape[1]
    model = vectors.shape[1]
    shapes = [(rows[0].shape, BF16)] * 2 + [(rows[0].shape, F32)] * 2
    matrices = [(3, part, width)] * 3 + [(part, units)] * 2 + [(part, width)] * 3 + [(part, units)] * 2
    matrices += [(size, model) for size in sizes] + [(2, width)] * 3 + [(units,)] * 2
    shapes += [(shape, F32) for shape in matrices]
    inputs = (flag, *rows, vectors, *grads)
    return pl.pallas_call(
        closing_kernel,
        out_shape=[jax.ShapeDtypeStruct(*shape) for shape in shapes],
        in_specs=[SCALARS] + [ANYWHERE] * (len(inputs) - 1),
        out_specs=[VECTORS] * len(shapes),
        scratch_shapes=[pltpu.VMEM(value.shape, value.dtype) for value in inputs[1:]]
        + [DMA((len(inputs) - 1,))],
        compiler_params=pltpu.CompilerParams(vmem_limit_bytes=62 << 20),
    )(*inputs)


class HandOut:
    def __init__(self, here, inputs, outputs, scratch, times):
        self.here, self.times = here, times
        self.sent, self.got = scratch
        self.copies = [
            remote(given, taken, self.sent.at[k], self.got.at[k], here.over_y)
            for k, (given, taken) in enumerate(zip(inputs, outputs))
        ]

    def event(self, time):
        owns = self.here.core == self.here.y
        for copy in self.copies:
            if time == self.times[0]:
                pl.when(owns)(copy.start)
            if time == self.times[1]:
                pl.when(owns)(copy.wait_send)
                pl.when(jnp.logical_not(owns))(copy.wait_recv)


def hand_out(rows, times):
    number = len(rows)
    return Part(
        tuple(rows),
        [VECTORS] * number,
        [jax.ShapeDtypeStruct(value.shape, value.dtype) for value in rows],
        [DMA((number,))] * 2,
        lambda here, *refs: HandOut(here, *refs, times),
    )


class Small:
    def __init__(self, here, rows, held_rows, given, result, refs, times):
        self.here, self.given, self.result, self.times = here, given, result, times
        self.rows, self.held_rows = rows, held_rows
        self.arrived, self.sent, self.got = refs
        self.bits = [lax.rem(here.z, 2), lax.div(here.z, 2)]

    def copies(self, stage):
        here = self.here
        low, high = self.bits

        def to(device, slot, source=self.result, target=None):
            target = self.arrived.at[slot] if target is None else target
            return remote(source, target, self.sent.at[slot], self.got.at[slot], device)

        if stage < 3:
            device = (
                here.over_x,
                (here.d, here.z + 1 - 2 * low, here.y),
                (here.d, here.z + 2 - 4 * high, here.y),
            )[stage]
            both = [(None, to(device, stage))]
            return both, both
        if stage == 3:
            sends = [
                (None, to(here.over_y, 3)),
                (here.core == 0, to(here.partner, 4)),
                (here.core == 1, to(here.diagonal, 4)),
            ]
            return sends, sends[:1] + [(None, to(here.partner, 4))]
        return [(here.core == 0, to(here.partner, 5))], [(here.core == 1, to(here.partner, 5))]

    def end(self, stage):
        sends, arrivals = self.copies(stage)
        Stage.each(arrivals, lambda copy: copy.wait_recv())
        Stage.each(sends, lambda copy: copy.wait_send())
        core = self.here.core
        if stage < 3:
            self.result[...] += self.arrived[stage]
        elif stage == 3:
            whole, halves = slice(0, self.held_rows), slice(self.held_rows, self.rows)
            self.result[whole, :] += self.arrived[3, whole, :]
            own = jnp.where(core == 0, self.result[halves, :], self.arrived[3, halves, :])
            self.result[halves, :] = own + self.arrived[4, halves, :]
        else:
            whole = slice(0, self.held_rows)

            @pl.when(core == 1)
            def _():
                self.result[whole, :] = self.arrived[5, whole, :]

    def event(self, time):
        for k, own in enumerate(self.times):
            if own == time:
                if k == 0:
                    self.result[...] = self.given[...]
                else:
                    self.end(k - 1)
                if k < 5:
                    Stage.each(self.copies(k)[0], lambda copy: copy.start())


def small_sums(whole, halves, times):
    both = jnp.concatenate([whole, halves])
    rows, columns = both.shape
    shape = jax.ShapeDtypeStruct(both.shape, F32)
    part = Part(
        (both,),
        [VECTORS],
        [shape],
        [pltpu.VMEM((6, rows, columns), F32), DMA((6,)), DMA((6,))],
        lambda here, inputs, outputs, refs: Small(
            here, rows, whole.shape[0], inputs[0], outputs[0], refs, times
        ),
    )
    part.rows, part.vectors = whole.shape[0], (whole.reshape(-1), halves.reshape(-1))
    return part


def run_chains(number, chains, events):
    def body(here, *bound):
        for time in range(events):
            for one in bound:
                one.event(time)

    return run_parts(number, body, chains)


class Back:
    def __init__(self, here, causal, apart, inputs, outputs, scratch):
        self.here, self.causal, self.apart = here, causal, apart
        self.starts, self.segments, self.q, self.kv, self.do, self.dot, self.out, self.lse = inputs[:8]
        self.weights = inputs[8]
        self.dq_out, self.dkv, self.sum = outputs[:3]
        self.query_sum = outputs[3] if apart else None
        self.work, scratch = scratch[:4], scratch[4:]
        self.terms, self.from_core, self.outgoing, self.arrived, self.total = scratch[:5]
        self.core_sent, self.core_got, self.sent, self.got, self.end_sent, self.end_got = scratch[5:11]
        if apart:
            self.query_low, self.query_got, self.query_sems = scratch[11:]
        self.count, self.width = self.q.shape
        self.part = self.count // 2
        self.mask = Mask(causal, self.starts, self.segments, here.z * self.count)

    def half(self, core):
        return pl.ds(pl.multiple_of(core * self.part, self.part), self.part)

    def shard_at(self, turn):
        ring, z, shard = self.here.ring, self.here.z, 0
        for device in range(ring):
            others = [t for t in range(ring) if t != device]
            others.sort(key=lambda t: (ring - t + device) if t > device else (t + ring - device))
            for k, other in enumerate(others):
                shard = jnp.where((z == device) & (turn == k + 1), other, shard)
        return shard

    def across(self, turn, shard):
        return remote(
            self.terms.at[lax.rem(turn, 2), self.half(1 - self.here.core)],
            self.from_core.at[shard],
            self.core_sent.at[shard],
            self.core_got.at[shard],
            self.here.partner,
        )

    def slot(self, way, shard, z):
        return jnp.where((way == 1) & (shard == z), self.here.ring, shard)

    def along(self, way, shard, device):
        return remote(
            self.outgoing.at[shard],
            self.arrived.at[self.slot(way, shard, device[1])],
            self.sent.at[shard],
            self.got.at[way, shard],
            device,
        )

    def put(self, turn, shard, terms):
        @pl.when(turn > 2)
        def _():
            self.across(turn - 2, self.shard_at(turn - 2)).wait_send()

        slot = lax.rem(turn, 2)
        self.terms[slot] = terms.astype(BF16)
        self.across(turn, shard).start()
        self.outgoing[shard] = self.terms[slot, self.half(self.here.core), :]

    def both(self, shard):
        self.across(0, shard).wait_recv()
        return self.outgoing[shard].astype(F32) + self.from_core[shard].astype(F32)

    def forward(self, shard):
        here = self.here
        self.total[...] = self.both(shard)
        for way, mine, comes, device in (
            (0, shard > here.z, here.z > 0, here.right),
            (1, shard < here.z, here.z + 1 < here.ring, here.left),
        ):

            @pl.when(mine & comes)
            def _(way=way):
                self.along(way, shard, here.partner).wait_recv()
                self.total[...] += self.arrived[self.slot(way, shard, here.z)].astype(F32)

        self.outgoing[shard] = self.total[...].astype(BF16)
        for way, mine, device in ((0, shard > here.z, here.right), (1, shard < here.z, here.left)):

            @pl.when(mine)
            def _(way=way, device=device):
                self.along(way, shard, device).start()

    def block(self, shard, between):
        rows = pl.ds(pl.multiple_of(shard * self.count, self.count), self.count)
        backward_block(
            shard, rows, self.count, self.mask, self.kv, self.lse, self.dkv, *self.work, between
        )
        return dot_last(self.dkv[rows, :], self.weights[:, self.width :])

    def run(self, event):
        here, ring = self.here, self.here.ring
        at_end = (here.z == 0) | (here.z == ring - 1)
        event(0)
        backward_start(self.q, self.do, self.dot, self.out, *self.work)

        @pl.loop(1, ring)
        def _(turn):
            shard = self.shard_at(turn)

            def between():
                @pl.when((turn > 1) & at_end)
                def _():
                    self.forward(self.shard_at(turn - 1))

            self.put(turn, shard, self.block(shard, between))
            for time in range(1, ring):
                pl.when(turn == time)(functools.partial(event, time))

        def between():
            self.forward(self.shard_at(jnp.where(at_end, ring - 1, 1)))

        own = self.block(here.z, between)
        event(ring)
        low = (self.work[3][...] * HEAD_DIM ** (-0.5)).T.astype(BF16)
        self.dq_out[...] = low
        query = dot_last(low, self.weights[:, : self.width])
        if self.apart:
            self.query_low[...] = query.astype(BF16)
            exchange = remote(
                self.query_low, self.query_got, self.query_sems.at[0], self.query_sems.at[1], here.partner
            )
            exchange.start()
        else:
            own = own + query
        self.put(jnp.int32(ring), here.z, own)
        if self.apart:
            exchange.wait()
            self.query_sum[...] = self.query_low[...].astype(F32) + self.query_got[...].astype(F32)

        @pl.when(jnp.logical_not(at_end))
        def _():
            @pl.loop(2, ring)
            def _(turn):
                self.forward(self.shard_at(turn))

        event(ring + 1)
        self.total[...] = self.both(here.z)
        for way, comes in ((0, here.z > 0), (1, here.z + 1 < ring)):

            @pl.when(comes)
            def _(way=way):
                self.along(way, here.z, here.partner).wait_recv()
                self.total[...] += self.arrived[self.slot(way, here.z, here.z)].astype(F32)

        own, other = self.half(here.core), self.half(1 - here.core)
        self.sum[own, :] = self.total[...].astype(BF16)
        for half, waits in ((own, False), (other, True)):
            view = self.sum.at[half]
            copy = remote(view, view, self.end_sent, self.end_got, here.partner)
            if waits:
                copy.wait_recv()
            else:
                copy.start()
                copy.wait_send()
        self.across(ring - 1, self.shard_at(ring - 1)).wait_send()
        self.across(ring, here.z).wait_send()
        for shard in range(ring):

            @pl.when(here.z != shard)
            def _(shard=shard):
                self.along(0, shard, here.partner).wait_send()

        event(ring + 2)


class Products:
    def __init__(self, back, inputs, of_bias, made, scratch, time):
        self.back, self.time = back, time
        self.query_in, self.key_in, self.grad_branch, self.mixed = inputs
        self.of_bias = of_bias
        self.of_q, self.of_out, self.of_kv = made
        self.blocks, self.copied = scratch

    def copy(self, index):
        part = pl.ds(pl.multiple_of(index * 256, 256), 256)
        slot = lax.rem(index, 2)
        return pltpu.make_async_copy(
            self.key_in.at[:, part], self.blocks.at[slot], self.copied.at[slot]
        )

    def event(self, time):
        if time == 0:
            self.copy(0).start()
        if time != self.time:
            return
        dq, dkv = self.back.dq_out, self.back.dkv
        width = dq.shape[1]
        number = self.of_kv.shape[0] // 256

        @pl.loop(0, number)
        def _(index):
            @pl.when(index + 1 < number)
            def _():
                self.copy(index + 1).start()

            self.copy(index).wait()
            part = pl.ds(pl.multiple_of(index * 256, 256), 256)
            block = self.blocks[lax.rem(index, 2)]
            self.of_kv[part, :] = dot_first(block, dkv[...]).astype(BF16)

        self.of_q[...] = dot_first(self.query_in[...], dq[...]).astype(BF16)
        self.of_out[...] = dot_first(self.grad_branch[...], self.mixed[...].T).astype(BF16)
        self.of_bias[0:1, :] = jnp.sum(dq[...].astype(F32), axis=0, keepdims=True)
        self.of_bias[1:2, :] = jnp.sum(dkv[:, width:].astype(F32), axis=0, keepdims=True)


def products(box, query_in, key_in, grad_branch, mixed, time, begins):
    model, width = query_in.shape[1], mixed.shape[0]
    shapes = ((model, width), (model, width), (model, 2 * width))

    def bind(here, inputs, outputs, refs):
        made = refs[2:] if begins else outputs[1:]
        for k in range(3):
            box[k] = made[k]
        return Products(box["back"], inputs, outputs[0], made, refs[:2], time)

    part = Part(
        (query_in, key_in, grad_branch, mixed),
        [VECTORS, ANYWHERE, VECTORS, VECTORS],
        [jax.ShapeDtypeStruct((2, width), F32)]
        + ([] if begins else [jax.ShapeDtypeStruct(shape, BF16) for shape in shapes]),
        [pltpu.VMEM((2, key_in.shape[0], 256), BF16), DMA((2,))]
        + ([pltpu.VMEM(shape, BF16) for shape in shapes] if begins else []),
        bind,
    )
    if not begins:
        return [part]
    firsts = [
        chain(None, kind, (time, 6), (box, k, shape)) for k, (kind, shape) in enumerate(zip("yyx", shapes))
    ]
    return [part, *firsts]


class FeedBack:
    def __init__(self, here, inputs, outputs, scratch, time):
        self.here, self.time = here, time
        self.grad, self.x_in = inputs[:2]
        self.streamed = inputs[2:]
        self.sum, self.of_bias, self.of_in, self.of_out = outputs
        self.blocks, (self.low, self.got, self.copied, self.sems) = scratch[:4], scratch[4:]

    def event(self, time):
        if time != self.time:
            return
        span = self.blocks[0].shape[2]
        number = self.of_in.shape[1] // span
        self.sum[...] = jnp.zeros_like(self.sum)

        def columns(index):
            return pl.ds(pl.multiple_of(index * span, span), span)

        def copies(index):
            slot, part = lax.rem(index, 2), columns(index)
            return [
                pltpu.make_async_copy(
                    ref.at[part] if k == 3 else ref.at[:, part],
                    self.blocks[k].at[slot],
                    self.copied.at[k, slot],
                )
                for k, ref in enumerate(self.streamed)
            ]

        for copy in copies(0):
            copy.start()

        @pl.loop(0, number)
        def _(index):
            part = columns(index)

            @pl.when(index + 1 < number)
            def _():
                for copy in copies(index + 1):
                    copy.start()

            for copy in copies(index):
                copy.wait()
            slope, active, w_in, w_out = (block.at[lax.rem(index, 2)] for block in self.blocks)
            hidden = (slope[...] * dot_last(self.grad[...], w_out[...])).astype(BF16)
            self.of_bias[:, part] = jnp.sum(hidden.astype(F32), axis=0, keepdims=True)
            self.sum[...] += dot_last(hidden, w_in[...])
            self.of_in[:, part] = dot_first(self.x_in[...], hidden).astype(BF16)
            self.of_out[:, part] = dot_first(self.grad[...], active[...]).astype(BF16)

        self.low[...] = self.sum[...].astype(BF16)
        exchange = remote(self.low, self.got, self.sems.at[0], self.sems.at[1], self.here.partner)
        exchange.start()
        exchange.wait()
        self.sum[...] = self.low[...].astype(F32) + self.got[...].astype(F32)


def feed_back(grad_branch, slope, w_in, w_out, x_in, active, time):
    count, model = x_in.shape
    units = w_in.shape[1]
    span = 256
    return Part(
        (grad_branch, x_in, slope, active, w_in, w_out),
        [VECTORS] * 2 + [ANYWHERE] * 4,
        [
            jax.ShapeDtypeStruct((count, model), F32),
            jax.ShapeDtypeStruct((1, units), F32),
            jax.ShapeDtypeStruct((model, units), BF16),
            jax.ShapeDtypeStruct((model, units), BF16),
        ],
        [
            pltpu.VMEM((2, count, span), slope.dtype),
            pltpu.VMEM((2, count, span), BF16),
            pltpu.VMEM((2, model, span), BF16),
            pltpu.VMEM((2, span, model), BF16),
            pltpu.VMEM((count, model), BF16),
            pltpu.VMEM((count, model), BF16),
            DMA((4, 2)),
            DMA((2,)),
        ],
        lambda here, *refs: FeedBack(here, *refs, time),
    )


def attend_back(number, saved, grad_mixed, grad_mixed_t, weights, mask, apart, more, box):
    queries, kv, output, lse, _ = saved
    causal, starts, segments = mask
    ring = lax.axis_size("seq")
    count, width = queries.shape
    model = weights.shape[0]
    part = count // 2
    shapes = [
        jax.ShapeDtypeStruct((count, width), BF16),
        jax.ShapeDtypeStruct(kv.shape, BF16),
        jax.ShapeDtypeStruct((count, model), BF16),
    ]
    scratch = backward_scratch(count, width) + [
        pltpu.VMEM((2, count, model), BF16),
        *[pltpu.VMEM((ring, part, model), BF16)] * 2,
        pltpu.VMEM((ring + 1, part, model), BF16),
        pltpu.VMEM((part, model), F32),
        *[DMA((ring,))] * 3,
        DMA((2, ring)),
        *[DMA] * 2,
    ]
    if apart:
        shapes.append(jax.ShapeDtypeStruct((count, model), F32))
        scratch += [pltpu.VMEM((count, model), BF16)] * 2 + [DMA((2,))]
    main = Part(
        (starts, segments, queries, kv, grad_mixed, grad_mixed_t, output, lse, weights),
        [SCALARS] + [VECTORS] * 8,
        shapes,
        scratch,
        lambda here, *refs: box.setdefault("back", Back(here, causal, apart, *refs)),
    )

    def body(here, back, *bound):
        def event(time):
            for one in bound:
                one.event(time)

        back.run(event)

    return run_parts(number, body, [main] + list(more), cost_of(kv, count, width, 7))


class Plan:
    def __init__(self, kernels):
        self.kernels = kernels

    def chains(self, wanted):
        return [chain(*one) for one in wanted] if self.kernels else []

    def given(self, wanted, results):
        return results if self.kernels else [one[0] for one in wanted]


class Places:
    def __init__(self, pairs, ring):
        self.pairs, self.ring = pairs, ring
        self.d = lax.axis_index("dp")
        self.x, self.core = self.d // 2, self.d % 2
        self.y, self.z = lax.axis_index("tensor"), lax.axis_index("seq")

    def swap_core(self, value):
        return lax.ppermute(value, "dp", [(i, i ^ 1) for i in range(self.pairs)])

    def swap_y(self, value):
        return lax.ppermute(value, "tensor", [(0, 1), (1, 0)])

    def swap_x(self, value, bit):
        return lax.ppermute(value, "dp", [(i, i ^ (2 << bit)) for i in range(self.pairs)])

    def swap_z(self, value, bit):
        return lax.ppermute(value, "seq", [(i, i ^ (1 << bit)) for i in range(self.ring)])

    def from_z(self, value, step):
        return lax.ppermute(value, "seq", [((i + step) % self.ring, i) for i in range(self.ring)])

    def to_z(self, value, step):
        return lax.ppermute(value, "seq", [(i, (i + step) % self.ring) for i in range(self.ring)])

    def permute(self, value, source_of):
        moves = []
        for d in range(self.pairs):
            for y in range(2):
                source = source_of(d, y)
                if source is not None:
                    moves.append((source[0] * 2 + source[1], d * 2 + y))
        return lax.ppermute(value, ("dp", "tensor"), moves)

    def fetch_weight(self, value):
        return self.permute(value, lambda d, y: (d + 1, y) if d % 2 == 0 else (d - 1, 1 - y))

    def core_sum(self, partial):
        low = rounded(partial)
        return low + self.swap_core(low.astype(BF16)).astype(F32)

    def own_pair(self, rows):
        return jnp.where(self.core == self.y, rows, self.swap_core(rows))

    def others(self, rows):
        return self.permute(rows, lambda d, y: (d, 1 - y) if d % 2 != y else None)

    def plan(self):
        return Plan(self.pairs == 4 and self.ring == 4)

    def scatter(self, grad, x_first):
        rows, columns = grad.shape
        owners = self.pairs // 2
        grad = grad.reshape(owners, 2, self.ring, rows // (self.pairs * self.ring), columns)
        for stage in "xyz" if x_first else "yxz":
            if stage == "y":
                kept = lax.dynamic_index_in_dim(grad, self.core, grad.ndim - 4, False)
                sent = lax.dynamic_index_in_dim(grad, 1 - self.core, grad.ndim - 4, False)
                first = self.permute(
                    sent, lambda d, y: (d + 1, 1 - y) if d % 2 == 0 else (d - 1, y)
                )
                second = self.permute(kept, lambda d, y: (d, 1 - y) if d % 2 else None)
                kept = jnp.where(self.core == 0, kept, second)
                grad = (kept.astype(F32) + first.astype(F32)).astype(BF16)
            else:
                axis = 0 if stage == "x" else grad.ndim - 3
                place, swap = (self.x, self.swap_x) if stage == "x" else (self.z, self.swap_z)
                size, bit = grad.shape[axis], 0
                while size > 1:
                    shape = grad.shape[:axis] + (size // 2, 2) + grad.shape[axis + 1 :]
                    grad = grad.reshape(shape)
                    mine = (place >> bit) & 1
                    kept = lax.dynamic_index_in_dim(grad, mine, axis + 1, False)
                    sent = lax.dynamic_index_in_dim(grad, 1 - mine, axis + 1, False)
                    grad = kept.astype(F32) + swap(sent, bit).astype(F32)
                    size, bit = size // 2, bit + 1
                    if stage == "x" or size > 1:
                        grad = grad.astype(BF16)
                grad = lax.squeeze(grad, (axis,))
        return grad.astype(F32)

    def all_sum(self, whole, halves):
        both = jnp.concatenate([whole, halves])
        for bit in range((self.pairs // 2).bit_length() - 1):
            both = both + self.swap_x(both, bit)
        for bit in range(self.ring.bit_length() - 1):
            both = both + self.swap_z(both, bit)
        whole, halves = both[: whole.shape[0]], both[whole.shape[0] :]
        whole = whole + self.swap_y(whole)
        whole = (whole + self.swap_core(whole)) * 0.5
        first = self.permute(halves, lambda d, y: (d + 1, 1 - y) if d % 2 == 0 else (d - 1, y))
        second = self.swap_y(halves)
        halves = jnp.where(self.core == 0, halves, second) + first
        return whole, halves


def starts_of(segments):
    numbers = jnp.arange(8, dtype=jnp.int32)
    return jnp.sum(segments[None, :] < numbers[:, None], axis=1, dtype=jnp.int32)


def mask_of(query_seg, key_starts, first_row, causal):
    ends = jnp.stack([query_seg[0], query_seg[-1], first_row])
    return (causal, key_starts, ends, query_seg[None])


def projected(query_in, key_in, weights, bias):
    width = bias.shape[1] // 3
    queries = (dot_plain(query_in, weights[:, :width]) + bias[:, :width]).astype(BF16)
    kv = (dot_plain(key_in, weights[:, width:]) + bias[:, width:]).astype(BF16)
    return (queries * HEAD_DIM ** (-0.5)).astype(BF16), kv


def attention_output(place, queries, kv, output, lse, out_weight, out_bias):
    mixed = output.astype(BF16)
    branch = place.core_sum(dot_first(mixed, out_weight)) + out_bias.astype(F32)
    return (branch, (queries, kv, output, lse, mixed))


def attention_backward(
    number,
    grad_branch,
    saved,
    query_in,
    key_in,
    weights,
    out_weight,
    mask,
    apart,
    plan,
    wanted,
    inside=(),
    begins=False,
):
    mixed = saved[4]
    grad_mixed = dot_last(grad_branch, out_weight).astype(BF16)
    grad_mixed_t = dot_last(out_weight, grad_branch).astype(BF16)
    box = {}
    more = []
    if plan.kernels:
        made = products(box, query_in, key_in, grad_branch, mixed, 5, begins)
        more = [*made, *plan.chains(wanted), *inside]
    (grad_q, grad_kv, *sums), *rest = attend_back(
        number, saved, grad_mixed, grad_mixed_t, weights, mask, apart, more, box
    )
    if plan.kernels:
        (grad_bias, *grads), *rest = rest
        if begins:
            grads, rest = [first[0] for first in rest[:3]], rest[3:]
    else:
        grads = (
            dot_first(query_in, grad_q).astype(BF16),
            dot_first(grad_branch, mixed.T).astype(BF16),
            dot_first(key_in, grad_kv).astype(BF16),
        )
        grad_bias = jnp.stack([column_sum(grad_q), column_sum(grad_kv[:, grad_q.shape[1] :])])
    given = [results[0] for results in rest[: len(rest) - len(inside)]]
    rest = rest[len(rest) - len(inside) :]
    return (sums, grads, grad_bias.reshape(-1), plan.given(wanted, given), rest)


def feed_forward(place, x_in, w_in, b_in, w_out, b_out):
    hidden = dot_plain(x_in, w_in) + b_in.astype(F32)
    spread = 0.5 * (1.0 + lax.erf(hidden * 0.5**0.5))
    active = (hidden * spread).astype(BF16)
    slope = spread + hidden * jnp.exp(-0.5 * hidden * hidden) * (2.0 * math.pi) ** (-0.5)
    branch = place.core_sum(dot_plain(active, w_out)) + b_out.astype(F32)
    return (branch, (slope, active))


def feed_backward(place, grad_branch, saved, x_in, w_in, w_out):
    slope, active = saved
    grad_hidden = (slope * dot_last(grad_branch, w_out)).astype(BF16)
    grad_in = place.core_sum(dot_last(grad_hidden, w_in))
    return (
        grad_in,
        dot_first(x_in, grad_hidden).astype(BF16),
        column_sum(grad_hidden),
        dot_first(grad_branch, active).astype(BF16),
    )


def shards(
    source,
    target,
    source_segments,
    target_segments,
    enc_qkv,
    enc_qv_bias,
    enc_proj,
    enc_ff_in,
    enc_ff_in_bias,
    enc_ff_out,
    enc_bias,
    enc_gains,
    enc_shifts,
    dec_self,
    dec_self_bias,
    dec_self_proj,
    dec_cross,
    dec_cross_bias,
    dec_cross_proj,
    dec_ff_in,
    dec_ff_in_bias,
    dec_ff_out,
    dec_bias,
    dec_gains,
    dec_shifts,
    enc_cotangent,
    dec_cotangent,
):
    count = source.shape[1]
    model = source.shape[2]
    place = Places(lax.axis_size("dp"), lax.axis_size("seq"))
    first_row = place.z * count

    ring = place.ring
    width = enc_qkv.shape[2]
    hidden_units = enc_ff_in.shape[1]

    x_all, ts, source_keys, target_keys, vectors, enc_qkv, enc_proj, dec_self = opening(
        ring,
        source[0],
        target[0],
        source_segments,
        target_segments,
        (
            enc_qv_bias,
            dec_self_bias,
            dec_cross_bias,
            enc_ff_in_bias,
            dec_ff_in_bias,
        ),
        (enc_qkv, enc_proj, dec_self),
    )
    source_keys, target_keys = source_keys[0], target_keys[0]
    xs = lax.dynamic_slice_in_dim(x_all, first_row, count, 0)
    enc_cot = place.own_pair(enc_cotangent[0])
    dec_cot = place.own_pair(dec_cotangent[0])
    enc_b, self_b, cross_b = (vectors[k : k + 1, : 3 * width] for k in range(3))
    enc_ff_in_bias, dec_ff_in_bias = vectors[3], vectors[4]
    source_own = lax.dynamic_slice_in_dim(source_keys, first_row, count, 0)
    target_own = lax.dynamic_slice_in_dim(target_keys, first_row, count, 0)
    source_starts, target_starts = starts_of(source_keys), starts_of(target_keys)
    enc_mask = mask_of(source_own, source_starts, first_row, False)
    self_mask = mask_of(target_own, target_starts, first_row, True)
    cross_mask = mask_of(target_own, source_starts, first_row, False)

    queries, kv, output, lse, t_all, enc_ff_in, enc_ff_out = gather_attend(
        7, ring, x_all, enc_qkv, enc_b, enc_mask, ts, (enc_ff_in, enc_ff_out)
    )
    dec_ff_in = place.fetch_weight(dec_ff_in + after(lse).astype(BF16))
    branch, enc_attn = attention_output(place, queries, kv, output, lse, enc_proj, enc_bias[0])
    first, enc_norm_one = norm_forward(xs.astype(F32) + branch, enc_gains[0], enc_shifts[0])
    first_low = first.astype(BF16)
    branch, enc_feed = feed_forward(
        place, first_low, enc_ff_in, enc_ff_in_bias, enc_ff_out, enc_bias[1]
    )
    encoded, enc_norm_two = norm_forward(first + branch, enc_gains[1], enc_shifts[1])
    encoded_low = encoded.astype(BF16)

    (
        queries,
        kv,
        output,
        lse,
        e_all,
        dec_self_proj,
        dec_cross,
        dec_cross_proj,
    ) = gather_attend(
        2,
        ring,
        t_all,
        dec_self,
        self_b,
        self_mask,
        encoded_low,
        (dec_self_proj, dec_cross, dec_cross_proj),
    )
    dec_ff_out = place.fetch_weight(dec_ff_out + after(lse).astype(BF16))
    branch, self_attn = attention_output(
        place, queries, kv, output, lse, dec_self_proj, dec_bias[0]
    )
    second, dec_norm_one = norm_forward(ts.astype(F32) + branch, dec_gains[0], dec_shifts[0])
    second_low = second.astype(BF16)
    queries, kv = projected(second_low, e_all, dec_cross, cross_b)
    output, lse = attend(queries, kv, cross_mask, (dec_ff_in,))
    branch, cross_attn = attention_output(
        place, queries, kv, output, lse, dec_cross_proj, dec_bias[1]
    )
    third, dec_norm_two = norm_forward(second + branch, dec_gains[1], dec_shifts[1])
    third_low = third.astype(BF16)
    branch, dec_feed = feed_forward(
        place, third_low, dec_ff_in, dec_ff_in_bias, dec_ff_out, dec_bias[2]
    )
    decoded, dec_norm_three = norm_forward(third + branch, dec_gains[2], dec_shifts[2])

    def back_mask(mask):
        return (mask[0], mask[1], mask[3])

    grad_hidden, dec_gain_three, dec_shift_three = norm_backward(
        dec_cot.astype(F32), dec_norm_three, dec_gains[2]
    )
    grad_branch = grad_hidden.astype(BF16)
    feed_in, dec_w_in, dec_b_in, dec_w_out = feed_backward(
        place, grad_branch, dec_feed, third_low, dec_ff_in, dec_ff_out
    )
    dec_bias_three = column_sum(grad_branch)
    grad_third = grad_hidden + feed_in
    grad_hidden, dec_gain_two, dec_shift_two = norm_backward(grad_third, dec_norm_two, dec_gains[1])
    grad_branch = grad_hidden.astype(BF16)
    plan = place.plan()
    (key_total, query_total), cross_grads, cross_bias, (dec_w_in, dec_w_out), _ = attention_backward(
        3,
        grad_branch,
        cross_attn,
        second_low,
        e_all,
        dec_cross,
        dec_cross_proj,
        back_mask(cross_mask),
        True,
        plan,
        [(dec_w_in, "x", (0, 6)), (dec_w_out, "y", (0, 6))],
    )
    dec_bias_two = column_sum(grad_branch)
    grad_second = grad_hidden + query_total
    grad_hidden, dec_gain_one, dec_shift_one = norm_backward(
        grad_second, dec_norm_one, dec_gains[0]
    )
    grad_branch = grad_hidden.astype(BF16)
    cross_q, cross_proj, cross_kv = cross_grads
    target_hidden, target_branch = grad_hidden, grad_branch
    grad_hidden, enc_gain_two, enc_shift_two = norm_backward(
        enc_cot.astype(F32) + key_total.astype(F32), enc_norm_two, enc_gains[1]
    )
    grad_branch = grad_hidden.astype(BF16)
    enc_bias_two = column_sum(grad_branch)
    slope, active = enc_feed
    (target_total,), self_grads, self_bias, given, inside = attention_backward(
        4,
        target_branch,
        self_attn,
        ts,
        t_all,
        dec_self,
        dec_self_proj,
        back_mask(self_mask),
        False,
        plan,
            [
                (dec_w_in, "yvw", (0, 3, 5, 6)),
                (dec_w_out, "xvw", (0, 3, 5, 6)),
                (cross_kv, "x", (3, 6)),
                (cross_q, "y", (3, 6)),
                (cross_proj, "y", (3, 6)),
            ],
        [feed_back(grad_branch, slope, enc_ff_in, enc_ff_out, first_low, active, 5)]
        if plan.kernels
        else (),
        begins=True,
    )
    dec_w_in, dec_w_out, cross_kv, cross_q, cross_proj = given
    if plan.kernels:
        feed_in, enc_b_in, enc_w_in, enc_w_out = inside[0]
        enc_b_in = enc_b_in.reshape(-1)
    else:
        feed_in, enc_w_in, enc_b_in, enc_w_out = feed_backward(
            place, grad_branch, enc_feed, first_low, enc_ff_in, enc_ff_out
        )
    dec_bias_one = column_sum(target_branch)
    grad_target = target_hidden + target_total.astype(F32)
    grad_first = grad_hidden + feed_in
    grad_hidden, enc_gain_one, enc_shift_one = norm_backward(grad_first, enc_norm_one, enc_gains[0])
    grad_branch = grad_hidden.astype(BF16)
    self_q, self_proj, self_kv = self_grads
    (source_total,), enc_grads, enc_bias_grad, given, _ = attention_backward(
        5,
        grad_branch,
        enc_attn,
        xs,
        x_all,
        enc_qkv,
        enc_proj,
        back_mask(enc_mask),
        False,
        plan,
            [
                (cross_kv, "yvw", (0, 1, 3, 6)),
                (cross_q, "xvw", (0, 1, 3, 6)),
                (cross_proj, "xvw", (0, 1, 3, 6)),
                (enc_w_in, "x", (1, 6)),
                (enc_w_out, "y", (1, 6)),
                (self_kv, "y", (4, 6)),
                (self_q, "x", (4, 6)),
                (self_proj, "x", (4, 6)),
            ],
    )
    cross_kv, cross_q, cross_proj, enc_w_in, enc_w_out, self_kv, self_q, self_proj = given
    enc_bias_one = column_sum(grad_branch)
    grad_source = grad_hidden + source_total.astype(F32)
    enc_q, enc_proj_grad, enc_kv = enc_grads
    rest = [
        (self_kv, "vw", (0, 1, 2)),
        (self_q, "vw", (0, 1, 2)),
        (self_proj, "vw", (0, 1, 2)),
        (enc_w_in, "yvw", (0, 2, 4, 7)),
        (enc_w_out, "xvw", (0, 2, 4, 7)),
        (enc_kv, "xyvw", (2, 3, 5, 6, 7)),
        (enc_q, "yxvw", (2, 3, 5, 6, 7)),
        (enc_proj_grad, "yxvw", (2, 3, 5, 6, 7)),
    ]
    source_low = rounded(grad_source).astype(BF16)
    target_low = rounded(grad_target).astype(BF16)
    decoded_low = decoded.astype(BF16)
    small = small_sums(
        jnp.concatenate(
            [
                enc_bias_one,
                enc_bias_two,
                enc_gain_one,
                enc_gain_two,
                enc_shift_one,
                enc_shift_two,
                dec_bias_one,
                dec_bias_two,
                dec_bias_three,
                dec_gain_one,
                dec_gain_two,
                dec_gain_three,
                dec_shift_one,
                dec_shift_two,
                dec_shift_three,
            ]
        ).reshape(15, model),
        jnp.concatenate([enc_bias_grad, self_bias, cross_bias, enc_b_in, dec_b_in]).reshape(-1, model),
        (0, 1, 2, 3, 4, 5),
    )
    if plan.kernels:
        (vectors,), (source_other, target_other), *given = run_chains(
            6, [small, hand_out((source_low, target_low), (4, 7))] + plan.chains(rest), 8
        )
        given = [results[0] for results in given]
    else:
        vectors = jnp.concatenate(place.all_sum(*small.vectors)).reshape(-1, model)
        source_other, target_other = place.others(source_low), place.others(target_low)
        given = [place.scatter(array, True) for array, _, _ in rest]
        dec_w_in, dec_w_out, cross_kv, cross_q, cross_proj = (
            place.scatter(array, True)
            for array in (dec_w_in, dec_w_out, cross_kv, cross_q, cross_proj)
        )
    self_kv, self_q, self_proj, enc_w_in, enc_w_out, enc_kv, enc_q, enc_proj_grad = given

    grads = (enc_q, enc_proj_grad, enc_kv, self_q, self_proj, self_kv, cross_q, cross_proj, cross_kv)
    grads += (enc_w_in, enc_w_out, dec_w_in, dec_w_out)
    flag = jnp.where(place.core == place.y, 1, 0).astype(jnp.int32).reshape(1)
    rows = (
        encoded_low,
        place.others(encoded_low),
        decoded_low,
        place.others(decoded_low),
        source_low,
        source_other,
        target_low,
        target_other,
    )
    results = closing(flag, rows, vectors, grads, (2, 2, 2, 3, 3, 3))
    of_rows, of_qkv, of_in = [value[None] for value in results[:4]], results[4:7], results[7:9]
    of_out, of_ff_out = [value.T for value in results[9:12]], [value.T for value in results[12:14]]
    of_whole, of_qv_bias, of_in_bias = results[14:20], results[20:23], results[23:]
    return (
        *of_rows,
        of_qkv[0],
        of_qv_bias[0],
        of_out[0],
        of_in[0],
        of_in_bias[0],
        of_ff_out[0],
        *of_whole[:3],
        of_qkv[1],
        of_qv_bias[1],
        of_out[1],
        of_qkv[2],
        of_qv_bias[2],
        of_out[2],
        of_in[1],
        of_in_bias[1],
        of_ff_out[1],
        *of_whole[3:],
    )


def solution(mesh):
    return jax.shard_map(
        shards,
        mesh=mesh,
        in_specs=(
            P("dp", "seq", None),
            P("dp", "seq", None),
            P("dp", None),
            P("dp", None),
            P(None, None, "tensor"),
            P(None, "tensor"),
            P("tensor", None),
            P(None, "tensor"),
            P("tensor"),
            P("tensor", None),
            P(),
            P(),
            P(),
            P(None, None, "tensor"),
            P(None, "tensor"),
            P("tensor", None),
            P(None, None, "tensor"),
            P(None, "tensor"),
            P("tensor", None),
            P(None, "tensor"),
            P("tensor"),
            P("tensor", None),
            P(),
            P(),
            P(),
            P("dp", "seq", None),
            P("dp", "seq", None),
        ),
        out_specs=(
            P("dp", "seq", None),
            P("dp", "seq", None),
            P("dp", "seq", None),
            P("dp", "seq", None),
            P(None, ("dp", "seq"), "tensor"),
            P(None, "tensor"),
            P("tensor", ("dp", "seq")),
            P(("dp", "seq"), "tensor"),
            P("tensor"),
            P("tensor", ("dp", "seq")),
            P(),
            P(),
            P(),
            P(None, ("dp", "seq"), "tensor"),
            P(None, "tensor"),
            P("tensor", ("dp", "seq")),
            P(None, ("dp", "seq"), "tensor"),
            P(None, "tensor"),
            P("tensor", ("dp", "seq")),
            P(("dp", "seq"), "tensor"),
            P("tensor"),
            P("tensor", ("dp", "seq")),
            P(),
            P(),
            P(),
        ),
        check_vma=False,
    )
```

```python
import functools
import math

import jax
import jax.numpy as jnp
from jax import lax
from jax.experimental import pallas as pl
from jax.experimental.pallas import tpu as pltpu
from jax.sharding import PartitionSpec as P

HEAD_DIM = 64
EPS = 1e-05
NEG = -1e30
BF16 = jnp.bfloat16
F32 = jnp.float32
NT = (((1,), (1,)), ((), ()))
TN = (((0,), (0,)), ((), ()))
KEY_BLOCK = 512
CHUNKS = 2
DOCS = 4


def dot_plain(left, right):
    return jnp.dot(left, right, preferred_element_type=F32)


def dot_last(left, right):
    return lax.dot_general(left, right, NT, preferred_element_type=F32)


def dot_first(left, right):
    return lax.dot_general(left, right, TN, preferred_element_type=F32)


def column_sum(value):
    return jnp.sum(value.astype(F32), axis=0)


def rounded(value):
    return lax.reduce_precision(value, 8, 7)


def after(array):
    return jnp.minimum(jnp.abs(array[0, 0].astype(F32)), 0.0)


def norm_forward(hidden, gain, shift):
    centered = hidden - jnp.mean(hidden, axis=-1, keepdims=True)
    spread = jnp.mean(centered * centered, axis=-1, keepdims=True)
    factor = lax.rsqrt(spread + EPS)
    normed = centered * factor
    return (normed * gain.astype(F32) + shift.astype(F32), (normed, factor))


def norm_backward(grad, saved, gain):
    normed, factor = saved
    scaled = grad * gain.astype(F32)
    centered = scaled - jnp.mean(scaled, axis=-1, keepdims=True)
    grad_hidden = factor * (centered - normed * jnp.mean(scaled * normed, axis=-1, keepdims=True))
    return (grad_hidden, jnp.sum(grad * normed, axis=0), jnp.sum(grad, axis=0))


def head_columns(head):
    return slice(head // 2 * 128, head // 2 * 128 + 128)


def head_rows(head):
    return slice(head * HEAD_DIM, (head + 1) * HEAD_DIM)


def own_lanes(shape, head):
    lanes = lax.broadcasted_iota(jnp.int32, shape, 1)
    return lanes >= HEAD_DIM if head % 2 else lanes < HEAD_DIM


class Mask:
    def __init__(self, causal, starts, segments, first_row):
        self.causal, self.starts, self.first_row = causal, starts, first_row
        segments = segments[...]
        low = high = jnp.zeros_like(segments)
        for number in range(DOCS):
            low = jnp.where(segments == number, starts[number], low)
            high = jnp.where(segments == number, starts[number + 1], high)
        self.count = segments.shape[1]
        if causal:
            place = first_row + lax.broadcasted_iota(jnp.int32, segments.shape, 1)
            high = jnp.minimum(high, place + 1)
        self.low, self.high = low, high

    def allowed(self, index, block):
        place = lax.broadcasted_iota(jnp.int32, (block, self.count), 0) + index * block
        return (place >= self.low) & (place < self.high)

    def flag(self, index, block, ends):
        start, stop = index * block, (index + 1) * block
        low, low_last = self.starts[ends[0]], self.starts[ends[1]]
        high_first, high = self.starts[ends[0] + 1], self.starts[ends[1] + 1]
        if self.causal:
            high = jnp.minimum(high, self.first_row + self.count)
            high_first = jnp.minimum(high_first, self.first_row + 1)
        active = (low < stop) & (high > start)
        full = (low_last <= start) & (high_first >= stop)
        return jnp.where(active, jnp.where(full, 2, 1), 0)


def over_blocks(mask, ends, length, block, body, skipped):
    @pl.loop(0, length // block)
    def _(index):
        flag = mask.flag(index, block, ends)
        rows = pl.ds(pl.multiple_of(index * block, block), block)

        @pl.when(flag == 0)
        def _():
            skipped(rows)

        @pl.when(flag == 1)
        def _():
            body(index, rows, True)

        @pl.when(flag == 2)
        def _():
            body(index, rows, False)


def forward_start(q_ref, masked_q, acc, top):
    heads = q_ref.shape[1] // HEAD_DIM
    for head in range(heads):
        pair = q_ref[:, head_columns(head)]
        masked_q[head] = jnp.where(own_lanes(pair.shape, head), pair, jnp.zeros_like(pair))
    acc[...] = jnp.zeros_like(acc)
    top[...] = jnp.full_like(top, NEG)


def forward_block(index, rows, partial, block, kv_ref, mask, masked_q, acc, top):
    heads, count = masked_q.shape[:2]
    width = heads * HEAD_DIM
    if partial:
        allowed = mask.allowed(index, block)
    for head in range(heads):
        cols = head_columns(head)
        scores = lax.dot_general(kv_ref[rows, cols], masked_q[head], NT, preferred_element_type=F32)
        if partial:
            scores = jnp.where(allowed, scores, NEG)
        old = top[head : head + 1, :]
        new = jnp.maximum(old, jnp.max(scores, axis=0, keepdims=True))
        weights = jnp.exp(scores - new).astype(BF16)
        vals = kv_ref[rows, width + cols.start : width + cols.stop]
        vals = jnp.where(own_lanes(vals.shape, head), vals, jnp.ones_like(vals))
        acc[head] = acc[head] * jnp.exp(old - new) + lax.dot_general(
            vals, weights, TN, preferred_element_type=F32
        )
        top[head : head + 1, :] = new


def forward_end(out_ref, lse_ref, acc, top):
    lse_ref[...] = jnp.zeros_like(lse_ref)
    for head in range(acc.shape[0]):
        first = head % 2 * HEAD_DIM
        total = acc[head, HEAD_DIM - first : HEAD_DIM - first + 1, :]
        out_ref[head_rows(head), :] = acc[head, first : first + HEAD_DIM, :] / total
        lse_ref[head : head + 1, :] = top[head : head + 1, :] + jnp.log(total)


def forward_kernel(block, causal, tokens, starts, ends, segments, q_ref, kv_ref, *refs):
    out_ref, lse_ref, masked_q, acc, top = refs[tokens:]
    mask = Mask(causal, starts, segments, ends[2])
    forward_start(q_ref, masked_q, acc, top)

    def body(index, rows, partial):
        forward_block(index, rows, partial, block, kv_ref, mask, masked_q, acc, top)

    over_blocks(mask, ends, kv_ref.shape[0], block, body, lambda rows: None)
    forward_end(out_ref, lse_ref, acc, top)


def backward_start(q_ref, do_ref, dot_ref, out_ref, masked_q, masked_do, delta, dq):
    for head in range(masked_q.shape[0]):
        pair = q_ref[:, head_columns(head)]
        keep = own_lanes(pair.shape, head)
        masked_q[head] = jnp.where(keep, pair, jnp.zeros_like(pair))
        pair = do_ref[:, head_columns(head)]
        masked_do[head] = jnp.where(keep, pair, jnp.zeros_like(pair))
        part = head_rows(head)
        delta[head : head + 1, :] = jnp.sum(
            dot_ref[part, :].astype(F32) * out_ref[part, :], axis=0, keepdims=True
        )
    dq[...] = jnp.zeros_like(dq)


def backward_block(
    index, rows, block, mask, kv_ref, lse_ref, dkv_ref, masked_q, masked_do, delta, dq, between
):
    heads = masked_q.shape[0]
    width = heads * HEAD_DIM
    allowed = mask.allowed(index, block)
    for pair in range(heads // 2):
        if pair == 1:
            between()
        cols = head_columns(2 * pair)
        later = slice(width + cols.start, width + cols.stop)
        keys, vals = kv_ref[rows, cols], kv_ref[rows, later]
        dk = dv = 0.0
        for head in (2 * pair, 2 * pair + 1):
            scores = lax.dot_general(keys, masked_q[head], NT, preferred_element_type=F32)
            probs = jnp.exp(scores - lse_ref[head : head + 1, :])
            probs = jnp.where(allowed, probs, 0.0)
            dprobs = lax.dot_general(vals, masked_do[head], NT, preferred_element_type=F32)
            draw = (probs * (dprobs - delta[head : head + 1, :])).astype(BF16)
            probs = probs.astype(BF16)
            dv = dv + jnp.dot(probs, masked_do[head], preferred_element_type=F32)
            dk = dk + jnp.dot(draw, masked_q[head], preferred_element_type=F32)
            first = head % 2 * HEAD_DIM
            both = lax.dot_general(keys, draw, TN, preferred_element_type=F32)
            dq[head_rows(head), :] += both[first : first + HEAD_DIM]
        dkv_ref[rows, cols] = dk.astype(BF16)
        dkv_ref[rows, later] = dv.astype(BF16)


SCALARS = pl.BlockSpec(memory_space=pltpu.SMEM)
VECTORS = pl.BlockSpec(memory_space=pltpu.VMEM)


ANYWHERE = pl.BlockSpec(memory_space=pl.ANY)


def cost_of(kv, count, width, products):
    flops = 2 * products * kv.shape[0] * count * width
    return pl.CostEstimate(flops=flops, bytes_accessed=flops // 512, transcendentals=0)


def forward_scratch(count, width):
    heads = width // HEAD_DIM
    return [
        pltpu.VMEM((heads, count, 128), BF16),
        pltpu.VMEM((heads, 128, count), F32),
        pltpu.VMEM((8, count), F32),
    ]


def backward_scratch(count, width):
    heads = width // HEAD_DIM
    return [
        pltpu.VMEM((heads, count, 128), BF16),
        pltpu.VMEM((heads, count, 128), BF16),
        pltpu.VMEM((8, count), F32),
        pltpu.VMEM((width, count), F32),
    ]


def attend(queries, kv, mask, tokens):
    count, width = queries.shape
    causal, starts, ends, segments = mask
    return pl.pallas_call(
        functools.partial(forward_kernel, KEY_BLOCK, causal, len(tokens)),
        out_shape=(
            jax.ShapeDtypeStruct((width, count), F32),
            jax.ShapeDtypeStruct((8, count), F32),
        ),
        in_specs=[SCALARS] * 2 + [VECTORS] * 3 + [ANYWHERE] * len(tokens),
        out_specs=(VECTORS,) * 2,
        scratch_shapes=forward_scratch(count, width),
        compiler_params=pltpu.CompilerParams(vmem_limit_bytes=40 << 20),
        cost_estimate=cost_of(kv, count, width, 2),
    )(starts, ends, segments, queries, kv, *tokens)


MESH = pl.DeviceIdType.MESH
DMA = pltpu.SemaphoreType.DMA


class Here:
    def __init__(self, ring):
        self.ring = ring
        self.d, self.z, self.y = (lax.axis_index(a) for a in ("dp", "seq", "tensor"))
        self.core, self.x = lax.rem(self.d, 2), lax.div(self.d, 2)
        self.other_d = self.d + 1 - 2 * self.core
        self.partner = (self.other_d, self.z, self.y)
        self.right = (self.d, self.z + 1, self.y)
        self.left = (self.d, self.z - 1, self.y)
        self.over_x = (self.d + 2 - 4 * lax.rem(self.x, 2), self.z, self.y)
        self.over_y = (self.d, self.z, 1 - self.y)
        self.diagonal = (self.other_d, self.z, 1 - self.y)

    def meet(self, devices):
        barrier = pltpu.get_barrier_semaphore()
        wanted = 0
        for condition, device in devices:

            @pl.when(condition)
            def _(device=device):
                pl.semaphore_signal(barrier, inc=1, device_id=device, device_id_type=MESH)

            wanted = wanted + jnp.where(condition, 1, 0)
        pl.semaphore_wait(barrier, wanted)

    def along_z(self, step):
        return (self.d, lax.rem(self.z + step, self.ring), self.y)

    def everyone(self):
        devices = [self.partner, self.over_x, self.over_y, self.diagonal]
        devices += [self.along_z(step) for step in range(1, self.ring)]
        return [(self.core >= 0, device) for device in devices]

    def crosswise(self):
        return [
            (self.z + 1 < self.ring, (self.other_d, self.z + 1, self.y)),
            (self.z > 0, (self.other_d, self.z - 1, self.y)),
        ]

    def neighbours(self):
        return [
            (self.core >= 0, self.partner),
            (self.z + 1 < self.ring, self.right),
            (self.z > 0, self.left),
        ]


def remote(source, target, sent, received, device):
    return pltpu.make_async_remote_copy(
        src_ref=source,
        dst_ref=target,
        send_sem=sent,
        recv_sem=received,
        device_id=device,
        device_id_type=MESH,
    )


class Gather:
    def __init__(self, here, rows_ref, sems, source=None, owner=None):
        self.here, self.rows_ref, self.source, self.owner = here, rows_ref, source, owner
        self.count = rows_ref.shape[0] // here.ring
        self.size = self.count // (2 * CHUNKS)
        self.sent, self.got, self.core_sent, self.core_got = sems

    def chunk(self, shard, core, chunk):
        start = shard * self.count + core * (self.count // 2) + chunk * self.size
        return self.rows_ref.at[pl.ds(pl.multiple_of(start, self.size), self.size)]

    def ways(self, step):
        here = self.here
        z, ring = here.z, here.ring
        return [
            (0, z - step, z >= step, z - step + 1, (z + 1 < ring) & (z + 1 >= step), here.right),
            (1, z + step, z + step < ring, z + step - 1, (z > 0) & (z + step <= ring), here.left),
        ]

    def along(self, way, step, shard, chunk, device):
        view = self.chunk(shard, self.here.core, chunk)
        k = way * CHUNKS + chunk
        return remote(view, view, self.sent.at[k, step], self.got.at[k, step], device)

    def across(self, way, step, shard, core, chunk):
        view = self.chunk(shard, core, chunk)
        k = way * CHUNKS + chunk
        return remote(
            view, view, self.core_sent.at[k, step], self.core_got.at[k, step], self.here.partner
        )

    def firsts(self):
        found = []
        for chunk in range(CHUNKS):
            for way, _, _, shard, sends, device in self.ways(1):
                if self.source is None:
                    found.append((sends, self.along(way, 1, shard, chunk, device)))
                    continue
                for core in range(2):
                    k = way * CHUNKS + chunk
                    start = core * (self.count // 2) + chunk * self.size
                    to = (self.here.d - self.here.core + core, *device[1:])
                    copy = remote(
                        self.source.at[pl.ds(start, self.size)],
                        self.chunk(shard, core, chunk),
                        self.sent.at[k, core],
                        self.got.at[k, 1],
                        to,
                    )
                    found.append((sends & self.owner, copy))
        return found

    def begin(self):
        for condition, copy in self.firsts():
            pl.when(condition)(copy.start)

    def advance(self, step):
        for chunk in range(CHUNKS):
            for way, shard, comes, _, _, _ in self.ways(step):

                @pl.when(comes)
                def _(way=way, shard=shard, chunk=chunk):
                    self.along(way, step, shard, chunk, self.here.partner).wait_recv()

                _, _, _, _, sends, device = self.ways(step + 1)[way]

                @pl.when(sends)
                def _(way=way, shard=shard, chunk=chunk, device=device):
                    self.along(way, step + 1, shard, chunk, device).start()

                @pl.when(comes)
                def _(way=way, shard=shard, chunk=chunk):
                    self.across(way, step, shard, self.here.core, chunk).start()

    def finish(self):
        for condition, copy in self.firsts():
            pl.when(condition)(copy.wait_send)

        @pl.loop(1, self.here.ring)
        def _(step):
            for chunk in range(CHUNKS):
                for way, shard, comes, out, sends, device in self.ways(step):

                    @pl.when(sends & (step > 1))
                    def _(way=way, out=out, device=device, chunk=chunk):
                        self.along(way, step, out, chunk, device).wait_send()

                    @pl.when(comes)
                    def _(way=way, shard=shard, chunk=chunk):
                        core = self.here.core
                        self.across(way, step, shard, core, chunk).wait_send()
                        self.across(way, step, shard, 1 - core, chunk).wait_recv()


def pieces_of(weights):
    found = []
    for k, weight in enumerate(weights):
        rows, columns = weight.shape[-2:]
        number = 1 if rows % 3 else 3
        while 2 * rows * columns > 655360 * number and rows % (64 * number) == 0:
            number *= 2
        for matrix in range(matrices_of(weight)):
            found += [(k, matrix, i * (rows // number), rows // number) for i in range(number)]
    return found


def matrices_of(weight):
    return weight.shape[0] if len(weight.shape) == 3 else 1


def beside(weight):
    rows, columns = weight.shape[-2:]
    return jax.ShapeDtypeStruct((rows, columns * matrices_of(weight)), weight.dtype)


AHEAD = 4


class Fetch:
    def __init__(self, here, inputs, outputs, sems):
        self.here, self.inputs, self.outputs = here, inputs, outputs
        self.y_sent, self.y_got, self.x_sent, self.x_got, self.core_sent, self.core_got = sems
        self.pieces = pieces_of(inputs)
        self.matrices = [
            (k, matrix)
            for k, given in enumerate(inputs)
            for matrix in range(matrices_of(given))
        ]
        self.number = len(self.pieces)
        self.own = lax.rem(here.x, 2)

    def devices(self):
        here = self.here
        return [(here.core >= 0, here.diagonal), (here.core == 1, here.over_x)]

    def matrix(self, k, matrix):
        given = self.inputs[k]
        return given.at[matrix] if len(given.shape) == 3 else given

    def part(self, p, which):
        k, matrix, start, rows = self.pieces[p]
        first = pl.multiple_of(start + which * (rows // 2), 16)
        return self.matrix(k, matrix).at[pl.ds(first, rows // 2)]

    def place(self, p, which):
        k, matrix, start, rows = self.pieces[p]
        columns = self.inputs[k].shape[-1]
        first = pl.multiple_of(start + which * (rows // 2), 16)
        return self.outputs[k].at[pl.ds(first, rows // 2), pl.ds(matrix * columns, columns)]

    def over_y(self, p):
        return remote(
            self.part(p, self.own),
            self.place(p, self.own),
            self.y_sent.at[p],
            self.y_got.at[p],
            self.here.diagonal,
        )

    def over_x(self, p, which):
        view = self.place(p, which)
        return remote(view, view, self.x_sent.at[p], self.x_got.at[p], self.here.over_x)

    def across(self, m):
        k, matrix = self.matrices[m]
        columns = self.inputs[k].shape[-1]
        return remote(
            self.matrix(k, matrix),
            self.outputs[k].at[:, pl.ds(matrix * columns, columns)],
            self.core_sent.at[m],
            self.core_got.at[m],
            self.here.partner,
        )

    def begin(self):
        @pl.when(self.here.core == 0)
        def _():
            for p in range(min(AHEAD, self.number)):
                self.over_y(p).start()

        @pl.when(self.here.core == 1)
        def _():
            for m in range(len(self.matrices)):
                self.across(m).start()

    def advance(self, p):
        @pl.when(self.here.core == 0)
        def _():
            self.over_y(p).wait_send()
            if p + AHEAD < self.number:
                self.over_y(p + AHEAD).start()

        @pl.when(self.here.core == 1)
        def _():
            self.over_y(p).wait_recv()
            self.over_x(p, self.own).start()

    def end(self):
        @pl.when(self.here.core == 0)
        def _():
            for m in range(len(self.matrices)):
                self.across(m).wait_recv()

        @pl.when(self.here.core == 1)
        def _():
            for p in range(self.number):
                self.over_x(p, self.own).wait_send()
                self.over_x(p, 1 - self.own).wait_recv()
            for m in range(len(self.matrices)):
                self.across(m).wait_send()


def gather_sems(ring):
    return [DMA((2 * CHUNKS, ring))] * 4


def fetch_sems(weights):
    number = len(pieces_of(weights))
    return [DMA((number,))] * 4 + [DMA((3 * len(weights),))] * 2


def opening_kernel(ring, number, *refs):
    inputs, refs = refs[: 9 + number], refs[9 + number :]
    outputs, (vectors, *sems) = refs[: 5 + number], refs[5 + number :]
    source, target, source_seg, target_seg = inputs[:4]
    source_all, target_out, source_seg_out, target_seg_out, vectors_out = outputs[:5]
    shard_sems, vector_sems = sems[:3], sems[3:6]
    here = Here(ring)
    fetch = Fetch(here, inputs[9:], outputs[5:], sems[10:])
    here.meet(here.neighbours() + here.crosswise() + fetch.devices())
    count = source.shape[0]
    own = pl.ds(pl.multiple_of(here.z * count, count), count)
    moves = [
        (source, source_all.at[own]),
        (target, target_out),
        (source_seg, source_seg_out),
        (target_seg, target_seg_out),
    ]
    owner = here.core == here.y

    def shard_copy(k):
        start, end = moves[k]
        sent, got, copied = shard_sems
        return (
            remote(start, end, sent.at[k], got.at[k], here.partner),
            pltpu.make_async_copy(start, end, copied.at[k]),
        )

    def vector_copy():
        sent, got, copied = vector_sems
        return (
            remote(vectors, vectors_out, sent, got, here.diagonal),
            pltpu.make_async_copy(vectors, vectors_out, copied),
        )

    def wait_shard(k):
        across, local = shard_copy(k)

        @pl.when(owner)
        def _():
            across.wait_send()
            local.wait()

        @pl.when(jnp.logical_not(owner))
        def _():
            across.wait_recv()

    gather = Gather(here, source_all, sems[6:10], source, owner)
    gather.begin()

    @pl.when(owner)
    def _():
        for k in range(len(moves)):
            across, local = shard_copy(k)
            across.start()
            local.start()

    fetch.begin()

    vectors[...] = jnp.zeros_like(vectors)
    for row, bias in enumerate(inputs[4:7]):
        width = bias.shape[1]
        for part in range(2):
            value = bias[part : part + 1, :].astype(F32)
            vectors[row : row + 1, 2 * part * width : (2 * part + 1) * width] = value
    for row, bias in enumerate(inputs[7:9]):
        vectors[3 + row : 4 + row, :] = bias[...].astype(F32).reshape(1, -1)

    @pl.when(here.core == 0)
    def _():
        across, local = vector_copy()
        across.start()
        local.start()

    done = 0
    for step in range(1, ring):
        while done < fetch.number * (2 * step - 1) // (2 * ring - 2):
            fetch.advance(done)
            done += 1
        gather.advance(step)
    while done < fetch.number:
        fetch.advance(done)
        done += 1
    gather.finish()
    for k in range(len(moves)):
        wait_shard(k)
    fetch.end()
    across, local = vector_copy()

    @pl.when(here.core == 0)
    def _():
        across.wait_send()
        local.wait()

    @pl.when(here.core == 1)
    def _():
        across.wait_recv()


def opening(ring, source, target, source_seg, target_seg, biases, weights):
    inputs = (source, target, source_seg, target_seg, *biases, *weights)
    count, model = source.shape
    number = len(weights)
    units = biases[-1].shape[0]
    shapes = (
        jax.ShapeDtypeStruct((ring * count, model), BF16),
        jax.ShapeDtypeStruct(target.shape, BF16),
        jax.ShapeDtypeStruct(source_seg.shape, jnp.int32),
        jax.ShapeDtypeStruct(target_seg.shape, jnp.int32),
        jax.ShapeDtypeStruct((8, units), F32),
    ) + tuple(beside(weight) for weight in weights)
    return pl.pallas_call(
        functools.partial(opening_kernel, ring, number),
        out_shape=shapes,
        in_specs=[VECTORS] * 9 + [ANYWHERE] * number,
        out_specs=(ANYWHERE,) + (VECTORS,) * 4 + (ANYWHERE,) * number,
        scratch_shapes=[pltpu.VMEM((8, units), F32)]
        + [DMA((4,))] * 3
        + [DMA] * 3
        + gather_sems(ring)
        + fetch_sems(weights),
        compiler_params=pltpu.CompilerParams(collective_id=1, has_side_effects=True),
    )(*inputs)


def gather_attend_kernel(
    block, causal, ring, number, tokens, starts, segments, bias_ref, own_ref, rows_ref, proj_ref, *refs
):
    weights, refs = refs[:number], refs[number + tokens :]
    q_ref, kv_ref, out_ref, lse_ref, all_ref = refs[:5]
    fetched, refs = refs[5 : 5 + number], refs[5 + number :]
    masked_q, acc, top, rows_in, proj, copied, rows_copied, proj_copied = refs[:8]
    here = Here(ring)
    gather = Gather(here, all_ref, refs[8:12])
    fetch = Fetch(here, weights, fetched, refs[12:])
    count, width = q_ref.shape
    first_row = pl.multiple_of(here.z * count, count)

    def rows_copy(shard):
        rows = pl.ds(pl.multiple_of(shard * count, count), count)
        return pltpu.make_async_copy(rows_ref.at[rows], rows_in.at[rows], rows_copied.at[shard])

    proj_copy = pltpu.make_async_copy(proj_ref, proj, proj_copied)
    proj_copy.start()
    for shard in range(ring):
        rows_copy(shard).start()
    here.meet(here.neighbours() + fetch.devices())
    local = pltpu.make_async_copy(own_ref, all_ref.at[pl.ds(first_row, count)], copied)
    local.start()
    fetch.begin()
    local.wait()
    gather.begin()
    mask = Mask(causal, starts, segments, first_row)
    proj_copy.wait()
    for shard in range(ring):
        rows_copy(shard).wait()
    queries = dot_plain(rows_in[pl.ds(first_row, count), :], proj[:, :width]) + bias_ref[:, :width]
    q_ref[...] = (queries.astype(BF16).astype(F32) * HEAD_DIM ** (-0.5)).astype(BF16)
    forward_start(q_ref, masked_q, acc, top)
    blocks = kv_ref.shape[0] // block

    @pl.loop(0, blocks)
    def _(index):
        rows = pl.ds(pl.multiple_of(index * block, block), block)
        both = dot_plain(rows_in[rows, :], proj[:, width:]) + bias_ref[:, width:]
        kv_ref[rows, :] = both.astype(BF16)
        forward_block(index, rows, True, block, kv_ref, mask, masked_q, acc, top)

        @pl.when((index >= 1) & (index < ring))
        def _():
            gather.advance(index)

        for p in range(fetch.number):
            pl.when(index == 1 + p * (blocks - 1) // fetch.number)(
                functools.partial(fetch.advance, p)
            )

    forward_end(out_ref, lse_ref, acc, top)
    gather.finish()
    fetch.end()


def gather_attend(number, ring, rows, proj, bias, mask, own, weights, tokens=()):
    length, model = rows.shape
    count, width = length // ring, proj.shape[1] // 3
    causal, starts, _, segments = mask
    fetched = len(weights)
    kv = jax.ShapeDtypeStruct((length, 2 * width), BF16)
    return pl.pallas_call(
        functools.partial(gather_attend_kernel, KEY_BLOCK, causal, ring, fetched, len(tokens)),
        out_shape=(
            jax.ShapeDtypeStruct((count, width), BF16),
            kv,
            jax.ShapeDtypeStruct((width, count), F32),
            jax.ShapeDtypeStruct((8, count), F32),
            jax.ShapeDtypeStruct((ring * own.shape[0], own.shape[1]), BF16),
        )
        + tuple(beside(weight) for weight in weights),
        in_specs=[SCALARS] + [VECTORS] * 3 + [ANYWHERE] * (2 + fetched + len(tokens)),
        out_specs=(VECTORS,) * 4 + (ANYWHERE,) * (1 + fetched),
        scratch_shapes=forward_scratch(count, width)
        + [
            pltpu.VMEM((length, model), BF16),
            pltpu.VMEM(proj.shape, BF16),
            DMA,
            DMA((ring,)),
            DMA,
        ]
        + gather_sems(ring)
        + fetch_sems(weights),
        compiler_params=pltpu.CompilerParams(
            vmem_limit_bytes=50 << 20, collective_id=number, has_side_effects=True
        ),
        cost_estimate=cost_of(kv, count, width, 4),
    )(starts, segments, bias, own, rows, proj, *weights, *tokens)


class Part:
    def __init__(self, inputs, in_specs, out_shapes, scratch, bind):
        self.inputs, self.in_specs, self.out_shapes = inputs, in_specs, out_shapes
        self.scratch, self.bind = scratch, bind


def run_parts(number, body, parts, cost=None):
    ring = lax.axis_size("seq")
    counts = [(len(p.inputs), len(p.out_shapes), len(p.scratch)) for p in parts]

    def kernel(*refs):
        here = Here(ring)
        taken, offset = [[] for _ in parts], 0
        for kind in range(3):
            for refs_of, count in zip(taken, counts):
                refs_of.append(refs[offset : offset + count[kind]])
                offset += count[kind]
        here.meet(here.everyone())
        body(here, *(p.bind(here, *refs_of) for p, refs_of in zip(parts, taken)))

    results = pl.pallas_call(
        kernel,
        out_shape=[shape for p in parts for shape in p.out_shapes],
        in_specs=[spec for p in parts for spec in p.in_specs],
        out_specs=[VECTORS for p in parts for _ in p.out_shapes],
        scratch_shapes=[shape for p in parts for shape in p.scratch],
        compiler_params=pltpu.CompilerParams(
            vmem_limit_bytes=62 << 20, collective_id=number, has_side_effects=True
        ),
        cost_estimate=cost,
    )(*(array for p in parts for array in p.inputs))
    given = []
    for _, count, _ in counts:
        given.append(results[:count])
        results = results[count:]
    return given


class Stage:
    def __init__(self, here, kind, source, result, buffers, sems):
        self.here, self.kind, self.source, self.result = here, kind, source, result
        self.buffers, (self.sent, self.got) = buffers, sems
        rows = source.shape[0]
        if kind == "x":
            half = rows // 2
            self.kept = [half * here.x]
            self.given = [half * (1 - here.x)]
            self.size, self.to = half, here.over_x
        elif kind == "y":
            self.size = 192
            self.starts = list(range(0, rows, 2 * self.size))
        elif kind == "v":
            bit = lax.rem(here.z, 2)
            self.size = rows // 4
            self.kept = [self.size * bit, self.size * (bit + 2)]
            self.given = [self.size * (1 - bit), self.size * (3 - bit)]
            self.to = (here.d, here.z + 1 - 2 * bit, here.y)
        else:
            bit = lax.div(here.z, 2)
            self.size = rows // 2
            self.kept, self.given = [self.size * bit], [self.size * (1 - bit)]
            self.to = (here.d, here.z + 2 - 4 * bit, here.y)

    def rows(self, start):
        if not isinstance(start, int):
            start = pl.multiple_of(start, 16)
        return pl.ds(start, self.size)

    def move(self, start, place, buffer, sem, to):
        return remote(
            self.source.at[self.rows(start)],
            self.buffers[buffer].at[self.rows(place * self.size)],
            self.sent.at[sem],
            self.got.at[sem],
            to,
        )

    def moves(self):
        here = self.here
        if self.kind != "y":
            both = [
                (None, self.move(start, k, 0, k, self.to)) for k, start in enumerate(self.given)
            ]
            return both, both
        sends, arrivals = [], []
        for k, start in enumerate(self.starts):
            upper = start + self.size
            sends.append((here.core == 0, self.move(upper, k, 0, 2 * k, here.partner)))
            sends.append((here.core == 1, self.move(start, k, 0, 2 * k, here.diagonal)))
            sends.append((here.core == 1, self.move(upper, k, 1, 2 * k + 1, here.over_y)))
            arrivals.append((None, self.move(upper, k, 0, 2 * k, here.partner)))
            arrivals.append((here.core == 1, self.move(upper, k, 1, 2 * k + 1, here.over_y)))
        return sends, arrivals

    @staticmethod
    def each(moves, act):
        for condition, copy in moves:
            if condition is None:
                act(copy)
            else:
                pl.when(condition)(functools.partial(act, copy))

    def begin(self):
        self.each(self.moves()[0], lambda copy: copy.start())

    def end(self):
        sends, arrivals = self.moves()
        self.each(arrivals, lambda copy: copy.wait_recv())
        kept = self.kept if self.kind != "y" else self.starts
        for k, start in enumerate(kept):
            place = self.rows(k * self.size)

            def add(own_ref, own, place=place):
                both = own_ref[own, :].astype(F32) + self.buffers[0][place, :].astype(F32)
                self.result[place, :] = both.astype(self.result.dtype)

            if self.kind == "y":
                pl.when(self.here.core == 0)(functools.partial(add, self.source, self.rows(start)))
                pl.when(self.here.core == 1)(functools.partial(add, self.buffers[1], place))
            else:
                add(self.source, self.rows(start))
        self.each(sends, lambda copy: copy.wait_send())


class Chain:
    def __init__(self, stages, times):
        self.stages, self.times = stages, times

    def event(self, time):
        for k, own in enumerate(self.times):
            if own == time:
                if k:
                    self.stages[k - 1].end()
                if k < len(self.stages):
                    self.stages[k].begin()


def chain(array, kinds, times, made=None):
    rows, columns = made[2] if made else array.shape
    scratch, shapes = [], []
    for kind in kinds:
        rows = rows // 2
        scratch += [pltpu.VMEM((rows, columns), BF16)] * (2 if kind == "y" else 1)
        scratch += [DMA((4,))] * 2
        shapes.append((rows, columns))
    scratch += [pltpu.VMEM(shape, BF16) for shape in shapes[:-1]]
    final = jax.ShapeDtypeStruct(shapes[-1], F32 if kinds[-1] == "w" else BF16)

    def bind(here, inputs, outputs, refs):
        refs = list(refs)
        results = refs[len(refs) - len(kinds) + 1 :] + [outputs[0]]
        source, stages = made[0][made[1]] if made else inputs[0], []
        for kind, result in zip(kinds, results):
            buffers = [refs.pop(0) for _ in range(2 if kind == "y" else 1)]
            sems = [refs.pop(0) for _ in range(2)]
            stages.append(Stage(here, kind, source, result, buffers, sems))
            source = result
        return Chain(stages, times)

    inputs = () if made else (array,)
    return Part(inputs, [VECTORS] * len(inputs), [final], scratch, bind)


def closing_kernel(flag, *refs):
    given, outputs, held, copied = refs[:22], refs[22:47], refs[47:69], refs[69]
    copies = [
        pltpu.make_async_copy(start, end, copied.at[k])
        for k, (start, end) in enumerate(zip(given, held))
    ]
    for copy in copies:
        copy.start()
    for copy in copies:
        copy.wait()
    rows, vectors, grads = held[:8], held[8], held[9:22]
    keeps = flag[0] == 1
    for k in range(4):
        own, other = rows[2 * k][...], rows[2 * k + 1][...]
        outputs[k][...] = jnp.where(keeps, own, other).astype(outputs[k].dtype)
    for k in range(3):
        of_q, of_kv = grads[3 * k], grads[3 * k + 2]
        qkv = outputs[4 + k]
        width = of_q.shape[1]
        qkv[0] = of_q[...]
        qkv[1] = of_kv[:, :width]
        qkv[2] = of_kv[:, width:]
    outputs[7][...] = grads[9][...]
    outputs[8][...] = grads[11][...]
    for k in range(3):
        outputs[9 + k][...] = grads[3 * k + 1][...]
    for k in range(2):
        outputs[12 + k][...] = grads[10 + 2 * k][...]
    row = 0
    for out in outputs[14:20]:
        out[...] = vectors[row : row + out.shape[0], :]
        row += out.shape[0]
    for out in outputs[20:23]:
        width = out.shape[1]
        out[0:1, :] = vectors[row : row + 1, :width]
        out[1:2, :] = vectors[row : row + 1, width:]
        row += 1
    columns = vectors.shape[1]
    for out in outputs[23:]:
        for part in range(out.shape[0] // columns):
            out[part * columns : (part + 1) * columns] = vectors[row, :]
            row += 1


def closing(flag, rows, vectors, grads, sizes):
    part, width = grads[0].shape
    units = grads[9].shape[1]
    model = vectors.shape[1]
    shapes = [(rows[0].shape, BF16)] * 2 + [(rows[0].shape, F32)] * 2
    matrices = [(3, part, width)] * 3 + [(part, units)] * 2 + [(part, width)] * 3 + [(part, units)] * 2
    matrices += [(size, model) for size in sizes] + [(2, width)] * 3 + [(units,)] * 2
    shapes += [(shape, F32) for shape in matrices]
    inputs = (flag, *rows, vectors, *grads)
    return pl.pallas_call(
        closing_kernel,
        out_shape=[jax.ShapeDtypeStruct(*shape) for shape in shapes],
        in_specs=[SCALARS] + [ANYWHERE] * (len(inputs) - 1),
        out_specs=[VECTORS] * len(shapes),
        scratch_shapes=[pltpu.VMEM(value.shape, value.dtype) for value in inputs[1:]]
        + [DMA((len(inputs) - 1,))],
        compiler_params=pltpu.CompilerParams(vmem_limit_bytes=62 << 20),
    )(*inputs)


class HandOut:
    def __init__(self, here, inputs, outputs, scratch, times):
        self.here, self.times = here, times
        self.sent, self.got = scratch
        self.copies = [
            remote(given, taken, self.sent.at[k], self.got.at[k], here.over_y)
            for k, (given, taken) in enumerate(zip(inputs, outputs))
        ]

    def event(self, time):
        owns = self.here.core == self.here.y
        for copy in self.copies:
            if time == self.times[0]:
                pl.when(owns)(copy.start)
            if time == self.times[1]:
                pl.when(owns)(copy.wait_send)
                pl.when(jnp.logical_not(owns))(copy.wait_recv)


def hand_out(rows, times):
    number = len(rows)
    return Part(
        tuple(rows),
        [VECTORS] * number,
        [jax.ShapeDtypeStruct(value.shape, value.dtype) for value in rows],
        [DMA((number,))] * 2,
        lambda here, *refs: HandOut(here, *refs, times),
    )


class Small:
    def __init__(self, here, rows, held_rows, given, result, refs, times):
        self.here, self.given, self.result, self.times = here, given, result, times
        self.rows, self.held_rows = rows, held_rows
        self.arrived, self.sent, self.got = refs
        self.bits = [lax.rem(here.z, 2), lax.div(here.z, 2)]

    def copies(self, stage):
        here = self.here
        low, high = self.bits

        def to(device, slot, source=self.result, target=None):
            target = self.arrived.at[slot] if target is None else target
            return remote(source, target, self.sent.at[slot], self.got.at[slot], device)

        if stage < 3:
            device = (
                here.over_x,
                (here.d, here.z + 1 - 2 * low, here.y),
                (here.d, here.z + 2 - 4 * high, here.y),
            )[stage]
            both = [(None, to(device, stage))]
            return both, both
        if stage == 3:
            sends = [
                (None, to(here.over_y, 3)),
                (here.core == 0, to(here.partner, 4)),
                (here.core == 1, to(here.diagonal, 4)),
            ]
            return sends, sends[:1] + [(None, to(here.partner, 4))]
        return [(here.core == 0, to(here.partner, 5))], [(here.core == 1, to(here.partner, 5))]

    def end(self, stage):
        sends, arrivals = self.copies(stage)
        Stage.each(arrivals, lambda copy: copy.wait_recv())
        Stage.each(sends, lambda copy: copy.wait_send())
        core = self.here.core
        if stage < 3:
            self.result[...] += self.arrived[stage]
        elif stage == 3:
            whole, halves = slice(0, self.held_rows), slice(self.held_rows, self.rows)
            self.result[whole, :] += self.arrived[3, whole, :]
            own = jnp.where(core == 0, self.result[halves, :], self.arrived[3, halves, :])
            self.result[halves, :] = own + self.arrived[4, halves, :]
        else:
            whole = slice(0, self.held_rows)

            @pl.when(core == 1)
            def _():
                self.result[whole, :] = self.arrived[5, whole, :]

    def event(self, time):
        for k, own in enumerate(self.times):
            if own == time:
                if k == 0:
                    self.result[...] = self.given[...]
                else:
                    self.end(k - 1)
                if k < 5:
                    Stage.each(self.copies(k)[0], lambda copy: copy.start())


def small_sums(whole, halves, times):
    both = jnp.concatenate([whole, halves])
    rows, columns = both.shape
    shape = jax.ShapeDtypeStruct(both.shape, F32)
    part = Part(
        (both,),
        [VECTORS],
        [shape],
        [pltpu.VMEM((6, rows, columns), F32), DMA((6,)), DMA((6,))],
        lambda here, inputs, outputs, refs: Small(
            here, rows, whole.shape[0], inputs[0], outputs[0], refs, times
        ),
    )
    part.rows, part.vectors = whole.shape[0], (whole.reshape(-1), halves.reshape(-1))
    return part


def run_chains(number, chains, events):
    def body(here, *bound):
        for time in range(events):
            for one in bound:
                one.event(time)

    return run_parts(number, body, chains)


class Back:
    def __init__(self, here, causal, apart, inputs, outputs, scratch):
        self.here, self.causal, self.apart = here, causal, apart
        self.starts, self.segments, self.q, self.kv, self.do, self.dot, self.out, self.lse = inputs[:8]
        self.weights = inputs[8]
        self.dq_out, self.dkv, self.sum = outputs[:3]
        self.query_sum = outputs[3] if apart else None
        self.work, scratch = scratch[:4], scratch[4:]
        self.terms, self.from_core, self.outgoing, self.arrived, self.total = scratch[:5]
        self.core_sent, self.core_got, self.sent, self.got, self.end_sent, self.end_got = scratch[5:11]
        if apart:
            self.query_low, self.query_got, self.query_sems = scratch[11:]
        self.count, self.width = self.q.shape
        self.part = self.count // 2
        self.mask = Mask(causal, self.starts, self.segments, here.z * self.count)

    def half(self, core):
        return pl.ds(pl.multiple_of(core * self.part, self.part), self.part)

    def shard_at(self, turn):
        ring, z, shard = self.here.ring, self.here.z, 0
        for device in range(ring):
            others = [t for t in range(ring) if t != device]
            others.sort(key=lambda t: (ring - t + device) if t > device else (t + ring - device))
            for k, other in enumerate(others):
                shard = jnp.where((z == device) & (turn == k + 1), other, shard)
        return shard

    def across(self, turn, shard):
        return remote(
            self.terms.at[lax.rem(turn, 2), self.half(1 - self.here.core)],
            self.from_core.at[shard],
            self.core_sent.at[shard],
            self.core_got.at[shard],
            self.here.partner,
        )

    def slot(self, way, shard, z):
        return jnp.where((way == 1) & (shard == z), self.here.ring, shard)

    def chunk(self, chunk):
        size = self.part // CHUNKS
        return pl.ds(chunk * size, size)

    def along(self, way, shard, chunk, device):
        rows = self.chunk(chunk)
        return remote(
            self.outgoing.at[shard, rows],
            self.arrived.at[self.slot(way, shard, device[1]), rows],
            self.sent.at[chunk, shard],
            self.got.at[way * CHUNKS + chunk, shard],
            device,
        )

    def put(self, turn, shard, terms):
        @pl.when(turn > 2)
        def _():
            self.across(turn - 2, self.shard_at(turn - 2)).wait_send()

        slot = lax.rem(turn, 2)
        self.terms[slot] = terms.astype(BF16)
        self.across(turn, shard).start()
        self.outgoing[shard] = self.terms[slot, self.half(self.here.core), :]

    def both(self, shard):
        self.across(0, shard).wait_recv()
        return self.outgoing[shard].astype(F32) + self.from_core[shard].astype(F32)

    def take(self, way, shard, chunk):
        rows = self.chunk(chunk)
        self.along(way, shard, chunk, self.here.partner).wait_recv()
        slot = self.slot(way, shard, self.here.z)
        self.total[rows, :] += self.arrived[slot, rows, :].astype(F32)

    def forward(self, shard):
        here = self.here
        self.total[...] = self.both(shard)
        ways = (
            (0, shard > here.z, here.z > 0, here.right),
            (1, shard < here.z, here.z + 1 < here.ring, here.left),
        )
        for chunk in range(CHUNKS):
            rows = self.chunk(chunk)
            for way, mine, comes, _ in ways:
                pl.when(mine & comes)(functools.partial(self.take, way, shard, chunk))
            self.outgoing[shard, rows, :] = self.total[rows, :].astype(BF16)
            for way, mine, _, device in ways:

                @pl.when(mine)
                def _(way=way, device=device, chunk=chunk):
                    self.along(way, shard, chunk, device).start()

    def block(self, shard, between):
        rows = pl.ds(pl.multiple_of(shard * self.count, self.count), self.count)
        backward_block(
            shard, rows, self.count, self.mask, self.kv, self.lse, self.dkv, *self.work, between
        )
        return dot_last(self.dkv[rows, :], self.weights[:, self.width :])

    def run(self, event):
        here, ring = self.here, self.here.ring
        at_end = (here.z == 0) | (here.z == ring - 1)
        event(0)
        backward_start(self.q, self.do, self.dot, self.out, *self.work)

        @pl.loop(1, ring)
        def _(turn):
            shard = self.shard_at(turn)

            def between():
                @pl.when((turn > 1) & at_end)
                def _():
                    self.forward(self.shard_at(turn - 1))

            self.put(turn, shard, self.block(shard, between))
            for time in range(1, ring):
                pl.when(turn == time)(functools.partial(event, time))

        def between():
            self.forward(self.shard_at(jnp.where(at_end, ring - 1, 1)))

        own = self.block(here.z, between)
        event(ring)
        low = (self.work[3][...] * HEAD_DIM ** (-0.5)).T.astype(BF16)
        self.dq_out[...] = low
        query = dot_last(low, self.weights[:, : self.width])
        if self.apart:
            self.query_low[...] = query.astype(BF16)
            exchange = remote(
                self.query_low, self.query_got, self.query_sems.at[0], self.query_sems.at[1], here.partner
            )
            exchange.start()
        else:
            own = own + query
        self.put(jnp.int32(ring), here.z, own)
        if self.apart:
            exchange.wait()
            self.query_sum[...] = self.query_low[...].astype(F32) + self.query_got[...].astype(F32)

        @pl.when(jnp.logical_not(at_end))
        def _():
            @pl.loop(2, ring)
            def _(turn):
                self.forward(self.shard_at(turn))

        event(ring + 1)
        self.total[...] = self.both(here.z)
        for chunk in range(CHUNKS):
            for way, comes in ((0, here.z > 0), (1, here.z + 1 < ring)):
                pl.when(comes)(functools.partial(self.take, way, here.z, chunk))

        own, other = self.half(here.core), self.half(1 - here.core)
        self.sum[own, :] = self.total[...].astype(BF16)
        for half, waits in ((own, False), (other, True)):
            view = self.sum.at[half]
            copy = remote(view, view, self.end_sent, self.end_got, here.partner)
            if waits:
                copy.wait_recv()
            else:
                copy.start()
                copy.wait_send()
        self.across(ring - 1, self.shard_at(ring - 1)).wait_send()
        self.across(ring, here.z).wait_send()
        for shard in range(ring):

            @pl.when(here.z != shard)
            def _(shard=shard):
                for chunk in range(CHUNKS):
                    self.along(0, shard, chunk, here.partner).wait_send()

        event(ring + 2)


class Products:
    def __init__(self, back, inputs, of_bias, made, scratch, time):
        self.back, self.time = back, time
        self.query_in, self.key_in, self.grad_branch, self.mixed = inputs
        self.of_bias = of_bias
        self.of_q, self.of_out, self.of_kv = made
        self.blocks, self.copied = scratch

    def copy(self, index):
        part = pl.ds(pl.multiple_of(index * 128, 128), 128)
        slot = lax.rem(index, 2)
        return pltpu.make_async_copy(
            self.key_in.at[:, part], self.blocks.at[slot], self.copied.at[slot]
        )

    def event(self, time):
        if time == 0:
            self.copy(0).start()
        if time != self.time:
            return
        dq, dkv = self.back.dq_out, self.back.dkv
        width = dq.shape[1]
        number = self.of_kv.shape[0] // 128

        @pl.loop(0, number)
        def _(index):
            @pl.when(index + 1 < number)
            def _():
                self.copy(index + 1).start()

            self.copy(index).wait()
            part = pl.ds(pl.multiple_of(index * 128, 128), 128)
            block = self.blocks[lax.rem(index, 2)]
            self.of_kv[part, :] = dot_first(block, dkv[...]).astype(BF16)

        self.of_q[...] = dot_first(self.query_in[...], dq[...]).astype(BF16)
        self.of_out[...] = dot_first(self.grad_branch[...], self.mixed[...].T).astype(BF16)
        self.of_bias[0:1, :] = jnp.sum(dq[...].astype(F32), axis=0, keepdims=True)
        self.of_bias[1:2, :] = jnp.sum(dkv[:, width:].astype(F32), axis=0, keepdims=True)


def products(box, query_in, key_in, grad_branch, mixed, time, begins):
    model, width = query_in.shape[1], mixed.shape[0]
    shapes = ((model, width), (model, width), (model, 2 * width))

    def bind(here, inputs, outputs, refs):
        made = refs[2:] if begins else outputs[1:]
        for k in range(3):
            box[k] = made[k]
        return Products(box["back"], inputs, outputs[0], made, refs[:2], time)

    part = Part(
        (query_in, key_in, grad_branch, mixed),
        [VECTORS, ANYWHERE, VECTORS, VECTORS],
        [jax.ShapeDtypeStruct((2, width), F32)]
        + ([] if begins else [jax.ShapeDtypeStruct(shape, BF16) for shape in shapes]),
        [pltpu.VMEM((2, key_in.shape[0], 128), BF16), DMA((2,))]
        + ([pltpu.VMEM(shape, BF16) for shape in shapes] if begins else []),
        bind,
    )
    if not begins:
        return [part]
    firsts = [
        chain(None, kind, (time, 6), (box, k, shape)) for k, (kind, shape) in enumerate(zip("yyx", shapes))
    ]
    return [part, *firsts]


class FeedBack:
    def __init__(self, here, inputs, outputs, scratch, time):
        self.here, self.time = here, time
        self.grad, self.x_in = inputs[:2]
        self.streamed = inputs[2:]
        self.sum, self.of_bias, self.of_in, self.of_out = outputs
        self.blocks, scratch = scratch[:4], scratch[4:]
        self.x_turned, self.grad_turned, self.low, self.got, self.copied, self.sems = scratch

    def event(self, time):
        if time != self.time:
            return
        span = self.blocks[0].shape[2]
        number = self.of_in.shape[1] // span
        self.sum[...] = jnp.zeros_like(self.sum)

        def columns(index):
            return pl.ds(pl.multiple_of(index * span, span), span)

        def copies(index):
            slot, part = lax.rem(index, 2), columns(index)
            return [
                pltpu.make_async_copy(
                    ref.at[part] if k == 3 else ref.at[:, part],
                    self.blocks[k].at[slot],
                    self.copied.at[k, slot],
                )
                for k, ref in enumerate(self.streamed)
            ]

        for copy in copies(0):
            copy.start()

        @pl.loop(0, self.x_turned.shape[0] // span)
        def _(index):
            part = columns(index)
            self.x_turned[part, :] = self.x_in[:, part].T
            self.grad_turned[part, :] = self.grad[:, part].T

        @pl.loop(0, number)
        def _(index):
            part = columns(index)

            @pl.when(index + 1 < number)
            def _():
                for copy in copies(index + 1):
                    copy.start()

            for copy in copies(index):
                copy.wait()
            slope, active, w_in, w_out = (block.at[lax.rem(index, 2)] for block in self.blocks)
            hidden = (slope[...] * dot_last(self.grad[...], w_out[...])).astype(BF16)
            self.of_bias[:, part] = jnp.sum(hidden.astype(F32), axis=0, keepdims=True)
            self.sum[...] += dot_last(hidden, w_in[...])
            self.of_in[:, part] = dot_plain(self.x_turned[...], hidden).astype(BF16)
            self.of_out[:, part] = dot_plain(self.grad_turned[...], active[...]).astype(BF16)

        self.low[...] = self.sum[...].astype(BF16)
        exchange = remote(self.low, self.got, self.sems.at[0], self.sems.at[1], self.here.partner)
        exchange.start()
        exchange.wait()
        self.sum[...] = self.low[...].astype(F32) + self.got[...].astype(F32)


def feed_back(grad_branch, slope, w_in, w_out, x_in, active, time):
    count, model = x_in.shape
    units = w_in.shape[1]
    span = 256
    return Part(
        (grad_branch, x_in, slope, active, w_in, w_out),
        [VECTORS] * 2 + [ANYWHERE] * 4,
        [
            jax.ShapeDtypeStruct((count, model), F32),
            jax.ShapeDtypeStruct((1, units), F32),
            jax.ShapeDtypeStruct((model, units), BF16),
            jax.ShapeDtypeStruct((model, units), BF16),
        ],
        [
            pltpu.VMEM((2, count, span), slope.dtype),
            pltpu.VMEM((2, count, span), BF16),
            pltpu.VMEM((2, model, span), BF16),
            pltpu.VMEM((2, span, model), BF16),
            pltpu.VMEM((model, count), BF16),
            pltpu.VMEM((model, count), BF16),
            pltpu.VMEM((count, model), BF16),
            pltpu.VMEM((count, model), BF16),
            DMA((4, 2)),
            DMA((2,)),
        ],
        lambda here, *refs: FeedBack(here, *refs, time),
    )


def attend_back(number, saved, grad_mixed, grad_mixed_t, weights, mask, apart, more, box):
    queries, kv, output, lse, _ = saved
    causal, starts, segments = mask
    ring = lax.axis_size("seq")
    count, width = queries.shape
    model = weights.shape[0]
    part = count // 2
    shapes = [
        jax.ShapeDtypeStruct((count, width), BF16),
        jax.ShapeDtypeStruct(kv.shape, BF16),
        jax.ShapeDtypeStruct((count, model), BF16),
    ]
    scratch = backward_scratch(count, width) + [
        pltpu.VMEM((2, count, model), BF16),
        *[pltpu.VMEM((ring, part, model), BF16)] * 2,
        pltpu.VMEM((ring + 1, part, model), BF16),
        pltpu.VMEM((part, model), F32),
        *[DMA((ring,))] * 2,
        DMA((CHUNKS, ring)),
        DMA((2 * CHUNKS, ring)),
        *[DMA] * 2,
    ]
    if apart:
        shapes.append(jax.ShapeDtypeStruct((count, model), F32))
        scratch += [pltpu.VMEM((count, model), BF16)] * 2 + [DMA((2,))]
    main = Part(
        (starts, segments, queries, kv, grad_mixed, grad_mixed_t, output, lse, weights),
        [SCALARS] + [VECTORS] * 8,
        shapes,
        scratch,
        lambda here, *refs: box.setdefault("back", Back(here, causal, apart, *refs)),
    )

    def body(here, back, *bound):
        def event(time):
            for one in bound:
                one.event(time)

        back.run(event)

    return run_parts(number, body, [main] + list(more), cost_of(kv, count, width, 7))


class Plan:
    def __init__(self, kernels):
        self.kernels = kernels

    def chains(self, wanted):
        return [chain(*one) for one in wanted] if self.kernels else []

    def given(self, wanted, results):
        return results if self.kernels else [one[0] for one in wanted]


class Places:
    def __init__(self, pairs, ring):
        self.pairs, self.ring = pairs, ring
        self.d = lax.axis_index("dp")
        self.x, self.core = self.d // 2, self.d % 2
        self.y, self.z = lax.axis_index("tensor"), lax.axis_index("seq")

    def swap_core(self, value):
        return lax.ppermute(value, "dp", [(i, i ^ 1) for i in range(self.pairs)])

    def swap_y(self, value):
        return lax.ppermute(value, "tensor", [(0, 1), (1, 0)])

    def swap_x(self, value, bit):
        return lax.ppermute(value, "dp", [(i, i ^ (2 << bit)) for i in range(self.pairs)])

    def swap_z(self, value, bit):
        return lax.ppermute(value, "seq", [(i, i ^ (1 << bit)) for i in range(self.ring)])

    def from_z(self, value, step):
        return lax.ppermute(value, "seq", [((i + step) % self.ring, i) for i in range(self.ring)])

    def to_z(self, value, step):
        return lax.ppermute(value, "seq", [(i, (i + step) % self.ring) for i in range(self.ring)])

    def permute(self, value, source_of):
        moves = []
        for d in range(self.pairs):
            for y in range(2):
                source = source_of(d, y)
                if source is not None:
                    moves.append((source[0] * 2 + source[1], d * 2 + y))
        return lax.ppermute(value, ("dp", "tensor"), moves)

    def fetch_weight(self, value):
        return self.permute(value, lambda d, y: (d + 1, y) if d % 2 == 0 else (d - 1, 1 - y))

    def core_sum(self, partial):
        low = rounded(partial)
        return low + self.swap_core(low.astype(BF16)).astype(F32)

    def own_pair(self, rows):
        return jnp.where(self.core == self.y, rows, self.swap_core(rows))

    def others(self, rows):
        return self.permute(rows, lambda d, y: (d, 1 - y) if d % 2 != y else None)

    def plan(self):
        return Plan(self.pairs == 4 and self.ring == 4)

    def scatter(self, grad, x_first):
        rows, columns = grad.shape
        owners = self.pairs // 2
        grad = grad.reshape(owners, 2, self.ring, rows // (self.pairs * self.ring), columns)
        for stage in "xyz" if x_first else "yxz":
            if stage == "y":
                kept = lax.dynamic_index_in_dim(grad, self.core, grad.ndim - 4, False)
                sent = lax.dynamic_index_in_dim(grad, 1 - self.core, grad.ndim - 4, False)
                first = self.permute(
                    sent, lambda d, y: (d + 1, 1 - y) if d % 2 == 0 else (d - 1, y)
                )
                second = self.permute(kept, lambda d, y: (d, 1 - y) if d % 2 else None)
                kept = jnp.where(self.core == 0, kept, second)
                grad = (kept.astype(F32) + first.astype(F32)).astype(BF16)
            else:
                axis = 0 if stage == "x" else grad.ndim - 3
                place, swap = (self.x, self.swap_x) if stage == "x" else (self.z, self.swap_z)
                size, bit = grad.shape[axis], 0
                while size > 1:
                    shape = grad.shape[:axis] + (size // 2, 2) + grad.shape[axis + 1 :]
                    grad = grad.reshape(shape)
                    mine = (place >> bit) & 1
                    kept = lax.dynamic_index_in_dim(grad, mine, axis + 1, False)
                    sent = lax.dynamic_index_in_dim(grad, 1 - mine, axis + 1, False)
                    grad = kept.astype(F32) + swap(sent, bit).astype(F32)
                    size, bit = size // 2, bit + 1
                    if stage == "x" or size > 1:
                        grad = grad.astype(BF16)
                grad = lax.squeeze(grad, (axis,))
        return grad.astype(F32)

    def all_sum(self, whole, halves):
        both = jnp.concatenate([whole, halves])
        for bit in range((self.pairs // 2).bit_length() - 1):
            both = both + self.swap_x(both, bit)
        for bit in range(self.ring.bit_length() - 1):
            both = both + self.swap_z(both, bit)
        whole, halves = both[: whole.shape[0]], both[whole.shape[0] :]
        whole = whole + self.swap_y(whole)
        whole = (whole + self.swap_core(whole)) * 0.5
        first = self.permute(halves, lambda d, y: (d + 1, 1 - y) if d % 2 == 0 else (d - 1, y))
        second = self.swap_y(halves)
        halves = jnp.where(self.core == 0, halves, second) + first
        return whole, halves


def starts_of(segments):
    numbers = jnp.arange(8, dtype=jnp.int32)
    return jnp.sum(segments[None, :] < numbers[:, None], axis=1, dtype=jnp.int32)


def mask_of(query_seg, key_starts, first_row, causal):
    ends = jnp.stack([query_seg[0], query_seg[-1], first_row])
    return (causal, key_starts, ends, query_seg[None])


def projected(query_in, key_in, weights, bias):
    width = bias.shape[1] // 3
    queries = (dot_plain(query_in, weights[:, :width]) + bias[:, :width]).astype(BF16)
    kv = (dot_plain(key_in, weights[:, width:]) + bias[:, width:]).astype(BF16)
    return (queries * HEAD_DIM ** (-0.5)).astype(BF16), kv


def attention_output(place, queries, kv, output, lse, out_weight, out_bias):
    mixed = output.astype(BF16)
    branch = place.core_sum(dot_first(mixed, out_weight)) + out_bias.astype(F32)
    return (branch, (queries, kv, output, lse, mixed))


def attention_backward(
    number,
    grad_branch,
    saved,
    query_in,
    key_in,
    weights,
    out_weight,
    mask,
    apart,
    plan,
    wanted,
    inside=(),
    begins=False,
):
    mixed = saved[4]
    grad_mixed = dot_last(grad_branch, out_weight).astype(BF16)
    grad_mixed_t = dot_last(out_weight, grad_branch).astype(BF16)
    box = {}
    more = []
    if plan.kernels:
        made = products(box, query_in, key_in, grad_branch, mixed, 5, begins)
        more = [*made, *plan.chains(wanted), *inside]
    (grad_q, grad_kv, *sums), *rest = attend_back(
        number, saved, grad_mixed, grad_mixed_t, weights, mask, apart, more, box
    )
    if plan.kernels:
        (grad_bias, *grads), *rest = rest
        if begins:
            grads, rest = [first[0] for first in rest[:3]], rest[3:]
    else:
        grads = (
            dot_first(query_in, grad_q).astype(BF16),
            dot_first(grad_branch, mixed.T).astype(BF16),
            dot_first(key_in, grad_kv).astype(BF16),
        )
        grad_bias = jnp.stack([column_sum(grad_q), column_sum(grad_kv[:, grad_q.shape[1] :])])
    given = [results[0] for results in rest[: len(rest) - len(inside)]]
    rest = rest[len(rest) - len(inside) :]
    return (sums, grads, grad_bias.reshape(-1), plan.given(wanted, given), rest)


def feed_forward(place, x_in, w_in, b_in, w_out, b_out):
    hidden = dot_plain(x_in, w_in) + b_in.astype(F32)
    spread = 0.5 * (1.0 + lax.erf(hidden * 0.5**0.5))
    active = (hidden * spread).astype(BF16)
    slope = spread + hidden * jnp.exp(-0.5 * hidden * hidden) * (2.0 * math.pi) ** (-0.5)
    branch = place.core_sum(dot_plain(active, w_out)) + b_out.astype(F32)
    return (branch, (slope, active))


def feed_backward(place, grad_branch, saved, x_in, w_in, w_out):
    slope, active = saved
    grad_hidden = (slope * dot_last(grad_branch, w_out)).astype(BF16)
    grad_in = place.core_sum(dot_last(grad_hidden, w_in))
    return (
        grad_in,
        dot_first(x_in, grad_hidden).astype(BF16),
        column_sum(grad_hidden),
        dot_first(grad_branch, active).astype(BF16),
    )


def shards(
    source,
    target,
    source_segments,
    target_segments,
    enc_qkv,
    enc_qv_bias,
    enc_proj,
    enc_ff_in,
    enc_ff_in_bias,
    enc_ff_out,
    enc_bias,
    enc_gains,
    enc_shifts,
    dec_self,
    dec_self_bias,
    dec_self_proj,
    dec_cross,
    dec_cross_bias,
    dec_cross_proj,
    dec_ff_in,
    dec_ff_in_bias,
    dec_ff_out,
    dec_bias,
    dec_gains,
    dec_shifts,
    enc_cotangent,
    dec_cotangent,
):
    count = source.shape[1]
    model = source.shape[2]
    place = Places(lax.axis_size("dp"), lax.axis_size("seq"))
    first_row = place.z * count

    ring = place.ring
    width = enc_qkv.shape[2]
    hidden_units = enc_ff_in.shape[1]

    x_all, ts, source_keys, target_keys, vectors, enc_qkv, enc_proj, dec_self = opening(
        ring,
        source[0],
        target[0],
        source_segments,
        target_segments,
        (
            enc_qv_bias,
            dec_self_bias,
            dec_cross_bias,
            enc_ff_in_bias,
            dec_ff_in_bias,
        ),
        (enc_qkv, enc_proj, dec_self),
    )
    source_keys, target_keys = source_keys[0], target_keys[0]
    xs = lax.dynamic_slice_in_dim(x_all, first_row, count, 0)
    enc_cot = place.own_pair(enc_cotangent[0])
    dec_cot = place.own_pair(dec_cotangent[0])
    enc_b, self_b, cross_b = (vectors[k : k + 1, : 3 * width] for k in range(3))
    enc_ff_in_bias, dec_ff_in_bias = vectors[3], vectors[4]
    source_own = lax.dynamic_slice_in_dim(source_keys, first_row, count, 0)
    target_own = lax.dynamic_slice_in_dim(target_keys, first_row, count, 0)
    source_starts, target_starts = starts_of(source_keys), starts_of(target_keys)
    enc_mask = mask_of(source_own, source_starts, first_row, False)
    self_mask = mask_of(target_own, target_starts, first_row, True)
    cross_mask = mask_of(target_own, source_starts, first_row, False)

    queries, kv, output, lse, t_all, enc_ff_in, enc_ff_out = gather_attend(
        7, ring, x_all, enc_qkv, enc_b, enc_mask, ts, (enc_ff_in, enc_ff_out)
    )
    dec_ff_in = place.fetch_weight(dec_ff_in + after(lse).astype(BF16))
    branch, enc_attn = attention_output(place, queries, kv, output, lse, enc_proj, enc_bias[0])
    first, enc_norm_one = norm_forward(xs.astype(F32) + branch, enc_gains[0], enc_shifts[0])
    first_low = first.astype(BF16)
    branch, enc_feed = feed_forward(
        place, first_low, enc_ff_in, enc_ff_in_bias, enc_ff_out, enc_bias[1]
    )
    encoded, enc_norm_two = norm_forward(first + branch, enc_gains[1], enc_shifts[1])
    encoded_low = encoded.astype(BF16)

    (
        queries,
        kv,
        output,
        lse,
        e_all,
        dec_self_proj,
        dec_cross,
        dec_cross_proj,
    ) = gather_attend(
        2,
        ring,
        t_all,
        dec_self,
        self_b,
        self_mask,
        encoded_low,
        (dec_self_proj, dec_cross, dec_cross_proj),
    )
    dec_ff_out = place.fetch_weight(dec_ff_out + after(lse).astype(BF16))
    branch, self_attn = attention_output(
        place, queries, kv, output, lse, dec_self_proj, dec_bias[0]
    )
    second, dec_norm_one = norm_forward(ts.astype(F32) + branch, dec_gains[0], dec_shifts[0])
    second_low = second.astype(BF16)
    queries, kv = projected(second_low, e_all, dec_cross, cross_b)
    output, lse = attend(queries, kv, cross_mask, (dec_ff_in,))
    branch, cross_attn = attention_output(
        place, queries, kv, output, lse, dec_cross_proj, dec_bias[1]
    )
    third, dec_norm_two = norm_forward(second + branch, dec_gains[1], dec_shifts[1])
    third_low = third.astype(BF16)
    branch, dec_feed = feed_forward(
        place, third_low, dec_ff_in, dec_ff_in_bias, dec_ff_out, dec_bias[2]
    )
    decoded, dec_norm_three = norm_forward(third + branch, dec_gains[2], dec_shifts[2])

    def back_mask(mask):
        return (mask[0], mask[1], mask[3])

    grad_hidden, dec_gain_three, dec_shift_three = norm_backward(
        dec_cot.astype(F32), dec_norm_three, dec_gains[2]
    )
    grad_branch = grad_hidden.astype(BF16)
    feed_in, dec_w_in, dec_b_in, dec_w_out = feed_backward(
        place, grad_branch, dec_feed, third_low, dec_ff_in, dec_ff_out
    )
    dec_bias_three = column_sum(grad_branch)
    grad_third = grad_hidden + feed_in
    grad_hidden, dec_gain_two, dec_shift_two = norm_backward(grad_third, dec_norm_two, dec_gains[1])
    grad_branch = grad_hidden.astype(BF16)
    plan = place.plan()
    (key_total, query_total), cross_grads, cross_bias, (dec_w_in, dec_w_out), _ = attention_backward(
        3,
        grad_branch,
        cross_attn,
        second_low,
        e_all,
        dec_cross,
        dec_cross_proj,
        back_mask(cross_mask),
        True,
        plan,
        [(dec_w_in, "x", (0, 6)), (dec_w_out, "y", (0, 6))],
    )
    dec_bias_two = column_sum(grad_branch)
    grad_second = grad_hidden + query_total
    grad_hidden, dec_gain_one, dec_shift_one = norm_backward(
        grad_second, dec_norm_one, dec_gains[0]
    )
    grad_branch = grad_hidden.astype(BF16)
    cross_q, cross_proj, cross_kv = cross_grads
    target_hidden, target_branch = grad_hidden, grad_branch
    grad_hidden, enc_gain_two, enc_shift_two = norm_backward(
        enc_cot.astype(F32) + key_total.astype(F32), enc_norm_two, enc_gains[1]
    )
    grad_branch = grad_hidden.astype(BF16)
    enc_bias_two = column_sum(grad_branch)
    slope, active = enc_feed
    (target_total,), self_grads, self_bias, given, inside = attention_backward(
        4,
        target_branch,
        self_attn,
        ts,
        t_all,
        dec_self,
        dec_self_proj,
        back_mask(self_mask),
        False,
        plan,
            [
                (dec_w_in, "yvw", (0, 3, 5, 6)),
                (dec_w_out, "xvw", (0, 3, 5, 6)),
                (cross_kv, "x", (3, 6)),
                (cross_q, "y", (3, 6)),
                (cross_proj, "y", (3, 6)),
            ],
        [feed_back(grad_branch, slope, enc_ff_in, enc_ff_out, first_low, active, 5)]
        if plan.kernels
        else (),
        begins=True,
    )
    dec_w_in, dec_w_out, cross_kv, cross_q, cross_proj = given
    if plan.kernels:
        feed_in, enc_b_in, enc_w_in, enc_w_out = inside[0]
        enc_b_in = enc_b_in.reshape(-1)
    else:
        feed_in, enc_w_in, enc_b_in, enc_w_out = feed_backward(
            place, grad_branch, enc_feed, first_low, enc_ff_in, enc_ff_out
        )
    dec_bias_one = column_sum(target_branch)
    grad_target = target_hidden + target_total.astype(F32)
    grad_first = grad_hidden + feed_in
    grad_hidden, enc_gain_one, enc_shift_one = norm_backward(grad_first, enc_norm_one, enc_gains[0])
    grad_branch = grad_hidden.astype(BF16)
    self_q, self_proj, self_kv = self_grads
    (source_total,), enc_grads, enc_bias_grad, given, _ = attention_backward(
        5,
        grad_branch,
        enc_attn,
        xs,
        x_all,
        enc_qkv,
        enc_proj,
        back_mask(enc_mask),
        False,
        plan,
            [
                (cross_kv, "yvw", (0, 1, 3, 6)),
                (cross_q, "xvw", (0, 1, 3, 6)),
                (cross_proj, "xvw", (0, 1, 3, 6)),
                (enc_w_in, "x", (1, 6)),
                (enc_w_out, "y", (1, 6)),
                (self_kv, "y", (4, 6)),
                (self_q, "x", (4, 6)),
                (self_proj, "x", (4, 6)),
            ],
    )
    cross_kv, cross_q, cross_proj, enc_w_in, enc_w_out, self_kv, self_q, self_proj = given
    enc_bias_one = column_sum(grad_branch)
    grad_source = grad_hidden + source_total.astype(F32)
    enc_q, enc_proj_grad, enc_kv = enc_grads
    rest = [
        (self_kv, "vw", (0, 1, 2)),
        (self_q, "vw", (0, 1, 2)),
        (self_proj, "vw", (0, 1, 2)),
        (enc_w_in, "yvw", (0, 2, 4, 7)),
        (enc_w_out, "xvw", (0, 2, 4, 7)),
        (enc_kv, "xyvw", (2, 3, 5, 6, 7)),
        (enc_q, "yxvw", (2, 3, 5, 6, 7)),
        (enc_proj_grad, "yxvw", (2, 3, 5, 6, 7)),
    ]
    source_low = rounded(grad_source).astype(BF16)
    target_low = rounded(grad_target).astype(BF16)
    decoded_low = decoded.astype(BF16)
    small = small_sums(
        jnp.concatenate(
            [
                enc_bias_one,
                enc_bias_two,
                enc_gain_one,
                enc_gain_two,
                enc_shift_one,
                enc_shift_two,
                dec_bias_one,
                dec_bias_two,
                dec_bias_three,
                dec_gain_one,
                dec_gain_two,
                dec_gain_three,
                dec_shift_one,
                dec_shift_two,
                dec_shift_three,
            ]
        ).reshape(15, model),
        jnp.concatenate([enc_bias_grad, self_bias, cross_bias, enc_b_in, dec_b_in]).reshape(-1, model),
        (0, 1, 2, 3, 4, 5),
    )
    if plan.kernels:
        (vectors,), (source_other, target_other), *given = run_chains(
            6, [small, hand_out((source_low, target_low), (4, 7))] + plan.chains(rest), 8
        )
        given = [results[0] for results in given]
    else:
        vectors = jnp.concatenate(place.all_sum(*small.vectors)).reshape(-1, model)
        source_other, target_other = place.others(source_low), place.others(target_low)
        given = [place.scatter(array, True) for array, _, _ in rest]
        dec_w_in, dec_w_out, cross_kv, cross_q, cross_proj = (
            place.scatter(array, True)
            for array in (dec_w_in, dec_w_out, cross_kv, cross_q, cross_proj)
        )
    self_kv, self_q, self_proj, enc_w_in, enc_w_out, enc_kv, enc_q, enc_proj_grad = given

    grads = (enc_q, enc_proj_grad, enc_kv, self_q, self_proj, self_kv, cross_q, cross_proj, cross_kv)
    grads += (enc_w_in, enc_w_out, dec_w_in, dec_w_out)
    flag = jnp.where(place.core == place.y, 1, 0).astype(jnp.int32).reshape(1)
    rows = (
        encoded_low,
        place.others(encoded_low),
        decoded_low,
        place.others(decoded_low),
        source_low,
        source_other,
        target_low,
        target_other,
    )
    results = closing(flag, rows, vectors, grads, (2, 2, 2, 3, 3, 3))
    of_rows, of_qkv, of_in = [value[None] for value in results[:4]], results[4:7], results[7:9]
    of_out, of_ff_out = [value.T for value in results[9:12]], [value.T for value in results[12:14]]
    of_whole, of_qv_bias, of_in_bias = results[14:20], results[20:23], results[23:]
    return (
        *of_rows,
        of_qkv[0],
        of_qv_bias[0],
        of_out[0],
        of_in[0],
        of_in_bias[0],
        of_ff_out[0],
        *of_whole[:3],
        of_qkv[1],
        of_qv_bias[1],
        of_out[1],
        of_qkv[2],
        of_qv_bias[2],
        of_out[2],
        of_in[1],
        of_in_bias[1],
        of_ff_out[1],
        *of_whole[3:],
    )


def solution(mesh):
    return jax.shard_map(
        shards,
        mesh=mesh,
        in_specs=(
            P("dp", "seq", None),
            P("dp", "seq", None),
            P("dp", None),
            P("dp", None),
            P(None, None, "tensor"),
            P(None, "tensor"),
            P("tensor", None),
            P(None, "tensor"),
            P("tensor"),
            P("tensor", None),
            P(),
            P(),
            P(),
            P(None, None, "tensor"),
            P(None, "tensor"),
            P("tensor", None),
            P(None, None, "tensor"),
            P(None, "tensor"),
            P("tensor", None),
            P(None, "tensor"),
            P("tensor"),
            P("tensor", None),
            P(),
            P(),
            P(),
            P("dp", "seq", None),
            P("dp", "seq", None),
        ),
        out_specs=(
            P("dp", "seq", None),
            P("dp", "seq", None),
            P("dp", "seq", None),
            P("dp", "seq", None),
            P(None, ("dp", "seq"), "tensor"),
            P(None, "tensor"),
            P("tensor", ("dp", "seq")),
            P(("dp", "seq"), "tensor"),
            P("tensor"),
            P("tensor", ("dp", "seq")),
            P(),
            P(),
            P(),
            P(None, ("dp", "seq"), "tensor"),
            P(None, "tensor"),
            P("tensor", ("dp", "seq")),
            P(None, ("dp", "seq"), "tensor"),
            P(None, "tensor"),
            P("tensor", ("dp", "seq")),
            P(("dp", "seq"), "tensor"),
            P("tensor"),
            P("tensor", ("dp", "seq")),
            P(),
            P(),
            P(),
        ),
        check_vma=False,
    )
```

```python
import functools
import math

import jax
import jax.numpy as jnp
from jax import lax
from jax.experimental import pallas as pl
from jax.experimental.pallas import tpu as pltpu
from jax.sharding import PartitionSpec as P

HEAD_DIM = 64
EPS = 1e-05
NEG = -1e30
BF16 = jnp.bfloat16
F32 = jnp.float32
NT = (((1,), (1,)), ((), ()))
TN = (((0,), (0,)), ((), ()))
KEY_BLOCK = 512
CHUNKS = 2
DOCS = 4


def dot_plain(left, right):
    return jnp.dot(left, right, preferred_element_type=F32)


def dot_last(left, right):
    return lax.dot_general(left, right, NT, preferred_element_type=F32)


def dot_first(left, right):
    return lax.dot_general(left, right, TN, preferred_element_type=F32)


def column_sum(value):
    return jnp.sum(value.astype(F32), axis=0)


def rounded(value):
    return lax.reduce_precision(value, 8, 7)


def after(array):
    return jnp.minimum(jnp.abs(array[0, 0].astype(F32)), 0.0)


def norm_forward(hidden, gain, shift):
    centered = hidden - jnp.mean(hidden, axis=-1, keepdims=True)
    spread = jnp.mean(centered * centered, axis=-1, keepdims=True)
    factor = lax.rsqrt(spread + EPS)
    normed = centered * factor
    return (normed * gain.astype(F32) + shift.astype(F32), (normed, factor))


def norm_backward(grad, saved, gain):
    normed, factor = saved
    scaled = grad * gain.astype(F32)
    centered = scaled - jnp.mean(scaled, axis=-1, keepdims=True)
    grad_hidden = factor * (centered - normed * jnp.mean(scaled * normed, axis=-1, keepdims=True))
    return (grad_hidden, jnp.sum(grad * normed, axis=0), jnp.sum(grad, axis=0))


def head_columns(head):
    return slice(head // 2 * 128, head // 2 * 128 + 128)


def head_rows(head):
    return slice(head * HEAD_DIM, (head + 1) * HEAD_DIM)


def own_lanes(shape, head):
    lanes = lax.broadcasted_iota(jnp.int32, shape, 1)
    return lanes >= HEAD_DIM if head % 2 else lanes < HEAD_DIM


class Mask:
    def __init__(self, causal, starts, segments, first_row):
        self.causal, self.starts, self.first_row = causal, starts, first_row
        segments = segments[...]
        low = high = jnp.zeros_like(segments)
        for number in range(DOCS):
            low = jnp.where(segments == number, starts[number], low)
            high = jnp.where(segments == number, starts[number + 1], high)
        self.count = segments.shape[1]
        if causal:
            place = first_row + lax.broadcasted_iota(jnp.int32, segments.shape, 1)
            high = jnp.minimum(high, place + 1)
        self.low, self.high = low, high

    def allowed(self, index, block):
        place = lax.broadcasted_iota(jnp.int32, (block, self.count), 0) + index * block
        return (place >= self.low) & (place < self.high)

    def flag(self, index, block, ends):
        start, stop = index * block, (index + 1) * block
        low, low_last = self.starts[ends[0]], self.starts[ends[1]]
        high_first, high = self.starts[ends[0] + 1], self.starts[ends[1] + 1]
        if self.causal:
            high = jnp.minimum(high, self.first_row + self.count)
            high_first = jnp.minimum(high_first, self.first_row + 1)
        active = (low < stop) & (high > start)
        full = (low_last <= start) & (high_first >= stop)
        return jnp.where(active, jnp.where(full, 2, 1), 0)


def over_blocks(mask, ends, length, block, body, skipped):
    @pl.loop(0, length // block)
    def _(index):
        flag = mask.flag(index, block, ends)
        rows = pl.ds(pl.multiple_of(index * block, block), block)

        @pl.when(flag == 0)
        def _():
            skipped(rows)

        @pl.when(flag == 1)
        def _():
            body(index, rows, True)

        @pl.when(flag == 2)
        def _():
            body(index, rows, False)


def forward_start(q_ref, masked_q, acc, top):
    heads = q_ref.shape[1] // HEAD_DIM
    for head in range(heads):
        pair = q_ref[:, head_columns(head)]
        masked_q[head] = jnp.where(own_lanes(pair.shape, head), pair, jnp.zeros_like(pair))
    acc[...] = jnp.zeros_like(acc)
    top[...] = jnp.full_like(top, NEG)


def forward_block(index, rows, partial, block, kv_ref, mask, masked_q, acc, top):
    heads, count = masked_q.shape[:2]
    width = heads * HEAD_DIM
    if partial:
        allowed = mask.allowed(index, block)
    for head in range(heads):
        cols = head_columns(head)
        scores = lax.dot_general(kv_ref[rows, cols], masked_q[head], NT, preferred_element_type=F32)
        if partial:
            scores = jnp.where(allowed, scores, NEG)
        old = top[head : head + 1, :]
        new = jnp.maximum(old, jnp.max(scores, axis=0, keepdims=True))
        weights = jnp.exp(scores - new).astype(BF16)
        vals = kv_ref[rows, width + cols.start : width + cols.stop]
        vals = jnp.where(own_lanes(vals.shape, head), vals, jnp.ones_like(vals))
        acc[head] = acc[head] * jnp.exp(old - new) + lax.dot_general(
            vals, weights, TN, preferred_element_type=F32
        )
        top[head : head + 1, :] = new


def forward_end(out_ref, lse_ref, acc, top):
    lse_ref[...] = jnp.zeros_like(lse_ref)
    for head in range(acc.shape[0]):
        first = head % 2 * HEAD_DIM
        total = acc[head, HEAD_DIM - first : HEAD_DIM - first + 1, :]
        out_ref[head_rows(head), :] = acc[head, first : first + HEAD_DIM, :] / total
        lse_ref[head : head + 1, :] = top[head : head + 1, :] + jnp.log(total)


def forward_kernel(block, causal, tokens, starts, ends, segments, q_ref, kv_ref, *refs):
    out_ref, lse_ref, masked_q, acc, top = refs[tokens:]
    mask = Mask(causal, starts, segments, ends[2])
    forward_start(q_ref, masked_q, acc, top)

    def body(index, rows, partial):
        forward_block(index, rows, partial, block, kv_ref, mask, masked_q, acc, top)

    over_blocks(mask, ends, kv_ref.shape[0], block, body, lambda rows: None)
    forward_end(out_ref, lse_ref, acc, top)


def backward_start(q_ref, do_ref, dot_ref, out_ref, masked_q, masked_do, delta, dq):
    for head in range(masked_q.shape[0]):
        pair = q_ref[:, head_columns(head)]
        keep = own_lanes(pair.shape, head)
        masked_q[head] = jnp.where(keep, pair, jnp.zeros_like(pair))
        pair = do_ref[:, head_columns(head)]
        masked_do[head] = jnp.where(keep, pair, jnp.zeros_like(pair))
        part = head_rows(head)
        delta[head : head + 1, :] = jnp.sum(
            dot_ref[part, :].astype(F32) * out_ref[part, :], axis=0, keepdims=True
        )
    dq[...] = jnp.zeros_like(dq)


def backward_block(
    index, rows, block, mask, kv_ref, lse_ref, dkv_ref, masked_q, masked_do, delta, dq, between
):
    heads = masked_q.shape[0]
    width = heads * HEAD_DIM
    allowed = mask.allowed(index, block)
    for pair in range(heads // 2):
        if pair == 0:
            between()
        cols = head_columns(2 * pair)
        later = slice(width + cols.start, width + cols.stop)
        keys, vals = kv_ref[rows, cols], kv_ref[rows, later]
        dk = dv = 0.0
        for head in (2 * pair, 2 * pair + 1):
            scores = lax.dot_general(keys, masked_q[head], NT, preferred_element_type=F32)
            probs = jnp.exp(scores - lse_ref[head : head + 1, :])
            probs = jnp.where(allowed, probs, 0.0)
            dprobs = lax.dot_general(vals, masked_do[head], NT, preferred_element_type=F32)
            draw = (probs * (dprobs - delta[head : head + 1, :])).astype(BF16)
            probs = probs.astype(BF16)
            dv = dv + jnp.dot(probs, masked_do[head], preferred_element_type=F32)
            dk = dk + jnp.dot(draw, masked_q[head], preferred_element_type=F32)
            first = head % 2 * HEAD_DIM
            both = lax.dot_general(keys, draw, TN, preferred_element_type=F32)
            dq[head_rows(head), :] += both[first : first + HEAD_DIM]
        dkv_ref[rows, cols] = dk.astype(BF16)
        dkv_ref[rows, later] = dv.astype(BF16)


SCALARS = pl.BlockSpec(memory_space=pltpu.SMEM)
VECTORS = pl.BlockSpec(memory_space=pltpu.VMEM)


ANYWHERE = pl.BlockSpec(memory_space=pl.ANY)


def cost_of(kv, count, width, products):
    flops = 2 * products * kv.shape[0] * count * width
    return pl.CostEstimate(flops=flops, bytes_accessed=flops // 512, transcendentals=0)


def forward_scratch(count, width):
    heads = width // HEAD_DIM
    return [
        pltpu.VMEM((heads, count, 128), BF16),
        pltpu.VMEM((heads, 128, count), F32),
        pltpu.VMEM((8, count), F32),
    ]


def backward_scratch(count, width):
    heads = width // HEAD_DIM
    return [
        pltpu.VMEM((heads, count, 128), BF16),
        pltpu.VMEM((heads, count, 128), BF16),
        pltpu.VMEM((8, count), F32),
        pltpu.VMEM((width, count), F32),
    ]


def attend(queries, kv, mask, tokens):
    count, width = queries.shape
    causal, starts, ends, segments = mask
    return pl.pallas_call(
        functools.partial(forward_kernel, KEY_BLOCK, causal, len(tokens)),
        out_shape=(
            jax.ShapeDtypeStruct((width, count), F32),
            jax.ShapeDtypeStruct((8, count), F32),
        ),
        in_specs=[SCALARS] * 2 + [VECTORS] * 3 + [ANYWHERE] * len(tokens),
        out_specs=(VECTORS,) * 2,
        scratch_shapes=forward_scratch(count, width),
        compiler_params=pltpu.CompilerParams(vmem_limit_bytes=40 << 20),
        cost_estimate=cost_of(kv, count, width, 2),
    )(starts, ends, segments, queries, kv, *tokens)


MESH = pl.DeviceIdType.MESH
DMA = pltpu.SemaphoreType.DMA


class Here:
    def __init__(self, ring):
        self.ring = ring
        self.d, self.z, self.y = (lax.axis_index(a) for a in ("dp", "seq", "tensor"))
        self.core, self.x = lax.rem(self.d, 2), lax.div(self.d, 2)
        self.other_d = self.d + 1 - 2 * self.core
        self.partner = (self.other_d, self.z, self.y)
        self.right = (self.d, self.z + 1, self.y)
        self.left = (self.d, self.z - 1, self.y)
        self.over_x = (self.d + 2 - 4 * lax.rem(self.x, 2), self.z, self.y)
        self.over_y = (self.d, self.z, 1 - self.y)
        self.diagonal = (self.other_d, self.z, 1 - self.y)

    def meet(self, devices):
        barrier = pltpu.get_barrier_semaphore()
        wanted = 0
        for condition, device in devices:

            @pl.when(condition)
            def _(device=device):
                pl.semaphore_signal(barrier, inc=1, device_id=device, device_id_type=MESH)

            wanted = wanted + jnp.where(condition, 1, 0)
        pl.semaphore_wait(barrier, wanted)

    def along_z(self, step):
        return (self.d, lax.rem(self.z + step, self.ring), self.y)

    def everyone(self):
        devices = [self.partner, self.over_x, self.over_y, self.diagonal]
        devices += [self.along_z(step) for step in range(1, self.ring)]
        return [(self.core >= 0, device) for device in devices]

    def crosswise(self):
        return [
            (self.z + 1 < self.ring, (self.other_d, self.z + 1, self.y)),
            (self.z > 0, (self.other_d, self.z - 1, self.y)),
        ]

    def neighbours(self):
        return [
            (self.core >= 0, self.partner),
            (self.z + 1 < self.ring, self.right),
            (self.z > 0, self.left),
        ]


def remote(source, target, sent, received, device):
    return pltpu.make_async_remote_copy(
        src_ref=source,
        dst_ref=target,
        send_sem=sent,
        recv_sem=received,
        device_id=device,
        device_id_type=MESH,
    )


class Gather:
    def __init__(self, here, rows_ref, sems, source=None, owner=None):
        self.here, self.rows_ref, self.source, self.owner = here, rows_ref, source, owner
        self.count = rows_ref.shape[0] // here.ring
        self.size = self.count // (2 * CHUNKS)
        self.sent, self.got, self.core_sent, self.core_got = sems

    def chunk(self, shard, core, chunk):
        start = shard * self.count + core * (self.count // 2) + chunk * self.size
        return self.rows_ref.at[pl.ds(pl.multiple_of(start, self.size), self.size)]

    def ways(self, step):
        here = self.here
        z, ring = here.z, here.ring
        return [
            (0, z - step, z >= step, z - step + 1, (z + 1 < ring) & (z + 1 >= step), here.right),
            (1, z + step, z + step < ring, z + step - 1, (z > 0) & (z + step <= ring), here.left),
        ]

    def along(self, way, step, shard, chunk, device):
        view = self.chunk(shard, self.here.core, chunk)
        k = way * CHUNKS + chunk
        return remote(view, view, self.sent.at[k, step], self.got.at[k, step], device)

    def across(self, way, step, shard, core, chunk):
        view = self.chunk(shard, core, chunk)
        k = way * CHUNKS + chunk
        return remote(
            view, view, self.core_sent.at[k, step], self.core_got.at[k, step], self.here.partner
        )

    def firsts(self):
        found = []
        for chunk in range(CHUNKS):
            for way, _, _, shard, sends, device in self.ways(1):
                if self.source is None:
                    found.append((sends, self.along(way, 1, shard, chunk, device)))
                    continue
                for core in range(2):
                    k = way * CHUNKS + chunk
                    start = core * (self.count // 2) + chunk * self.size
                    to = (self.here.d - self.here.core + core, *device[1:])
                    copy = remote(
                        self.source.at[pl.ds(start, self.size)],
                        self.chunk(shard, core, chunk),
                        self.sent.at[k, core],
                        self.got.at[k, 1],
                        to,
                    )
                    found.append((sends & self.owner, copy))
        return found

    def begin(self):
        for condition, copy in self.firsts():
            pl.when(condition)(copy.start)

    def advance(self, step):
        for chunk in range(CHUNKS):
            for way, shard, comes, _, _, _ in self.ways(step):

                @pl.when(comes)
                def _(way=way, shard=shard, chunk=chunk):
                    self.along(way, step, shard, chunk, self.here.partner).wait_recv()

                _, _, _, _, sends, device = self.ways(step + 1)[way]

                @pl.when(sends)
                def _(way=way, shard=shard, chunk=chunk, device=device):
                    self.along(way, step + 1, shard, chunk, device).start()

                @pl.when(comes)
                def _(way=way, shard=shard, chunk=chunk):
                    self.across(way, step, shard, self.here.core, chunk).start()

    def finish(self):
        for condition, copy in self.firsts():
            pl.when(condition)(copy.wait_send)

        @pl.loop(1, self.here.ring)
        def _(step):
            for chunk in range(CHUNKS):
                for way, shard, comes, out, sends, device in self.ways(step):

                    @pl.when(sends & (step > 1))
                    def _(way=way, out=out, device=device, chunk=chunk):
                        self.along(way, step, out, chunk, device).wait_send()

                    @pl.when(comes)
                    def _(way=way, shard=shard, chunk=chunk):
                        core = self.here.core
                        self.across(way, step, shard, core, chunk).wait_send()
                        self.across(way, step, shard, 1 - core, chunk).wait_recv()


def pieces_of(weights):
    found = []
    for k, weight in enumerate(weights):
        rows, columns = weight.shape[-2:]
        number = 1 if rows % 3 else 3
        while 2 * rows * columns > 655360 * number and rows % (64 * number) == 0:
            number *= 2
        for matrix in range(matrices_of(weight)):
            found += [(k, matrix, i * (rows // number), rows // number) for i in range(number)]
    return found


def matrices_of(weight):
    return weight.shape[0] if len(weight.shape) == 3 else 1


def beside(weight):
    rows, columns = weight.shape[-2:]
    return jax.ShapeDtypeStruct((rows, columns * matrices_of(weight)), weight.dtype)


AHEAD = 4


class Fetch:
    def __init__(self, here, inputs, outputs, sems):
        self.here, self.inputs, self.outputs = here, inputs, outputs
        self.y_sent, self.y_got, self.x_sent, self.x_got, self.core_sent, self.core_got = sems
        self.pieces = pieces_of(inputs)
        self.matrices = [
            (k, matrix)
            for k, given in enumerate(inputs)
            for matrix in range(matrices_of(given))
        ]
        self.number = len(self.pieces)
        self.own = lax.rem(here.x, 2)

    def devices(self):
        here = self.here
        return [(here.core >= 0, here.diagonal), (here.core == 1, here.over_x)]

    def matrix(self, k, matrix):
        given = self.inputs[k]
        return given.at[matrix] if len(given.shape) == 3 else given

    def part(self, p, which):
        k, matrix, start, rows = self.pieces[p]
        first = pl.multiple_of(start + which * (rows // 2), 16)
        return self.matrix(k, matrix).at[pl.ds(first, rows // 2)]

    def place(self, p, which):
        k, matrix, start, rows = self.pieces[p]
        columns = self.inputs[k].shape[-1]
        first = pl.multiple_of(start + which * (rows // 2), 16)
        return self.outputs[k].at[pl.ds(first, rows // 2), pl.ds(matrix * columns, columns)]

    def over_y(self, p):
        return remote(
            self.part(p, self.own),
            self.place(p, self.own),
            self.y_sent.at[p],
            self.y_got.at[p],
            self.here.diagonal,
        )

    def over_x(self, p, which):
        view = self.place(p, which)
        return remote(view, view, self.x_sent.at[p], self.x_got.at[p], self.here.over_x)

    def across(self, m):
        k, matrix = self.matrices[m]
        columns = self.inputs[k].shape[-1]
        return remote(
            self.matrix(k, matrix),
            self.outputs[k].at[:, pl.ds(matrix * columns, columns)],
            self.core_sent.at[m],
            self.core_got.at[m],
            self.here.partner,
        )

    def begin(self):
        @pl.when(self.here.core == 0)
        def _():
            for p in range(min(AHEAD, self.number)):
                self.over_y(p).start()

        @pl.when(self.here.core == 1)
        def _():
            for m in range(len(self.matrices)):
                self.across(m).start()

    def advance(self, p):
        @pl.when(self.here.core == 0)
        def _():
            self.over_y(p).wait_send()
            if p + AHEAD < self.number:
                self.over_y(p + AHEAD).start()

        @pl.when(self.here.core == 1)
        def _():
            self.over_y(p).wait_recv()
            self.over_x(p, self.own).start()

    def end(self):
        @pl.when(self.here.core == 0)
        def _():
            for m in range(len(self.matrices)):
                self.across(m).wait_recv()

        @pl.when(self.here.core == 1)
        def _():
            for p in range(self.number):
                self.over_x(p, self.own).wait_send()
                self.over_x(p, 1 - self.own).wait_recv()
            for m in range(len(self.matrices)):
                self.across(m).wait_send()


def gather_sems(ring):
    return [DMA((2 * CHUNKS, ring))] * 4


def fetch_sems(weights):
    number = len(pieces_of(weights))
    return [DMA((number,))] * 4 + [DMA((3 * len(weights),))] * 2


def opening_kernel(ring, number, *refs):
    inputs, refs = refs[: 9 + number], refs[9 + number :]
    outputs, (vectors, *sems) = refs[: 5 + number], refs[5 + number :]
    source, target, source_seg, target_seg = inputs[:4]
    source_all, target_out, source_seg_out, target_seg_out, vectors_out = outputs[:5]
    shard_sems, vector_sems = sems[:3], sems[3:6]
    here = Here(ring)
    fetch = Fetch(here, inputs[9:], outputs[5:], sems[10:])
    here.meet(here.neighbours() + here.crosswise() + fetch.devices())
    count = source.shape[0]
    own = pl.ds(pl.multiple_of(here.z * count, count), count)
    moves = [
        (source, source_all.at[own]),
        (target, target_out),
        (source_seg, source_seg_out),
        (target_seg, target_seg_out),
    ]
    owner = here.core == here.y

    def shard_copy(k):
        start, end = moves[k]
        sent, got, copied = shard_sems
        return (
            remote(start, end, sent.at[k], got.at[k], here.partner),
            pltpu.make_async_copy(start, end, copied.at[k]),
        )

    def vector_copy():
        sent, got, copied = vector_sems
        return (
            remote(vectors, vectors_out, sent, got, here.diagonal),
            pltpu.make_async_copy(vectors, vectors_out, copied),
        )

    def wait_shard(k):
        across, local = shard_copy(k)

        @pl.when(owner)
        def _():
            across.wait_send()
            local.wait()

        @pl.when(jnp.logical_not(owner))
        def _():
            across.wait_recv()

    gather = Gather(here, source_all, sems[6:10], source, owner)
    gather.begin()

    @pl.when(owner)
    def _():
        for k in range(len(moves)):
            across, local = shard_copy(k)
            across.start()
            local.start()

    fetch.begin()

    vectors[...] = jnp.zeros_like(vectors)
    for row, bias in enumerate(inputs[4:7]):
        width = bias.shape[1]
        for part in range(2):
            value = bias[part : part + 1, :].astype(F32)
            vectors[row : row + 1, 2 * part * width : (2 * part + 1) * width] = value
    for row, bias in enumerate(inputs[7:9]):
        vectors[3 + row : 4 + row, :] = bias[...].astype(F32).reshape(1, -1)

    @pl.when(here.core == 0)
    def _():
        across, local = vector_copy()
        across.start()
        local.start()

    done = 0
    for step in range(1, ring):
        while done < fetch.number * (2 * step - 1) // (2 * ring - 2):
            fetch.advance(done)
            done += 1
        gather.advance(step)
    while done < fetch.number:
        fetch.advance(done)
        done += 1
    gather.finish()
    for k in range(len(moves)):
        wait_shard(k)
    fetch.end()
    across, local = vector_copy()

    @pl.when(here.core == 0)
    def _():
        across.wait_send()
        local.wait()

    @pl.when(here.core == 1)
    def _():
        across.wait_recv()


def opening(ring, source, target, source_seg, target_seg, biases, weights):
    inputs = (source, target, source_seg, target_seg, *biases, *weights)
    count, model = source.shape
    number = len(weights)
    units = biases[-1].shape[0]
    shapes = (
        jax.ShapeDtypeStruct((ring * count, model), BF16),
        jax.ShapeDtypeStruct(target.shape, BF16),
        jax.ShapeDtypeStruct(source_seg.shape, jnp.int32),
        jax.ShapeDtypeStruct(target_seg.shape, jnp.int32),
        jax.ShapeDtypeStruct((8, units), F32),
    ) + tuple(beside(weight) for weight in weights)
    return pl.pallas_call(
        functools.partial(opening_kernel, ring, number),
        out_shape=shapes,
        in_specs=[VECTORS] * 9 + [ANYWHERE] * number,
        out_specs=(ANYWHERE,) + (VECTORS,) * 4 + (ANYWHERE,) * number,
        scratch_shapes=[pltpu.VMEM((8, units), F32)]
        + [DMA((4,))] * 3
        + [DMA] * 3
        + gather_sems(ring)
        + fetch_sems(weights),
        compiler_params=pltpu.CompilerParams(collective_id=1, has_side_effects=True),
    )(*inputs)


def gather_attend_kernel(
    block, causal, ring, number, tokens, starts, segments, bias_ref, own_ref, rows_ref, proj_ref, *refs
):
    weights, refs = refs[:number], refs[number + tokens :]
    q_ref, kv_ref, out_ref, lse_ref, all_ref = refs[:5]
    fetched, refs = refs[5 : 5 + number], refs[5 + number :]
    masked_q, acc, top, rows_in, proj, copied, rows_copied, proj_copied = refs[:8]
    here = Here(ring)
    gather = Gather(here, all_ref, refs[8:12])
    fetch = Fetch(here, weights, fetched, refs[12:])
    count, width = q_ref.shape
    first_row = pl.multiple_of(here.z * count, count)

    def rows_copy(shard):
        rows = pl.ds(pl.multiple_of(shard * count, count), count)
        return pltpu.make_async_copy(rows_ref.at[rows], rows_in.at[rows], rows_copied.at[shard])

    proj_copy = pltpu.make_async_copy(proj_ref, proj, proj_copied)
    proj_copy.start()
    for shard in range(ring):
        rows_copy(shard).start()
    here.meet(here.neighbours() + fetch.devices())
    local = pltpu.make_async_copy(own_ref, all_ref.at[pl.ds(first_row, count)], copied)
    local.start()
    fetch.begin()
    local.wait()
    gather.begin()
    mask = Mask(causal, starts, segments, first_row)
    proj_copy.wait()
    for shard in range(ring):
        rows_copy(shard).wait()
    queries = dot_plain(rows_in[pl.ds(first_row, count), :], proj[:, :width]) + bias_ref[:, :width]
    q_ref[...] = (queries.astype(BF16).astype(F32) * HEAD_DIM ** (-0.5)).astype(BF16)
    forward_start(q_ref, masked_q, acc, top)
    blocks = kv_ref.shape[0] // block

    @pl.loop(0, blocks)
    def _(index):
        rows = pl.ds(pl.multiple_of(index * block, block), block)
        both = dot_plain(rows_in[rows, :], proj[:, width:]) + bias_ref[:, width:]
        kv_ref[rows, :] = both.astype(BF16)
        forward_block(index, rows, True, block, kv_ref, mask, masked_q, acc, top)

        @pl.when((index >= 1) & (index < ring))
        def _():
            gather.advance(index)

        for p in range(fetch.number):
            pl.when(index == 1 + p * (blocks - 1) // fetch.number)(
                functools.partial(fetch.advance, p)
            )

    forward_end(out_ref, lse_ref, acc, top)
    gather.finish()
    fetch.end()


def gather_attend(number, ring, rows, proj, bias, mask, own, weights, tokens=()):
    length, model = rows.shape
    count, width = length // ring, proj.shape[1] // 3
    causal, starts, _, segments = mask
    fetched = len(weights)
    kv = jax.ShapeDtypeStruct((length, 2 * width), BF16)
    return pl.pallas_call(
        functools.partial(gather_attend_kernel, KEY_BLOCK, causal, ring, fetched, len(tokens)),
        out_shape=(
            jax.ShapeDtypeStruct((count, width), BF16),
            kv,
            jax.ShapeDtypeStruct((width, count), F32),
            jax.ShapeDtypeStruct((8, count), F32),
            jax.ShapeDtypeStruct((ring * own.shape[0], own.shape[1]), BF16),
        )
        + tuple(beside(weight) for weight in weights),
        in_specs=[SCALARS] + [VECTORS] * 3 + [ANYWHERE] * (2 + fetched + len(tokens)),
        out_specs=(VECTORS,) * 4 + (ANYWHERE,) * (1 + fetched),
        scratch_shapes=forward_scratch(count, width)
        + [
            pltpu.VMEM((length, model), BF16),
            pltpu.VMEM(proj.shape, BF16),
            DMA,
            DMA((ring,)),
            DMA,
        ]
        + gather_sems(ring)
        + fetch_sems(weights),
        compiler_params=pltpu.CompilerParams(
            vmem_limit_bytes=50 << 20, collective_id=number, has_side_effects=True
        ),
        cost_estimate=cost_of(kv, count, width, 4),
    )(starts, segments, bias, own, rows, proj, *weights, *tokens)


class Part:
    def __init__(self, inputs, in_specs, out_shapes, scratch, bind):
        self.inputs, self.in_specs, self.out_shapes = inputs, in_specs, out_shapes
        self.scratch, self.bind = scratch, bind


def run_parts(number, body, parts, cost=None):
    ring = lax.axis_size("seq")
    counts = [(len(p.inputs), len(p.out_shapes), len(p.scratch)) for p in parts]

    def kernel(*refs):
        here = Here(ring)
        taken, offset = [[] for _ in parts], 0
        for kind in range(3):
            for refs_of, count in zip(taken, counts):
                refs_of.append(refs[offset : offset + count[kind]])
                offset += count[kind]
        here.meet(here.everyone())
        body(here, *(p.bind(here, *refs_of) for p, refs_of in zip(parts, taken)))

    results = pl.pallas_call(
        kernel,
        out_shape=[shape for p in parts for shape in p.out_shapes],
        in_specs=[spec for p in parts for spec in p.in_specs],
        out_specs=[VECTORS for p in parts for _ in p.out_shapes],
        scratch_shapes=[shape for p in parts for shape in p.scratch],
        compiler_params=pltpu.CompilerParams(
            vmem_limit_bytes=62 << 20, collective_id=number, has_side_effects=True
        ),
        cost_estimate=cost,
    )(*(array for p in parts for array in p.inputs))
    given = []
    for _, count, _ in counts:
        given.append(results[:count])
        results = results[count:]
    return given


class Stage:
    def __init__(self, here, kind, source, result, buffers, sems):
        self.here, self.kind, self.source, self.result = here, kind, source, result
        self.buffers, (self.sent, self.got) = buffers, sems
        rows = source.shape[0]
        if kind == "x":
            half = rows // 2
            self.kept = [half * here.x]
            self.given = [half * (1 - here.x)]
            self.size, self.to = half, here.over_x
        elif kind == "y":
            self.size = 192
            self.starts = list(range(0, rows, 2 * self.size))
        elif kind == "v":
            bit = lax.rem(here.z, 2)
            self.size = rows // 4
            self.kept = [self.size * bit, self.size * (bit + 2)]
            self.given = [self.size * (1 - bit), self.size * (3 - bit)]
            self.to = (here.d, here.z + 1 - 2 * bit, here.y)
        else:
            bit = lax.div(here.z, 2)
            self.size = rows // 2
            self.kept, self.given = [self.size * bit], [self.size * (1 - bit)]
            self.to = (here.d, here.z + 2 - 4 * bit, here.y)

    def rows(self, start):
        if not isinstance(start, int):
            start = pl.multiple_of(start, 16)
        return pl.ds(start, self.size)

    def move(self, start, place, buffer, sem, to):
        return remote(
            self.source.at[self.rows(start)],
            self.buffers[buffer].at[self.rows(place * self.size)],
            self.sent.at[sem],
            self.got.at[sem],
            to,
        )

    def moves(self):
        here = self.here
        if self.kind != "y":
            both = [
                (None, self.move(start, k, 0, k, self.to)) for k, start in enumerate(self.given)
            ]
            return both, both
        sends, arrivals = [], []
        for k, start in enumerate(self.starts):
            upper = start + self.size
            sends.append((here.core == 0, self.move(upper, k, 0, 2 * k, here.partner)))
            sends.append((here.core == 1, self.move(start, k, 0, 2 * k, here.diagonal)))
            sends.append((here.core == 1, self.move(upper, k, 1, 2 * k + 1, here.over_y)))
            arrivals.append((None, self.move(upper, k, 0, 2 * k, here.partner)))
            arrivals.append((here.core == 1, self.move(upper, k, 1, 2 * k + 1, here.over_y)))
        return sends, arrivals

    @staticmethod
    def each(moves, act):
        for condition, copy in moves:
            if condition is None:
                act(copy)
            else:
                pl.when(condition)(functools.partial(act, copy))

    def begin(self):
        self.each(self.moves()[0], lambda copy: copy.start())

    def end(self):
        sends, arrivals = self.moves()
        self.each(arrivals, lambda copy: copy.wait_recv())
        kept = self.kept if self.kind != "y" else self.starts
        for k, start in enumerate(kept):
            place = self.rows(k * self.size)

            def add(own_ref, own, place=place):
                both = own_ref[own, :].astype(F32) + self.buffers[0][place, :].astype(F32)
                self.result[place, :] = both.astype(self.result.dtype)

            if self.kind == "y":
                pl.when(self.here.core == 0)(functools.partial(add, self.source, self.rows(start)))
                pl.when(self.here.core == 1)(functools.partial(add, self.buffers[1], place))
            else:
                add(self.source, self.rows(start))
        self.each(sends, lambda copy: copy.wait_send())


class Chain:
    def __init__(self, stages, times):
        self.stages, self.times = stages, times

    def event(self, time):
        for k, own in enumerate(self.times):
            if own == time:
                if k:
                    self.stages[k - 1].end()
                if k < len(self.stages):
                    self.stages[k].begin()


def chain(array, kinds, times, made=None):
    rows, columns = made[2] if made else array.shape
    scratch, shapes = [], []
    for kind in kinds:
        rows = rows // 2
        scratch += [pltpu.VMEM((rows, columns), BF16)] * (2 if kind == "y" else 1)
        scratch += [DMA((4,))] * 2
        shapes.append((rows, columns))
    scratch += [pltpu.VMEM(shape, BF16) for shape in shapes[:-1]]
    final = jax.ShapeDtypeStruct(shapes[-1], F32 if kinds[-1] == "w" else BF16)

    def bind(here, inputs, outputs, refs):
        refs = list(refs)
        results = refs[len(refs) - len(kinds) + 1 :] + [outputs[0]]
        source, stages = made[0][made[1]] if made else inputs[0], []
        for kind, result in zip(kinds, results):
            buffers = [refs.pop(0) for _ in range(2 if kind == "y" else 1)]
            sems = [refs.pop(0) for _ in range(2)]
            stages.append(Stage(here, kind, source, result, buffers, sems))
            source = result
        return Chain(stages, times)

    inputs = () if made else (array,)
    return Part(inputs, [VECTORS] * len(inputs), [final], scratch, bind)


def closing_kernel(flag, *refs):
    given, outputs, held, copied = refs[:22], refs[22:47], refs[47:69], refs[69]
    copies = [
        pltpu.make_async_copy(start, end, copied.at[k])
        for k, (start, end) in enumerate(zip(given, held))
    ]
    for copy in copies:
        copy.start()
    for copy in copies:
        copy.wait()
    rows, vectors, grads = held[:8], held[8], held[9:22]
    keeps = flag[0] == 1
    for k in range(4):
        own, other = rows[2 * k][...], rows[2 * k + 1][...]
        outputs[k][...] = jnp.where(keeps, own, other).astype(outputs[k].dtype)
    for k in range(3):
        of_q, of_kv = grads[3 * k], grads[3 * k + 2]
        qkv = outputs[4 + k]
        width = of_q.shape[1]
        qkv[0] = of_q[...]
        qkv[1] = of_kv[:, :width]
        qkv[2] = of_kv[:, width:]
    outputs[7][...] = grads[9][...]
    outputs[8][...] = grads[11][...]
    for k in range(3):
        outputs[9 + k][...] = grads[3 * k + 1][...]
    for k in range(2):
        outputs[12 + k][...] = grads[10 + 2 * k][...]
    row = 0
    for out in outputs[14:20]:
        out[...] = vectors[row : row + out.shape[0], :]
        row += out.shape[0]
    for out in outputs[20:23]:
        width = out.shape[1]
        out[0:1, :] = vectors[row : row + 1, :width]
        out[1:2, :] = vectors[row : row + 1, width:]
        row += 1
    columns = vectors.shape[1]
    for out in outputs[23:]:
        for part in range(out.shape[0] // columns):
            out[part * columns : (part + 1) * columns] = vectors[row, :]
            row += 1


def closing(flag, rows, vectors, grads, sizes):
    part, width = grads[0].shape
    units = grads[9].shape[1]
    model = vectors.shape[1]
    shapes = [(rows[0].shape, BF16)] * 2 + [(rows[0].shape, F32)] * 2
    matrices = [(3, part, width)] * 3 + [(part, units)] * 2 + [(part, width)] * 3 + [(part, units)] * 2
    matrices += [(size, model) for size in sizes] + [(2, width)] * 3 + [(units,)] * 2
    shapes += [(shape, F32) for shape in matrices]
    inputs = (flag, *rows, vectors, *grads)
    return pl.pallas_call(
        closing_kernel,
        out_shape=[jax.ShapeDtypeStruct(*shape) for shape in shapes],
        in_specs=[SCALARS] + [ANYWHERE] * (len(inputs) - 1),
        out_specs=[VECTORS] * len(shapes),
        scratch_shapes=[pltpu.VMEM(value.shape, value.dtype) for value in inputs[1:]]
        + [DMA((len(inputs) - 1,))],
        compiler_params=pltpu.CompilerParams(vmem_limit_bytes=62 << 20),
    )(*inputs)


class HandOut:
    def __init__(self, here, inputs, outputs, scratch, times):
        self.here, self.times = here, times
        self.sent, self.got = scratch
        self.copies = [
            remote(given, taken, self.sent.at[k], self.got.at[k], here.over_y)
            for k, (given, taken) in enumerate(zip(inputs, outputs))
        ]

    def event(self, time):
        owns = self.here.core == self.here.y
        for copy in self.copies:
            if time == self.times[0]:
                pl.when(owns)(copy.start)
            if time == self.times[1]:
                pl.when(owns)(copy.wait_send)
                pl.when(jnp.logical_not(owns))(copy.wait_recv)


def hand_out(rows, times):
    number = len(rows)
    return Part(
        tuple(rows),
        [VECTORS] * number,
        [jax.ShapeDtypeStruct(value.shape, value.dtype) for value in rows],
        [DMA((number,))] * 2,
        lambda here, *refs: HandOut(here, *refs, times),
    )


class Small:
    def __init__(self, here, rows, held_rows, given, result, refs, times):
        self.here, self.given, self.result, self.times = here, given, result, times
        self.rows, self.held_rows = rows, held_rows
        self.arrived, self.sent, self.got = refs
        self.bits = [lax.rem(here.z, 2), lax.div(here.z, 2)]

    def copies(self, stage):
        here = self.here
        low, high = self.bits

        def to(device, slot, source=self.result, target=None):
            target = self.arrived.at[slot] if target is None else target
            return remote(source, target, self.sent.at[slot], self.got.at[slot], device)

        if stage < 3:
            device = (
                here.over_x,
                (here.d, here.z + 1 - 2 * low, here.y),
                (here.d, here.z + 2 - 4 * high, here.y),
            )[stage]
            both = [(None, to(device, stage))]
            return both, both
        if stage == 3:
            sends = [
                (None, to(here.over_y, 3)),
                (here.core == 0, to(here.partner, 4)),
                (here.core == 1, to(here.diagonal, 4)),
            ]
            return sends, sends[:1] + [(None, to(here.partner, 4))]
        return [(here.core == 0, to(here.partner, 5))], [(here.core == 1, to(here.partner, 5))]

    def end(self, stage):
        sends, arrivals = self.copies(stage)
        Stage.each(arrivals, lambda copy: copy.wait_recv())
        Stage.each(sends, lambda copy: copy.wait_send())
        core = self.here.core
        if stage < 3:
            self.result[...] += self.arrived[stage]
        elif stage == 3:
            whole, halves = slice(0, self.held_rows), slice(self.held_rows, self.rows)
            self.result[whole, :] += self.arrived[3, whole, :]
            own = jnp.where(core == 0, self.result[halves, :], self.arrived[3, halves, :])
            self.result[halves, :] = own + self.arrived[4, halves, :]
        else:
            whole = slice(0, self.held_rows)

            @pl.when(core == 1)
            def _():
                self.result[whole, :] = self.arrived[5, whole, :]

    def event(self, time):
        for k, own in enumerate(self.times):
            if own == time:
                if k == 0:
                    self.result[...] = self.given[...]
                else:
                    self.end(k - 1)
                if k < 5:
                    Stage.each(self.copies(k)[0], lambda copy: copy.start())


def small_sums(whole, halves, times):
    both = jnp.concatenate([whole, halves])
    rows, columns = both.shape
    shape = jax.ShapeDtypeStruct(both.shape, F32)
    part = Part(
        (both,),
        [VECTORS],
        [shape],
        [pltpu.VMEM((6, rows, columns), F32), DMA((6,)), DMA((6,))],
        lambda here, inputs, outputs, refs: Small(
            here, rows, whole.shape[0], inputs[0], outputs[0], refs, times
        ),
    )
    part.rows, part.vectors = whole.shape[0], (whole.reshape(-1), halves.reshape(-1))
    return part


def run_chains(number, chains, events):
    def body(here, *bound):
        for time in range(events):
            for one in bound:
                one.event(time)

    return run_parts(number, body, chains)


class Back:
    def __init__(self, here, causal, apart, inputs, outputs, scratch):
        self.here, self.causal, self.apart = here, causal, apart
        self.starts, self.segments, self.q, self.kv, self.do, self.dot, self.out, self.lse = inputs[:8]
        self.weights = inputs[8]
        self.dq_out, self.dkv, self.sum = outputs[:3]
        self.query_sum = outputs[3] if apart else None
        self.work, scratch = scratch[:4], scratch[4:]
        self.terms, self.from_core, self.outgoing, self.arrived, self.total = scratch[:5]
        self.core_sent, self.core_got, self.sent, self.got, self.end_sent, self.end_got = scratch[5:11]
        if apart:
            self.query_low, self.query_got, self.query_sems = scratch[11:]
        self.count, self.width = self.q.shape
        self.part = self.count // 2
        self.mask = Mask(causal, self.starts, self.segments, here.z * self.count)

    def half(self, core):
        return pl.ds(pl.multiple_of(core * self.part, self.part), self.part)

    def shard_at(self, turn):
        ring, z, shard = self.here.ring, self.here.z, 0
        for device in range(ring):
            others = [t for t in range(ring) if t != device]
            others.sort(key=lambda t: (ring - t + device) if t > device else (t + ring - device))
            for k, other in enumerate(others):
                shard = jnp.where((z == device) & (turn == k + 1), other, shard)
        return shard

    def across(self, turn, shard):
        return remote(
            self.terms.at[lax.rem(turn, 2), self.half(1 - self.here.core)],
            self.from_core.at[shard],
            self.core_sent.at[shard],
            self.core_got.at[shard],
            self.here.partner,
        )

    def slot(self, way, shard, z):
        return jnp.where((way == 1) & (shard == z), self.here.ring, shard)

    def chunk(self, chunk):
        size = self.part // CHUNKS
        return pl.ds(chunk * size, size)

    def along(self, way, shard, chunk, device):
        rows = self.chunk(chunk)
        return remote(
            self.outgoing.at[shard, rows],
            self.arrived.at[self.slot(way, shard, device[1]), rows],
            self.sent.at[chunk, shard],
            self.got.at[way * CHUNKS + chunk, shard],
            device,
        )

    def put(self, turn, shard, terms):
        @pl.when(turn > 2)
        def _():
            self.across(turn - 2, self.shard_at(turn - 2)).wait_send()

        slot = lax.rem(turn, 2)
        self.terms[slot] = terms.astype(BF16)
        self.across(turn, shard).start()
        self.outgoing[shard] = self.terms[slot, self.half(self.here.core), :]

    def both(self, shard):
        self.across(0, shard).wait_recv()
        return self.outgoing[shard].astype(F32) + self.from_core[shard].astype(F32)

    def take(self, way, shard, chunk):
        rows = self.chunk(chunk)
        self.along(way, shard, chunk, self.here.partner).wait_recv()
        slot = self.slot(way, shard, self.here.z)
        self.total[rows, :] += self.arrived[slot, rows, :].astype(F32)

    def forward(self, shard):
        here = self.here
        self.total[...] = self.both(shard)
        ways = (
            (0, shard > here.z, here.z > 0, here.right),
            (1, shard < here.z, here.z + 1 < here.ring, here.left),
        )
        for chunk in range(CHUNKS):
            rows = self.chunk(chunk)
            for way, mine, comes, _ in ways:
                pl.when(mine & comes)(functools.partial(self.take, way, shard, chunk))
            self.outgoing[shard, rows, :] = self.total[rows, :].astype(BF16)
            for way, mine, _, device in ways:

                @pl.when(mine)
                def _(way=way, device=device, chunk=chunk):
                    self.along(way, shard, chunk, device).start()

    def block(self, shard, between):
        rows = pl.ds(pl.multiple_of(shard * self.count, self.count), self.count)
        backward_block(
            shard, rows, self.count, self.mask, self.kv, self.lse, self.dkv, *self.work, between
        )
        return dot_last(self.dkv[rows, :], self.weights[:, self.width :])

    def run(self, event):
        here, ring = self.here, self.here.ring
        at_end = (here.z == 0) | (here.z == ring - 1)
        event(0)
        backward_start(self.q, self.do, self.dot, self.out, *self.work)

        @pl.loop(1, ring)
        def _(turn):
            shard = self.shard_at(turn)

            def between():
                @pl.when((turn > 1) & at_end)
                def _():
                    self.forward(self.shard_at(turn - 1))

            self.put(turn, shard, self.block(shard, between))
            for time in range(1, ring):
                pl.when(turn == time)(functools.partial(event, time))

        def between():
            self.forward(self.shard_at(jnp.where(at_end, ring - 1, 1)))

        own = self.block(here.z, between)
        event(ring)
        low = (self.work[3][...] * HEAD_DIM ** (-0.5)).T.astype(BF16)
        self.dq_out[...] = low
        query = dot_last(low, self.weights[:, : self.width])
        if self.apart:
            self.query_low[...] = query.astype(BF16)
            exchange = remote(
                self.query_low, self.query_got, self.query_sems.at[0], self.query_sems.at[1], here.partner
            )
            exchange.start()
        else:
            own = own + query
        self.put(jnp.int32(ring), here.z, own)
        if self.apart:
            exchange.wait()
            self.query_sum[...] = self.query_low[...].astype(F32) + self.query_got[...].astype(F32)

        @pl.when(jnp.logical_not(at_end))
        def _():
            @pl.loop(2, ring)
            def _(turn):
                self.forward(self.shard_at(turn))

        event(ring + 1)
        self.total[...] = self.both(here.z)
        for chunk in range(CHUNKS):
            for way, comes in ((0, here.z > 0), (1, here.z + 1 < ring)):
                pl.when(comes)(functools.partial(self.take, way, here.z, chunk))

        own, other = self.half(here.core), self.half(1 - here.core)
        self.sum[own, :] = self.total[...].astype(BF16)
        for half, waits in ((own, False), (other, True)):
            view = self.sum.at[half]
            copy = remote(view, view, self.end_sent, self.end_got, here.partner)
            if waits:
                copy.wait_recv()
            else:
                copy.start()
                copy.wait_send()
        self.across(ring - 1, self.shard_at(ring - 1)).wait_send()
        self.across(ring, here.z).wait_send()
        for shard in range(ring):

            @pl.when(here.z != shard)
            def _(shard=shard):
                for chunk in range(CHUNKS):
                    self.along(0, shard, chunk, here.partner).wait_send()

        event(ring + 2)


class Products:
    def __init__(self, back, inputs, of_bias, made, scratch, time):
        self.back, self.time = back, time
        self.query_in, self.key_in, self.grad_branch, self.mixed = inputs
        self.of_bias = of_bias
        self.of_q, self.of_out, self.of_kv = made
        self.blocks, self.copied = scratch

    def copy(self, index):
        part = pl.ds(pl.multiple_of(index * 128, 128), 128)
        slot = lax.rem(index, 2)
        return pltpu.make_async_copy(
            self.key_in.at[:, part], self.blocks.at[slot], self.copied.at[slot]
        )

    def event(self, time):
        if time == 0:
            self.copy(0).start()
        if time != self.time:
            return
        dq, dkv = self.back.dq_out, self.back.dkv
        width = dq.shape[1]
        number = self.of_kv.shape[0] // 128

        @pl.loop(0, number)
        def _(index):
            @pl.when(index + 1 < number)
            def _():
                self.copy(index + 1).start()

            self.copy(index).wait()
            part = pl.ds(pl.multiple_of(index * 128, 128), 128)
            block = self.blocks[lax.rem(index, 2)]
            self.of_kv[part, :] = dot_first(block, dkv[...]).astype(BF16)

        self.of_q[...] = dot_first(self.query_in[...], dq[...]).astype(BF16)
        self.of_out[...] = dot_first(self.grad_branch[...], self.mixed[...].T).astype(BF16)
        self.of_bias[0:1, :] = jnp.sum(dq[...].astype(F32), axis=0, keepdims=True)
        self.of_bias[1:2, :] = jnp.sum(dkv[:, width:].astype(F32), axis=0, keepdims=True)


def products(box, query_in, key_in, grad_branch, mixed, time, begins):
    model, width = query_in.shape[1], mixed.shape[0]
    shapes = ((model, width), (model, width), (model, 2 * width))

    def bind(here, inputs, outputs, refs):
        made = refs[2:] if begins else outputs[1:]
        for k in range(3):
            box[k] = made[k]
        return Products(box["back"], inputs, outputs[0], made, refs[:2], time)

    part = Part(
        (query_in, key_in, grad_branch, mixed),
        [VECTORS, ANYWHERE, VECTORS, VECTORS],
        [jax.ShapeDtypeStruct((2, width), F32)]
        + ([] if begins else [jax.ShapeDtypeStruct(shape, BF16) for shape in shapes]),
        [pltpu.VMEM((2, key_in.shape[0], 128), BF16), DMA((2,))]
        + ([pltpu.VMEM(shape, BF16) for shape in shapes] if begins else []),
        bind,
    )
    if not begins:
        return [part]
    firsts = [
        chain(None, kind, (time, 6), (box, k, shape)) for k, (kind, shape) in enumerate(zip("yyx", shapes))
    ]
    return [part, *firsts]


class FeedBack:
    def __init__(self, here, inputs, outputs, scratch, time):
        self.here, self.time = here, time
        self.grad, self.x_in = inputs[:2]
        self.streamed = inputs[2:]
        self.sum, self.of_bias, self.of_in, self.of_out = outputs
        self.blocks, scratch = scratch[:4], scratch[4:]
        self.x_turned, self.grad_turned, self.low, self.got, self.copied, self.sems = scratch

    def event(self, time):
        if time != self.time:
            return
        span = self.blocks[0].shape[2]
        number = self.of_in.shape[1] // span
        self.sum[...] = jnp.zeros_like(self.sum)

        def columns(index):
            return pl.ds(pl.multiple_of(index * span, span), span)

        def copies(index):
            slot, part = lax.rem(index, 2), columns(index)
            return [
                pltpu.make_async_copy(
                    ref.at[part] if k == 3 else ref.at[:, part],
                    self.blocks[k].at[slot],
                    self.copied.at[k, slot],
                )
                for k, ref in enumerate(self.streamed)
            ]

        for copy in copies(0):
            copy.start()

        @pl.loop(0, self.x_turned.shape[0] // span)
        def _(index):
            part = columns(index)
            self.x_turned[part, :] = self.x_in[:, part].T
            self.grad_turned[part, :] = self.grad[:, part].T

        @pl.loop(0, number)
        def _(index):
            part = columns(index)

            @pl.when(index + 1 < number)
            def _():
                for copy in copies(index + 1):
                    copy.start()

            for copy in copies(index):
                copy.wait()
            slope, active, w_in, w_out = (block.at[lax.rem(index, 2)] for block in self.blocks)
            hidden = (slope[...] * dot_last(self.grad[...], w_out[...])).astype(BF16)
            self.of_bias[:, part] = jnp.sum(hidden.astype(F32), axis=0, keepdims=True)
            self.sum[...] += dot_last(hidden, w_in[...])
            self.of_in[:, part] = dot_plain(self.x_turned[...], hidden).astype(BF16)
            self.of_out[:, part] = dot_plain(self.grad_turned[...], active[...]).astype(BF16)

        self.low[...] = self.sum[...].astype(BF16)
        exchange = remote(self.low, self.got, self.sems.at[0], self.sems.at[1], self.here.partner)
        exchange.start()
        exchange.wait()
        self.sum[...] = self.low[...].astype(F32) + self.got[...].astype(F32)


def feed_back(grad_branch, slope, w_in, w_out, x_in, active, time):
    count, model = x_in.shape
    units = w_in.shape[1]
    span = 256
    return Part(
        (grad_branch, x_in, slope, active, w_in, w_out),
        [VECTORS] * 2 + [ANYWHERE] * 4,
        [
            jax.ShapeDtypeStruct((count, model), F32),
            jax.ShapeDtypeStruct((1, units), F32),
            jax.ShapeDtypeStruct((model, units), BF16),
            jax.ShapeDtypeStruct((model, units), BF16),
        ],
        [
            pltpu.VMEM((2, count, span), slope.dtype),
            pltpu.VMEM((2, count, span), BF16),
            pltpu.VMEM((2, model, span), BF16),
            pltpu.VMEM((2, span, model), BF16),
            pltpu.VMEM((model, count), BF16),
            pltpu.VMEM((model, count), BF16),
            pltpu.VMEM((count, model), BF16),
            pltpu.VMEM((count, model), BF16),
            DMA((4, 2)),
            DMA((2,)),
        ],
        lambda here, *refs: FeedBack(here, *refs, time),
    )


def attend_back(number, saved, grad_mixed, grad_mixed_t, weights, mask, apart, more, box):
    queries, kv, output, lse, _ = saved
    causal, starts, segments = mask
    ring = lax.axis_size("seq")
    count, width = queries.shape
    model = weights.shape[0]
    part = count // 2
    shapes = [
        jax.ShapeDtypeStruct((count, width), BF16),
        jax.ShapeDtypeStruct(kv.shape, BF16),
        jax.ShapeDtypeStruct((count, model), BF16),
    ]
    scratch = backward_scratch(count, width) + [
        pltpu.VMEM((2, count, model), BF16),
        *[pltpu.VMEM((ring, part, model), BF16)] * 2,
        pltpu.VMEM((ring + 1, part, model), BF16),
        pltpu.VMEM((part, model), F32),
        *[DMA((ring,))] * 2,
        DMA((CHUNKS, ring)),
        DMA((2 * CHUNKS, ring)),
        *[DMA] * 2,
    ]
    if apart:
        shapes.append(jax.ShapeDtypeStruct((count, model), F32))
        scratch += [pltpu.VMEM((count, model), BF16)] * 2 + [DMA((2,))]
    main = Part(
        (starts, segments, queries, kv, grad_mixed, grad_mixed_t, output, lse, weights),
        [SCALARS] + [VECTORS] * 8,
        shapes,
        scratch,
        lambda here, *refs: box.setdefault("back", Back(here, causal, apart, *refs)),
    )

    def body(here, back, *bound):
        def event(time):
            for one in bound:
                one.event(time)

        back.run(event)

    return run_parts(number, body, [main] + list(more), cost_of(kv, count, width, 7))


class Plan:
    def __init__(self, kernels):
        self.kernels = kernels

    def chains(self, wanted):
        return [chain(*one) for one in wanted] if self.kernels else []

    def given(self, wanted, results):
        return results if self.kernels else [one[0] for one in wanted]


class Places:
    def __init__(self, pairs, ring):
        self.pairs, self.ring = pairs, ring
        self.d = lax.axis_index("dp")
        self.x, self.core = self.d // 2, self.d % 2
        self.y, self.z = lax.axis_index("tensor"), lax.axis_index("seq")

    def swap_core(self, value):
        return lax.ppermute(value, "dp", [(i, i ^ 1) for i in range(self.pairs)])

    def swap_y(self, value):
        return lax.ppermute(value, "tensor", [(0, 1), (1, 0)])

    def swap_x(self, value, bit):
        return lax.ppermute(value, "dp", [(i, i ^ (2 << bit)) for i in range(self.pairs)])

    def swap_z(self, value, bit):
        return lax.ppermute(value, "seq", [(i, i ^ (1 << bit)) for i in range(self.ring)])

    def from_z(self, value, step):
        return lax.ppermute(value, "seq", [((i + step) % self.ring, i) for i in range(self.ring)])

    def to_z(self, value, step):
        return lax.ppermute(value, "seq", [(i, (i + step) % self.ring) for i in range(self.ring)])

    def permute(self, value, source_of):
        moves = []
        for d in range(self.pairs):
            for y in range(2):
                source = source_of(d, y)
                if source is not None:
                    moves.append((source[0] * 2 + source[1], d * 2 + y))
        return lax.ppermute(value, ("dp", "tensor"), moves)

    def fetch_weight(self, value):
        return self.permute(value, lambda d, y: (d + 1, y) if d % 2 == 0 else (d - 1, 1 - y))

    def core_sum(self, partial):
        low = rounded(partial)
        return low + self.swap_core(low.astype(BF16)).astype(F32)

    def own_pair(self, rows):
        return jnp.where(self.core == self.y, rows, self.swap_core(rows))

    def others(self, rows):
        return self.permute(rows, lambda d, y: (d, 1 - y) if d % 2 != y else None)

    def plan(self):
        return Plan(self.pairs == 4 and self.ring == 4)

    def scatter(self, grad, x_first):
        rows, columns = grad.shape
        owners = self.pairs // 2
        grad = grad.reshape(owners, 2, self.ring, rows // (self.pairs * self.ring), columns)
        for stage in "xyz" if x_first else "yxz":
            if stage == "y":
                kept = lax.dynamic_index_in_dim(grad, self.core, grad.ndim - 4, False)
                sent = lax.dynamic_index_in_dim(grad, 1 - self.core, grad.ndim - 4, False)
                first = self.permute(
                    sent, lambda d, y: (d + 1, 1 - y) if d % 2 == 0 else (d - 1, y)
                )
                second = self.permute(kept, lambda d, y: (d, 1 - y) if d % 2 else None)
                kept = jnp.where(self.core == 0, kept, second)
                grad = (kept.astype(F32) + first.astype(F32)).astype(BF16)
            else:
                axis = 0 if stage == "x" else grad.ndim - 3
                place, swap = (self.x, self.swap_x) if stage == "x" else (self.z, self.swap_z)
                size, bit = grad.shape[axis], 0
                while size > 1:
                    shape = grad.shape[:axis] + (size // 2, 2) + grad.shape[axis + 1 :]
                    grad = grad.reshape(shape)
                    mine = (place >> bit) & 1
                    kept = lax.dynamic_index_in_dim(grad, mine, axis + 1, False)
                    sent = lax.dynamic_index_in_dim(grad, 1 - mine, axis + 1, False)
                    grad = kept.astype(F32) + swap(sent, bit).astype(F32)
                    size, bit = size // 2, bit + 1
                    if stage == "x" or size > 1:
                        grad = grad.astype(BF16)
                grad = lax.squeeze(grad, (axis,))
        return grad.astype(F32)

    def all_sum(self, whole, halves):
        both = jnp.concatenate([whole, halves])
        for bit in range((self.pairs // 2).bit_length() - 1):
            both = both + self.swap_x(both, bit)
        for bit in range(self.ring.bit_length() - 1):
            both = both + self.swap_z(both, bit)
        whole, halves = both[: whole.shape[0]], both[whole.shape[0] :]
        whole = whole + self.swap_y(whole)
        whole = (whole + self.swap_core(whole)) * 0.5
        first = self.permute(halves, lambda d, y: (d + 1, 1 - y) if d % 2 == 0 else (d - 1, y))
        second = self.swap_y(halves)
        halves = jnp.where(self.core == 0, halves, second) + first
        return whole, halves


def starts_of(segments):
    numbers = jnp.arange(8, dtype=jnp.int32)
    return jnp.sum(segments[None, :] < numbers[:, None], axis=1, dtype=jnp.int32)


def mask_of(query_seg, key_starts, first_row, causal):
    ends = jnp.stack([query_seg[0], query_seg[-1], first_row])
    return (causal, key_starts, ends, query_seg[None])


def projected(query_in, key_in, weights, bias):
    width = bias.shape[1] // 3
    queries = (dot_plain(query_in, weights[:, :width]) + bias[:, :width]).astype(BF16)
    kv = (dot_plain(key_in, weights[:, width:]) + bias[:, width:]).astype(BF16)
    return (queries * HEAD_DIM ** (-0.5)).astype(BF16), kv


def attention_output(place, queries, kv, output, lse, out_weight, out_bias):
    mixed = output.astype(BF16)
    branch = place.core_sum(dot_first(mixed, out_weight)) + out_bias.astype(F32)
    return (branch, (queries, kv, output, lse, mixed))


def attention_backward(
    number,
    grad_branch,
    saved,
    query_in,
    key_in,
    weights,
    out_weight,
    mask,
    apart,
    plan,
    wanted,
    inside=(),
    begins=False,
):
    mixed = saved[4]
    grad_mixed = dot_last(grad_branch, out_weight).astype(BF16)
    grad_mixed_t = dot_last(out_weight, grad_branch).astype(BF16)
    box = {}
    more = []
    if plan.kernels:
        made = products(box, query_in, key_in, grad_branch, mixed, 5, begins)
        more = [*made, *plan.chains(wanted), *inside]
    (grad_q, grad_kv, *sums), *rest = attend_back(
        number, saved, grad_mixed, grad_mixed_t, weights, mask, apart, more, box
    )
    if plan.kernels:
        (grad_bias, *grads), *rest = rest
        if begins:
            grads, rest = [first[0] for first in rest[:3]], rest[3:]
    else:
        grads = (
            dot_first(query_in, grad_q).astype(BF16),
            dot_first(grad_branch, mixed.T).astype(BF16),
            dot_first(key_in, grad_kv).astype(BF16),
        )
        grad_bias = jnp.stack([column_sum(grad_q), column_sum(grad_kv[:, grad_q.shape[1] :])])
    given = [results[0] for results in rest[: len(rest) - len(inside)]]
    rest = rest[len(rest) - len(inside) :]
    return (sums, grads, grad_bias.reshape(-1), plan.given(wanted, given), rest)


def feed_forward(place, x_in, w_in, b_in, w_out, b_out):
    hidden = dot_plain(x_in, w_in) + b_in.astype(F32)
    spread = 0.5 * (1.0 + lax.erf(hidden * 0.5**0.5))
    active = (hidden * spread).astype(BF16)
    slope = spread + hidden * jnp.exp(-0.5 * hidden * hidden) * (2.0 * math.pi) ** (-0.5)
    branch = place.core_sum(dot_plain(active, w_out)) + b_out.astype(F32)
    return (branch, (slope, active))


def feed_backward(place, grad_branch, saved, x_in, w_in, w_out):
    slope, active = saved
    grad_hidden = (slope * dot_last(grad_branch, w_out)).astype(BF16)
    grad_in = place.core_sum(dot_last(grad_hidden, w_in))
    return (
        grad_in,
        dot_first(x_in, grad_hidden).astype(BF16),
        column_sum(grad_hidden),
        dot_first(grad_branch, active).astype(BF16),
    )


def shards(
    source,
    target,
    source_segments,
    target_segments,
    enc_qkv,
    enc_qv_bias,
    enc_proj,
    enc_ff_in,
    enc_ff_in_bias,
    enc_ff_out,
    enc_bias,
    enc_gains,
    enc_shifts,
    dec_self,
    dec_self_bias,
    dec_self_proj,
    dec_cross,
    dec_cross_bias,
    dec_cross_proj,
    dec_ff_in,
    dec_ff_in_bias,
    dec_ff_out,
    dec_bias,
    dec_gains,
    dec_shifts,
    enc_cotangent,
    dec_cotangent,
):
    count = source.shape[1]
    model = source.shape[2]
    place = Places(lax.axis_size("dp"), lax.axis_size("seq"))
    first_row = place.z * count

    ring = place.ring
    width = enc_qkv.shape[2]
    hidden_units = enc_ff_in.shape[1]

    x_all, ts, source_keys, target_keys, vectors, enc_qkv, enc_proj, dec_self = opening(
        ring,
        source[0],
        target[0],
        source_segments,
        target_segments,
        (
            enc_qv_bias,
            dec_self_bias,
            dec_cross_bias,
            enc_ff_in_bias,
            dec_ff_in_bias,
        ),
        (enc_qkv, enc_proj, dec_self),
    )
    source_keys, target_keys = source_keys[0], target_keys[0]
    xs = lax.dynamic_slice_in_dim(x_all, first_row, count, 0)
    enc_cot = place.own_pair(enc_cotangent[0])
    dec_cot = place.own_pair(dec_cotangent[0])
    enc_b, self_b, cross_b = (vectors[k : k + 1, : 3 * width] for k in range(3))
    enc_ff_in_bias, dec_ff_in_bias = vectors[3], vectors[4]
    source_own = lax.dynamic_slice_in_dim(source_keys, first_row, count, 0)
    target_own = lax.dynamic_slice_in_dim(target_keys, first_row, count, 0)
    source_starts, target_starts = starts_of(source_keys), starts_of(target_keys)
    enc_mask = mask_of(source_own, source_starts, first_row, False)
    self_mask = mask_of(target_own, target_starts, first_row, True)
    cross_mask = mask_of(target_own, source_starts, first_row, False)

    queries, kv, output, lse, t_all, enc_ff_in, enc_ff_out = gather_attend(
        7, ring, x_all, enc_qkv, enc_b, enc_mask, ts, (enc_ff_in, enc_ff_out)
    )
    dec_ff_in = place.fetch_weight(dec_ff_in + after(lse).astype(BF16))
    branch, enc_attn = attention_output(place, queries, kv, output, lse, enc_proj, enc_bias[0])
    first, enc_norm_one = norm_forward(xs.astype(F32) + branch, enc_gains[0], enc_shifts[0])
    first_low = first.astype(BF16)
    branch, enc_feed = feed_forward(
        place, first_low, enc_ff_in, enc_ff_in_bias, enc_ff_out, enc_bias[1]
    )
    encoded, enc_norm_two = norm_forward(first + branch, enc_gains[1], enc_shifts[1])
    encoded_low = encoded.astype(BF16)

    (
        queries,
        kv,
        output,
        lse,
        e_all,
        dec_self_proj,
        dec_cross,
        dec_cross_proj,
    ) = gather_attend(
        2,
        ring,
        t_all,
        dec_self,
        self_b,
        self_mask,
        encoded_low,
        (dec_self_proj, dec_cross, dec_cross_proj),
    )
    dec_ff_out = place.fetch_weight(dec_ff_out + after(lse).astype(BF16))
    branch, self_attn = attention_output(
        place, queries, kv, output, lse, dec_self_proj, dec_bias[0]
    )
    second, dec_norm_one = norm_forward(ts.astype(F32) + branch, dec_gains[0], dec_shifts[0])
    second_low = second.astype(BF16)
    queries, kv = projected(second_low, e_all, dec_cross, cross_b)
    output, lse = attend(queries, kv, cross_mask, (dec_ff_in,))
    branch, cross_attn = attention_output(
        place, queries, kv, output, lse, dec_cross_proj, dec_bias[1]
    )
    third, dec_norm_two = norm_forward(second + branch, dec_gains[1], dec_shifts[1])
    third_low = third.astype(BF16)
    branch, dec_feed = feed_forward(
        place, third_low, dec_ff_in, dec_ff_in_bias, dec_ff_out, dec_bias[2]
    )
    decoded, dec_norm_three = norm_forward(third + branch, dec_gains[2], dec_shifts[2])

    def back_mask(mask):
        return (mask[0], mask[1], mask[3])

    grad_hidden, dec_gain_three, dec_shift_three = norm_backward(
        dec_cot.astype(F32), dec_norm_three, dec_gains[2]
    )
    grad_branch = grad_hidden.astype(BF16)
    feed_in, dec_w_in, dec_b_in, dec_w_out = feed_backward(
        place, grad_branch, dec_feed, third_low, dec_ff_in, dec_ff_out
    )
    dec_bias_three = column_sum(grad_branch)
    grad_third = grad_hidden + feed_in
    grad_hidden, dec_gain_two, dec_shift_two = norm_backward(grad_third, dec_norm_two, dec_gains[1])
    grad_branch = grad_hidden.astype(BF16)
    plan = place.plan()
    (key_total, query_total), cross_grads, cross_bias, (dec_w_in, dec_w_out), _ = attention_backward(
        3,
        grad_branch,
        cross_attn,
        second_low,
        e_all,
        dec_cross,
        dec_cross_proj,
        back_mask(cross_mask),
        True,
        plan,
        [(dec_w_in, "x", (0, 6)), (dec_w_out, "y", (0, 6))],
    )
    dec_bias_two = column_sum(grad_branch)
    grad_second = grad_hidden + query_total
    grad_hidden, dec_gain_one, dec_shift_one = norm_backward(
        grad_second, dec_norm_one, dec_gains[0]
    )
    grad_branch = grad_hidden.astype(BF16)
    cross_q, cross_proj, cross_kv = cross_grads
    target_hidden, target_branch = grad_hidden, grad_branch
    grad_hidden, enc_gain_two, enc_shift_two = norm_backward(
        enc_cot.astype(F32) + key_total.astype(F32), enc_norm_two, enc_gains[1]
    )
    grad_branch = grad_hidden.astype(BF16)
    enc_bias_two = column_sum(grad_branch)
    slope, active = enc_feed
    (target_total,), self_grads, self_bias, given, inside = attention_backward(
        4,
        target_branch,
        self_attn,
        ts,
        t_all,
        dec_self,
        dec_self_proj,
        back_mask(self_mask),
        False,
        plan,
            [
                (dec_w_in, "yvw", (0, 3, 5, 6)),
                (dec_w_out, "xvw", (0, 3, 5, 6)),
                (cross_kv, "x", (3, 6)),
                (cross_q, "y", (3, 6)),
                (cross_proj, "y", (3, 6)),
            ],
        [feed_back(grad_branch, slope, enc_ff_in, enc_ff_out, first_low, active, 5)]
        if plan.kernels
        else (),
        begins=True,
    )
    dec_w_in, dec_w_out, cross_kv, cross_q, cross_proj = given
    if plan.kernels:
        feed_in, enc_b_in, enc_w_in, enc_w_out = inside[0]
        enc_b_in = enc_b_in.reshape(-1)
    else:
        feed_in, enc_w_in, enc_b_in, enc_w_out = feed_backward(
            place, grad_branch, enc_feed, first_low, enc_ff_in, enc_ff_out
        )
    dec_bias_one = column_sum(target_branch)
    grad_target = target_hidden + target_total.astype(F32)
    grad_first = grad_hidden + feed_in
    grad_hidden, enc_gain_one, enc_shift_one = norm_backward(grad_first, enc_norm_one, enc_gains[0])
    grad_branch = grad_hidden.astype(BF16)
    self_q, self_proj, self_kv = self_grads
    (source_total,), enc_grads, enc_bias_grad, given, _ = attention_backward(
        5,
        grad_branch,
        enc_attn,
        xs,
        x_all,
        enc_qkv,
        enc_proj,
        back_mask(enc_mask),
        False,
        plan,
            [
                (cross_kv, "yvw", (0, 1, 3, 6)),
                (cross_q, "xvw", (0, 1, 3, 6)),
                (cross_proj, "xvw", (0, 1, 3, 6)),
                (enc_w_in, "x", (1, 6)),
                (enc_w_out, "y", (1, 6)),
                (self_kv, "y", (4, 6)),
                (self_q, "x", (4, 6)),
                (self_proj, "x", (4, 6)),
            ],
    )
    cross_kv, cross_q, cross_proj, enc_w_in, enc_w_out, self_kv, self_q, self_proj = given
    enc_bias_one = column_sum(grad_branch)
    grad_source = grad_hidden + source_total.astype(F32)
    enc_q, enc_proj_grad, enc_kv = enc_grads
    rest = [
        (self_kv, "vw", (0, 1, 2)),
        (self_q, "vw", (0, 1, 2)),
        (self_proj, "vw", (0, 1, 2)),
        (enc_w_in, "yvw", (0, 2, 4, 7)),
        (enc_w_out, "xvw", (0, 2, 4, 7)),
        (enc_kv, "xyvw", (2, 3, 5, 6, 7)),
        (enc_q, "yxvw", (2, 3, 5, 6, 7)),
        (enc_proj_grad, "yxvw", (2, 3, 5, 6, 7)),
    ]
    source_low = rounded(grad_source).astype(BF16)
    target_low = rounded(grad_target).astype(BF16)
    decoded_low = decoded.astype(BF16)
    small = small_sums(
        jnp.concatenate(
            [
                enc_bias_one,
                enc_bias_two,
                enc_gain_one,
                enc_gain_two,
                enc_shift_one,
                enc_shift_two,
                dec_bias_one,
                dec_bias_two,
                dec_bias_three,
                dec_gain_one,
                dec_gain_two,
                dec_gain_three,
                dec_shift_one,
                dec_shift_two,
                dec_shift_three,
            ]
        ).reshape(15, model),
        jnp.concatenate([enc_bias_grad, self_bias, cross_bias, enc_b_in, dec_b_in]).reshape(-1, model),
        (0, 1, 2, 3, 4, 5),
    )
    if plan.kernels:
        (vectors,), (source_other, target_other), *given = run_chains(
            6, [small, hand_out((source_low, target_low), (4, 7))] + plan.chains(rest), 8
        )
        given = [results[0] for results in given]
    else:
        vectors = jnp.concatenate(place.all_sum(*small.vectors)).reshape(-1, model)
        source_other, target_other = place.others(source_low), place.others(target_low)
        given = [place.scatter(array, True) for array, _, _ in rest]
        dec_w_in, dec_w_out, cross_kv, cross_q, cross_proj = (
            place.scatter(array, True)
            for array in (dec_w_in, dec_w_out, cross_kv, cross_q, cross_proj)
        )
    self_kv, self_q, self_proj, enc_w_in, enc_w_out, enc_kv, enc_q, enc_proj_grad = given

    grads = (enc_q, enc_proj_grad, enc_kv, self_q, self_proj, self_kv, cross_q, cross_proj, cross_kv)
    grads += (enc_w_in, enc_w_out, dec_w_in, dec_w_out)
    flag = jnp.where(place.core == place.y, 1, 0).astype(jnp.int32).reshape(1)
    rows = (
        encoded_low,
        place.others(encoded_low),
        decoded_low,
        place.others(decoded_low),
        source_low,
        source_other,
        target_low,
        target_other,
    )
    results = closing(flag, rows, vectors, grads, (2, 2, 2, 3, 3, 3))
    of_rows, of_qkv, of_in = [value[None] for value in results[:4]], results[4:7], results[7:9]
    of_out, of_ff_out = [value.T for value in results[9:12]], [value.T for value in results[12:14]]
    of_whole, of_qv_bias, of_in_bias = results[14:20], results[20:23], results[23:]
    return (
        *of_rows,
        of_qkv[0],
        of_qv_bias[0],
        of_out[0],
        of_in[0],
        of_in_bias[0],
        of_ff_out[0],
        *of_whole[:3],
        of_qkv[1],
        of_qv_bias[1],
        of_out[1],
        of_qkv[2],
        of_qv_bias[2],
        of_out[2],
        of_in[1],
        of_in_bias[1],
        of_ff_out[1],
        *of_whole[3:],
    )


def solution(mesh):
    return jax.shard_map(
        shards,
        mesh=mesh,
        in_specs=(
            P("dp", "seq", None),
            P("dp", "seq", None),
            P("dp", None),
            P("dp", None),
            P(None, None, "tensor"),
            P(None, "tensor"),
            P("tensor", None),
            P(None, "tensor"),
            P("tensor"),
            P("tensor", None),
            P(),
            P(),
            P(),
            P(None, None, "tensor"),
            P(None, "tensor"),
            P("tensor", None),
            P(None, None, "tensor"),
            P(None, "tensor"),
            P("tensor", None),
            P(None, "tensor"),
            P("tensor"),
            P("tensor", None),
            P(),
            P(),
            P(),
            P("dp", "seq", None),
            P("dp", "seq", None),
        ),
        out_specs=(
            P("dp", "seq", None),
            P("dp", "seq", None),
            P("dp", "seq", None),
            P("dp", "seq", None),
            P(None, ("dp", "seq"), "tensor"),
            P(None, "tensor"),
            P("tensor", ("dp", "seq")),
            P(("dp", "seq"), "tensor"),
            P("tensor"),
            P("tensor", ("dp", "seq")),
            P(),
            P(),
            P(),
            P(None, ("dp", "seq"), "tensor"),
            P(None, "tensor"),
            P("tensor", ("dp", "seq")),
            P(None, ("dp", "seq"), "tensor"),
            P(None, "tensor"),
            P("tensor", ("dp", "seq")),
            P(("dp", "seq"), "tensor"),
            P("tensor"),
            P("tensor", ("dp", "seq")),
            P(),
            P(),
            P(),
        ),
        check_vma=False,
    )
```
